32 devices in a mesh: win: 16 (over z, y, core), rep: 2 (over x).
Axes of the slice: x: 2, y: 2, z: 4, core: 2. Of those that a mesh axis runs over, the one named last changes fastest.
Arguments:
- tokens: bfloat16 [2, 320, 50, 512], P('rep', 'win'), may hold values from -6 to 6
- patch_mask: int32 [2, 320, 49], P('rep', 'win'), may hold values 0 or 1
- keep_mask: int32 [2, 320, 3], P('rep', 'win'), may hold values 0 or 1
- image_map: int32 [2, 320], P('rep'), may hold values from 0 to 7
- qkv_weight: bfloat16 [3, 512, 512], replicated, may hold values from -0.25 to 0.25
- out_weight: bfloat16 [512, 512], replicated, may hold values from -0.75 to 0.75
- up_weight: bfloat16 [512, 2048], replicated, may hold values from -0.25 to 0.25
- down_weight: bfloat16 [2048, 512], replicated, may hold values from -0.125 to 0.125
- vectors: float32 [14, 512], replicated
- qkv_mom: float32 [3, 512, 512], P(None, 'win'), may hold values from -512 to 512
- out_mom: float32 [512, 512], P('win'), may hold values from -512 to 512
- up_mom: float32 [512, 2048], P('win'), may hold values from -512 to 512
- down_mom: float32 [2048, 512], P('win'), may hold values from -512 to 512
- vec_mom: float32 [7168], P('win'), may hold values from -512 to 512
- cotangent: bfloat16 [2, 320, 50, 512], P('rep', 'win'), may hold values from -6 to 6
Outputs:
- out_tokens: bfloat16 [2, 320, 50, 512], P('rep', 'win')
- grad_tokens: float32 [2, 320, 50, 512], P('rep', 'win')
- new_qkv_mom: float32 [3, 512, 512], P(None, 'win')
- new_qkv: float32 [3, 512, 512], P(None, 'win')
- new_out_mom: float32 [512, 512], P('win')
- new_out: float32 [512, 512], P('win')
- new_up_mom: float32 [512, 2048], P('win')
- new_up: float32 [512, 2048], P('win')
- new_down_mom: float32 [2048, 512], P('win')
- new_down: float32 [2048, 512], P('win')
- new_vec_mom: float32 [7168], P('win')
- new_vectors: float32 [7168], P('win')
The draws below stay inside these ranges and needn't reach their ends.
Inputs may be any that keep to these rules, and one draw needn't show every extreme that they name: `image_map`: each window's image is independent of its position, so the windows of one image lie scattered over all devices of its group.
All inputs are finite; a program needn't handle non-finite values. No bound on the sum of `patch_mask` or of `keep_mask` on one device may be relied on, other than what follows from the above.
Results may differ from the reference program's by a relative error of at most 0.011.
Values may be sent and summed in bfloat16 or wider, within the bound.
No kernel may reach another device: no remote copies, remote signals or barrier semaphores. Data moves between devices by JAX's collectives and lax.ppermute only.
A program may use at most 192 MiB of HBM per device.

```python
import jax
import jax.numpy as jnp
from jax import lax

C = 512
HEADS = 16
HEAD_DIM = 32
FF = 2048
PATCH = 49
IMGS = 8
SEQ = 50
RGN = 320
VROWS = 14
N_REP = 2


def draw_vectors(key, part):
    key = jax.random.fold_in(key, 11)
    noise = 0.3 * jax.random.normal(key, (VROWS, C), jnp.float32)
    row_ids = jnp.arange(VROWS)
    gain_rows = ((row_ids == 0) | (row_ids == 2) | (row_ids == 4)).astype(jnp.float32)[:, None]
    return noise + gain_rows


def with_ends(drawn, rng, low, high):
    longest = drawn.shape.index(max(drawn.shape))
    spots = []
    for shift in (0, 1):
        where = [jax.random.randint(jax.random.fold_in(rng, axis), (), 0, length) for axis, length in enumerate(drawn.shape)]
        where[longest] = (where[longest] + shift) % drawn.shape[longest]
        spots.append(tuple(where))
    return drawn.at[spots[0]].set(low).at[spots[1]].set(high)


def level_of(rng, shape, shards, least, largest):
    def one(position, parts):
        heights = jax.random.uniform(jax.random.fold_in(jax.random.fold_in(rng, 6), position), (parts,), jnp.float32, least / len(shards), largest / len(shards))
        return jnp.repeat(jnp.exp(heights), shape[position] // parts).reshape((-1,) + (1,) * (len(shape) - position - 1))

    factor_of = one(*shards[0])
    for cut in shards[1:]:
        factor_of = factor_of * one(*cut)
    return factor_of


def centred(stream_key, dims, scale, most, cuts=(), dtype=jnp.bfloat16):
    values = scale * jax.random.normal(stream_key, dims, jnp.float32)
    if cuts:
        values = values * level_of(stream_key, dims, cuts, -0.22, 0.18)
    return jnp.clip(values, -most, most).astype(dtype)


def setup_inputs(seed: int = 0) -> dict:
    arg_keys = jax.random.split(jax.random.key(seed), 16)
    return {
        "tokens": centred(arg_keys[0], (N_REP, RGN, SEQ, C), 1.0, 6.0, ((0, 2), (1, 16))),
        "patch_mask": with_ends((jax.random.randint(arg_keys[1], (N_REP, RGN, PATCH), 0, 4) < 3).astype(jnp.int32), jax.random.fold_in(arg_keys[1], 1), 0, 1),
        "keep_mask": with_ends((jax.random.randint(arg_keys[2], (N_REP, RGN, 3), 0, 4) < 3).astype(jnp.int32), jax.random.fold_in(arg_keys[2], 1), 0, 1),
        "image_map": with_ends(jax.random.randint(arg_keys[3], (N_REP, RGN), 0, IMGS), jax.random.fold_in(arg_keys[3], 1), 0, IMGS - 1).astype(jnp.int32),
        "qkv_weight": centred(arg_keys[4], (3, C, C), C ** -0.5, 0.25),
        "out_weight": centred(arg_keys[5], (C, C), (C // 8) ** -0.5, 0.75),
        "up_weight": centred(arg_keys[6], (C, FF), C ** -0.5, 0.25),
        "down_weight": centred(arg_keys[7], (FF, C), FF ** -0.5, 0.125),
        "vectors": draw_vectors(jax.random.fold_in(arg_keys[15], 71), 0),
        "qkv_mom": centred(arg_keys[9], (3, C, C), (0.5 * (N_REP * RGN * SEQ) ** 0.5), 512.0, ((1, 16),), jnp.float32),
        "out_mom": centred(arg_keys[10], (C, C), (0.5 * (N_REP * RGN * SEQ) ** 0.5), 512.0, ((0, 16),), jnp.float32),
        "up_mom": centred(arg_keys[11], (C, FF), (0.5 * (N_REP * RGN * SEQ) ** 0.5), 512.0, ((0, 16),), jnp.float32),
        "down_mom": centred(arg_keys[12], (FF, C), (0.5 * (N_REP * RGN * SEQ) ** 0.5), 512.0, ((0, 16),), jnp.float32),
        "vec_mom": centred(arg_keys[13], (VROWS * C,), (0.5 * (N_REP * RGN * SEQ) ** 0.5), 512.0, ((0, 16),), jnp.float32),
        "cotangent": centred(arg_keys[14], (N_REP, RGN, SEQ, C), 1.0, 6.0, ((0, 2), (1, 16))),
    }


EPSILON = 1e-06
MOMENTUM_DECAY = 0.95
MATRIX_RATE = 0.5
VECTOR_RATE = 0.0002
KEEP_SHARE = 0.75
NEWTON_COEFFS = (3.4445, -4.775, 2.0315)
HIGHEST = lax.Precision.HIGHEST

@jax.custom_vjp
def low(v):
    return lax.optimization_barrier(v.astype(jnp.bfloat16)).astype(jnp.float32)

@jax.custom_vjp
def low_back(v):
    return v

def low_keep(v):
    return (low(v), None)

def low_pass(kept, grad):
    return (grad,)

def back_keep(v):
    return (v, None)

def back_low(kept, grad):
    return (low(grad),)
low.defvjp(low_keep, low_pass)
low_back.defvjp(back_keep, back_low)

def round_both(values):
    return low(low_back(values))

def norm_rows(values, gain_row, shift_row):
    center = values - lax.optimization_barrier(jnp.mean(values, -1, keepdims=True))
    spread = lax.optimization_barrier(jnp.mean(center * center, -1, keepdims=True))
    return center * lax.rsqrt(spread + EPSILON) * gain_row + shift_row

def matmul(left_side, right_side):
    return jnp.matmul(left_side, right_side, precision=HIGHEST)

def attend(queries, keyset, values, allowed):
    logits = jnp.einsum('...qhd,...khd->...hqk', queries, keyset, precision=HIGHEST) * HEAD_DIM ** (-0.5)
    logits = low_back(logits)
    logits = jnp.where(allowed, logits, -1e+30)
    row_top = lax.optimization_barrier(jnp.max(logits, -1, keepdims=True))
    raised = jnp.exp(logits - row_top)
    attn_probs = low(raised / lax.optimization_barrier(jnp.sum(raised, -1, keepdims=True)))
    return jnp.einsum('...hqk,...khd->...qhd', attn_probs, values, precision=HIGHEST)

def project_heads(normed, weights, shape):
    wqkv, wout, wup, wdown, vectors = weights
    queries = round_both(matmul(normed, wqkv[0]) + vectors[6]).reshape(shape)
    keyset = round_both(matmul(normed, wqkv[1])).reshape(shape)
    values = round_both(matmul(normed, wqkv[2]) + vectors[7]).reshape(shape)
    return (queries, keyset, values)

def group_forward(inputs, patch_mask, keep_mask, images, weights):
    wqkv, wout, wup, wdown, vectors = weights
    windows = inputs.shape[0]
    seq_len = inputs.shape[1]
    model_width = inputs.shape[2]
    keeper = keep_mask.astype(jnp.float32) / KEEP_SHARE
    region = inputs[:, 0]
    region_norm = low(norm_rows(region, vectors[0], vectors[1]))
    queries, keyset, values = project_heads(region_norm, weights, (windows, HEADS, HEAD_DIM))
    allowed = (images[:, None] == images[None, :])[None]
    region_mix = round_both(attend(queries, keyset, values, allowed).reshape(windows, model_width))
    region_branch = low_back(matmul(region_mix, wout) + vectors[8])
    region_new = region + keeper[:, 0:1] * region_branch
    sequence = jnp.concatenate([region_new[:, None], inputs[:, 1:]], axis=1)
    seq_norm = low(norm_rows(sequence, vectors[2], vectors[3]))
    queries, keyset, values = project_heads(seq_norm, weights, (windows, seq_len, HEADS, HEAD_DIM))
    key_valid = jnp.concatenate([jnp.ones((windows, 1), jnp.int32), patch_mask], axis=1) == 1
    local_mix = round_both(attend(queries, keyset, values, key_valid[:, None, None, :]).reshape(windows, seq_len, model_width))
    local_branch = low_back(matmul(local_mix, wout) + vectors[8])
    after_attn = sequence + keeper[:, 1][:, None, None] * local_branch
    mlp_norm = low(norm_rows(after_attn, vectors[4], vectors[5]))
    up_value = low_back(matmul(mlp_norm, wup) + vectors[10:].reshape(-1))
    activated = low(jax.nn.gelu(up_value))
    mlp_branch = low_back(matmul(activated, wdown) + vectors[9])
    return after_attn + keeper[:, 2][:, None, None] * mlp_branch

def newton(matrix):
    is_tall = matrix.shape[0] > matrix.shape[1]
    iterate = matrix.T if is_tall else matrix
    iterate = iterate / (jnp.sqrt(jnp.sum(iterate * iterate)) + EPSILON)
    for sweep_count in range(5):
        gram_matrix = jnp.matmul(iterate, iterate.T, precision=HIGHEST)
        polynomial = NEWTON_COEFFS[1] * gram_matrix + NEWTON_COEFFS[2] * jnp.matmul(gram_matrix, gram_matrix, precision=HIGHEST)
        iterate = NEWTON_COEFFS[0] * iterate + jnp.matmul(polynomial, iterate, precision=HIGHEST)
    result = iterate.T if is_tall else iterate
    return result * max(1.0, matrix.shape[0] / matrix.shape[1]) ** 0.5

def reference(tokens, patch_mask, keep_mask, image_map, qkv_weight, out_weight, up_weight, down_weight, vectors, qkv_mom, out_mom, up_mom, down_mom, vec_mom, cotangent):
    params = (qkv_weight.astype(jnp.float32), out_weight.astype(jnp.float32), up_weight.astype(jnp.float32), down_weight.astype(jnp.float32), vectors)

    def forward(inputs, weights):

        def one_group(group_items):
            return group_forward(group_items[0], group_items[1], group_items[2], group_items[3], weights)
        return lax.map(jax.checkpoint(one_group), (inputs, patch_mask, keep_mask, image_map))
    output, pullback = jax.vjp(forward, tokens.astype(jnp.float32), params)
    input_grad, param_grads = pullback(cotangent.astype(jnp.float32))
    grad_qkv, grad_out, grad_up, grad_down, grad_vec = param_grads
    new_qkv_mom = MOMENTUM_DECAY * qkv_mom + grad_qkv
    new_qkv = params[0] - MATRIX_RATE * jnp.stack([newton(new_qkv_mom[number]) for number in range(3)])
    new_out_mom = MOMENTUM_DECAY * out_mom + grad_out
    new_out = params[1] - MATRIX_RATE * newton(new_out_mom)
    new_up_mom = MOMENTUM_DECAY * up_mom + grad_up
    new_up = params[2] - MATRIX_RATE * newton(new_up_mom)
    new_down_mom = MOMENTUM_DECAY * down_mom + grad_down
    new_down = params[3] - MATRIX_RATE * newton(new_down_mom)
    new_vec_mom = MOMENTUM_DECAY * vec_mom + grad_vec.reshape(-1)
    new_vectors = vectors.reshape(-1) - VECTOR_RATE * new_vec_mom
    return (output.astype(jnp.bfloat16), input_grad, new_qkv_mom, new_qkv, new_out_mom, new_out, new_up_mom, new_up, new_down_mom, new_down, new_vec_mom, new_vectors)
```

```python
import jax
import jax.numpy as jnp
from jax import lax
from jax.sharding import PartitionSpec as P

HEADS = 16
HEAD_DIM = 32


EPSILON = 1e-06
MOMENTUM_DECAY = 0.95
MATRIX_RATE = 0.5
VECTOR_RATE = 0.0002
KEEP_SHARE = 0.75
NEWTON_COEFFS = (3.4445, -4.775, 2.0315)
NEWTON_PRECISION = lax.Precision.HIGH


def bfloat(values):
    return values.astype(jnp.bfloat16)


def product(left_side, right_side):
    return jnp.dot(left_side, right_side, preferred_element_type=jnp.float32)


def norm_rows(values, gain_row, shift_row):
    center = values - jnp.mean(values, -1, keepdims=True)
    spread = jnp.mean(center * center, -1, keepdims=True)
    return center * lax.rsqrt(spread + EPSILON) * gain_row + shift_row


def soft_scores(queries, keyset, allowed):
    logits = jnp.einsum(
        "bqhd,bkhd->bhqk", queries, keyset, preferred_element_type=jnp.float32
    ) * HEAD_DIM ** (-0.5)
    logits = jnp.where(allowed, logits, -1e30)
    row_top = jnp.max(logits, -1, keepdims=True)
    raised = jnp.exp(logits - row_top)
    total = jnp.sum(raised, -1, keepdims=True)
    return raised / total, row_top + jnp.log(total)


def mix_values(probs_low, values):
    return jnp.einsum("bhqk,bkhd->bqhd", probs_low, values, preferred_element_type=jnp.float32)


def attend_back(attn_probs, probs_low, queries, keyset, values, mix_grad):
    value_grad = jnp.einsum(
        "bhqk,bqhd->bkhd", probs_low, mix_grad, preferred_element_type=jnp.float32
    )
    prob_grad = jnp.einsum("bqhd,bkhd->bhqk", mix_grad, values, preferred_element_type=jnp.float32)
    score_low = bfloat(
        attn_probs * (prob_grad - jnp.sum(attn_probs * prob_grad, -1, keepdims=True))
    )
    factor = HEAD_DIM ** (-0.5)
    query_grad = (
        jnp.einsum("bhqk,bkhd->bqhd", score_low, keyset, preferred_element_type=jnp.float32)
        * factor
    )
    key_grad = (
        jnp.einsum("bhqk,bqhd->bkhd", score_low, queries, preferred_element_type=jnp.float32)
        * factor
    )
    return (query_grad, key_grad, value_grad)


def bit_count(axis):
    return lax.axis_size(axis).bit_length() - 1


def swap(values, axis, bit):
    size = lax.axis_size(axis)
    return lax.ppermute(values, axis, [(i, i ^ (1 << bit)) for i in range(size)])


def my_bit(axis, bit):
    return (lax.axis_index(axis) >> bit) & 1


def gather_blocks(values, axis):
    done = []
    for bit in list(range(2, bit_count(axis))) + [1, 0]:
        other = swap(values, axis, bit)
        first = my_bit(axis, bit) == 0
        place = sum(1 for earlier in done if earlier > bit)
        values = jnp.stack(
            [jnp.where(first, values, other), jnp.where(first, other, values)], axis=place
        )
        done.append(bit)
    return values.reshape((lax.axis_size(axis),) + values.shape[len(done) :])


def scatter_sum(values, order):
    win_bits = bit_count("win")
    values = values.reshape((2,) * win_bits + values.shape[1:])
    left = list(range(win_bits))[::-1]
    rep_done = []
    for axis, bit in order:
        mine = my_bit(axis, bit)
        if axis == "win":
            place = left.index(bit)
            left.remove(bit)
            kept = lax.dynamic_index_in_dim(values, mine, place, keepdims=False)
            sent = lax.dynamic_index_in_dim(values, 1 - mine, place, keepdims=False)
        else:
            half = values.shape[-1] // 2
            last = values.ndim - 1
            kept = lax.dynamic_slice_in_dim(values, mine * half, half, last)
            sent = lax.dynamic_slice_in_dim(values, (1 - mine) * half, half, last)
            rep_done.append(bit)
        values = kept + swap(bfloat(sent), axis, bit).astype(jnp.float32)
    values = bfloat(values)
    for bit in reversed(rep_done):
        other = swap(values, "rep", bit)
        first = my_bit("rep", bit) == 0
        values = jnp.concatenate(
            [jnp.where(first, values, other), jnp.where(first, other, values)], axis=-1
        )
    return values.astype(jnp.float32)


def sum_everywhere(values):
    for axis in ("win", "rep"):
        for bit in range(bit_count(axis)):
            values = values + swap(values, axis, bit)
    return values


def hop_orders():
    win_far = [("win", bit) for bit in range(2, bit_count("win"))]
    rep = [("rep", bit) for bit in range(bit_count("rep"))]
    core, side = [("win", 0)], [("win", 1)]
    return core + rep + side + win_far, core + side + rep + win_far


def times(left_side, right_side, dims):
    return lax.dot_general(
        left_side,
        right_side,
        (dims, ((), ())),
        precision=NEWTON_PRECISION,
        preferred_element_type=jnp.float32,
    )


def newton_wide(matrix):
    iterate = matrix / (jnp.sqrt(jnp.sum(matrix * matrix)) + EPSILON)
    for _ in range(5):
        gram = times(iterate, iterate, ((1,), (1,)))
        poly = NEWTON_COEFFS[1] * gram + NEWTON_COEFFS[2] * times(gram, gram, ((1,), (0,)))
        iterate = NEWTON_COEFFS[0] * iterate + times(poly, iterate, ((1,), (0,)))
    return iterate


def newton_tall(matrix):
    iterate = matrix / (jnp.sqrt(jnp.sum(matrix * matrix)) + EPSILON)
    for _ in range(5):
        gram = times(iterate, iterate, ((0,), (0,)))
        poly = NEWTON_COEFFS[1] * gram + NEWTON_COEFFS[2] * times(gram, gram, ((1,), (0,)))
        iterate = NEWTON_COEFFS[0] * iterate + times(iterate, poly, ((1,), (0,)))
    return iterate * max(1.0, matrix.shape[0] / matrix.shape[1]) ** 0.5


def own_rows(matrix, rows_here):
    return lax.dynamic_slice_in_dim(matrix, lax.axis_index("win") * rows_here, rows_here, 0)


def updates_two_owners(qkv_mom, out_mom, up_mom, down_mom):
    first = lax.axis_index("rep") == 0
    up_rows, up_cols = up_mom.shape
    width = qkv_mom.shape[2]
    folds = up_cols // width
    big = jnp.where(
        first,
        bfloat(up_mom).reshape(up_rows, folds, width).swapaxes(0, 1).reshape(-1, width),
        bfloat(down_mom),
    )
    small = bfloat(
        jnp.where(
            first, jnp.stack([qkv_mom[0], qkv_mom[2]]), jnp.stack([qkv_mom[1], out_mom])
        )
    )
    big = gather_blocks(big, "win")
    small = gather_blocks(small, "win")

    def wide_branch():
        matrix = big.reshape(-1, folds, up_rows, width).swapaxes(1, 2).reshape(-1, up_cols)
        rows = own_rows(newton_wide(matrix.astype(jnp.float32)), up_rows)
        return bfloat(rows).reshape(up_rows, folds, width).swapaxes(0, 1).reshape(-1, width)

    def tall_branch():
        matrix = big.reshape(-1, width)
        return bfloat(own_rows(newton_tall(matrix.astype(jnp.float32)), big.shape[1]))

    big_mine = lax.cond(first, wide_branch, tall_branch)
    big_other = swap(big_mine, "rep", 0)
    small = small.swapaxes(0, 1).reshape(2, -1, width).astype(jnp.float32)
    small_mine = bfloat(
        jnp.stack([own_rows(newton_wide(small[number]), up_rows) for number in range(2)])
    )
    small_other = swap(small_mine, "rep", 0)
    up = jnp.where(first, big_mine, big_other)
    up = up.reshape(folds, up_rows, width).swapaxes(0, 1).reshape(up_rows, up_cols)
    down = jnp.where(first, big_other, big_mine)
    even = jnp.where(first, small_mine, small_other)
    odd = jnp.where(first, small_other, small_mine)
    return even[0], odd[0], even[1], odd[1], up, down


def updates_any_owners(qkv_mom, out_mom, up_mom, down_mom):
    rep_count = lax.axis_size("rep")
    shards = [up_mom, down_mom, qkv_mom[0], qkv_mom[1], qkv_mom[2], out_mom]
    updates = []
    for number, shard in enumerate(shards):
        whole = gather_blocks(bfloat(shard), "win").reshape(-1, shard.shape[1])
        solve = newton_tall if whole.shape[0] > whole.shape[1] else newton_wide
        mine = lax.axis_index("rep") == number % rep_count
        rows = lax.cond(
            mine,
            lambda m=whole, s=solve, r=shard.shape[0]: own_rows(s(m.astype(jnp.float32)), r),
            lambda shape=shard.shape: jnp.zeros(shape, jnp.float32),
        )
        updates.append(lax.psum(bfloat(rows), "rep"))
    up, down, query, key, value, out = updates
    return query, key, value, out, up, down


def local(
    tokens,
    patch_mask,
    keep_mask,
    image_map,
    qkv_weight,
    out_weight,
    up_weight,
    down_weight,
    vectors,
    qkv_mom,
    out_mom,
    up_mom,
    down_mom,
    vec_mom,
    cotangent,
):
    windows = tokens.shape[1]
    seq_len = tokens.shape[2]
    model_width = tokens.shape[3]
    hidden_width = up_weight.shape[1]
    row_count = windows * seq_len
    win_count = lax.axis_size("win")
    win_index = lax.axis_index("win")
    factor = HEAD_DIM ** (-0.5)
    order_a, order_b = hop_orders()
    region_all = gather_blocks(tokens[0, :, 0], "win").reshape(-1, model_width)
    region_all = region_all.astype(jnp.float32)
    group_rows = region_all.shape[0]
    inputs = tokens[0].astype(jnp.float32)
    keeper = keep_mask[0].astype(jnp.float32) / KEEP_SHARE
    all_images = image_map[0]
    own_images = lax.dynamic_slice_in_dim(all_images, win_index * windows, windows)
    qkv_flat = jnp.concatenate([qkv_weight[0], qkv_weight[1], qkv_weight[2]], axis=1)
    qkv_bias = jnp.concatenate([vectors[6], jnp.zeros((model_width,), jnp.float32), vectors[7]])
    bias_up = vectors[10:].reshape(hidden_width)
    region = inputs[:, 0]

    all_norm1 = bfloat(norm_rows(region_all, vectors[0], vectors[1]))
    all_proj = bfloat(product(all_norm1, qkv_flat) + qkv_bias)
    own_proj = lax.dynamic_slice_in_dim(all_proj, win_index * windows, windows)
    region_norm = lax.dynamic_slice_in_dim(all_norm1, win_index * windows, windows)
    head_shape = (1, -1, HEADS, HEAD_DIM)

    def split_heads(proj):
        return [
            proj[:, number * model_width : (number + 1) * model_width].reshape(head_shape)
            for number in range(3)
        ]

    query_all4, key_all4, value_all4 = split_heads(all_proj)
    query_own4, key_own4, value_own4 = split_heads(own_proj)
    region_allowed = (own_images[:, None] == all_images[None, :])[None, None]
    region_probs, region_lse = soft_scores(query_own4, key_all4, region_allowed)
    region_plow = bfloat(region_probs)
    region_mix = bfloat(mix_values(region_plow, value_all4).reshape(windows, model_width))
    region_branch = product(region_mix, out_weight) + vectors[8]
    region_new = region + keeper[:, 0:1] * region_branch

    sequence = jnp.concatenate([region_new[:, None], inputs[:, 1:]], axis=1)
    flat_seq = sequence.reshape(row_count, model_width)
    seq_norm = bfloat(norm_rows(flat_seq, vectors[2], vectors[3]))
    seq_proj = product(seq_norm, qkv_flat) + qkv_bias
    window_shape = (windows, seq_len, HEADS, HEAD_DIM)
    local_query = bfloat(seq_proj[:, :model_width]).reshape(window_shape)
    local_key = bfloat(seq_proj[:, model_width : 2 * model_width]).reshape(window_shape)
    local_value = bfloat(seq_proj[:, 2 * model_width :]).reshape(window_shape)
    key_valid = jnp.concatenate([jnp.ones((windows, 1), jnp.int32), patch_mask[0]], axis=1) == 1
    local_probs, _ = soft_scores(local_query, local_key, key_valid[:, None, None, :])
    local_plow = bfloat(local_probs)
    local_mix = bfloat(mix_values(local_plow, local_value).reshape(row_count, model_width))
    local_branch = product(local_mix, out_weight) + vectors[8]
    keep_attn = jnp.broadcast_to(keeper[:, 1:2], (windows, seq_len)).reshape(row_count, 1)
    keep_mlp = jnp.broadcast_to(keeper[:, 2:3], (windows, seq_len)).reshape(row_count, 1)
    after_attn = flat_seq + keep_attn * local_branch

    mlp_norm = bfloat(norm_rows(after_attn, vectors[4], vectors[5]))
    up_value = product(mlp_norm, up_weight) + bias_up
    activated, gelu_back = jax.vjp(jax.nn.gelu, up_value)
    act_low = bfloat(activated)
    mlp_branch = product(act_low, down_weight) + vectors[9]
    output = after_attn + keep_mlp * mlp_branch
    grad_out = cotangent[0].astype(jnp.float32).reshape(row_count, model_width)
    mlp_grad = bfloat(keep_mlp * grad_out)
    grad_down = product(act_low.T, mlp_grad)
    grad_bm = jnp.sum(mlp_grad.astype(jnp.float32), 0)
    up_grad = bfloat(gelu_back(product(mlp_grad, down_weight.T))[0])
    grad_up = product(mlp_norm.T, up_grad)
    grad_bu = jnp.sum(up_grad.astype(jnp.float32), 0)
    up_total = scatter_sum(grad_up.reshape(win_count, -1, hidden_width), order_a)
    down_total = scatter_sum(grad_down.reshape(win_count, -1, model_width), order_b)
    norm3_back = jax.vjp(norm_rows, after_attn, vectors[4], vectors[5])[1](
        product(up_grad, up_weight.T)
    )
    attn_res_grad = grad_out + norm3_back[0]

    local_branch_grad = bfloat(keep_attn * attn_res_grad)
    grad_outw = product(local_mix.T, local_branch_grad)
    local_mix_grad = bfloat(product(local_branch_grad, out_weight.T)).reshape(window_shape)
    local_qg, local_kg, local_vg = attend_back(
        local_probs, local_plow, local_query, local_key, local_value, local_mix_grad
    )
    local_qkv_grad = bfloat(
        jnp.concatenate(
            [
                local_qg.reshape(row_count, model_width),
                local_kg.reshape(row_count, model_width),
                local_vg.reshape(row_count, model_width),
            ],
            axis=1,
        )
    )
    norm2_back = jax.vjp(norm_rows, flat_seq, vectors[2], vectors[3])[1](
        product(local_qkv_grad, qkv_flat.T)
    )
    seq_grad = (attn_res_grad + norm2_back[0]).reshape(windows, seq_len, model_width)

    region_new_grad = seq_grad[:, 0]
    region_branch_grad = bfloat(keeper[:, 0:1] * region_new_grad)
    grad_outw = grad_outw + product(region_mix.T, region_branch_grad)
    grad_bo = jnp.sum(local_branch_grad.astype(jnp.float32), 0) + jnp.sum(
        region_branch_grad.astype(jnp.float32), 0
    )
    region_mix_grad = bfloat(product(region_branch_grad, out_weight.T))
    mix_grad4 = region_mix_grad.reshape(head_shape)
    prob_grad = jnp.einsum(
        "bqhd,bkhd->bhqk", mix_grad4, value_all4, preferred_element_type=jnp.float32
    )
    grad_mean = jnp.sum(region_probs * prob_grad, -1, keepdims=True)
    score_low = bfloat(region_probs * (prob_grad - grad_mean))
    region_qg = (
        jnp.einsum("bhqk,bkhd->bqhd", score_low, key_all4, preferred_element_type=jnp.float32)
        * factor
    )
    stats = jnp.concatenate([region_lse[0, :, :, 0], grad_mean[0, :, :, 0]], axis=0).T
    sent = jnp.concatenate(
        [
            region_mix_grad.astype(jnp.float32),
            stats,
            jnp.zeros((windows, 128 - 2 * HEADS), jnp.float32),
        ],
        axis=1,
    )
    sent = gather_blocks(sent, "win").reshape(group_rows, -1)
    mix_grad_all4 = bfloat(sent[:, :model_width]).reshape(head_shape)
    lse_all = sent[:, model_width : model_width + HEADS].T[None, :, :, None]
    mean_all = sent[:, model_width + HEADS : model_width + 2 * HEADS].T[None, :, :, None]
    logits_back = (
        jnp.einsum(
            "bqhd,bkhd->bhqk", query_all4, key_own4, preferred_element_type=jnp.float32
        )
        * factor
    )
    back_allowed = (all_images[:, None] == own_images[None, :])[None, None]
    probs_back = jnp.where(back_allowed, jnp.exp(jnp.minimum(logits_back - lse_all, 0.0)), 0.0)
    prob_grad_back = jnp.einsum(
        "bqhd,bkhd->bhqk", mix_grad_all4, value_own4, preferred_element_type=jnp.float32
    )
    score_back = bfloat(probs_back * (prob_grad_back - mean_all))
    region_kg = (
        jnp.einsum("bhqk,bqhd->bkhd", score_back, query_all4, preferred_element_type=jnp.float32)
        * factor
    )
    region_vg = jnp.einsum(
        "bhqk,bqhd->bkhd", bfloat(probs_back), mix_grad_all4, preferred_element_type=jnp.float32
    )
    region_qkv_grad = bfloat(
        jnp.concatenate(
            [part.reshape(windows, model_width) for part in (region_qg, region_kg, region_vg)],
            axis=1,
        )
    )
    norm1_back = jax.vjp(norm_rows, region, vectors[0], vectors[1])[1](
        product(region_qkv_grad, qkv_flat.T)
    )
    region_grad = region_new_grad + norm1_back[0]
    input_grad = jnp.concatenate([region_grad[:, None], seq_grad[:, 1:]], axis=1)
    all_norm = jnp.concatenate([seq_norm, region_norm], axis=0)
    all_qkv_grad = jnp.concatenate([local_qkv_grad, region_qkv_grad], axis=0)
    grad_qkv = [
        product(all_norm.T, all_qkv_grad[:, number * model_width : (number + 1) * model_width])
        for number in range(3)
    ]
    qkv_bias_grad = jnp.sum(all_qkv_grad.astype(jnp.float32), 0)
    grad_vec = jnp.concatenate(
        [
            jnp.stack(
                [
                    norm1_back[1],
                    norm1_back[2],
                    norm2_back[1],
                    norm2_back[2],
                    norm3_back[1],
                    norm3_back[2],
                    qkv_bias_grad[:model_width],
                    qkv_bias_grad[2 * model_width :],
                    grad_bo,
                    grad_bm,
                ]
            ),
            grad_bu.reshape(-1, model_width),
        ],
        axis=0,
    ).reshape(-1)
    shard_rows = out_mom.shape[0]
    ff_rows = down_mom.shape[0]
    vec_rows = vec_mom.shape[0]

    def blocks(first, second):
        pair = jnp.stack([first, second]).reshape(2, win_count, shard_rows, model_width)
        return pair.swapaxes(0, 1).reshape(win_count, 2 * shard_rows, model_width)

    query_key_total = scatter_sum(blocks(grad_qkv[0], grad_qkv[1]), order_a)
    value_out_total = scatter_sum(blocks(grad_qkv[2], grad_outw), order_b)
    vec_total = lax.dynamic_slice_in_dim(sum_everywhere(grad_vec), win_index * vec_rows, vec_rows)
    new_qkv_mom = MOMENTUM_DECAY * qkv_mom + jnp.stack(
        [query_key_total[:shard_rows], query_key_total[shard_rows:], value_out_total[:shard_rows]]
    )
    new_out_mom = MOMENTUM_DECAY * out_mom + value_out_total[shard_rows:]
    new_up_mom = MOMENTUM_DECAY * up_mom + up_total
    new_down_mom = MOMENTUM_DECAY * down_mom + down_total
    new_vec_mom = MOMENTUM_DECAY * vec_mom + vec_total
    new_vectors = (
        lax.dynamic_slice_in_dim(vectors.reshape(-1), win_index * vec_rows, vec_rows)
        - VECTOR_RATE * new_vec_mom
    )
    find_updates = updates_two_owners if lax.axis_size("rep") == 2 else updates_any_owners
    updates = find_updates(new_qkv_mom, new_out_mom, new_up_mom, new_down_mom)

    def stepped(weight, rows_here, update):
        rows = own_rows(weight, rows_here).astype(jnp.float32)
        return rows - MATRIX_RATE * update.astype(jnp.float32)

    new_qkv = jnp.stack(
        [stepped(qkv_weight[number], shard_rows, updates[number]) for number in range(3)]
    )
    new_out = stepped(out_weight, shard_rows, updates[3])
    new_up = stepped(up_weight, shard_rows, updates[4])
    new_down = stepped(down_weight, ff_rows, updates[5])
    out_tokens = bfloat(output.reshape(1, windows, seq_len, model_width))
    return (
        out_tokens,
        input_grad[None],
        new_qkv_mom,
        new_qkv,
        new_out_mom,
        new_out,
        new_up_mom,
        new_up,
        new_down_mom,
        new_down,
        new_vec_mom,
        new_vectors,
    )


def solution(mesh):
    placed = (
        P("rep", "win", None, None),
        P("rep", "win", None),
        P("rep", "win", None),
        P("rep", None),
        P(),
        P(),
        P(),
        P(),
        P(),
        P(None, "win", None),
        P("win", None),
        P("win", None),
        P("win", None),
        P("win"),
        P("rep", "win", None, None),
    )
    return jax.shard_map(
        local,
        mesh=mesh,
        in_specs=placed,
        out_specs=(
            P("rep", "win", None, None),
            P("rep", "win", None, None),
            P(None, "win", None),
            P(None, "win", None),
            P("win", None),
            P("win", None),
            P("win", None),
            P("win", None),
            P("win", None),
            P("win", None),
            P("win"),
            P("win"),
        ),
        check_vma=False,
    )
```

```python
import functools

import jax
import jax.numpy as jnp
from jax import lax
from jax.experimental import pallas as pl
from jax.experimental.pallas import tpu as pltpu
from jax.sharding import PartitionSpec as P

HEADS = 16
HEAD_DIM = 32


EPSILON = 1e-06
MOMENTUM_DECAY = 0.95
MATRIX_RATE = 0.5
VECTOR_RATE = 0.0002
KEEP_SHARE = 0.75
NEWTON_COEFFS = (3.4445, -4.775, 2.0315)


def bfloat(values):
    return values.astype(jnp.bfloat16)


def product(left_side, right_side):
    return jnp.dot(left_side, right_side, preferred_element_type=jnp.float32)


def norm_rows(values, gain_row, shift_row):
    center = values - jnp.mean(values, -1, keepdims=True)
    spread = jnp.mean(center * center, -1, keepdims=True)
    return center * lax.rsqrt(spread + EPSILON) * gain_row + shift_row


def bit_count(axis):
    return lax.axis_size(axis).bit_length() - 1


def swap(values, axis, bit):
    size = lax.axis_size(axis)
    return lax.ppermute(values, axis, [(i, i ^ (1 << bit)) for i in range(size)])


def my_bit(axis, bit):
    return (lax.axis_index(axis) >> bit) & 1


def gather_blocks(values, axis):
    done = []
    for bit in list(range(2, bit_count(axis))) + [1, 0]:
        other = swap(values, axis, bit)
        first = my_bit(axis, bit) == 0
        place = sum(1 for earlier in done if earlier > bit)
        values = jnp.stack(
            [jnp.where(first, values, other), jnp.where(first, other, values)], axis=place
        )
        done.append(bit)
    return values.reshape((lax.axis_size(axis),) + values.shape[len(done) :])


def halve_blocks(values, bit, bits_left):
    place = bits_left.index(bit)
    split = values.reshape((2,) * len(bits_left) + values.shape[1:])
    mine = my_bit("win", bit)
    kept = lax.dynamic_index_in_dim(split, mine, place, keepdims=False)
    sent = lax.dynamic_index_in_dim(split, 1 - mine, place, keepdims=False)
    total = kept + swap(bfloat(sent), "win", bit).astype(jnp.float32)
    left = [other for other in bits_left if other != bit]
    return total.reshape((-1,) + values.shape[1:]), left


def halve_columns(values):
    for bit in range(bit_count("rep")):
        half = values.shape[-1] // 2
        last = values.ndim - 1
        mine = my_bit("rep", bit)
        kept = lax.dynamic_slice_in_dim(values, mine * half, half, last)
        sent = lax.dynamic_slice_in_dim(values, (1 - mine) * half, half, last)
        values = kept + swap(bfloat(sent), "rep", bit).astype(jnp.float32)
    return values


def join_columns(values):
    values = bfloat(values)
    for bit in reversed(range(bit_count("rep"))):
        other = swap(values, "rep", bit)
        first = my_bit("rep", bit) == 0
        values = jnp.concatenate(
            [jnp.where(first, values, other), jnp.where(first, other, values)], axis=-1
        )
    return values.astype(jnp.float32)


def scatter_pair(first, second):
    bits = list(range(1, bit_count("win")))[::-1]
    first, left = halve_blocks(halve_columns(first), 1, bits)
    second = halve_columns(halve_blocks(second, 1, bits)[0])
    values = jnp.concatenate([first, second], axis=1)
    for bit in sorted(left):
        values, left = halve_blocks(values, bit, left)
    return join_columns(values)[0]


def sum_over_rep(values):
    for bit in range(bit_count("rep")):
        low = bfloat(values)
        values = low.astype(jnp.float32) + swap(low, "rep", bit).astype(jnp.float32)
    return values


def off_diagonal_step(iterate, exact):
    high = bfloat(iterate)
    gram = dot_as(high, high, NT)
    if exact:
        rest = bfloat(iterate - high.astype(jnp.float32))
        gram = gram + dot_as(high, rest, NT) + dot_as(rest, high, NT)
    size = gram.shape[0]
    row_ids = lax.broadcasted_iota(jnp.int32, (size, size), 0)
    on_diagonal = row_ids == lax.broadcasted_iota(jnp.int32, (size, size), 1)
    own = jnp.where(on_diagonal, gram, 0.0)
    own_column = jnp.sum(own, 1, keepdims=True)
    own_row = jnp.sum(own, 0, keepdims=True)
    off = jnp.where(on_diagonal, 0.0, gram)
    off_low = bfloat(off)
    square = product(off_low, off_low) + (own_column + own_row) * off
    poly = NEWTON_COEFFS[1] * off + NEWTON_COEFFS[2] * square
    poly_own = jnp.sum(jnp.where(on_diagonal, poly, 0.0), 1, keepdims=True)
    factor = (
        NEWTON_COEFFS[0]
        + poly_own
        + own_column * (NEWTON_COEFFS[1] + NEWTON_COEFFS[2] * own_column)
    )
    poly = jnp.where(on_diagonal, 0.0, poly)
    poly_high = bfloat(poly)
    moved = product(poly_high, high)
    if exact:
        poly_rest = bfloat(poly - poly_high.astype(jnp.float32))
        moved = moved + product(poly_high, rest) + product(poly_rest, high)
    return factor * iterate + moved


def unit_scale(values):
    total = jnp.sum(jnp.sum(values * values, 1, keepdims=True), 0, keepdims=True)
    return values * (1.0 / (jnp.sqrt(total) + EPSILON))


def big_newton_kernel(folds, place_ref, blocks_ref, out_ref, iterate_ref, turned_ref):
    blocks, rows, width = blocks_ref.shape
    part = rows // folds

    @pl.when(place_ref[0] == 0)
    def _():
        for block in range(blocks):
            for fold in range(folds):
                iterate_ref[
                    block * part : (block + 1) * part, fold * width : (fold + 1) * width
                ] = blocks_ref[block, fold * part : (fold + 1) * part, :].astype(jnp.float32)

    @pl.when(place_ref[0] != 0)
    def _():
        for block in range(blocks):
            iterate_ref[:, block * rows : (block + 1) * rows] = blocks_ref[block].astype(
                jnp.float32
            ).T

    iterate_ref[...] = unit_scale(iterate_ref[...])

    @pl.loop(0, 5)
    def _(_):
        iterate_ref[...] = off_diagonal_step(iterate_ref[...], False)

    @pl.when(place_ref[0] == 0)
    def _():
        start = pl.multiple_of(place_ref[1] * part, part)
        for fold in range(folds):
            out_ref[fold * part : (fold + 1) * part, :] = bfloat(
                iterate_ref[pl.ds(start, part), fold * width : (fold + 1) * width]
            )

    @pl.when(place_ref[0] != 0)
    def _():
        span = max(rows, 128)
        start = pl.multiple_of(place_ref[1] * rows // span * span, span)
        turned_ref[...] = iterate_ref[:, pl.ds(start, span)].T * float(folds) ** 0.5
        inner = pl.multiple_of(place_ref[1] * rows - start, rows)
        out_ref[...] = bfloat(turned_ref[pl.ds(inner, rows), :])


def small_newton_kernel(place_ref, blocks_ref, out_ref, iterate_ref):
    blocks, matrices, rows, width = blocks_ref.shape
    for number in range(matrices):
        for block in range(blocks):
            iterate_ref[number, block * rows : (block + 1) * rows, :] = blocks_ref[
                block, number
            ].astype(jnp.float32)

    @pl.loop(0, matrices)
    def _(number):
        iterate_ref[number] = unit_scale(iterate_ref[number])

        @pl.loop(0, 2)
        def _(_):
            iterate_ref[number] = off_diagonal_step(iterate_ref[number], False)

        @pl.loop(0, 3)
        def _(_):
            iterate_ref[number] = off_diagonal_step(iterate_ref[number], True)

    start = pl.multiple_of(place_ref[1] * rows, rows)
    for number in range(matrices):
        out_ref[number] = bfloat(iterate_ref[number, pl.ds(start, rows), :])


def newton_call(kernel, name, place, blocks, out_dims, scratch_dims, flops):
    return pl.pallas_call(
        kernel,
        in_specs=[
            pl.BlockSpec(memory_space=pltpu.SMEM),
            pl.BlockSpec(memory_space=pltpu.VMEM),
        ],
        out_specs=pl.BlockSpec(memory_space=pltpu.VMEM),
        out_shape=shape_of(out_dims, jnp.bfloat16),
        scratch_shapes=[pltpu.VMEM(dims, jnp.float32) for dims in scratch_dims],
        compiler_params=pltpu.CompilerParams(vmem_limit_bytes=VMEM_LIMIT),
        cost_estimate=pl.CostEstimate(
            flops=flops, bytes_accessed=2 * blocks.size, transcendentals=0
        ),
        name=name,
    )(place, blocks)


def big_update(place, blocks, folds):
    win, rows, width = blocks.shape
    return newton_call(
        functools.partial(big_newton_kernel, folds),
        "big_newton",
        place,
        blocks,
        (rows, width),
        [(width, win * rows), (max(rows, 128), width)],
        2 * 5 * width * width * (2 * win * rows + width),
    )


def small_update(place, blocks):
    win, matrices, rows, width = blocks.shape
    return newton_call(
        small_newton_kernel,
        "small_newton",
        place,
        blocks,
        (matrices, rows, width),
        [(matrices, width, width)],
        2 * 27 * matrices * width**3,
    )


def own_rows(matrix, rows_here):
    return lax.dynamic_slice_in_dim(matrix, lax.axis_index("win") * rows_here, rows_here, 0)


def own_block(values):
    return lax.dynamic_index_in_dim(values, lax.axis_index("win"), 0, keepdims=False)


def fold_columns(rows, width):
    count, columns = rows.shape
    return rows.reshape(count, columns // width, width).swapaxes(0, 1).reshape(-1, width)


def unfold_columns(rows, folds):
    total, width = rows.shape
    return rows.reshape(folds, total // folds, width).swapaxes(0, 1).reshape(-1, folds * width)


def pick_owner(first, here, there):
    return jnp.where(first, here, there), jnp.where(first, there, here)


def big_updates(up_folded, down_rows, folds):
    win_index = lax.axis_index("win")
    rep_index = lax.axis_index("rep")
    if lax.axis_size("rep") == 2:
        first = rep_index == 0
        place = jnp.stack([rep_index, win_index]).astype(jnp.int32)
        blocks = gather_blocks(bfloat(jnp.where(first, up_folded, down_rows)), "win")
        mine = big_update(place, blocks, folds)
        return pick_owner(first, mine, swap(mine, "rep", 0))
    updates = []
    for number, rows in enumerate([up_folded, down_rows]):
        place = jnp.stack([jnp.int32(number), win_index]).astype(jnp.int32)
        updates.append(big_update(place, gather_blocks(bfloat(rows), "win"), folds))
    return updates


def small_updates(rows):
    win_index = lax.axis_index("win")
    rep_index = lax.axis_index("rep")
    place = jnp.stack([rep_index, win_index]).astype(jnp.int32)
    if lax.axis_size("rep") == 2:
        first = rep_index == 0
        blocks = gather_blocks(bfloat(jnp.where(first, rows[:2], rows[2:])), "win")
        mine = small_update(place, blocks)
        return jnp.concatenate(pick_owner(first, mine, swap(mine, "rep", 0)))
    return small_update(place, gather_blocks(bfloat(rows), "win"))


GROUP_HEADS = 128 // HEAD_DIM
SCORE_SCALE = HEAD_DIM ** (-0.5)
LOG2_E = 1.4426950408889634
VMEM_LIMIT = 48 * 1024 * 1024
NT = (((1,), (1,)), ((), ()))
TN = (((0,), (0,)), ((), ()))


def dot_as(left_side, right_side, dims):
    return lax.dot_general(left_side, right_side, dims, preferred_element_type=jnp.float32)


def spread_heads(part, lane_head):
    return bfloat(
        jnp.concatenate(
            [jnp.where(lane_head == head, part, 0.0) for head in range(GROUP_HEADS)], axis=0
        )
    )


def join_heads(spread, lane_head, rows):
    joined = spread[:rows]
    for head in range(1, GROUP_HEADS):
        joined = jnp.where(lane_head == head, spread[head * rows : (head + 1) * rows], joined)
    return joined


def column_softmax(scores, bias_column):
    scores = scores + bias_column
    raised = jnp.exp2((scores - jnp.max(scores, 0, keepdims=True)) * (SCORE_SCALE * LOG2_E))
    return raised * (1.0 / jnp.sum(raised, 0, keepdims=True))


def load_windows(tokens_ref, region_ref, fill_ref, count, seq_len, padded, step):
    for window in range(count):
        base = window * padded
        fill_ref[base : base + seq_len, :] = tokens_ref[0, window].astype(jnp.float32)
        fill_ref[base : base + 1, :] = region_ref[pl.ds(step * count + window, 1), :]


def window_forward_kernel(
    count,
    seq_len,
    padded,
    tokens_ref,
    region_ref,
    bias_ref,
    keep_ref,
    qkv_ref,
    out_ref,
    vec_ref,
    norm_out,
    proj_out,
    mix_out,
    after_out,
    fill_ref,
    mix_ref,
):
    step = pl.program_id(0)
    width = tokens_ref.shape[-1]

    @pl.when(step == 0)
    def _():
        fill_ref[...] = jnp.zeros_like(fill_ref)

    load_windows(tokens_ref, region_ref, fill_ref, count, seq_len, padded, step)
    flat = fill_ref[...]
    normed = bfloat(norm_rows(flat, vec_ref[2:3, :], vec_ref[3:4, :]))
    lane_head = lax.broadcasted_iota(jnp.int32, (padded, 128), 1) // HEAD_DIM
    proj = product(normed, qkv_ref[...])
    query = proj[:, :width] + vec_ref[6:7, :]
    keyset = proj[:, width : 2 * width]
    values = proj[:, 2 * width :] + vec_ref[7:8, :]
    for window in range(count):
        rows = slice(window * padded, (window + 1) * padded)
        norm_out[window] = normed[rows]
        bias_column = bias_ref[window]
        for group in range(width // 128):
            lanes = slice(group * 128, (group + 1) * 128)
            spread = spread_heads(query[rows, lanes], lane_head)
            key_low = bfloat(keyset[rows, lanes])
            value_low = bfloat(values[rows, lanes])
            probs = column_softmax(dot_as(key_low, spread, NT), bias_column)
            mixed = dot_as(bfloat(probs), value_low, TN)
            mix_ref[rows, lanes] = join_heads(mixed, lane_head, padded)
            proj_out[window, :, lanes] = bfloat(query[rows, lanes])
            proj_out[window, :, width + group * 128 : width + (group + 1) * 128] = key_low
            proj_out[window, :, 2 * width + group * 128 : 2 * width + (group + 1) * 128] = value_low
    mixed_low = bfloat(mix_ref[...])
    branch = product(mixed_low, out_ref[...]) + vec_ref[8:9, :]
    for window in range(count):
        rows = slice(window * padded, (window + 1) * padded)
        mix_out[window] = mixed_low[rows]
        after_out[window] = flat[rows] + keep_ref[window] * branch[rows]


def window_backward_kernel(
    count,
    seq_len,
    padded,
    tokens_ref,
    region_ref,
    bias_ref,
    keep_ref,
    qkv_ref,
    out_ref,
    vec_ref,
    proj_ref,
    after_grad_ref,
    region_keep_ref,
    grad_out,
    region_grad_out,
    proj_grad_out,
    branch_grad_out,
    sums_out,
    region_branch_out,
    region_mix_out,
    fill_ref,
    proj_grad_ref,
):
    step = pl.program_id(0)
    width = tokens_ref.shape[-1]

    @pl.when(step == 0)
    def _():
        fill_ref[...] = jnp.zeros_like(fill_ref)
        sums_out[...] = jnp.zeros_like(sums_out)
        region_grad_out[...] = jnp.zeros_like(region_grad_out)

    load_windows(tokens_ref, region_ref, fill_ref, count, seq_len, padded, step)
    lane_head = lax.broadcasted_iota(jnp.int32, (padded, 128), 1) // HEAD_DIM
    branch_grad = bfloat(
        jnp.concatenate(
            [keep_ref[window] * after_grad_ref[window] for window in range(count)], axis=0
        )
    )
    mix_grad = dot_as(branch_grad, out_ref[...], NT)
    for window in range(count):
        rows = slice(window * padded, (window + 1) * padded)
        branch_grad_out[window] = branch_grad[rows]
        bias_column = bias_ref[window]
        for group in range(width // 128):
            lanes = slice(group * 128, (group + 1) * 128)
            key_lanes = slice(width + group * 128, width + (group + 1) * 128)
            value_lanes = slice(2 * width + group * 128, 2 * width + (group + 1) * 128)
            spread = spread_heads(proj_ref[window, :, lanes].astype(jnp.float32), lane_head)
            key_low = proj_ref[window, :, key_lanes]
            value_low = proj_ref[window, :, value_lanes]
            spread_grad = spread_heads(mix_grad[rows, lanes], lane_head)
            probs = column_softmax(dot_as(key_low, spread, NT), bias_column)
            probs_grad = dot_as(value_low, spread_grad, NT)
            weighted = probs * probs_grad
            score_grad = bfloat(weighted - probs * jnp.sum(weighted, 0, keepdims=True))
            value_grad = product(bfloat(probs), spread_grad)
            key_grad = product(score_grad, spread) * SCORE_SCALE
            query_grad = join_heads(dot_as(score_grad, key_low, TN), lane_head, padded)
            proj_grad_ref[rows, lanes] = query_grad * SCORE_SCALE
            proj_grad_ref[rows, key_lanes] = key_grad
            proj_grad_ref[rows, value_lanes] = value_grad
    proj_grad = bfloat(proj_grad_ref[...])
    norm_grad = dot_as(proj_grad, qkv_ref[...], NT)
    flat = fill_ref[...]
    center = flat - jnp.mean(flat, -1, keepdims=True)
    scale = lax.rsqrt(jnp.mean(center * center, -1, keepdims=True) + EPSILON)
    hat = center * scale
    hat_grad = norm_grad * vec_ref[2:3, :]
    flat_grad = scale * (
        hat_grad
        - jnp.mean(hat_grad, -1, keepdims=True)
        - hat * jnp.mean(hat_grad * hat, -1, keepdims=True)
    )
    sums_out[0:1, :width] += jnp.sum(norm_grad * hat, 0, keepdims=True)
    sums_out[1:2, :width] += jnp.sum(norm_grad, 0, keepdims=True)
    sums_out[2:3, :width] += jnp.sum(branch_grad.astype(jnp.float32), 0, keepdims=True)
    sums_out[3:4, :] += jnp.sum(proj_grad.astype(jnp.float32), 0, keepdims=True)
    for window in range(count):
        rows = slice(window * padded, (window + 1) * padded)
        proj_grad_out[window] = proj_grad[rows]
        seq_grad = after_grad_ref[window] + flat_grad[rows]
        grad_out[0, window] = seq_grad[:seq_len]
        region_grad_out[pl.ds(step * count + window, 1), :] = seq_grad[0:1]

    @pl.when(step == pl.num_programs(0) - 1)
    def _():
        region_branch = bfloat(region_keep_ref[...] * region_grad_out[...])
        sums_out[2:3, :width] += jnp.sum(region_branch.astype(jnp.float32), 0, keepdims=True)
        region_branch_out[...] = region_branch
        region_mix_out[...] = bfloat(dot_as(region_branch, out_ref[...], NT))


def window_step(windows):
    return next(count for count in (4, 2, 1) if windows % count == 0)


def whole_spec(shape):
    return pl.BlockSpec(shape, lambda step: (0,) * len(shape))


def step_spec(count, *rest):
    return pl.BlockSpec((count,) + rest, lambda step: (step,) + (0,) * len(rest))


def token_spec(count, *rest):
    return pl.BlockSpec((1, count) + rest, lambda step: (0, step) + (0,) * len(rest))


def shape_of(dims, kind=jnp.float32):
    return jax.ShapeDtypeStruct(dims, kind)


def window_forward(tokens, region, bias, keep, qkv_flat, out_weight, vectors, padded):
    _, windows, seq_len, width = tokens.shape
    count = window_step(windows)
    return pl.pallas_call(
        functools.partial(window_forward_kernel, count, seq_len, padded),
        grid=(windows // count,),
        in_specs=[
            token_spec(count, seq_len, width),
            whole_spec(region.shape),
            step_spec(count, padded, 1),
            step_spec(count, 1, 1),
            whole_spec(qkv_flat.shape),
            whole_spec(out_weight.shape),
            whole_spec(vectors.shape),
        ],
        out_specs=[
            step_spec(count, padded, width),
            step_spec(count, padded, 3 * width),
            step_spec(count, padded, width),
            step_spec(count, padded, width),
        ],
        out_shape=[
            shape_of((windows, padded, width), jnp.bfloat16),
            shape_of((windows, padded, 3 * width), jnp.bfloat16),
            shape_of((windows, padded, width), jnp.bfloat16),
            shape_of((windows, padded, width)),
        ],
        scratch_shapes=[
            pltpu.VMEM((count * padded, width), jnp.float32),
            pltpu.VMEM((count * padded, width), jnp.float32),
        ],
        compiler_params=pltpu.CompilerParams(vmem_limit_bytes=VMEM_LIMIT),
        name="window_forward",
    )(tokens, region, bias, keep, qkv_flat, out_weight, vectors)


def window_backward(
    tokens, region, bias, keep, qkv_flat, out_weight, vectors, proj, after_grad, region_keep, padded
):
    _, windows, seq_len, width = tokens.shape
    count = window_step(windows)
    return pl.pallas_call(
        functools.partial(window_backward_kernel, count, seq_len, padded),
        grid=(windows // count,),
        in_specs=[
            token_spec(count, seq_len, width),
            whole_spec(region.shape),
            step_spec(count, padded, 1),
            step_spec(count, 1, 1),
            whole_spec(qkv_flat.shape),
            whole_spec(out_weight.shape),
            whole_spec(vectors.shape),
            step_spec(count, padded, 3 * width),
            step_spec(count, padded, width),
            whole_spec(region_keep.shape),
        ],
        out_specs=[
            token_spec(count, seq_len, width),
            whole_spec(region.shape),
            step_spec(count, padded, 3 * width),
            step_spec(count, padded, width),
            whole_spec((8, 3 * width)),
            whole_spec(region.shape),
            whole_spec(region.shape),
        ],
        out_shape=[
            shape_of(tokens.shape),
            shape_of(region.shape),
            shape_of((windows, padded, 3 * width), jnp.bfloat16),
            shape_of((windows, padded, width), jnp.bfloat16),
            shape_of((8, 3 * width)),
            shape_of(region.shape, jnp.bfloat16),
            shape_of(region.shape, jnp.bfloat16),
        ],
        scratch_shapes=[
            pltpu.VMEM((count * padded, width), jnp.float32),
            pltpu.VMEM((count * padded, 3 * width), jnp.float32),
        ],
        compiler_params=pltpu.CompilerParams(vmem_limit_bytes=VMEM_LIMIT),
        name="window_backward",
    )(tokens, region, bias, keep, qkv_flat, out_weight, vectors, proj, after_grad, region_keep)


def image_bias(keys_ref, queries_ref):
    return jnp.where(keys_ref[...] == queries_ref[...], 0.0, -1e30)


def region_forward_kernel(
    all_ref,
    own_ref,
    keep_ref,
    key_image_ref,
    query_image_ref,
    qkv_ref,
    out_ref,
    vec_ref,
    norm_out,
    proj_out,
    mix_out,
    new_out,
):
    rows, width = own_ref.shape
    vec = vec_ref[...]
    normed = bfloat(norm_rows(all_ref[...].astype(jnp.float32), vec[0:1], vec[1:2]))
    norm_out[...] = normed
    proj = product(normed, qkv_ref[...])
    query = bfloat(proj[:, :width] + vec[6:7])
    keyset = bfloat(proj[:, width : 2 * width])
    values = bfloat(proj[:, 2 * width :] + vec[7:8])
    proj_out[:, :width] = query
    proj_out[:, width : 2 * width] = keyset
    proj_out[:, 2 * width :] = values
    region = own_ref[...].astype(jnp.float32)
    own_norm = bfloat(norm_rows(region, vec[0:1], vec[1:2]))
    own_query = product(own_norm, qkv_ref[:, :width]) + vec[6:7]
    bias = image_bias(key_image_ref, query_image_ref)
    lane_head = lax.broadcasted_iota(jnp.int32, (rows, 128), 1) // HEAD_DIM
    parts = []
    for group in range(width // 128):
        lanes = slice(group * 128, (group + 1) * 128)
        spread = spread_heads(own_query[:, lanes], lane_head)
        probs = column_softmax(dot_as(keyset[:, lanes], spread, NT), bias)
        mixed = dot_as(bfloat(probs), values[:, lanes], TN)
        parts.append(join_heads(mixed, lane_head, rows))
    mixed_low = bfloat(jnp.concatenate(parts, axis=1))
    mix_out[...] = mixed_low
    branch = product(mixed_low, out_ref[...]) + vec[8:9]
    new_out[...] = region + keep_ref[...] * branch


def region_forward(all_rows, own_rows_, keep, key_images, query_images, qkv_flat, out_weight, vectors):
    total, width = all_rows.shape
    return pl.pallas_call(
        region_forward_kernel,
        out_shape=[
            shape_of((total, width), jnp.bfloat16),
            shape_of((total, 3 * width), jnp.bfloat16),
            shape_of(own_rows_.shape, jnp.bfloat16),
            shape_of(own_rows_.shape),
        ],
        compiler_params=pltpu.CompilerParams(vmem_limit_bytes=VMEM_LIMIT),
        name="region_forward",
    )(all_rows, own_rows_, keep, key_images, query_images, qkv_flat, out_weight, vectors)


def region_backward_kernel(
    place_ref,
    all_ref,
    norm_ref,
    proj_ref,
    mix_grad_ref,
    key_image_ref,
    query_image_ref,
    new_grad_ref,
    qkv_ref,
    vec_ref,
    grad_out,
    weight_out,
    sums_out,
    bias_ref,
    proj_grad_ref,
    region_grad_ref,
    weight_ref,
):
    total, width = all_ref.shape
    rows = new_grad_ref.shape[0]
    bias_ref[...] = image_bias(key_image_ref, query_image_ref)
    lane_head = lax.broadcasted_iota(jnp.int32, (total, 128), 1) // HEAD_DIM

    @pl.loop(0, width // 128)
    def _(group):
        query_lanes = pl.ds(pl.multiple_of(group * 128, 128), 128)
        key_lanes = pl.ds(pl.multiple_of(width + group * 128, 128), 128)
        value_lanes = pl.ds(pl.multiple_of(2 * width + group * 128, 128), 128)
        query = proj_ref[:, query_lanes]
        key_low = proj_ref[:, key_lanes]
        value_low = proj_ref[:, value_lanes]
        mix_grad = mix_grad_ref[:, query_lanes]
        zero = jnp.zeros((total, 128), jnp.float32)
        query_grad, key_grad, value_grad = zero, zero, zero
        for head in range(GROUP_HEADS):
            here = lane_head == head
            head_query = jnp.where(here, query, jnp.zeros_like(query))
            head_grad = jnp.where(here, mix_grad, jnp.zeros_like(mix_grad))
            probs = column_softmax(dot_as(key_low, head_query, NT), bias_ref[...])
            probs_grad = dot_as(value_low, head_grad, NT)
            weighted = probs * probs_grad
            score_grad = bfloat(weighted - probs * jnp.sum(weighted, 0, keepdims=True))
            value_grad += product(bfloat(probs), head_grad)
            key_grad += product(score_grad, head_query)
            query_grad = jnp.where(here, dot_as(score_grad, key_low, TN), query_grad)
        proj_grad_ref[:, query_lanes] = bfloat(query_grad * SCORE_SCALE)
        proj_grad_ref[:, key_lanes] = bfloat(key_grad * SCORE_SCALE)
        proj_grad_ref[:, value_lanes] = bfloat(value_grad)

    proj_grad = proj_grad_ref[...]
    norm_grad = dot_as(proj_grad, qkv_ref[...], NT)
    region = all_ref[...].astype(jnp.float32)
    center = region - jnp.mean(region, -1, keepdims=True)
    scale = lax.rsqrt(jnp.mean(center * center, -1, keepdims=True) + EPSILON)
    hat = center * scale
    hat_grad = norm_grad * vec_ref[0:1, :]
    region_grad_ref[...] = scale * (
        hat_grad
        - jnp.mean(hat_grad, -1, keepdims=True)
        - hat * jnp.mean(hat_grad * hat, -1, keepdims=True)
    )
    start = pl.multiple_of(place_ref[1] * rows, 8)
    grad_out[...] = new_grad_ref[...] + region_grad_ref[pl.ds(start, rows), :]
    bias_sums = jnp.sum(proj_grad.astype(jnp.float32), 0, keepdims=True)
    sums_out[0:1, :] = jnp.sum(norm_grad * hat, 0, keepdims=True)
    sums_out[1:2, :] = jnp.sum(norm_grad, 0, keepdims=True)
    sums_out[2:3, :] = bias_sums[:, :width]
    sums_out[3:4, :] = bias_sums[:, 2 * width :]
    sums_out[4:8, :] = jnp.zeros((4, width), jnp.float32)
    weight_ref[...] = dot_as(norm_ref[...], proj_grad, TN)
    weight_rows = weight_out.shape[1]
    weight_start = pl.multiple_of(place_ref[1] * weight_rows, 8)
    for number in range(3):
        weight_out[number] = weight_ref[
            pl.ds(weight_start, weight_rows), number * width : (number + 1) * width
        ]


def region_backward(
    place, all_rows, normed, proj, mix_grad, key_images, query_images, new_grad, qkv_flat, vectors, weight_rows
):
    total, width = all_rows.shape
    vmem = pl.BlockSpec(memory_space=pltpu.VMEM)
    return pl.pallas_call(
        region_backward_kernel,
        in_specs=[pl.BlockSpec(memory_space=pltpu.SMEM)] + [vmem] * 9,
        out_specs=[vmem] * 3,
        out_shape=[
            shape_of(new_grad.shape),
            shape_of((3, weight_rows, width)),
            shape_of((8, width)),
        ],
        scratch_shapes=[
            pltpu.VMEM((total, total), jnp.float32),
            pltpu.VMEM((total, 3 * width), jnp.bfloat16),
            pltpu.VMEM((total, width), jnp.float32),
            pltpu.VMEM((width, 3 * width), jnp.float32),
        ],
        compiler_params=pltpu.CompilerParams(vmem_limit_bytes=VMEM_LIMIT),
        name="region_backward",
    )(place, all_rows, normed, proj, mix_grad, key_images, query_images, new_grad, qkv_flat, vectors)


def split_cores(values, core):
    own_first = core == 0
    kept = jnp.where(own_first, values[:, 0], values[:, 1])
    sent = jnp.where(own_first, values[:, 1], values[:, 0])
    return kept, bfloat(sent)


def big_gradient_kernel(
    place_ref, norm_ref, up_grad_ref, act_ref, down_grad_ref, up_kept, up_sent, down_kept, down_sent
):
    core = place_ref[1] % 2
    width = norm_ref.shape[1]
    blocks, _, rows, _ = up_kept.shape
    total = dot_as(norm_ref[...], up_grad_ref[...], TN).reshape(blocks, 2, rows, width)
    up_kept[:, 0], up_sent[:, 0] = split_cores(total, core)
    blocks, rows, _ = down_kept.shape
    total = dot_as(act_ref[...], down_grad_ref[...], TN).reshape(blocks, 2, rows, width)
    down_kept[...], down_sent[...] = split_cores(total, core)


def big_gradients(place, normed, up_grad, act, down_grad, win_count):
    rows, width = normed.shape
    folds = up_grad.shape[1] // width
    half = win_count // 2
    up_rows = width // win_count
    whole = pl.BlockSpec((rows, width), lambda fold: (0, 0))
    part = pl.BlockSpec((rows, width), lambda fold: (0, fold))
    up_spec = pl.BlockSpec((half, 1, up_rows, width), lambda fold: (0, fold, 0, 0))
    down_spec = pl.BlockSpec((half // folds, up_rows * folds, width), lambda fold: (fold, 0, 0))
    up_dims = (half, folds, up_rows, width)
    down_dims = (half, up_rows * folds, width)
    kept_up, sent_up, kept_down, sent_down = pl.pallas_call(
        big_gradient_kernel,
        grid=(folds,),
        in_specs=[pl.BlockSpec(memory_space=pltpu.SMEM), whole, part, part, whole],
        out_specs=[up_spec, up_spec, down_spec, down_spec],
        out_shape=[
            shape_of(up_dims),
            shape_of(up_dims, jnp.bfloat16),
            shape_of(down_dims),
            shape_of(down_dims, jnp.bfloat16),
        ],
        compiler_params=pltpu.CompilerParams(vmem_limit_bytes=VMEM_LIMIT),
        cost_estimate=pl.CostEstimate(
            flops=4 * rows * width * width * folds,
            bytes_accessed=4 * rows * width * (folds + 1) + 12 * width * width * folds,
            transcendentals=0,
        ),
        name="big_gradients",
    )(place, normed, up_grad, act, down_grad)
    return (kept_up.reshape(down_dims), sent_up.reshape(down_dims)), (kept_down, sent_down)


def small_gradient_kernel(
    place_ref, norm_ref, proj_grad_ref, mix_ref, branch_ref, region_mix_ref, region_branch_ref, kept, sent
):
    core = place_ref[1] % 2
    number = pl.program_id(0)
    width = norm_ref.shape[1]
    blocks, _, rows, _ = kept.shape

    @pl.when(number < 3)
    def _():
        total = dot_as(norm_ref[...], proj_grad_ref[...], TN).reshape(blocks, 2, rows, width)
        kept[:, 0], sent[:, 0] = split_cores(total, core)

    @pl.when(number == 3)
    def _():
        total = dot_as(mix_ref[...], branch_ref[...], TN)
        total = total + dot_as(region_mix_ref[...], region_branch_ref[...], TN)
        total = total.reshape(blocks, 2, rows, width)
        kept[:, 0], sent[:, 0] = split_cores(total, core)


def small_gradients(place, normed, proj_grad, mix, branch, region_mix, region_branch, win_count):
    rows, width = normed.shape
    half = win_count // 2
    weight_rows = width // win_count
    whole = pl.BlockSpec((rows, width), lambda number: (0, 0))
    part = pl.BlockSpec((rows, width), lambda number: (0, jnp.minimum(number, 2)))
    region = pl.BlockSpec(region_mix.shape, lambda number: (0, 0))
    out_spec = pl.BlockSpec((half, 1, weight_rows, width), lambda number: (0, number, 0, 0))
    dims = (half, 4, weight_rows, width)
    kept, sent = pl.pallas_call(
        small_gradient_kernel,
        grid=(4,),
        in_specs=[pl.BlockSpec(memory_space=pltpu.SMEM), whole, part, whole, whole, region, region],
        out_specs=[out_spec, out_spec],
        out_shape=[shape_of(dims), shape_of(dims, jnp.bfloat16)],
        compiler_params=pltpu.CompilerParams(vmem_limit_bytes=VMEM_LIMIT),
        cost_estimate=pl.CostEstimate(
            flops=8 * rows * width * width,
            bytes_accessed=12 * rows * width + 24 * width * width,
            transcendentals=0,
        ),
        name="small_gradients",
    )(place, normed, proj_grad, mix, branch, region_mix, region_branch)
    flat = (half, 4 * weight_rows, width)
    return kept.reshape(flat), sent.reshape(flat)


def core_hop(kept, sent):
    return kept + swap(sent, "win", 0).astype(jnp.float32)


def local(
    tokens,
    patch_mask,
    keep_mask,
    image_map,
    qkv_weight,
    out_weight,
    up_weight,
    down_weight,
    vectors,
    qkv_mom,
    out_mom,
    up_mom,
    down_mom,
    vec_mom,
    cotangent,
):
    windows = tokens.shape[1]
    seq_len = tokens.shape[2]
    model_width = tokens.shape[3]
    hidden_width = up_weight.shape[1]
    folds = hidden_width // model_width
    shard_rows = out_mom.shape[0]
    ff_rows = down_mom.shape[0]
    vec_rows = vec_mom.shape[0]
    padded = (seq_len + 7) // 8 * 8
    region_rows = (windows + 7) // 8 * 8
    row_count = windows * padded
    win_count = lax.axis_size("win")
    win_index = lax.axis_index("win")
    place = jnp.stack([lax.axis_index("rep"), win_index]).astype(jnp.int32)

    def pad_rows(values, rows, fill=0):
        widths = ((0, rows - values.shape[0]),) + ((0, 0),) * (values.ndim - 1)
        return jnp.pad(values, widths, constant_values=fill)

    region_own = pad_rows(tokens[0, :, 0], region_rows)
    region_all = gather_blocks(region_own, "win").reshape(-1, model_width)
    keeper = keep_mask[0].astype(jnp.float32) / KEEP_SHARE
    images = image_map[0].reshape(win_count, windows)
    images = jnp.pad(images, ((0, 0), (0, region_rows - windows)), constant_values=-1)
    key_images = images.reshape(-1, 1)
    own_images = jnp.tile(own_block(images)[None], (1, GROUP_HEADS))
    qkv_flat = jnp.concatenate([qkv_weight[0], qkv_weight[1], qkv_weight[2]], axis=1)
    bias_up = vectors[10:].reshape(hidden_width)
    region_keep = pad_rows(keeper[:, 0:1], region_rows)

    region_norm, region_proj, region_mix, region_new = region_forward(
        region_all, region_own, region_keep, key_images, own_images, qkv_flat, out_weight, vectors
    )

    key_valid = jnp.concatenate([jnp.ones((windows, 1), jnp.int32), patch_mask[0]], axis=1) == 1
    key_bias = jnp.where(key_valid, 0.0, -1e30)
    key_bias = jnp.pad(key_bias, ((0, 0), (0, padded - seq_len)), constant_values=-1e30)
    key_bias = key_bias[:, :, None]
    keep_window = keeper[:, 1].reshape(windows, 1, 1)
    seq_norm, seq_proj, local_mix, after_attn = window_forward(
        tokens, region_new, key_bias, keep_window, qkv_flat, out_weight, vectors, padded
    )
    seq_norm = seq_norm.reshape(row_count, model_width)
    local_mix = local_mix.reshape(row_count, model_width)
    after_attn = after_attn.reshape(row_count, model_width)
    keep_mlp = jnp.broadcast_to(keeper[:, 2:3], (windows, padded)).reshape(row_count, 1)

    mlp_norm = bfloat(norm_rows(after_attn, vectors[4], vectors[5]))
    up_value = product(mlp_norm, up_weight) + bias_up
    activated, gelu_back = jax.vjp(jax.nn.gelu, up_value)
    act_low = bfloat(activated)
    mlp_branch = product(act_low, down_weight) + vectors[9]
    output = after_attn + keep_mlp * mlp_branch
    grad_out = jnp.pad(cotangent[0], ((0, 0), (0, padded - seq_len), (0, 0)))
    grad_out = grad_out.astype(jnp.float32).reshape(row_count, model_width)
    mlp_grad = bfloat(keep_mlp * grad_out)
    grad_bm = jnp.sum(mlp_grad.astype(jnp.float32), 0)
    up_grad = bfloat(gelu_back(product(mlp_grad, down_weight.T))[0])
    grad_bu = jnp.sum(up_grad.astype(jnp.float32), 0)
    norm3_back = jax.vjp(norm_rows, after_attn, vectors[4], vectors[5])[1](
        product(up_grad, up_weight.T)
    )
    attn_res_grad = grad_out + norm3_back[0]
    up_half, down_half = big_gradients(place, mlp_norm, up_grad, act_low, mlp_grad, win_count)
    up_half, down_half, attn_res_grad = lax.optimization_barrier(
        (up_half, down_half, attn_res_grad)
    )
    big_total = scatter_pair(core_hop(*up_half), core_hop(*down_half))

    (
        seq_grad,
        region_new_grad,
        local_qkv_grad,
        local_branch_grad,
        seq_sums,
        region_branch_grad,
        region_mix_grad,
    ) = window_backward(
        tokens,
        region_new,
        key_bias,
        keep_window,
        qkv_flat,
        out_weight,
        vectors,
        seq_proj,
        attn_res_grad.reshape(windows, padded, model_width),
        region_keep,
        padded,
    )

    region_grad, region_weight_grad, region_sums = region_backward(
        place,
        region_all,
        region_norm,
        region_proj,
        gather_blocks(region_mix_grad, "win").reshape(-1, model_width),
        key_images,
        key_images.reshape(1, -1),
        region_new_grad,
        qkv_flat,
        vectors,
        shard_rows,
    )
    input_grad = lax.dynamic_update_slice(
        seq_grad, region_grad[None, :windows, None], (0, 0, 0, 0)
    )

    small_kept, small_sent = small_gradients(
        place,
        seq_norm,
        local_qkv_grad.reshape(row_count, 3 * model_width),
        local_mix,
        local_branch_grad.reshape(row_count, model_width),
        region_mix,
        region_branch_grad,
        win_count,
    )

    def vector_blocks(rows):
        blocks = jnp.concatenate(rows, axis=0).reshape(win_count, vec_rows)
        return jnp.pad(blocks, ((0, 0), (0, model_width - vec_rows)))

    zero_row = jnp.zeros((1, model_width), jnp.float32)
    seq_vectors = vector_blocks(
        [
            zero_row,
            zero_row,
            seq_sums[0:1, :model_width],
            seq_sums[1:2, :model_width],
            norm3_back[1][None],
            norm3_back[2][None],
            seq_sums[3:4, :model_width],
            seq_sums[3:4, 2 * model_width :],
            seq_sums[2:3, :model_width],
            grad_bm[None],
            grad_bu.reshape(-1, model_width),
        ]
    )
    region_vectors = vector_blocks(
        [region_sums[0:2], jnp.tile(zero_row, (4, 1)), region_sums[2:4], jnp.tile(zero_row, (6, 1))]
    )
    core = win_index % 2
    vector_pairs = seq_vectors.reshape(win_count // 2, 2, 1, model_width)
    vector_pairs = jnp.pad(vector_pairs, ((0, 0), (0, 0), (0, 7), (0, 0)))
    small_kept = jnp.concatenate(
        [small_kept, lax.dynamic_index_in_dim(vector_pairs, core, 1, keepdims=False)], axis=1
    )
    small_sent = jnp.concatenate(
        [
            small_sent,
            bfloat(lax.dynamic_index_in_dim(vector_pairs, 1 - core, 1, keepdims=False)),
        ],
        axis=1,
    )
    small_half = core_hop(small_kept, small_sent)
    small_total = scatter_pair(
        small_half[:, : 2 * shard_rows], small_half[:, 2 * shard_rows :]
    )
    region_total = sum_over_rep(
        jnp.concatenate(
            [
                region_weight_grad.reshape(-1, model_width),
                pad_rows(own_block(region_vectors)[None], 8),
            ],
            axis=0,
        )
    )
    matrix_rows = 4 * shard_rows
    region_matrix = region_total[: 3 * shard_rows].reshape(3, shard_rows, model_width)
    small_matrix = small_total[:matrix_rows].reshape(4, shard_rows, model_width)
    new_qkv_mom = MOMENTUM_DECAY * qkv_mom + (small_matrix[:3] + region_matrix)
    new_out_mom = MOMENTUM_DECAY * out_mom + small_matrix[3]
    vec_total = small_total[matrix_rows, :vec_rows] + region_total[3 * shard_rows, :vec_rows]
    new_vec_mom = MOMENTUM_DECAY * vec_mom + vec_total
    new_vectors = (
        lax.dynamic_slice_in_dim(vectors.reshape(-1), win_index * vec_rows, vec_rows)
        - VECTOR_RATE * new_vec_mom
    )
    folded_up_mom = MOMENTUM_DECAY * fold_columns(up_mom, model_width) + big_total[:ff_rows]
    new_up_mom = unfold_columns(folded_up_mom, folds)
    new_down_mom = MOMENTUM_DECAY * down_mom + big_total[ff_rows:]
    up_update, down_update = big_updates(folded_up_mom, new_down_mom, folds)
    updates = small_updates(jnp.concatenate([new_qkv_mom, new_out_mom[None]]))

    def stepped(weight, rows_here, update):
        rows = own_rows(weight, rows_here).astype(jnp.float32)
        return rows - MATRIX_RATE * update.astype(jnp.float32)

    new_qkv = jnp.stack(
        [stepped(qkv_weight[number], shard_rows, updates[number]) for number in range(3)]
    )
    new_out = stepped(out_weight, shard_rows, updates[3])
    new_up = stepped(up_weight, shard_rows, unfold_columns(up_update, folds))
    new_down = stepped(down_weight, ff_rows, down_update)
    out_tokens = bfloat(output.reshape(1, windows, padded, model_width)[:, :, :seq_len])
    return (
        out_tokens,
        input_grad,
        new_qkv_mom,
        new_qkv,
        new_out_mom,
        new_out,
        new_up_mom,
        new_up,
        new_down_mom,
        new_down,
        new_vec_mom,
        new_vectors,
    )


def solution(mesh):
    placed = (
        P("rep", "win", None, None),
        P("rep", "win", None),
        P("rep", "win", None),
        P("rep", None),
        P(),
        P(),
        P(),
        P(),
        P(),
        P(None, "win", None),
        P("win", None),
        P("win", None),
        P("win", None),
        P("win"),
        P("rep", "win", None, None),
    )
    return jax.shard_map(
        local,
        mesh=mesh,
        in_specs=placed,
        out_specs=(
            P("rep", "win", None, None),
            P("rep", "win", None, None),
            P(None, "win", None),
            P(None, "win", None),
            P("win", None),
            P("win", None),
            P("win", None),
            P("win", None),
            P("win", None),
            P("win", None),
            P("win"),
            P("win"),
        ),
        check_vma=False,
    )
```

```python
import functools

import jax
import jax.numpy as jnp
from jax import lax
from jax.experimental import pallas as pl
from jax.experimental.pallas import tpu as pltpu
from jax.sharding import PartitionSpec as P

HEADS = 16
HEAD_DIM = 32


EPSILON = 1e-06
MOMENTUM_DECAY = 0.95
MATRIX_RATE = 0.5
VECTOR_RATE = 0.0002
KEEP_SHARE = 0.75
NEWTON_COEFFS = (3.4445, -4.775, 2.0315)


def bfloat(values):
    return values.astype(jnp.bfloat16)


def product(left_side, right_side):
    return jnp.dot(left_side, right_side, preferred_element_type=jnp.float32)


def norm_rows(values, gain_row, shift_row):
    center = values - jnp.mean(values, -1, keepdims=True)
    spread = jnp.mean(center * center, -1, keepdims=True)
    return center * lax.rsqrt(spread + EPSILON) * gain_row + shift_row


def bit_count(axis):
    return lax.axis_size(axis).bit_length() - 1


def swap(values, axis, bit):
    size = lax.axis_size(axis)
    return lax.ppermute(values, axis, [(i, i ^ (1 << bit)) for i in range(size)])


def my_bit(axis, bit):
    return (lax.axis_index(axis) >> bit) & 1


def far_bits():
    return list(range(2, bit_count("win")))


def gather_masks(low=0):
    masks = [0]
    for bit in far_bits() + [1, 0]:
        if bit >= low:
            masks += [mask | (1 << bit) for mask in masks]
    return masks


def gather_far(values):
    size = lax.axis_size("win")
    values = values[None]
    if len(far_bits()) == 2:
        others = [
            lax.ppermute(values, "win", [(i, i ^ mask) for i in range(size)]) for mask in (4, 8, 12)
        ]
        return jnp.concatenate([values] + others)
    for bit in far_bits():
        values = gather_bit(values, bit)
    return values


def gather_bit(values, bit):
    return jnp.concatenate([values, swap(values, "win", bit)])


def gather_stages(low=0):
    stages = [gather_far]
    for bit in (1, 0):
        if bit >= low:
            stages.append(functools.partial(gather_bit, bit=bit))
    return stages


def gather_blocks(values, low=0):
    for stage in gather_stages(low):
        values = stage(values)
    return values


def index_order(blocks):
    masks = gather_masks()
    by_mask = sorted(range(len(masks)), key=masks.__getitem__)
    places = lax.axis_index("win") ^ jnp.arange(len(masks))
    return blocks[jnp.array(by_mask)][places]


class Chain:
    def __init__(self, value, stages):
        self.value = value
        self.stages = list(stages)

    def step(self):
        if self.stages:
            self.value = self.stages.pop(0)(self.value)


def tie(*values):
    return lax.optimization_barrier(values)


def step_together(*chains):
    for chain in chains:
        chain.step()
    for chain, value in zip(chains, tie(*[chain.value for chain in chains])):
        chain.value = value


def halve_blocks(values, bit, bits_left):
    place = bits_left.index(bit)
    split = values.reshape((2,) * len(bits_left) + values.shape[1:])
    mine = my_bit("win", bit)
    kept = lax.dynamic_index_in_dim(split, mine, place, keepdims=False)
    sent = lax.dynamic_index_in_dim(split, 1 - mine, place, keepdims=False)
    total = kept + swap(bfloat(sent), "win", bit).astype(jnp.float32)
    left = [other for other in bits_left if other != bit]
    return total.reshape((-1,) + values.shape[1:]), left


def halve_columns(values):
    for bit in range(bit_count("rep")):
        half = values.shape[-1] // 2
        last = values.ndim - 1
        mine = my_bit("rep", bit)
        kept = lax.dynamic_slice_in_dim(values, mine * half, half, last)
        sent = lax.dynamic_slice_in_dim(values, (1 - mine) * half, half, last)
        values = kept + swap(bfloat(sent), "rep", bit).astype(jnp.float32)
    return values


def join_columns(values):
    values = bfloat(values)
    for bit in reversed(range(bit_count("rep"))):
        other = swap(values, "rep", bit)
        first = my_bit("rep", bit) == 0
        values = jnp.concatenate(
            [jnp.where(first, values, other), jnp.where(first, other, values)], axis=-1
        )
    return values.astype(jnp.float32)


def scatter_stages():
    bits = list(range(1, bit_count("win")))[::-1]
    left = bits[:-1]

    def first_stage(pair):
        return halve_columns(pair[0]), halve_blocks(pair[1], 1, bits)[0]

    def second_stage(pair):
        return halve_blocks(pair[0], 1, bits)[0], halve_columns(pair[1])

    def far_stage(number):
        def stage(values):
            if number == 0:
                values = jnp.concatenate(values, axis=1)
            rest = [other for other in left if other not in far_bits()[:number]]
            return halve_blocks(values, far_bits()[number], rest)[0]

        return stage

    return (
        [first_stage, second_stage]
        + [far_stage(number) for number in range(len(far_bits()))]
        + [lambda values: join_columns(values)[0]]
    )


def sum_over_rep(values):
    for bit in range(bit_count("rep")):
        low = bfloat(values)
        values = low.astype(jnp.float32) + swap(low, "rep", bit).astype(jnp.float32)
    return values


def off_diagonal_step(iterate, exact):
    high = bfloat(iterate)
    gram = dot_as(high, high, NT)
    if exact:
        rest = bfloat(iterate - high.astype(jnp.float32))
        gram = gram + dot_as(high, rest, NT) + dot_as(rest, high, NT)
    size = gram.shape[0]
    row_ids = lax.broadcasted_iota(jnp.int32, (size, size), 0)
    on_diagonal = row_ids == lax.broadcasted_iota(jnp.int32, (size, size), 1)
    own = jnp.where(on_diagonal, gram, 0.0)
    own_column = jnp.sum(own, 1, keepdims=True)
    own_row = jnp.sum(own, 0, keepdims=True)
    off = jnp.where(on_diagonal, 0.0, gram)
    off_low = bfloat(off)
    square = product(off_low, off_low) + (own_column + own_row) * off
    poly = NEWTON_COEFFS[1] * off + NEWTON_COEFFS[2] * square
    poly_own = jnp.sum(jnp.where(on_diagonal, poly, 0.0), 1, keepdims=True)
    factor = (
        NEWTON_COEFFS[0]
        + poly_own
        + own_column * (NEWTON_COEFFS[1] + NEWTON_COEFFS[2] * own_column)
    )
    poly = jnp.where(on_diagonal, 0.0, poly)
    poly_high = bfloat(poly)
    moved = product(poly_high, high)
    if exact:
        poly_rest = bfloat(poly - poly_high.astype(jnp.float32))
        moved = moved + product(poly_high, rest) + product(poly_rest, high)
    return factor * iterate + moved


def unit_scale(values):
    total = jnp.sum(jnp.sum(values * values, 1, keepdims=True), 0, keepdims=True)
    return values * (1.0 / (jnp.sqrt(total) + EPSILON))


def block_start(place_ref, masks, block, rows, shift=0):
    if masks is None:
        return block * rows
    return pl.multiple_of(((place_ref[1] ^ masks[block]) >> shift) * rows, rows)


def big_newton_kernel(folds, masks, place_ref, blocks_ref, out_ref, iterate_ref, turned_ref):
    blocks, rows, width = blocks_ref.shape
    part = rows // folds

    @pl.when(place_ref[0] == 0)
    def _():
        for block in range(blocks):
            for fold in range(folds):
                start = block_start(place_ref, masks, block, part)
                iterate_ref[pl.ds(start, part), fold * width : (fold + 1) * width] = blocks_ref[block, fold * part : (fold + 1) * part, :].astype(jnp.float32)

    @pl.when(place_ref[0] != 0)
    def _():
        for block in range(blocks):
            start = block_start(place_ref, masks, block, rows)
            iterate_ref[:, pl.ds(start, rows)] = blocks_ref[block].astype(jnp.float32).T

    iterate_ref[...] = unit_scale(iterate_ref[...])

    @pl.loop(0, 5)
    def _(_):
        iterate_ref[...] = off_diagonal_step(iterate_ref[...], False)

    @pl.when(place_ref[0] == 0)
    def _():
        start = pl.multiple_of(place_ref[1] * part, part)
        for fold in range(folds):
            out_ref[fold * part : (fold + 1) * part, :] = bfloat(
                iterate_ref[pl.ds(start, part), fold * width : (fold + 1) * width]
            )

    @pl.when(place_ref[0] != 0)
    def _():
        span = max(rows, 128)
        start = pl.multiple_of(place_ref[1] * rows // span * span, span)
        turned_ref[...] = iterate_ref[:, pl.ds(start, span)].T * float(folds) ** 0.5
        inner = pl.multiple_of(place_ref[1] * rows - start, rows)
        out_ref[...] = bfloat(turned_ref[pl.ds(inner, rows), :])


def small_newton_kernel(masks, place_ref, blocks_ref, out_ref, iterate_ref):
    blocks, matrices, rows, width = blocks_ref.shape
    for number in range(matrices):
        for block in range(blocks):
            start = block_start(place_ref, masks, block, rows, 1)
            iterate_ref[number, pl.ds(start, rows), :] = blocks_ref[block, number].astype(
                jnp.float32
            )

    @pl.loop(0, matrices)
    def _(number):
        iterate_ref[number] = unit_scale(iterate_ref[number])

        @pl.loop(0, 2)
        def _(_):
            iterate_ref[number] = off_diagonal_step(iterate_ref[number], False)

        @pl.loop(0, 3)
        def _(_):
            iterate_ref[number] = off_diagonal_step(iterate_ref[number], True)

    start = pl.multiple_of((place_ref[1] if masks is None else place_ref[1] >> 1) * rows, rows)
    for number in range(matrices):
        out_ref[number] = bfloat(iterate_ref[number, pl.ds(start, rows), :])


def newton_call(kernel, name, place, blocks, out_dims, scratch_dims, flops):
    return pl.pallas_call(
        kernel,
        in_specs=[
            pl.BlockSpec(memory_space=pltpu.SMEM),
            pl.BlockSpec(memory_space=pltpu.VMEM),
        ],
        out_specs=pl.BlockSpec(memory_space=pltpu.VMEM),
        out_shape=shape_of(out_dims, jnp.bfloat16),
        scratch_shapes=[pltpu.VMEM(dims, jnp.float32) for dims in scratch_dims],
        compiler_params=pltpu.CompilerParams(vmem_limit_bytes=VMEM_LIMIT),
        cost_estimate=pl.CostEstimate(
            flops=flops, bytes_accessed=2 * blocks.size, transcendentals=0
        ),
        name=name,
    )(place, blocks)


def big_update(place, blocks, folds, masks):
    win, rows, width = blocks.shape
    return newton_call(
        functools.partial(big_newton_kernel, folds, masks),
        "big_newton",
        place,
        blocks,
        (rows, width),
        [(width, win * rows), (max(rows, 128), width)],
        2 * 5 * width * width * (2 * win * rows + width),
    )


def small_update(place, blocks, masks):
    win, matrices, rows, width = blocks.shape
    return newton_call(
        functools.partial(small_newton_kernel, masks),
        "small_newton",
        place,
        blocks,
        (matrices, rows, width),
        [(matrices, width, width)],
        2 * 27 * matrices * width**3,
    )


def own_rows(matrix, rows_here):
    return lax.dynamic_slice_in_dim(matrix, lax.axis_index("win") * rows_here, rows_here, 0)


def fold_columns(rows, width):
    count, columns = rows.shape
    return rows.reshape(count, columns // width, width).swapaxes(0, 1).reshape(-1, width)


def unfold_columns(rows, folds):
    total, width = rows.shape
    return rows.reshape(folds, total // folds, width).swapaxes(0, 1).reshape(-1, folds * width)


def pick_owner(first, here, there):
    return jnp.where(first, here, there), jnp.where(first, there, here)


def every_update(place, big_rows, small_rows, folds):
    updates = []
    for number, rows in enumerate(big_rows):
        here = jnp.stack([jnp.int32(number), place[1]])
        blocks = index_order(gather_blocks(bfloat(rows)))
        updates.append(big_update(here, blocks, folds, None))
    blocks = index_order(gather_blocks(bfloat(small_rows)))
    return updates[0], updates[1], small_update(place, blocks, None)


GROUP_HEADS = 128 // HEAD_DIM
SCORE_SCALE = HEAD_DIM ** (-0.5)
LOG2_E = 1.4426950408889634
VMEM_LIMIT = 44 * 1024 * 1024
WINDOW_COST = 10**9
NT = (((1,), (1,)), ((), ()))
TN = (((0,), (0,)), ((), ()))


def dot_as(left_side, right_side, dims):
    return lax.dot_general(left_side, right_side, dims, preferred_element_type=jnp.float32)


def spread_heads(part, lane_head):
    return bfloat(
        jnp.concatenate(
            [jnp.where(lane_head == head, part, 0.0) for head in range(GROUP_HEADS)], axis=0
        )
    )


def join_heads(spread, lane_head, rows):
    joined = spread[:rows]
    for head in range(1, GROUP_HEADS):
        joined = jnp.where(lane_head == head, spread[head * rows : (head + 1) * rows], joined)
    return joined


def column_softmax(scores, bias_column):
    scores = scores + bias_column
    raised = jnp.exp2((scores - jnp.max(scores, 0, keepdims=True)) * (SCORE_SCALE * LOG2_E))
    return raised * (1.0 / jnp.sum(raised, 0, keepdims=True))


def load_windows(tokens_ref, region_ref, fill_ref, count, seq_len, padded, step):
    for window in range(count):
        base = window * padded
        fill_ref[base : base + seq_len, :] = tokens_ref[0, window].astype(jnp.float32)
        fill_ref[base : base + 1, :] = region_ref[pl.ds(step * count + window, 1), :]


def window_forward_kernel(
    count,
    seq_len,
    padded,
    tokens_ref,
    region_ref,
    bias_ref,
    keep_ref,
    qkv_ref,
    out_ref,
    vec_ref,
    norm_out,
    proj_out,
    mix_out,
    after_out,
    fill_ref,
    mix_ref,
    scores_ref,
    probs_ref,
):
    step = pl.program_id(0)
    width = tokens_ref.shape[-1]

    @pl.when(step == 0)
    def _():
        fill_ref[...] = jnp.zeros_like(fill_ref)

    load_windows(tokens_ref, region_ref, fill_ref, count, seq_len, padded, step)
    flat = fill_ref[...]
    normed = bfloat(norm_rows(flat, vec_ref[2:3, :], vec_ref[3:4, :]))
    lane_head = lax.broadcasted_iota(jnp.int32, (padded, 128), 1) // HEAD_DIM
    query = product(normed, qkv_ref[0]) + vec_ref[6:7, :]
    keyset = product(normed, qkv_ref[1])
    values = product(normed, qkv_ref[2]) + vec_ref[7:8, :]
    pairs = [(window, group) for window in range(count) for group in range(width // 128)]
    for window in range(count):
        rows = slice(window * padded, (window + 1) * padded)
        norm_out[window] = normed[rows]
        proj_out[window, :, :width] = bfloat(query[rows])
        proj_out[window, :, width : 2 * width] = bfloat(keyset[rows])
        proj_out[window, :, 2 * width :] = bfloat(values[rows])
    for number, (window, group) in enumerate(pairs):
        rows = slice(window * padded, (window + 1) * padded)
        lanes = slice(group * 128, (group + 1) * 128)
        spread = spread_heads(query[rows, lanes], lane_head)
        scores_ref[number] = dot_as(bfloat(keyset[rows, lanes]), spread, NT)
    for number, (window, group) in enumerate(pairs):
        probs_ref[number] = bfloat(column_softmax(scores_ref[number], bias_ref[window]))
    for number, (window, group) in enumerate(pairs):
        rows = slice(window * padded, (window + 1) * padded)
        lanes = slice(group * 128, (group + 1) * 128)
        mixed = dot_as(probs_ref[number], bfloat(values[rows, lanes]), TN)
        mix_ref[rows, lanes] = join_heads(mixed, lane_head, padded)
    mixed_low = bfloat(mix_ref[...])
    branch = product(mixed_low, out_ref[...]) + vec_ref[8:9, :]
    for window in range(count):
        rows = slice(window * padded, (window + 1) * padded)
        mix_out[window] = mixed_low[rows]
        after_out[window] = flat[rows] + keep_ref[window] * branch[rows]


def window_backward_kernel(
    count,
    first_step,
    last,
    seq_len,
    padded,
    tokens_ref,
    region_ref,
    bias_ref,
    keep_ref,
    qkv_ref,
    out_ref,
    vec_ref,
    proj_ref,
    after_grad_ref,
    region_keep_ref,
    sums_before_ref,
    *rest,
):
    scratch_count = 8
    if last:
        region_branch_out, region_mix_out = rest[-scratch_count - 2 : -scratch_count]
        rest = rest[: -scratch_count - 2] + rest[-scratch_count:]
    (
        region_grad_out,
        sums_out,
        grad_out,
        proj_grad_out,
        branch_grad_out,
        fill_ref,
        proj_grad_ref,
        spread_ref,
        spread_grad_ref,
        scores_ref,
        probs_grad_ref,
        probs_ref,
        score_grad_ref,
    ) = rest[-13:]
    step = pl.program_id(0) + first_step
    width = tokens_ref.shape[-1]

    @pl.when(pl.program_id(0) == 0)
    def _():
        fill_ref[...] = jnp.zeros_like(fill_ref)
        sums_out[...] = sums_before_ref[...]
        if first_step == 0:
            region_grad_out[...] = jnp.zeros_like(region_grad_out)
        else:
            region_grad_out[...] = rest[0][...]

    load_windows(tokens_ref, region_ref, fill_ref, count, seq_len, padded, step)
    lane_head = lax.broadcasted_iota(jnp.int32, (padded, 128), 1) // HEAD_DIM
    branch_grad = bfloat(
        jnp.concatenate(
            [keep_ref[window] * after_grad_ref[window] for window in range(count)], axis=0
        )
    )
    mix_grad = dot_as(branch_grad, out_ref[...], NT)
    for window in range(count):
        branch_grad_out[window] = branch_grad[window * padded : (window + 1) * padded]
    pairs = [(window, group) for window in range(count) for group in range(width // 128)]

    def lanes_of(part, group):
        return slice(part * width + group * 128, part * width + (group + 1) * 128)

    for number, (window, group) in enumerate(pairs):
        query = proj_ref[window, :, lanes_of(0, group)].astype(jnp.float32)
        spread_ref[number] = spread_heads(query, lane_head)
        rows = slice(window * padded, (window + 1) * padded)
        spread_grad_ref[number] = spread_heads(mix_grad[rows, lanes_of(0, group)], lane_head)
    for number, (window, group) in enumerate(pairs):
        scores_ref[number] = dot_as(
            proj_ref[window, :, lanes_of(1, group)], spread_ref[number], NT
        )
        probs_grad_ref[number] = dot_as(
            proj_ref[window, :, lanes_of(2, group)], spread_grad_ref[number], NT
        )
    for number, (window, group) in enumerate(pairs):
        probs = column_softmax(scores_ref[number], bias_ref[window])
        weighted = probs * probs_grad_ref[number]
        probs_ref[number] = bfloat(probs)
        score_grad_ref[number] = bfloat(weighted - probs * jnp.sum(weighted, 0, keepdims=True))
    for number, (window, group) in enumerate(pairs):
        rows = slice(window * padded, (window + 1) * padded)
        proj_grad_ref[rows, lanes_of(2, group)] = product(
            probs_ref[number], spread_grad_ref[number]
        )
        proj_grad_ref[rows, lanes_of(1, group)] = (
            product(score_grad_ref[number], spread_ref[number]) * SCORE_SCALE
        )
    for number, (window, group) in enumerate(pairs):
        rows = slice(window * padded, (window + 1) * padded)
        query_grad = dot_as(score_grad_ref[number], proj_ref[window, :, lanes_of(1, group)], TN)
        proj_grad_ref[rows, lanes_of(0, group)] = (
            join_heads(query_grad, lane_head, padded) * SCORE_SCALE
        )
    proj_grad = bfloat(proj_grad_ref[...])
    norm_grad = sum(
        dot_as(proj_grad[:, number * width : (number + 1) * width], qkv_ref[number], NT)
        for number in range(3)
    )
    flat = fill_ref[...]
    center = flat - jnp.mean(flat, -1, keepdims=True)
    scale = lax.rsqrt(jnp.mean(center * center, -1, keepdims=True) + EPSILON)
    hat = center * scale
    hat_grad = norm_grad * vec_ref[2:3, :]
    flat_grad = scale * (
        hat_grad
        - jnp.mean(hat_grad, -1, keepdims=True)
        - hat * jnp.mean(hat_grad * hat, -1, keepdims=True)
    )
    proj_sums = jnp.sum(proj_grad.astype(jnp.float32), 0, keepdims=True)
    sums_out[2:3, :] += jnp.sum(norm_grad * hat, 0, keepdims=True)
    sums_out[3:4, :] += jnp.sum(norm_grad, 0, keepdims=True)
    sums_out[6:7, :] += proj_sums[:, :width]
    sums_out[7:8, :] += proj_sums[:, 2 * width :]
    sums_out[8:9, :] += jnp.sum(branch_grad.astype(jnp.float32), 0, keepdims=True)
    for window in range(count):
        rows = slice(window * padded, (window + 1) * padded)
        proj_grad_out[window] = proj_grad[rows]
        seq_grad = after_grad_ref[window] + flat_grad[rows]
        for group in range(width // 128):
            lanes = slice(group * 128, (group + 1) * 128)
            grad_out[window, pl.ds(group, seq_len, stride=width // 128), :] = seq_grad[
                :seq_len, lanes
            ]
        region_grad_out[pl.ds(step * count + window, 1), :] = seq_grad[0:1]

    if last:

        @pl.when(pl.program_id(0) == pl.num_programs(0) - 1)
        def _():
            region_branch = bfloat(region_keep_ref[...] * region_grad_out[...])
            sums_out[8:9, :] += jnp.sum(region_branch.astype(jnp.float32), 0, keepdims=True)
            region_branch_out[...] = region_branch
            region_mix_out[...] = bfloat(dot_as(region_branch, out_ref[...], NT))


def window_step(windows):
    return next(count for count in (4, 2, 1) if windows % count == 0)


def whole_spec(shape):
    return pl.BlockSpec(shape, lambda step: (0,) * len(shape))


def step_spec(count, *rest):
    return pl.BlockSpec((count,) + rest, lambda step: (step,) + (0,) * len(rest))


def token_spec(count, *rest):
    return pl.BlockSpec((1, count) + rest, lambda step: (0, step) + (0,) * len(rest))


def kept_spec():
    return pl.BlockSpec(memory_space=pltpu.VMEM)


def in_hbm(values):
    return pltpu.with_memory_space_constraint(values, pltpu.HBM)


def hbm_shape(dims, kind=jnp.float32):
    return pltpu.HBM(dims, kind)


def shape_of(dims, kind=jnp.float32):
    return jax.ShapeDtypeStruct(dims, kind)


def window_forward(tokens, region, bias, keep, qkv_weight, out_weight, vectors, padded):
    _, windows, seq_len, width = tokens.shape
    count = window_step(windows)
    pairs = count * width // 128
    return pl.pallas_call(
        functools.partial(window_forward_kernel, count, seq_len, padded),
        grid=(windows // count,),
        in_specs=[
            token_spec(count, seq_len, width),
            whole_spec(region.shape),
            step_spec(count, padded, 1),
            step_spec(count, 1, 1),
            kept_spec(),
            kept_spec(),
            whole_spec(vectors.shape),
        ],
        out_specs=[
            step_spec(count, padded, width),
            step_spec(count, padded, 3 * width),
            step_spec(count, padded, width),
            step_spec(count, padded, width),
        ],
        out_shape=[
            hbm_shape((windows, padded, width), jnp.bfloat16),
            hbm_shape((windows, padded, 3 * width), jnp.bfloat16),
            hbm_shape((windows, padded, width), jnp.bfloat16),
            hbm_shape((windows, padded, width)),
        ],
        scratch_shapes=[
            pltpu.VMEM((count * padded, width), jnp.float32),
            pltpu.VMEM((count * padded, width), jnp.float32),
            pltpu.VMEM((pairs, padded, GROUP_HEADS * padded), jnp.float32),
            pltpu.VMEM((pairs, padded, GROUP_HEADS * padded), jnp.bfloat16),
        ],
        compiler_params=pltpu.CompilerParams(vmem_limit_bytes=VMEM_LIMIT),
        name="window_forward",
    )(in_hbm(tokens), region, bias, keep, qkv_weight, out_weight, vectors)


def window_backward(
    tokens,
    region,
    bias,
    keep,
    qkv_weight,
    out_weight,
    vectors,
    proj,
    after_grad,
    region_keep,
    before,
    steps,
    padded,
):
    _, windows, seq_len, width = tokens.shape
    count = window_step(windows)
    first_step, last_step = steps
    here = (last_step - first_step) * count
    pairs = count * width // 128
    spread_rows = GROUP_HEADS * padded

    def moved(*dims, lead=0):
        zeros = (0,) * (len(dims) - 1)
        if lead:
            return pl.BlockSpec((1,) + dims, lambda step: (0, step + first_step) + zeros)
        return pl.BlockSpec(dims, lambda step: (step + first_step,) + zeros)

    flat_rows = seq_len * width // 128

    grad_before, sums_before, region_before = before
    operands = [in_hbm(tokens), region, bias, keep, qkv_weight, out_weight, vectors]
    operands += [in_hbm(proj), in_hbm(after_grad), region_keep, in_hbm(sums_before)]
    in_specs = [
        moved(count, seq_len, width, lead=1),
        whole_spec(region.shape),
        moved(count, padded, 1),
        moved(count, 1, 1),
        kept_spec(),
        kept_spec(),
        whole_spec(vectors.shape),
        moved(count, padded, 3 * width),
        moved(count, padded, width),
        whole_spec(region_keep.shape),
        whole_spec(sums_before.shape),
    ]
    aliases = {}
    if first_step:
        aliases = {len(operands) + 1: 2}
        operands += [in_hbm(region_before), in_hbm(grad_before)]
        in_specs += [whole_spec(region.shape), pl.BlockSpec(memory_space=pl.ANY)]
    last = last_step * count == windows
    out_specs = [
        whole_spec(region.shape),
        whole_spec(vectors.shape),
        moved(count, flat_rows, 128),
        step_spec(count, padded, 3 * width),
        step_spec(count, padded, width),
    ]
    out_shape = [
        hbm_shape(region.shape),
        hbm_shape(vectors.shape),
        hbm_shape((windows, flat_rows, 128)),
        hbm_shape((here, padded, 3 * width), jnp.bfloat16),
        hbm_shape((here, padded, width), jnp.bfloat16),
    ]
    if last:
        out_specs += [whole_spec(region.shape)] * 2
        out_shape += [shape_of(region.shape, jnp.bfloat16)] * 2
    return pl.pallas_call(
        functools.partial(window_backward_kernel, count, first_step, last, seq_len, padded),
        grid=(last_step - first_step,),
        in_specs=in_specs,
        out_specs=out_specs,
        out_shape=out_shape,
        scratch_shapes=[
            pltpu.VMEM((count * padded, width), jnp.float32),
            pltpu.VMEM((count * padded, 3 * width), jnp.float32),
            pltpu.VMEM((pairs, spread_rows, 128), jnp.bfloat16),
            pltpu.VMEM((pairs, spread_rows, 128), jnp.bfloat16),
            pltpu.VMEM((pairs, padded, spread_rows), jnp.float32),
            pltpu.VMEM((pairs, padded, spread_rows), jnp.float32),
            pltpu.VMEM((pairs, padded, spread_rows), jnp.bfloat16),
            pltpu.VMEM((pairs, padded, spread_rows), jnp.bfloat16),
        ],
        input_output_aliases=aliases,
        compiler_params=pltpu.CompilerParams(vmem_limit_bytes=VMEM_LIMIT),
        cost_estimate=pl.CostEstimate(
            flops=here * WINDOW_COST, bytes_accessed=here * padded * width * 20, transcendentals=0
        ),
        name="window_backward",
    )(*operands)


def insert_kernel(rows_ref, region_ref, out_ref):
    out_ref[...] = rows_ref[...]
    for window in range(rows_ref.shape[0]):
        for group in range(region_ref.shape[1] // 128):
            out_ref[window, group : group + 1, :] = region_ref[
                window : window + 1, group * 128 : (group + 1) * 128
            ]


def insert_regions(grad, region_grad):
    rows = pl.BlockSpec((grad.shape[0], 8, 128), lambda step: (0, 0, 0))
    return pl.pallas_call(
        insert_kernel,
        grid=(1,),
        in_specs=[rows, whole_spec(region_grad.shape)],
        out_specs=rows,
        out_shape=shape_of(grad.shape),
        input_output_aliases={0: 0},
        compiler_params=pltpu.CompilerParams(vmem_limit_bytes=VMEM_LIMIT),
        name="insert_regions",
    )(grad, region_grad)


GELU_IN = 0.7978845608028654
GELU_CUBE = 0.044715


def gelu_both(values):
    square = values * values
    bent = jnp.tanh(values * (GELU_IN + (GELU_IN * GELU_CUBE) * square))
    share = 0.5 + 0.5 * bent
    slope = share + (0.5 * values) * (1.0 - bent * bent) * (
        GELU_IN + (3.0 * GELU_IN * GELU_CUBE) * square
    )
    return values * share, slope


def split_cores(values, core):
    own_first = core == 0
    kept = jnp.where(own_first, values[:, 0], values[:, 1])
    sent = jnp.where(own_first, values[:, 1], values[:, 0])
    return kept, bfloat(sent)


def mlp_kernel(
    count,
    seq_len,
    padded,
    place_ref,
    after_ref,
    cot_ref,
    keep_ref,
    vec_ref,
    up_ref,
    down_ref,
    out_ref,
    grad_ref,
    sums_ref,
    up_kept,
    up_sent,
    down_kept,
    down_sent,
    cot_fill,
    up_total,
    down_total,
):
    step = pl.program_id(0)
    width = up_ref.shape[0]
    folds = up_ref.shape[1] // width

    @pl.when(step == 0)
    def _():
        cot_fill[...] = jnp.zeros_like(cot_fill)
        sums_ref[...] = jnp.zeros_like(sums_ref)
        up_total[...] = jnp.zeros_like(up_total)
        down_total[...] = jnp.zeros_like(down_total)

    keeps = []
    for window in range(count):
        base = window * padded
        cot_fill[base : base + seq_len, :] = cot_ref[0, window].astype(jnp.float32)
        keeps.append(jnp.broadcast_to(keep_ref[window], (padded, 1)))
    keep = jnp.concatenate(keeps, axis=0)
    flat = after_ref[...]
    center = flat - jnp.mean(flat, -1, keepdims=True)
    scale = lax.rsqrt(jnp.mean(center * center, -1, keepdims=True) + EPSILON)
    hat = center * scale
    normed = bfloat(hat * vec_ref[4:5, :] + vec_ref[5:6, :])
    normed_turned = normed.T
    cot = cot_fill[...]
    branch_grad = bfloat(keep * cot)
    branch = jnp.zeros_like(flat)
    norm_grad = jnp.zeros_like(flat)
    for fold in range(folds):
        lanes = slice(fold * width, (fold + 1) * width)
        up_part, down_part = up_ref[:, lanes], down_ref[lanes, :]
        hidden = product(normed, up_part) + vec_ref[10 + fold : 11 + fold, :]
        act, slope = gelu_both(hidden)
        act = bfloat(act)
        branch += product(act, down_part)
        hidden_grad = bfloat(slope * dot_as(branch_grad, down_part, NT))
        norm_grad += dot_as(hidden_grad, up_part, NT)
        up_total[fold] += product(normed_turned, hidden_grad)
        down_total[fold] += dot_as(act, branch_grad, TN)
        sums_ref[10 + fold : 11 + fold, :] += jnp.sum(
            hidden_grad.astype(jnp.float32), 0, keepdims=True
        )
    output = bfloat(flat + keep * (branch + vec_ref[9:10, :]))
    hat_grad = norm_grad * vec_ref[4:5, :]
    flat_grad = cot + scale * (
        hat_grad
        - jnp.mean(hat_grad, -1, keepdims=True)
        - hat * jnp.mean(hat_grad * hat, -1, keepdims=True)
    )
    sums_ref[4:5, :] += jnp.sum(norm_grad * hat, 0, keepdims=True)
    sums_ref[5:6, :] += jnp.sum(norm_grad, 0, keepdims=True)
    sums_ref[9:10, :] += jnp.sum(branch_grad.astype(jnp.float32), 0, keepdims=True)
    grad_ref[...] = flat_grad
    for window in range(count):
        out_ref[0, window] = output[window * padded : window * padded + seq_len]

    @pl.when(step == pl.num_programs(0) - 1)
    def _():
        core = place_ref[1] % 2
        blocks, _, rows, _ = up_kept.shape
        for fold in range(folds):
            total = up_total[fold].reshape(blocks, 2, rows, width)
            up_kept[:, fold], up_sent[:, fold] = split_cores(total, core)
        blocks, rows, _ = down_kept.shape
        here = blocks // folds
        for fold in range(folds):
            total = down_total[fold].reshape(here, 2, rows, width)
            part = slice(fold * here, (fold + 1) * here)
            down_kept[part], down_sent[part] = split_cores(total, core)


def mlp(place, after, cotangent, keep, vectors, up_weight, down_weight, padded, win_count):
    _, windows, seq_len, width = cotangent.shape
    count = window_step(windows)
    rows = count * padded
    folds = up_weight.shape[1] // width
    half = win_count // 2
    up_rows = width // win_count
    up_dims = (half, folds, up_rows, width)
    down_dims = (half, up_rows * folds, width)
    flat_rows = pl.BlockSpec((rows, width), lambda step: (step, 0))
    output, grad, sums, kept_up, sent_up, kept_down, sent_down = pl.pallas_call(
        functools.partial(mlp_kernel, count, seq_len, padded),
        grid=(windows // count,),
        in_specs=[
            pl.BlockSpec(memory_space=pltpu.SMEM),
            flat_rows,
            token_spec(count, seq_len, width),
            step_spec(count, 1, 1),
            whole_spec(vectors.shape),
            kept_spec(),
            kept_spec(),
        ],
        out_specs=[
            token_spec(count, seq_len, width),
            flat_rows,
            whole_spec(vectors.shape),
            whole_spec(up_dims),
            whole_spec(up_dims),
            whole_spec(down_dims),
            whole_spec(down_dims),
        ],
        out_shape=[
            hbm_shape(cotangent.shape, jnp.bfloat16),
            hbm_shape(after.shape),
            hbm_shape(vectors.shape),
            hbm_shape(up_dims),
            hbm_shape(up_dims, jnp.bfloat16),
            hbm_shape(down_dims),
            hbm_shape(down_dims, jnp.bfloat16),
        ],
        scratch_shapes=[
            pltpu.VMEM((rows, width), jnp.float32),
            pltpu.VMEM((folds, width, width), jnp.float32),
            pltpu.VMEM((folds, width, width), jnp.float32),
        ],
        compiler_params=pltpu.CompilerParams(vmem_limit_bytes=VMEM_LIMIT),
        cost_estimate=pl.CostEstimate(
            flops=12 * after.size * width * folds,
            bytes_accessed=16 * after.size,
            transcendentals=0,
        ),
        name="mlp",
    )(place, in_hbm(after), in_hbm(cotangent), keep, vectors, up_weight, down_weight)
    up_half = (kept_up.reshape(down_dims), sent_up.reshape(down_dims))
    return output, grad, sums, up_half, (kept_down, sent_down)


def image_bias(keys_ref, queries_ref):
    return jnp.where(keys_ref[...] == queries_ref[...], 0.0, -1e30)


def region_forward_kernel(
    all_ref,
    own_ref,
    keep_ref,
    key_image_ref,
    query_image_ref,
    qkv_ref,
    out_ref,
    vec_ref,
    norm_out,
    proj_out,
    mix_out,
    new_out,
):
    rows, width = own_ref.shape
    vec = vec_ref[...]
    normed = bfloat(norm_rows(all_ref[...].astype(jnp.float32), vec[0:1], vec[1:2]))
    norm_out[...] = normed
    query = bfloat(product(normed, qkv_ref[0]) + vec[6:7])
    keyset = bfloat(product(normed, qkv_ref[1]))
    values = bfloat(product(normed, qkv_ref[2]) + vec[7:8])
    proj_out[:, :width] = query
    proj_out[:, width : 2 * width] = keyset
    proj_out[:, 2 * width :] = values
    region = own_ref[...].astype(jnp.float32)
    own_norm = bfloat(norm_rows(region, vec[0:1], vec[1:2]))
    own_query = product(own_norm, qkv_ref[0]) + vec[6:7]
    bias = image_bias(key_image_ref, query_image_ref)
    lane_head = lax.broadcasted_iota(jnp.int32, (rows, 128), 1) // HEAD_DIM
    parts = []
    for group in range(width // 128):
        lanes = slice(group * 128, (group + 1) * 128)
        spread = spread_heads(own_query[:, lanes], lane_head)
        probs = column_softmax(dot_as(keyset[:, lanes], spread, NT), bias)
        mixed = dot_as(bfloat(probs), values[:, lanes], TN)
        parts.append(join_heads(mixed, lane_head, rows))
    mixed_low = bfloat(jnp.concatenate(parts, axis=1))
    mix_out[...] = mixed_low
    branch = product(mixed_low, out_ref[...]) + vec[8:9]
    new_out[...] = region + keep_ref[...] * branch


def region_forward(all_rows, own_rows_, keep, key_images, query_images, qkv_weight, out_weight, vectors):
    total, width = all_rows.shape
    return pl.pallas_call(
        region_forward_kernel,
        out_shape=[
            hbm_shape((total, width), jnp.bfloat16),
            hbm_shape((total, 3 * width), jnp.bfloat16),
            hbm_shape(own_rows_.shape, jnp.bfloat16),
            shape_of(own_rows_.shape),
        ],
        compiler_params=pltpu.CompilerParams(vmem_limit_bytes=VMEM_LIMIT),
        name="region_forward",
    )(all_rows, own_rows_, keep, key_images, query_images, qkv_weight, out_weight, vectors)


def region_backward_kernel(
    place_ref,
    all_ref,
    norm_ref,
    proj_ref,
    mix_grad_ref,
    key_image_ref,
    query_image_ref,
    new_grad_ref,
    qkv_ref,
    vec_ref,
    grad_out,
    weight_out,
    sums_out,
    bias_ref,
    proj_grad_ref,
    region_grad_ref,
    weight_ref,
    scores_ref,
    probs_grad_ref,
    probs_ref,
    score_grad_ref,
):
    total, width = all_ref.shape
    rows = new_grad_ref.shape[0]
    bias_ref[...] = image_bias(key_image_ref, query_image_ref)
    lane_head = lax.broadcasted_iota(jnp.int32, (total, 128), 1) // HEAD_DIM

    @pl.loop(0, width // 128)
    def _(group):
        query_lanes = pl.ds(pl.multiple_of(group * 128, 128), 128)
        key_lanes = pl.ds(pl.multiple_of(width + group * 128, 128), 128)
        value_lanes = pl.ds(pl.multiple_of(2 * width + group * 128, 128), 128)
        query = proj_ref[:, query_lanes]
        key_low = proj_ref[:, key_lanes]
        value_low = proj_ref[:, value_lanes]
        mix_grad = mix_grad_ref[:, query_lanes]
        heads = range(GROUP_HEADS)
        head_query = [jnp.where(lane_head == head, query, jnp.zeros_like(query)) for head in heads]
        head_grad = [
            jnp.where(lane_head == head, mix_grad, jnp.zeros_like(mix_grad)) for head in heads
        ]
        for head in heads:
            scores_ref[head] = dot_as(key_low, head_query[head], NT)
            probs_grad_ref[head] = dot_as(value_low, head_grad[head], NT)
        for head in heads:
            probs = column_softmax(scores_ref[head], bias_ref[...])
            weighted = probs * probs_grad_ref[head]
            probs_ref[head] = bfloat(probs)
            score_grad_ref[head] = bfloat(weighted - probs * jnp.sum(weighted, 0, keepdims=True))
        zero = jnp.zeros((total, 128), jnp.float32)
        value_grad = sum((product(probs_ref[head], head_grad[head]) for head in heads), zero)
        key_grad = sum((product(score_grad_ref[head], head_query[head]) for head in heads), zero)
        query_grad = zero
        for head in heads:
            head_part = dot_as(score_grad_ref[head], key_low, TN)
            query_grad = jnp.where(lane_head == head, head_part, query_grad)
        proj_grad_ref[:, query_lanes] = bfloat(query_grad * SCORE_SCALE)
        proj_grad_ref[:, key_lanes] = bfloat(key_grad * SCORE_SCALE)
        proj_grad_ref[:, value_lanes] = bfloat(value_grad)

    proj_grad = proj_grad_ref[...]
    norm_grad = sum(
        dot_as(proj_grad[:, number * width : (number + 1) * width], qkv_ref[number], NT)
        for number in range(3)
    )
    region = all_ref[...].astype(jnp.float32)
    center = region - jnp.mean(region, -1, keepdims=True)
    scale = lax.rsqrt(jnp.mean(center * center, -1, keepdims=True) + EPSILON)
    hat = center * scale
    hat_grad = norm_grad * vec_ref[0:1, :]
    region_grad_ref[...] = scale * (
        hat_grad
        - jnp.mean(hat_grad, -1, keepdims=True)
        - hat * jnp.mean(hat_grad * hat, -1, keepdims=True)
    )
    grad_out[...] = new_grad_ref[...] + region_grad_ref[:rows, :]
    bias_sums = jnp.sum(proj_grad.astype(jnp.float32), 0, keepdims=True)
    sums_out[...] = jnp.zeros_like(sums_out)
    sums_out[0:1, :] = jnp.sum(norm_grad * hat, 0, keepdims=True)
    sums_out[1:2, :] = jnp.sum(norm_grad, 0, keepdims=True)
    sums_out[6:7, :] = bias_sums[:, :width]
    sums_out[7:8, :] = bias_sums[:, 2 * width :]
    weight_ref[...] = dot_as(norm_ref[...], proj_grad, TN)
    weight_rows = weight_out.shape[1]
    weight_start = pl.multiple_of(place_ref[1] * weight_rows, 8)
    for number in range(3):
        weight_out[number] = weight_ref[
            pl.ds(weight_start, weight_rows), number * width : (number + 1) * width
        ]


def region_backward(
    place, all_rows, normed, proj, mix_grad, key_images, query_images, new_grad, qkv_weight, vectors, weight_rows
):
    total, width = all_rows.shape
    vmem = pl.BlockSpec(memory_space=pltpu.VMEM)
    return pl.pallas_call(
        region_backward_kernel,
        in_specs=[pl.BlockSpec(memory_space=pltpu.SMEM)] + [vmem] * 9,
        out_specs=[vmem] * 3,
        out_shape=[
            shape_of(new_grad.shape),
            shape_of((3, weight_rows, width)),
            shape_of(vectors.shape),
        ],
        scratch_shapes=[
            pltpu.VMEM((total, total), jnp.float32),
            pltpu.VMEM((total, 3 * width), jnp.bfloat16),
            pltpu.VMEM((total, width), jnp.float32),
            pltpu.VMEM((width, 3 * width), jnp.float32),
            pltpu.VMEM((GROUP_HEADS, total, total), jnp.float32),
            pltpu.VMEM((GROUP_HEADS, total, total), jnp.float32),
            pltpu.VMEM((GROUP_HEADS, total, total), jnp.bfloat16),
            pltpu.VMEM((GROUP_HEADS, total, total), jnp.bfloat16),
        ],
        compiler_params=pltpu.CompilerParams(vmem_limit_bytes=VMEM_LIMIT),
        name="region_backward",
    )(place, all_rows, normed, proj, mix_grad, key_images, query_images, new_grad, qkv_weight, vectors)


def small_gradient_kernel(pieces, place_ref, *refs):
    norm_refs = refs[:pieces]
    proj_grad_refs = refs[pieces : 2 * pieces]
    mix_refs = refs[2 * pieces : 3 * pieces]
    branch_refs = refs[3 * pieces : 4 * pieces]
    region_mix_ref, region_branch_ref, kept, sent = refs[4 * pieces :]
    core = place_ref[1] % 2
    number = pl.program_id(0)
    blocks, _, rows, width = kept.shape

    def write(total):
        kept[:, 0], sent[:, 0] = split_cores(total.reshape(blocks, 2, rows, width), core)

    @pl.when(number < 3)
    def _():
        write(
            sum(
                dot_as(norm_ref[...], grad_ref[...], TN)
                for norm_ref, grad_ref in zip(norm_refs, proj_grad_refs)
            )
        )

    @pl.when(number == 3)
    def _():
        write(
            sum(
                dot_as(mix_ref[...], branch_ref[...], TN)
                for mix_ref, branch_ref in zip(mix_refs, branch_refs)
            )
            + dot_as(region_mix_ref[...], region_branch_ref[...], TN)
        )


def small_gradients(place, normed, proj_grads, mix, branches, region_mix, region_branch, win_count):
    width = normed.shape[1]
    half = win_count // 2
    weight_rows = width // win_count
    pieces = len(proj_grads)
    operands, in_specs = [place], [pl.BlockSpec(memory_space=pltpu.SMEM)]

    def add_rows(whole):
        start = 0
        for piece in branches:
            here = piece.shape[0]
            if start % here:
                operands.append(whole[start : start + here])
                block = 0
            else:
                operands.append(in_hbm(whole))
                block = start // here
            in_specs.append(pl.BlockSpec(piece.shape, lambda number, block=block: (block, 0)))
            start += here

    add_rows(normed)
    for piece in proj_grads:
        operands.append(in_hbm(piece))
        in_specs.append(
            pl.BlockSpec((piece.shape[0], width), lambda number: (0, jnp.minimum(number, 2)))
        )
    add_rows(mix)
    for piece in branches + [region_mix, region_branch]:
        operands.append(in_hbm(piece))
        in_specs.append(pl.BlockSpec(piece.shape, lambda number: (0, 0)))
    out_spec = pl.BlockSpec((half, 1, weight_rows, width), lambda number: (0, number, 0, 0))
    dims = (half, 4, weight_rows, width)
    rows = normed.shape[0]
    kept, sent = pl.pallas_call(
        functools.partial(small_gradient_kernel, pieces),
        grid=(4,),
        in_specs=in_specs,
        out_specs=[out_spec, out_spec],
        out_shape=[hbm_shape(dims), hbm_shape(dims, jnp.bfloat16)],
        compiler_params=pltpu.CompilerParams(vmem_limit_bytes=VMEM_LIMIT),
        cost_estimate=pl.CostEstimate(
            flops=8 * rows * width * width,
            bytes_accessed=12 * rows * width + 24 * width * width,
            transcendentals=0,
        ),
        name="small_gradients",
    )(*operands)
    flat = (half, 4 * weight_rows, width)
    return kept.reshape(flat), sent.reshape(flat)


def core_hop(kept, sent):
    return kept + swap(sent, "win", 0).astype(jnp.float32)


def local(
    tokens,
    patch_mask,
    keep_mask,
    image_map,
    qkv_weight,
    out_weight,
    up_weight,
    down_weight,
    vectors,
    qkv_mom,
    out_mom,
    up_mom,
    down_mom,
    vec_mom,
    cotangent,
):
    windows = tokens.shape[1]
    seq_len = tokens.shape[2]
    model_width = tokens.shape[3]
    hidden_width = up_weight.shape[1]
    folds = hidden_width // model_width
    shard_rows = out_mom.shape[0]
    ff_rows = down_mom.shape[0]
    vec_rows = vec_mom.shape[0]
    padded = (seq_len + 7) // 8 * 8
    region_rows = (windows + 7) // 8 * 8
    row_count = windows * padded
    win_count = lax.axis_size("win")
    win_index = lax.axis_index("win")
    place = jnp.stack([lax.axis_index("rep"), win_index]).astype(jnp.int32)

    def pad_rows(values, rows, fill=0):
        widths = ((0, rows - values.shape[0]),) + ((0, 0),) * (values.ndim - 1)
        return jnp.pad(values, widths, constant_values=fill)

    region_own = pad_rows(tokens[0, :, 0], region_rows)
    region_all = gather_blocks(region_own).reshape(-1, model_width)
    keeper = keep_mask[0].astype(jnp.float32) / KEEP_SHARE
    images = image_map[0].reshape(win_count, windows)[win_index ^ jnp.array(gather_masks())]
    images = jnp.pad(images, ((0, 0), (0, region_rows - windows)), constant_values=-1)
    key_images = images.reshape(-1, 1)
    own_images = jnp.tile(images[:1], (1, GROUP_HEADS))
    region_keep = pad_rows(keeper[:, 0:1], region_rows)

    region_norm, region_proj, region_mix, region_new = region_forward(
        region_all, region_own, region_keep, key_images, own_images, qkv_weight, out_weight, vectors
    )

    key_valid = jnp.concatenate([jnp.ones((windows, 1), jnp.int32), patch_mask[0]], axis=1) == 1
    key_bias = jnp.where(key_valid, 0.0, -1e30)
    key_bias = jnp.pad(key_bias, ((0, 0), (0, padded - seq_len)), constant_values=-1e30)
    key_bias = key_bias[:, :, None]
    keep_window = keeper[:, 1].reshape(windows, 1, 1)
    seq_norm, seq_proj, local_mix, after_attn = window_forward(
        tokens, region_new, key_bias, keep_window, qkv_weight, out_weight, vectors, padded
    )
    seq_norm = seq_norm.reshape(row_count, model_width)
    local_mix = local_mix.reshape(row_count, model_width)
    after_attn = after_attn.reshape(row_count, model_width)

    out_tokens, attn_res_grad, mlp_sums, up_half, down_half = mlp(
        place,
        after_attn,
        cotangent,
        keeper[:, 2].reshape(windows, 1, 1),
        vectors,
        up_weight,
        down_weight,
        padded,
        win_count,
    )

    steps = windows // window_step(windows)
    cuts = [0, steps * 2 // 5, steps * 4 // 5, steps]
    after_grad = attn_res_grad.reshape(windows, padded, model_width)
    big = Chain(
        (up_half, down_half),
        [lambda halves: (core_hop(*halves[0]), core_hop(*halves[1]))] + scatter_stages(),
    )
    before = (None, mlp_sums, None)
    proj_grads, branch_grads = [], []
    for piece in range(3):
        region_new_grad, sums, seq_grad, proj_grad, branch_grad, *region_parts = window_backward(
            tokens,
            region_new,
            key_bias,
            keep_window,
            qkv_weight,
            out_weight,
            vectors,
            seq_proj,
            after_grad,
            region_keep,
            before,
            (cuts[piece], cuts[piece + 1]),
            padded,
        )
        before = (seq_grad, sums, region_new_grad)
        proj_grads.append(proj_grad.reshape(-1, 3 * model_width))
        branch_grads.append(branch_grad.reshape(-1, model_width))
        big.step()
        if piece < 2:
            big.value, after_grad = tie(big.value, after_grad)
    region_branch_grad, region_mix_grad = region_parts

    small_kept, small_sent = small_gradients(
        place,
        seq_norm,
        proj_grads,
        local_mix,
        branch_grads,
        region_mix,
        region_branch_grad,
        win_count,
    )
    core = win_index % 2
    vector_pairs = sums.reshape(win_count // 2, 2, 1, vec_rows)
    vector_pairs = jnp.pad(
        vector_pairs, ((0, 0), (0, 0), (0, 7), (0, model_width - vec_rows))
    )
    small_kept = jnp.concatenate(
        [small_kept, lax.dynamic_index_in_dim(vector_pairs, core, 1, keepdims=False)], axis=1
    )
    small_sent = jnp.concatenate(
        [
            small_sent,
            bfloat(lax.dynamic_index_in_dim(vector_pairs, 1 - core, 1, keepdims=False)),
        ],
        axis=1,
    )

    def split_pair(halves):
        total = core_hop(*halves)
        return total[:, : 2 * shard_rows], total[:, 2 * shard_rows :]

    small = Chain((small_kept, small_sent), [split_pair] + scatter_stages())
    mixes = Chain(region_mix_grad, gather_stages())
    for _ in range(3):
        step_together(big, small, mixes)

    region_grad, region_weight_grad, region_sums = region_backward(
        place,
        region_all,
        region_norm,
        region_proj,
        mixes.value.reshape(-1, model_width),
        key_images,
        key_images.reshape(1, -1),
        region_new_grad,
        qkv_weight,
        vectors,
        shard_rows,
    )
    input_grad = insert_regions(seq_grad, region_grad).reshape(tokens.shape)
    region_vectors = jnp.pad(
        lax.dynamic_slice_in_dim(region_sums.reshape(-1), win_index * vec_rows, vec_rows)[None],
        ((0, 7), (0, model_width - vec_rows)),
    )
    region_part = Chain(
        jnp.concatenate([region_weight_grad.reshape(-1, model_width), region_vectors], axis=0),
        [sum_over_rep],
    )

    first = lax.axis_index("rep") == 0
    low_core = core == 0
    two_owners = lax.axis_size("rep") == 2
    while big.stages:
        big.step()
    folded_up_mom = MOMENTUM_DECAY * fold_columns(up_mom, model_width) + big.value[:ff_rows]
    new_down_mom = MOMENTUM_DECAY * down_mom + big.value[ff_rows:]
    if two_owners:
        big = Chain(bfloat(jnp.where(first, folded_up_mom, new_down_mom)), gather_stages())
        big.step()
        small.step()
        big.value, small.value, region_part.value = tie(
            big.value, small.value, region_part.value
        )
        step_together(big, small, region_part)
        step_together(big, small)
    while small.stages or region_part.stages:
        small.step()
        region_part.step()
    small_total, region_total = small.value, region_part.value
    matrix_rows = 4 * shard_rows
    region_matrix = region_total[: 3 * shard_rows].reshape(3, shard_rows, model_width)
    small_matrix = small_total[:matrix_rows].reshape(4, shard_rows, model_width)
    new_qkv_mom = MOMENTUM_DECAY * qkv_mom + (small_matrix[:3] + region_matrix)
    new_out_mom = MOMENTUM_DECAY * out_mom + small_matrix[3]
    vec_total = small_total[matrix_rows, :vec_rows] + region_total[3 * shard_rows, :vec_rows]
    new_vec_mom = MOMENTUM_DECAY * vec_mom + vec_total
    new_vectors = (
        lax.dynamic_slice_in_dim(vectors.reshape(-1), win_index * vec_rows, vec_rows)
        - VECTOR_RATE * new_vec_mom
    )
    new_up_mom = unfold_columns(folded_up_mom, folds)
    small_rows = jnp.concatenate([new_qkv_mom, new_out_mom[None]])
    if two_owners:
        pair = bfloat(jnp.where(first, small_rows[:2], small_rows[2:]))
        kept, sent = pick_owner(low_core, pair[0], pair[1])
        shards = jnp.concatenate(pick_owner(low_core, kept, swap(sent, "win", 0)))
        shards, big.value = tie(shards, big.value)
        small = Chain(shards, gather_stages(1))
        small.step()
        big_mine = big_update(place, big.value, folds, gather_masks())
        big_mine, small.value = tie(big_mine, small.value)
        small.step()
        up_update, down_update = pick_owner(first, big_mine, swap(big_mine, "rep", 0))
        small_mine = small_update(place, small.value[:, None], gather_masks(1))[0]
        small_mine = small_mine.reshape(2, shard_rows, model_width)
        kept, sent = pick_owner(low_core, small_mine[0], small_mine[1])
        pair = jnp.stack(pick_owner(low_core, kept, swap(sent, "win", 0)))
        updates = jnp.concatenate(pick_owner(first, pair, swap(pair, "rep", 0)))
    else:
        up_update, down_update, updates = every_update(
            place, (folded_up_mom, new_down_mom), small_rows, folds
        )

    def stepped(weight, rows_here, update):
        rows = own_rows(weight, rows_here).astype(jnp.float32)
        return rows - MATRIX_RATE * update.astype(jnp.float32)

    new_qkv = jnp.stack(
        [stepped(qkv_weight[number], shard_rows, updates[number]) for number in range(3)]
    )
    new_out = stepped(out_weight, shard_rows, updates[3])
    new_up = stepped(up_weight, shard_rows, unfold_columns(up_update, folds))
    new_down = stepped(down_weight, ff_rows, down_update)
    return (
        out_tokens,
        input_grad,
        new_qkv_mom,
        new_qkv,
        new_out_mom,
        new_out,
        new_up_mom,
        new_up,
        new_down_mom,
        new_down,
        new_vec_mom,
        new_vectors,
    )


def solution(mesh):
    placed = (
        P("rep", "win", None, None),
        P("rep", "win", None),
        P("rep", "win", None),
        P("rep", None),
        P(),
        P(),
        P(),
        P(),
        P(),
        P(None, "win", None),
        P("win", None),
        P("win", None),
        P("win", None),
        P("win"),
        P("rep", "win", None, None),
    )
    return jax.shard_map(
        local,
        mesh=mesh,
        in_specs=placed,
        out_specs=(
            P("rep", "win", None, None),
            P("rep", "win", None, None),
            P(None, "win", None),
            P(None, "win", None),
            P("win", None),
            P("win", None),
            P("win", None),
            P("win", None),
            P("win", None),
            P("win", None),
            P("win"),
            P("win"),
        ),
        check_vma=False,
    )
```

```python
import functools

import jax
import jax.numpy as jnp
from jax import lax
from jax.experimental import pallas as pl
from jax.experimental.pallas import tpu as pltpu
from jax.sharding import PartitionSpec as P

HEADS = 16
HEAD_DIM = 32


EPSILON = 1e-06
MOMENTUM_DECAY = 0.95
MATRIX_RATE = 0.5
VECTOR_RATE = 0.0002
KEEP_SHARE = 0.75
NEWTON_COEFFS = (3.4445, -4.775, 2.0315)


def bfloat(values):
    return values.astype(jnp.bfloat16)


def product(left_side, right_side):
    return jnp.dot(left_side, right_side, preferred_element_type=jnp.float32)


def norm_rows(values, gain_row, shift_row):
    center = values - jnp.mean(values, -1, keepdims=True)
    spread = jnp.mean(center * center, -1, keepdims=True)
    return center * lax.rsqrt(spread + EPSILON) * gain_row + shift_row


def bit_count(axis):
    return lax.axis_size(axis).bit_length() - 1


def swap(values, axis, bit):
    size = lax.axis_size(axis)
    return lax.ppermute(values, axis, [(i, i ^ (1 << bit)) for i in range(size)])


def my_bit(axis, bit):
    return (lax.axis_index(axis) >> bit) & 1


def far_bits():
    return list(range(2, bit_count("win")))


def gather_masks(low=0):
    masks = [0]
    for bit in far_bits() + [1, 0]:
        if bit >= low:
            masks += [mask | (1 << bit) for mask in masks]
    return masks


def gather_far(values):
    size = lax.axis_size("win")
    values = values[None]
    if len(far_bits()) == 2:
        others = [
            lax.ppermute(values, "win", [(i, i ^ mask) for i in range(size)]) for mask in (4, 8, 12)
        ]
        return [jnp.concatenate([values] + others)]
    for bit in far_bits():
        values = jnp.concatenate([values, swap(values, "win", bit)])
    return [values]


def gather_bit(pieces, bit):
    return pieces + [swap(piece, "win", bit) for piece in pieces]


def gather_stages(low=0):
    stages = [gather_far]
    for bit in (1, 0):
        if bit >= low:
            stages.append(functools.partial(gather_bit, bit=bit))
    return stages


def gather_blocks(values, low=0):
    for stage in gather_stages(low):
        values = stage(values)
    return values


def index_order(pieces):
    masks = gather_masks()
    by_mask = sorted(range(len(masks)), key=masks.__getitem__)
    places = lax.axis_index("win") ^ jnp.arange(len(masks))
    return [jnp.concatenate(pieces)[jnp.array(by_mask)][places]]


def tie(*values):
    return lax.optimization_barrier(values)


def after(value, *others):
    return lax.optimization_barrier((value,) + others)[0]


class Order:
    def __init__(self):
        self.sent = ()

    def launch(self, *hops):
        self.sent = tuple(array for array, _, _ in hops)
        return [
            lax.ppermute(array, axis, [(i, i ^ mask) for i in range(lax.axis_size(axis))])
            for array, axis, mask in hops
        ]

    def land(self, values):
        return after(values, *self.sent)


def pick(values, index, axis=0):
    return lax.dynamic_index_in_dim(values, index, axis, keepdims=False)


def wide(values):
    return values.astype(jnp.float32)


def rounded(values):
    return lax.reduce_precision(values, 8, 7)


def same_sum(values, axis, bit):
    low = rounded(values)
    return low + wide(swap(bfloat(low), axis, bit))


def place_bits():
    win_index = lax.axis_index("win")
    return lax.axis_index("rep"), win_index >> 2, (win_index >> 1) & 1, win_index & 1


def first_parts(total):
    rep, _, side, _ = place_bits()
    half = total.shape[-1] // 2
    left, right = total[..., :half], total[..., half:]
    right = right.reshape(2, -1, 2, right.shape[2], half)
    kept = pick(left, rep), pick(right, side, 2)
    sent = bfloat(pick(left, 1 - rep)), bfloat(pick(right, 1 - side, 2))
    return kept, ((sent[0], "rep", 1), (sent[1], "win", 2))


def first_parts_of_two(totals):
    rep, _, side, _ = place_bits()
    half = totals[0].shape[-1] // 2
    left = [total[..., :half] for total in totals]
    right = [total[..., half:].reshape(-1, 2, total.shape[1], half) for total in totals]
    own, other = pick_owner(rep == 0, *left)
    kept = own, jnp.stack([pick(part, side, 1) for part in right])
    sent = bfloat(other), bfloat(jnp.stack([pick(part, 1 - side, 1) for part in right]))
    return kept, ((sent[0], "rep", 1), (sent[1], "win", 2))


def second_parts(left, right):
    rep, _, side, _ = place_bits()
    left = left.reshape(-1, 2, *left.shape[1:])
    kept = pick(left, side, 1), pick(right, rep)
    sent = bfloat(pick(left, 1 - side, 1)), bfloat(pick(right, 1 - rep))
    return kept, ((sent[0], "win", 2), (sent[1], "rep", 1))


def far_parts(total):
    far = place_bits()[1]
    hops = tuple((bfloat(pick(total, far ^ mask)), "win", mask << 2) for mask in (1, 2, 3))
    return pick(total, far), hops


def add_pair(kept, taken):
    return kept[0] + wide(taken[0]), kept[1] + wide(taken[1])


def add_far(kept, taken):
    return (kept + wide(taken[0])) + (wide(taken[1]) + wide(taken[2]))


def join_halves(pair):
    return jnp.concatenate(pair, axis=-1)


def spread_far(values):
    return tuple((values[None], "win", mask) for mask in (4, 8, 12))


def far_piece(values, taken):
    return jnp.concatenate([values[None], *taken])


def sum_everywhere(values, skip_core=True):
    for bit in range(1 if skip_core else 0, bit_count("win")):
        values = same_sum(values, "win", bit)
    for bit in range(bit_count("rep")):
        values = same_sum(values, "rep", bit)
    return values


def off_diagonal_step(iterate, exact):
    high = bfloat(iterate)
    gram = dot_as(high, high, NT)
    if exact:
        rest = bfloat(iterate - high.astype(jnp.float32))
        gram = gram + dot_as(high, rest, NT) + dot_as(rest, high, NT)
    size = gram.shape[0]
    row_ids = lax.broadcasted_iota(jnp.int32, (size, size), 0)
    on_diagonal = row_ids == lax.broadcasted_iota(jnp.int32, (size, size), 1)
    own = jnp.where(on_diagonal, gram, 0.0)
    own_column = jnp.sum(own, 1, keepdims=True)
    own_row = jnp.sum(own, 0, keepdims=True)
    off = jnp.where(on_diagonal, 0.0, gram)
    off_low = bfloat(off)
    square = product(off_low, off_low) + (own_column + own_row) * off
    poly = NEWTON_COEFFS[1] * off + NEWTON_COEFFS[2] * square
    poly_own = jnp.sum(jnp.where(on_diagonal, poly, 0.0), 1, keepdims=True)
    factor = (
        NEWTON_COEFFS[0]
        + poly_own
        + own_column * (NEWTON_COEFFS[1] + NEWTON_COEFFS[2] * own_column)
    )
    poly = jnp.where(on_diagonal, 0.0, poly)
    poly_high = bfloat(poly)
    moved = product(poly_high, high)
    if exact:
        poly_rest = bfloat(poly - poly_high.astype(jnp.float32))
        moved = moved + product(poly_high, rest) + product(poly_rest, high)
    return factor * iterate + moved


def unit_scale(values):
    total = jnp.sum(jnp.sum(values * values, 1, keepdims=True), 0, keepdims=True)
    return values * (1.0 / (jnp.sqrt(total) + EPSILON))


def block_start(place_ref, masks, block, rows, shift=0):
    if masks is None:
        return block * rows
    return pl.multiple_of(((place_ref[1] ^ masks[block]) >> shift) * rows, rows)


def numbered_blocks(piece_refs):
    for piece, piece_ref in enumerate(piece_refs):
        blocks = piece_ref.shape[0]
        for block in range(blocks):
            yield piece * blocks + block, piece_ref.at[block]


def big_newton_kernel(folds, masks, place_ref, *refs):
    piece_refs, (out_ref, iterate_ref, turned_ref) = refs[:-3], refs[-3:]
    _, rows, width = piece_refs[0].shape
    part = rows // folds

    @pl.when(place_ref[0] == 0)
    def _():
        for block, block_ref in numbered_blocks(piece_refs):
            start = block_start(place_ref, masks, block, part)
            for fold in range(folds):
                lanes = slice(fold * width, (fold + 1) * width)
                inner = slice(fold * part, (fold + 1) * part)
                iterate_ref[pl.ds(start, part), lanes] = block_ref[inner, :].astype(jnp.float32)

    @pl.when(place_ref[0] != 0)
    def _():
        for block, block_ref in numbered_blocks(piece_refs):
            start = block_start(place_ref, masks, block, rows)
            iterate_ref[:, pl.ds(start, rows)] = block_ref[...].astype(jnp.float32).T

    iterate_ref[...] = unit_scale(iterate_ref[...])

    @pl.loop(0, 5)
    def _(_):
        iterate_ref[...] = off_diagonal_step(iterate_ref[...], False)

    @pl.when(place_ref[0] == 0)
    def _():
        start = pl.multiple_of(place_ref[1] * part, part)
        for fold in range(folds):
            out_ref[fold * part : (fold + 1) * part, :] = bfloat(
                iterate_ref[pl.ds(start, part), fold * width : (fold + 1) * width]
            )

    @pl.when(place_ref[0] != 0)
    def _():
        span = max(rows, 128)
        start = pl.multiple_of(place_ref[1] * rows // span * span, span)
        turned_ref[...] = iterate_ref[:, pl.ds(start, span)].T * float(folds) ** 0.5
        inner = pl.multiple_of(place_ref[1] * rows - start, rows)
        out_ref[...] = bfloat(turned_ref[pl.ds(inner, rows), :])


def small_newton_kernel(masks, place_ref, *refs):
    piece_refs, (out_ref, iterate_ref) = refs[:-2], refs[-2:]
    _, matrices, rows, width = piece_refs[0].shape
    for block, block_ref in numbered_blocks(piece_refs):
        start = block_start(place_ref, masks, block, rows, 1)
        for number in range(matrices):
            iterate_ref[number, pl.ds(start, rows), :] = block_ref[number].astype(jnp.float32)

    @pl.loop(0, matrices)
    def _(number):
        iterate_ref[number] = unit_scale(iterate_ref[number])

        @pl.loop(0, 2)
        def _(_):
            iterate_ref[number] = off_diagonal_step(iterate_ref[number], False)

        @pl.loop(0, 3)
        def _(_):
            iterate_ref[number] = off_diagonal_step(iterate_ref[number], True)

    start = pl.multiple_of((place_ref[1] if masks is None else place_ref[1] >> 1) * rows, rows)
    for number in range(matrices):
        out_ref[number] = bfloat(iterate_ref[number, pl.ds(start, rows), :])


def newton_call(kernel, name, place, pieces, out_dims, scratch_dims, flops):
    return pl.pallas_call(
        kernel,
        in_specs=[pl.BlockSpec(memory_space=pltpu.SMEM)]
        + [pl.BlockSpec(memory_space=pltpu.VMEM)] * len(pieces),
        out_specs=pl.BlockSpec(memory_space=pltpu.VMEM),
        out_shape=shape_of(out_dims, jnp.bfloat16),
        scratch_shapes=[pltpu.VMEM(dims, jnp.float32) for dims in scratch_dims],
        compiler_params=pltpu.CompilerParams(vmem_limit_bytes=VMEM_LIMIT),
        cost_estimate=pl.CostEstimate(flops=1, bytes_accessed=1, transcendentals=0),
        name=name,
    )(place, *pieces)


def big_update(place, pieces, folds, masks):
    blocks, rows, width = pieces[0].shape
    columns = len(pieces) * blocks * rows
    return newton_call(
        functools.partial(big_newton_kernel, folds, masks),
        "big_newton",
        place,
        pieces,
        (rows, width),
        [(width, columns), (max(rows, 128), width)],
        2 * 5 * width * width * (2 * columns + width),
    )


def small_update(place, pieces, masks):
    _, matrices, rows, width = pieces[0].shape
    return newton_call(
        functools.partial(small_newton_kernel, masks),
        "small_newton",
        place,
        pieces,
        (matrices, rows, width),
        [(matrices, width, width)],
        2 * 27 * matrices * width**3,
    )


def fold_columns(rows, width):
    count, columns = rows.shape
    return rows.reshape(count, columns // width, width).swapaxes(0, 1).reshape(-1, width)


def pick_owner(first, here, there):
    return jnp.where(first, here, there), jnp.where(first, there, here)


def every_update(place, big_rows, small_rows, folds):
    updates = []
    for number, rows in enumerate(big_rows):
        here = jnp.stack([jnp.int32(number), place[1]])
        blocks = index_order(gather_blocks(bfloat(rows)))
        updates.append(big_update(here, blocks, folds, None))
    blocks = index_order(gather_blocks(bfloat(small_rows)))
    return updates[0], updates[1], small_update(place, blocks, None)


GROUP_HEADS = 128 // HEAD_DIM
SCORE_SCALE = HEAD_DIM ** (-0.5)
LOG2_E = 1.4426950408889634
VMEM_LIMIT = 44 * 1024 * 1024
WINDOW_COST = 10**9
VECTOR_ROWS = 16
NT = (((1,), (1,)), ((), ()))
TN = (((0,), (0,)), ((), ()))


def dot_as(left_side, right_side, dims):
    return lax.dot_general(left_side, right_side, dims, preferred_element_type=jnp.float32)


def spread_heads(part, lane_head):
    return bfloat(
        jnp.concatenate(
            [jnp.where(lane_head == head, part, 0.0) for head in range(GROUP_HEADS)], axis=0
        )
    )


def join_heads(spread, lane_head, rows):
    joined = spread[:rows]
    for head in range(1, GROUP_HEADS):
        joined = jnp.where(lane_head == head, spread[head * rows : (head + 1) * rows], joined)
    return joined


def column_softmax(scores, bias_column):
    scores = scores + bias_column
    raised = jnp.exp2((scores - jnp.max(scores, 0, keepdims=True)) * (SCORE_SCALE * LOG2_E))
    return raised * (1.0 / jnp.sum(raised, 0, keepdims=True))


def load_windows(tokens_ref, region_ref, fill_ref, count, seq_len, padded, step):
    for window in range(count):
        base = window * padded
        fill_ref[base : base + seq_len, :] = tokens_ref[0, window].astype(jnp.float32)
        fill_ref[base : base + 1, :] = region_ref[pl.ds(step * count + window, 1), :]


def window_forward_kernel(
    count,
    seq_len,
    padded,
    tokens_ref,
    region_ref,
    bias_ref,
    keep_ref,
    qkv_ref,
    out_ref,
    vec_ref,
    norm_out,
    proj_out,
    mix_out,
    after_out,
    fill_ref,
    mix_ref,
    scores_ref,
    probs_ref,
):
    step = pl.program_id(0)
    width = tokens_ref.shape[-1]

    @pl.when(step == 0)
    def _():
        fill_ref[...] = jnp.zeros_like(fill_ref)

    load_windows(tokens_ref, region_ref, fill_ref, count, seq_len, padded, step)
    flat = fill_ref[...]
    normed = bfloat(norm_rows(flat, vec_ref[2:3, :], vec_ref[3:4, :]))
    lane_head = lax.broadcasted_iota(jnp.int32, (padded, 128), 1) // HEAD_DIM
    query = product(normed, qkv_ref[0]) + vec_ref[6:7, :]
    keyset = product(normed, qkv_ref[1])
    values = product(normed, qkv_ref[2]) + vec_ref[7:8, :]
    pairs = [(window, group) for window in range(count) for group in range(width // 128)]
    for window in range(count):
        rows = slice(window * padded, (window + 1) * padded)
        norm_out[window] = normed[rows]
        proj_out[window, :, :width] = bfloat(query[rows])
        proj_out[window, :, width : 2 * width] = bfloat(keyset[rows])
        proj_out[window, :, 2 * width :] = bfloat(values[rows])
    for number, (window, group) in enumerate(pairs):
        rows = slice(window * padded, (window + 1) * padded)
        lanes = slice(group * 128, (group + 1) * 128)
        spread = spread_heads(query[rows, lanes], lane_head)
        scores_ref[number] = dot_as(bfloat(keyset[rows, lanes]), spread, NT)
    for number, (window, group) in enumerate(pairs):
        probs_ref[number] = bfloat(column_softmax(scores_ref[number], bias_ref[window]))
    for number, (window, group) in enumerate(pairs):
        rows = slice(window * padded, (window + 1) * padded)
        lanes = slice(group * 128, (group + 1) * 128)
        mixed = dot_as(probs_ref[number], bfloat(values[rows, lanes]), TN)
        mix_ref[rows, lanes] = join_heads(mixed, lane_head, padded)
    mixed_low = bfloat(mix_ref[...])
    branch = product(mixed_low, out_ref[...]) + vec_ref[8:9, :]
    for window in range(count):
        rows = slice(window * padded, (window + 1) * padded)
        mix_out[window] = mixed_low[rows]
        after_out[window] = flat[rows] + keep_ref[window] * branch[rows]


def window_backward_kernel(
    count,
    first_step,
    last,
    seq_len,
    padded,
    tokens_ref,
    region_ref,
    bias_ref,
    keep_ref,
    qkv_ref,
    out_ref,
    vec_ref,
    proj_ref,
    after_grad_ref,
    region_keep_ref,
    sums_before_ref,
    *rest,
):
    scratch_count = 8
    if last:
        region_branch_out, region_mix_out = rest[-scratch_count - 2 : -scratch_count]
        rest = rest[: -scratch_count - 2] + rest[-scratch_count:]
    (
        region_grad_out,
        sums_out,
        grad_out,
        proj_grad_out,
        branch_grad_out,
        fill_ref,
        proj_grad_ref,
        spread_ref,
        spread_grad_ref,
        scores_ref,
        probs_grad_ref,
        probs_ref,
        score_grad_ref,
    ) = rest[-13:]
    step = pl.program_id(0) + first_step
    width = tokens_ref.shape[-1]

    @pl.when(pl.program_id(0) == 0)
    def _():
        fill_ref[...] = jnp.zeros_like(fill_ref)
        sums_out[...] = sums_before_ref[...]
        if first_step == 0:
            region_grad_out[...] = jnp.zeros_like(region_grad_out)
        else:
            region_grad_out[...] = rest[0][...]

    load_windows(tokens_ref, region_ref, fill_ref, count, seq_len, padded, step)
    lane_head = lax.broadcasted_iota(jnp.int32, (padded, 128), 1) // HEAD_DIM
    branch_grad = bfloat(
        jnp.concatenate(
            [keep_ref[window] * after_grad_ref[window] for window in range(count)], axis=0
        )
    )
    mix_grad = dot_as(branch_grad, out_ref[...], NT)
    for window in range(count):
        branch_grad_out[window] = branch_grad[window * padded : (window + 1) * padded]
    pairs = [(window, group) for window in range(count) for group in range(width // 128)]

    def lanes_of(part, group):
        return slice(part * width + group * 128, part * width + (group + 1) * 128)

    for number, (window, group) in enumerate(pairs):
        query = proj_ref[window, :, lanes_of(0, group)].astype(jnp.float32)
        spread_ref[number] = spread_heads(query, lane_head)
        rows = slice(window * padded, (window + 1) * padded)
        spread_grad_ref[number] = spread_heads(mix_grad[rows, lanes_of(0, group)], lane_head)
    for number, (window, group) in enumerate(pairs):
        scores_ref[number] = dot_as(
            proj_ref[window, :, lanes_of(1, group)], spread_ref[number], NT
        )
        probs_grad_ref[number] = dot_as(
            proj_ref[window, :, lanes_of(2, group)], spread_grad_ref[number], NT
        )
    for number, (window, group) in enumerate(pairs):
        probs = column_softmax(scores_ref[number], bias_ref[window])
        weighted = probs * probs_grad_ref[number]
        probs_ref[number] = bfloat(probs)
        score_grad_ref[number] = bfloat(weighted - probs * jnp.sum(weighted, 0, keepdims=True))
    for number, (window, group) in enumerate(pairs):
        rows = slice(window * padded, (window + 1) * padded)
        proj_grad_ref[rows, lanes_of(2, group)] = product(
            probs_ref[number], spread_grad_ref[number]
        )
        proj_grad_ref[rows, lanes_of(1, group)] = (
            product(score_grad_ref[number], spread_ref[number]) * SCORE_SCALE
        )
    for number, (window, group) in enumerate(pairs):
        rows = slice(window * padded, (window + 1) * padded)
        query_grad = dot_as(score_grad_ref[number], proj_ref[window, :, lanes_of(1, group)], TN)
        proj_grad_ref[rows, lanes_of(0, group)] = (
            join_heads(query_grad, lane_head, padded) * SCORE_SCALE
        )
    proj_grad = bfloat(proj_grad_ref[...])
    norm_grad = sum(
        dot_as(proj_grad[:, number * width : (number + 1) * width], qkv_ref[number], NT)
        for number in range(3)
    )
    flat = fill_ref[...]
    center = flat - jnp.mean(flat, -1, keepdims=True)
    scale = lax.rsqrt(jnp.mean(center * center, -1, keepdims=True) + EPSILON)
    hat = center * scale
    hat_grad = norm_grad * vec_ref[2:3, :]
    flat_grad = scale * (
        hat_grad
        - jnp.mean(hat_grad, -1, keepdims=True)
        - hat * jnp.mean(hat_grad * hat, -1, keepdims=True)
    )
    proj_sums = jnp.sum(proj_grad.astype(jnp.float32), 0, keepdims=True)
    sums_out[2:3, :] += jnp.sum(norm_grad * hat, 0, keepdims=True)
    sums_out[3:4, :] += jnp.sum(norm_grad, 0, keepdims=True)
    sums_out[6:7, :] += proj_sums[:, :width]
    sums_out[7:8, :] += proj_sums[:, 2 * width :]
    sums_out[8:9, :] += jnp.sum(branch_grad.astype(jnp.float32), 0, keepdims=True)
    for window in range(count):
        rows = slice(window * padded, (window + 1) * padded)
        proj_grad_out[window] = proj_grad[rows]
        seq_grad = after_grad_ref[window] + flat_grad[rows]
        for group in range(width // 128):
            lanes = slice(group * 128, (group + 1) * 128)
            grad_out[window, pl.ds(group, seq_len, stride=width // 128), :] = seq_grad[
                :seq_len, lanes
            ]
        region_grad_out[pl.ds(step * count + window, 1), :] = seq_grad[0:1]

    if last:

        @pl.when(pl.program_id(0) == pl.num_programs(0) - 1)
        def _():
            region_branch = bfloat(region_keep_ref[...] * region_grad_out[...])
            sums_out[8:9, :] += jnp.sum(region_branch.astype(jnp.float32), 0, keepdims=True)
            region_branch_out[...] = region_branch
            regions = region_branch.shape[0]
            spare_rows = region_mix_out.shape[0] - regions - sums_out.shape[0]
            region_mix_out[:regions, :] = bfloat(dot_as(region_branch, out_ref[...], NT))
            sums_low = jnp.concatenate(
                [sums_out[...], jnp.zeros((spare_rows, width), jnp.float32)], axis=0
            )
            region_mix_out[regions:, :] = bfloat(sums_low)


def window_step(windows):
    return next(count for count in (4, 2, 1) if windows % count == 0)


def whole_spec(shape):
    return pl.BlockSpec(shape, lambda step: (0,) * len(shape))


def step_spec(count, *rest):
    return pl.BlockSpec((count,) + rest, lambda step: (step,) + (0,) * len(rest))


def token_spec(count, *rest):
    return pl.BlockSpec((1, count) + rest, lambda step: (0, step) + (0,) * len(rest))


def kept_spec():
    return pl.BlockSpec(memory_space=pltpu.VMEM)


def in_hbm(values):
    return pltpu.with_memory_space_constraint(values, pltpu.HBM)


def hbm_shape(dims, kind=jnp.float32):
    return pltpu.HBM(dims, kind)


def shape_of(dims, kind=jnp.float32):
    return jax.ShapeDtypeStruct(dims, kind)


def window_forward(tokens, region, bias, keep, qkv_weight, out_weight, vectors, padded):
    _, windows, seq_len, width = tokens.shape
    count = window_step(windows)
    pairs = count * width // 128
    return pl.pallas_call(
        functools.partial(window_forward_kernel, count, seq_len, padded),
        grid=(windows // count,),
        in_specs=[
            token_spec(count, seq_len, width),
            whole_spec(region.shape),
            step_spec(count, padded, 1),
            step_spec(count, 1, 1),
            kept_spec(),
            kept_spec(),
            whole_spec(vectors.shape),
        ],
        out_specs=[
            step_spec(count, padded, width),
            step_spec(count, padded, 3 * width),
            step_spec(count, padded, width),
            step_spec(count, padded, width),
        ],
        out_shape=[
            hbm_shape((windows, padded, width), jnp.bfloat16),
            hbm_shape((windows, padded, 3 * width), jnp.bfloat16),
            hbm_shape((windows, padded, width), jnp.bfloat16),
            hbm_shape((windows, padded, width)),
        ],
        scratch_shapes=[
            pltpu.VMEM((count * padded, width), jnp.float32),
            pltpu.VMEM((count * padded, width), jnp.float32),
            pltpu.VMEM((pairs, padded, GROUP_HEADS * padded), jnp.float32),
            pltpu.VMEM((pairs, padded, GROUP_HEADS * padded), jnp.bfloat16),
        ],
        compiler_params=pltpu.CompilerParams(vmem_limit_bytes=VMEM_LIMIT),
        name="window_forward",
    )(in_hbm(tokens), region, bias, keep, qkv_weight, out_weight, vectors)


def window_backward(
    tokens,
    region,
    bias,
    keep,
    qkv_weight,
    out_weight,
    vectors,
    proj,
    after_grad,
    region_keep,
    before,
    steps,
    padded,
):
    _, windows, seq_len, width = tokens.shape
    count = window_step(windows)
    first_step, last_step = steps
    here = (last_step - first_step) * count
    pairs = count * width // 128
    spread_rows = GROUP_HEADS * padded

    def moved(*dims, lead=0):
        zeros = (0,) * (len(dims) - 1)
        if lead:
            return pl.BlockSpec((1,) + dims, lambda step: (0, step + first_step) + zeros)
        return pl.BlockSpec(dims, lambda step: (step + first_step,) + zeros)

    flat_rows = seq_len * width // 128

    grad_before, sums_before, region_before = before
    operands = [in_hbm(tokens), region, bias, keep, qkv_weight, out_weight, vectors]
    operands += [in_hbm(proj), in_hbm(after_grad), region_keep, in_hbm(sums_before)]
    in_specs = [
        moved(count, seq_len, width, lead=1),
        whole_spec(region.shape),
        moved(count, padded, 1),
        moved(count, 1, 1),
        kept_spec(),
        kept_spec(),
        whole_spec(vectors.shape),
        moved(count, padded, 3 * width),
        moved(count, padded, width),
        whole_spec(region_keep.shape),
        whole_spec(sums_before.shape),
    ]
    aliases = {}
    if first_step:
        aliases = {len(operands) + 1: 2}
        operands += [in_hbm(region_before), in_hbm(grad_before)]
        in_specs += [whole_spec(region.shape), pl.BlockSpec(memory_space=pl.ANY)]
    last = last_step * count == windows
    out_specs = [
        whole_spec(region.shape),
        whole_spec(vectors.shape),
        moved(count, flat_rows, 128),
        step_spec(count, padded, 3 * width),
        step_spec(count, padded, width),
    ]
    out_shape = [
        hbm_shape(region.shape),
        hbm_shape(vectors.shape),
        hbm_shape((windows, flat_rows, 128)),
        hbm_shape((here, padded, 3 * width), jnp.bfloat16),
        hbm_shape((here, padded, width), jnp.bfloat16),
    ]
    if last:
        payload = (region.shape[0] + VECTOR_ROWS, width)
        out_specs += [whole_spec(region.shape), whole_spec(payload)]
        out_shape += [shape_of(region.shape, jnp.bfloat16), shape_of(payload, jnp.bfloat16)]
    return pl.pallas_call(
        functools.partial(window_backward_kernel, count, first_step, last, seq_len, padded),
        grid=(last_step - first_step,),
        in_specs=in_specs,
        out_specs=out_specs,
        out_shape=out_shape,
        scratch_shapes=[
            pltpu.VMEM((count * padded, width), jnp.float32),
            pltpu.VMEM((count * padded, 3 * width), jnp.float32),
            pltpu.VMEM((pairs, spread_rows, 128), jnp.bfloat16),
            pltpu.VMEM((pairs, spread_rows, 128), jnp.bfloat16),
            pltpu.VMEM((pairs, padded, spread_rows), jnp.float32),
            pltpu.VMEM((pairs, padded, spread_rows), jnp.float32),
            pltpu.VMEM((pairs, padded, spread_rows), jnp.bfloat16),
            pltpu.VMEM((pairs, padded, spread_rows), jnp.bfloat16),
        ],
        input_output_aliases=aliases,
        compiler_params=pltpu.CompilerParams(vmem_limit_bytes=VMEM_LIMIT),
        cost_estimate=pl.CostEstimate(
            flops=here * WINDOW_COST, bytes_accessed=here * padded * width * 20, transcendentals=0
        ),
        name="window_backward",
    )(*operands)


def insert_kernel(rows_ref, region_ref, out_ref):
    out_ref[...] = rows_ref[...]
    for window in range(rows_ref.shape[0]):
        for group in range(region_ref.shape[1] // 128):
            out_ref[window, group : group + 1, :] = region_ref[
                window : window + 1, group * 128 : (group + 1) * 128
            ]


def insert_regions(grad, region_grad):
    rows = pl.BlockSpec((grad.shape[0], 8, 128), lambda step: (0, 0, 0))
    return pl.pallas_call(
        insert_kernel,
        grid=(1,),
        in_specs=[rows, whole_spec(region_grad.shape)],
        out_specs=rows,
        out_shape=shape_of(grad.shape),
        input_output_aliases={0: 0},
        compiler_params=pltpu.CompilerParams(vmem_limit_bytes=VMEM_LIMIT),
        name="insert_regions",
    )(grad, region_grad)


GELU_IN = 0.7978845608028654
GELU_CUBE = 0.044715


def gelu_both(values):
    square = values * values
    bent = jnp.tanh(values * (GELU_IN + (GELU_IN * GELU_CUBE) * square))
    share = 0.5 + 0.5 * bent
    slope = share + (0.5 * values) * (1.0 - bent * bent) * (
        GELU_IN + (3.0 * GELU_IN * GELU_CUBE) * square
    )
    return values * share, slope


def split_cores(values, core):
    own_first = core == 0
    kept = jnp.where(own_first, values[:, 0], values[:, 1])
    sent = jnp.where(own_first, values[:, 1], values[:, 0])
    return kept, bfloat(sent)


def mlp_kernel(
    count,
    seq_len,
    padded,
    place_ref,
    after_ref,
    cot_ref,
    keep_ref,
    vec_ref,
    up_ref,
    down_ref,
    out_ref,
    grad_ref,
    sums_ref,
    kept_ref,
    sent_ref,
    cot_fill,
    up_total,
    down_total,
):
    step = pl.program_id(0)
    width = up_ref.shape[0]
    folds = up_ref.shape[1] // width

    @pl.when(step == 0)
    def _():
        cot_fill[...] = jnp.zeros_like(cot_fill)
        sums_ref[...] = jnp.zeros_like(sums_ref)
        up_total[...] = jnp.zeros_like(up_total)
        down_total[...] = jnp.zeros_like(down_total)

    keeps = []
    for window in range(count):
        base = window * padded
        cot_fill[base : base + seq_len, :] = cot_ref[0, window].astype(jnp.float32)
        keeps.append(jnp.broadcast_to(keep_ref[window], (padded, 1)))
    keep = jnp.concatenate(keeps, axis=0)
    flat = after_ref[...]
    center = flat - jnp.mean(flat, -1, keepdims=True)
    scale = lax.rsqrt(jnp.mean(center * center, -1, keepdims=True) + EPSILON)
    hat = center * scale
    normed = bfloat(hat * vec_ref[4:5, :] + vec_ref[5:6, :])
    normed_turned = normed.T
    cot = cot_fill[...]
    branch_grad = bfloat(keep * cot)
    branch = jnp.zeros_like(flat)
    norm_grad = jnp.zeros_like(flat)
    for fold in range(folds):
        lanes = slice(fold * width, (fold + 1) * width)
        up_part, down_part = up_ref[:, lanes], down_ref[lanes, :]
        hidden = product(normed, up_part) + vec_ref[10 + fold : 11 + fold, :]
        act, slope = gelu_both(hidden)
        act = bfloat(act)
        branch += product(act, down_part)
        hidden_grad = bfloat(slope * dot_as(branch_grad, down_part, NT))
        norm_grad += dot_as(hidden_grad, up_part, NT)
        up_total[fold] += product(normed_turned, hidden_grad)
        down_total[fold] += dot_as(act, branch_grad, TN)
        sums_ref[10 + fold : 11 + fold, :] += jnp.sum(
            hidden_grad.astype(jnp.float32), 0, keepdims=True
        )
    output = bfloat(flat + keep * (branch + vec_ref[9:10, :]))
    hat_grad = norm_grad * vec_ref[4:5, :]
    flat_grad = cot + scale * (
        hat_grad
        - jnp.mean(hat_grad, -1, keepdims=True)
        - hat * jnp.mean(hat_grad * hat, -1, keepdims=True)
    )
    sums_ref[4:5, :] += jnp.sum(norm_grad * hat, 0, keepdims=True)
    sums_ref[5:6, :] += jnp.sum(norm_grad, 0, keepdims=True)
    sums_ref[9:10, :] += jnp.sum(branch_grad.astype(jnp.float32), 0, keepdims=True)
    grad_ref[...] = flat_grad
    for window in range(count):
        out_ref[0, window] = output[window * padded : window * padded + seq_len]

    @pl.when(step == pl.num_programs(0) - 1)
    def _():
        core = place_ref[1] % 2
        _, blocks, rows, _ = kept_ref.shape
        part, here = rows // folds, blocks // folds
        for fold in range(folds):
            total = up_total[fold].reshape(blocks, 2, part, width)
            inner = slice(fold * part, (fold + 1) * part)
            kept_ref[0, :, inner], sent_ref[0, :, inner] = split_cores(total, core)
        for fold in range(folds):
            total = down_total[fold].reshape(here, 2, rows, width)
            inner = slice(fold * here, (fold + 1) * here)
            kept_ref[1, inner], sent_ref[1, inner] = split_cores(total, core)


def mlp(place, after, cotangent, keep, vectors, up_weight, down_weight, padded, win_count):
    _, windows, seq_len, width = cotangent.shape
    count = window_step(windows)
    rows = count * padded
    folds = up_weight.shape[1] // width
    half = win_count // 2
    up_rows = width // win_count
    dims = (2, half, up_rows * folds, width)
    flat_rows = pl.BlockSpec((rows, width), lambda step: (step, 0))
    output, grad, sums, kept, sent = pl.pallas_call(
        functools.partial(mlp_kernel, count, seq_len, padded),
        grid=(windows // count,),
        in_specs=[
            pl.BlockSpec(memory_space=pltpu.SMEM),
            flat_rows,
            token_spec(count, seq_len, width),
            step_spec(count, 1, 1),
            whole_spec(vectors.shape),
            kept_spec(),
            kept_spec(),
        ],
        out_specs=[
            token_spec(count, seq_len, width),
            flat_rows,
            whole_spec(vectors.shape),
            whole_spec(dims),
            whole_spec(dims),
        ],
        out_shape=[
            hbm_shape(cotangent.shape, jnp.bfloat16),
            hbm_shape(after.shape),
            hbm_shape(vectors.shape),
            hbm_shape(dims),
            hbm_shape(dims, jnp.bfloat16),
        ],
        scratch_shapes=[
            pltpu.VMEM((rows, width), jnp.float32),
            pltpu.VMEM((folds, width, width), jnp.float32),
            pltpu.VMEM((folds, width, width), jnp.float32),
        ],
        compiler_params=pltpu.CompilerParams(vmem_limit_bytes=VMEM_LIMIT),
        cost_estimate=pl.CostEstimate(flops=1, bytes_accessed=1, transcendentals=0),
        name="mlp",
    )(place, in_hbm(after), in_hbm(cotangent), keep, vectors, up_weight, down_weight)
    return output, grad, sums, (kept, sent)


def image_bias(keys_ref, queries_ref):
    return jnp.where(keys_ref[...] == queries_ref[...], 0.0, -1e30)


def region_forward_kernel(
    pieces,
    *refs,
):
    piece_refs, refs = refs[:pieces], refs[pieces:]
    region_forward_rows(piece_refs, *refs)


def region_forward_rows(
    piece_refs,
    own_ref,
    keep_ref,
    key_image_ref,
    query_image_ref,
    qkv_ref,
    out_ref,
    vec_ref,
    norm_out,
    proj_out,
    mix_out,
    new_out,
    all_ref,
):
    rows, width = own_ref.shape
    vec = vec_ref[...]
    for block, block_ref in numbered_blocks(piece_refs):
        all_ref[block * rows : (block + 1) * rows, :] = block_ref[...].astype(jnp.float32)
    normed = bfloat(norm_rows(all_ref[...], vec[0:1], vec[1:2]))
    norm_out[...] = normed
    query = bfloat(product(normed, qkv_ref[0]) + vec[6:7])
    keyset = bfloat(product(normed, qkv_ref[1]))
    values = bfloat(product(normed, qkv_ref[2]) + vec[7:8])
    proj_out[:, :width] = query
    proj_out[:, width : 2 * width] = keyset
    proj_out[:, 2 * width :] = values
    region = own_ref[...].astype(jnp.float32)
    own_norm = bfloat(norm_rows(region, vec[0:1], vec[1:2]))
    own_query = product(own_norm, qkv_ref[0]) + vec[6:7]
    bias = image_bias(key_image_ref, query_image_ref)
    lane_head = lax.broadcasted_iota(jnp.int32, (rows, 128), 1) // HEAD_DIM
    parts = []
    for group in range(width // 128):
        lanes = slice(group * 128, (group + 1) * 128)
        spread = spread_heads(own_query[:, lanes], lane_head)
        probs = column_softmax(dot_as(keyset[:, lanes], spread, NT), bias)
        mixed = dot_as(bfloat(probs), values[:, lanes], TN)
        parts.append(join_heads(mixed, lane_head, rows))
    mixed_low = bfloat(jnp.concatenate(parts, axis=1))
    mix_out[...] = mixed_low
    branch = product(mixed_low, out_ref[...]) + vec[8:9]
    new_out[...] = region + keep_ref[...] * branch


def region_forward(pieces, own, keep, key_images, query_images, qkv_weight, out_weight, vectors):
    rows, width = own.shape
    total = len(pieces) * pieces[0].shape[0] * rows
    return pl.pallas_call(
        functools.partial(region_forward_kernel, len(pieces)),
        out_shape=[
            hbm_shape((total, width), jnp.bfloat16),
            hbm_shape((total, 3 * width), jnp.bfloat16),
            hbm_shape(own.shape, jnp.bfloat16),
            shape_of(own.shape),
        ],
        scratch_shapes=[pltpu.VMEM((total, width), jnp.float32)],
        compiler_params=pltpu.CompilerParams(vmem_limit_bytes=VMEM_LIMIT),
        name="region_forward",
    )(*pieces, own, keep, key_images, query_images, qkv_weight, out_weight, vectors)


def region_backward_kernel(pieces, place_ref, *refs):
    region_refs, refs = refs[:pieces], refs[pieces:]
    gathered_refs, refs = refs[:pieces], refs[pieces:]
    region_backward_rows(place_ref, region_refs, gathered_refs, *refs)


def region_backward_rows(
    place_ref,
    region_refs,
    gathered_refs,
    norm_ref,
    proj_ref,
    key_image_ref,
    query_image_ref,
    new_grad_ref,
    qkv_ref,
    vec_ref,
    grad_out,
    weight_out,
    sums_out,
    bias_ref,
    proj_grad_ref,
    region_grad_ref,
    weight_ref,
    mix_grad_ref,
    all_ref,
    scores_ref,
    probs_grad_ref,
    probs_ref,
    score_grad_ref,
):
    total, width = all_ref.shape
    rows = new_grad_ref.shape[0]
    bias_ref[...] = image_bias(key_image_ref, query_image_ref)
    lane_head = lax.broadcasted_iota(jnp.int32, (total, 128), 1) // HEAD_DIM
    for block, block_ref in numbered_blocks(region_refs):
        all_ref[block * rows : (block + 1) * rows, :] = block_ref[...].astype(jnp.float32)
    vector_sum = jnp.zeros((VECTOR_ROWS, width), jnp.float32)
    for block, block_ref in numbered_blocks(gathered_refs):
        part = block_ref[...].astype(jnp.float32)
        mix_grad_ref[block * rows : (block + 1) * rows, :] = part[:rows]
        vector_sum += part[rows:]

    @pl.loop(0, width // 128)
    def _(group):
        query_lanes = pl.ds(pl.multiple_of(group * 128, 128), 128)
        key_lanes = pl.ds(pl.multiple_of(width + group * 128, 128), 128)
        value_lanes = pl.ds(pl.multiple_of(2 * width + group * 128, 128), 128)
        key_low = proj_ref[:, key_lanes]
        value_low = proj_ref[:, value_lanes]
        spread = spread_heads(proj_ref[:, query_lanes].astype(jnp.float32), lane_head)
        spread_grad = spread_heads(mix_grad_ref[:, query_lanes], lane_head)
        scores_ref[...] = dot_as(key_low, spread, NT)
        probs_grad_ref[...] = dot_as(value_low, spread_grad, NT)
        for head in range(GROUP_HEADS):
            lanes = slice(head * total, (head + 1) * total)
            probs = column_softmax(scores_ref[:, lanes], bias_ref[...])
            weighted = probs * probs_grad_ref[:, lanes]
            probs_ref[:, lanes] = bfloat(probs)
            score_grad_ref[:, lanes] = bfloat(
                weighted - probs * jnp.sum(weighted, 0, keepdims=True)
            )
        value_grad = product(probs_ref[...], spread_grad)
        key_grad = product(score_grad_ref[...], spread)
        turned = product(key_low.T, score_grad_ref[...])
        query_grad = jnp.concatenate(
            [
                turned[head * HEAD_DIM : (head + 1) * HEAD_DIM, head * total : (head + 1) * total]
                for head in range(GROUP_HEADS)
            ],
            axis=0,
        ).T
        proj_grad_ref[:, query_lanes] = bfloat(query_grad * SCORE_SCALE)
        proj_grad_ref[:, key_lanes] = bfloat(key_grad * SCORE_SCALE)
        proj_grad_ref[:, value_lanes] = bfloat(value_grad)

    proj_grad = proj_grad_ref[...]
    norm_grad = sum(
        dot_as(proj_grad[:, number * width : (number + 1) * width], qkv_ref[number], NT)
        for number in range(3)
    )
    region = all_ref[...]
    center = region - jnp.mean(region, -1, keepdims=True)
    scale = lax.rsqrt(jnp.mean(center * center, -1, keepdims=True) + EPSILON)
    hat = center * scale
    hat_grad = norm_grad * vec_ref[0:1, :]
    region_grad_ref[...] = scale * (
        hat_grad
        - jnp.mean(hat_grad, -1, keepdims=True)
        - hat * jnp.mean(hat_grad * hat, -1, keepdims=True)
    )
    grad_out[...] = new_grad_ref[...] + region_grad_ref[:rows, :]
    bias_sums = jnp.sum(proj_grad.astype(jnp.float32), 0, keepdims=True)
    sums_out[...] = vector_sum
    sums_out[0:1, :] += jnp.sum(norm_grad * hat, 0, keepdims=True)
    sums_out[1:2, :] += jnp.sum(norm_grad, 0, keepdims=True)
    sums_out[6:7, :] += bias_sums[:, :width]
    sums_out[7:8, :] += bias_sums[:, 2 * width :]
    weight_ref[...] = dot_as(norm_ref[...], proj_grad, TN)
    weight_rows = weight_out.shape[1]
    weight_start = pl.multiple_of((place_ref[1] >> 1) * weight_rows, 8)
    for number in range(3):
        weight_out[number] = weight_ref[
            pl.ds(weight_start, weight_rows), number * width : (number + 1) * width
        ]


def region_backward(
    place,
    regions,
    gathered,
    normed,
    proj,
    key_images,
    query_images,
    new_grad,
    qkv_weight,
    vectors,
    weight_rows,
):
    total, width = normed.shape
    vmem = pl.BlockSpec(memory_space=pltpu.VMEM)
    operands = [*regions, *gathered, in_hbm(normed), in_hbm(proj), key_images, query_images]
    operands += [new_grad, qkv_weight, vectors]
    return pl.pallas_call(
        functools.partial(region_backward_kernel, len(regions)),
        grid=(1,),
        in_specs=[pl.BlockSpec(memory_space=pltpu.SMEM)]
        + [whole_spec(operand.shape) for operand in operands[:-2]]
        + [vmem, whole_spec(vectors.shape)],
        out_specs=[vmem] * 3,
        out_shape=[
            shape_of(new_grad.shape),
            shape_of((3, weight_rows, width)),
            shape_of((VECTOR_ROWS, width)),
        ],
        scratch_shapes=[
            pltpu.VMEM((total, total), jnp.float32),
            pltpu.VMEM((total, 3 * width), jnp.bfloat16),
            pltpu.VMEM((total, width), jnp.float32),
            pltpu.VMEM((width, 3 * width), jnp.float32),
            pltpu.VMEM((total, width), jnp.float32),
            pltpu.VMEM((total, width), jnp.float32),
            pltpu.VMEM((total, GROUP_HEADS * total), jnp.float32),
            pltpu.VMEM((total, GROUP_HEADS * total), jnp.float32),
            pltpu.VMEM((total, GROUP_HEADS * total), jnp.bfloat16),
            pltpu.VMEM((total, GROUP_HEADS * total), jnp.bfloat16),
        ],
        compiler_params=pltpu.CompilerParams(vmem_limit_bytes=VMEM_LIMIT),
        name="region_backward",
    )(place, *operands)


def pair_gradient_kernel(first_count, second_count, place_ref, *refs):
    own_first = place_ref[1] % 2 == 0
    kept, sent = refs[-2:]

    def total(pairs):
        lefts, rights = pairs[0::2], pairs[1::2]
        return sum(dot_as(left[...], right[...], TN) for left, right in zip(lefts, rights))

    first = total(refs[: 2 * first_count])
    second = total(refs[2 * first_count : 2 * (first_count + second_count)])
    kept[...] = jnp.where(own_first, first, second)
    sent[...] = bfloat(jnp.where(own_first, second, first))


def pair_gradients(place, first, second, width):
    operands, in_specs = [place], [pl.BlockSpec(memory_space=pltpu.SMEM)]
    for left, row, right, column, rows in first + second:
        operands += [in_hbm(left), in_hbm(right)]
        in_specs.append(pl.BlockSpec((rows, width), lambda step, row=row: (row, 0)))
        in_specs.append(pl.BlockSpec((rows, width), lambda step, column=column: (0, column)))
    return pl.pallas_call(
        functools.partial(pair_gradient_kernel, len(first), len(second)),
        grid=(1,),
        in_specs=in_specs,
        out_specs=[whole_spec((width, width))] * 2,
        out_shape=[hbm_shape((width, width)), hbm_shape((width, width), jnp.bfloat16)],
        compiler_params=pltpu.CompilerParams(vmem_limit_bytes=VMEM_LIMIT),
        cost_estimate=pl.CostEstimate(flops=1, bytes_accessed=1, transcendentals=0),
        name="pair_gradients",
    )(*operands)


def row_pieces(whole, rights, column):
    pairs, start = [], 0
    for right in rights:
        rows = right.shape[0]
        left, row = (whole, start // rows) if start % rows == 0 else (whole[start : start + rows], 0)
        pairs.append((left, row, right, column, rows))
        start += rows
    return pairs


def finish_big_kernel(
    place_ref, mine, other, mom_mine, mom_other, up_ref, down_ref, up_new, down_new, up_mom, down_mom
):
    first = place_ref[0] == 0

    def ordered(here, there):
        return jnp.where(first, here, there), jnp.where(first, there, here)

    updates = ordered(mine[...].astype(jnp.float32), other[...].astype(jnp.float32))
    momenta = ordered(mom_mine[...], mom_other[...])
    down_new[...] = down_ref[...].astype(jnp.float32) - MATRIX_RATE * updates[1]
    down_mom[...] = momenta[1]
    rows, columns = up_ref.shape
    width = down_ref.shape[1]
    for fold in range(columns // width):
        lanes = slice(fold * width, (fold + 1) * width)
        inner = slice(fold * rows, (fold + 1) * rows)
        up_new[:, lanes] = up_ref[:, lanes].astype(jnp.float32) - MATRIX_RATE * updates[0][inner]
        up_mom[:, lanes] = momenta[0][inner]


def finish_small_kernel(place_ref, *refs):
    updates, momenta = refs[:4], refs[4:8]
    qkv_ref, out_ref, qkv_new, out_new, qkv_mom, out_mom = refs[8:]
    first, low = place_ref[0] == 0, place_ref[2] == 0

    def ordered(parts):
        own, side, across, corner = [part[...].astype(jnp.float32) for part in parts]
        here = jnp.where(low, own, side), jnp.where(low, side, own)
        there = jnp.where(low, across, corner), jnp.where(low, corner, across)
        return [jnp.where(first, one, two) for one, two in zip(here + there, there + here)]

    for number, (update, momentum) in enumerate(zip(ordered(updates), ordered(momenta))):
        if number < 3:
            qkv_new[number] = qkv_ref[number].astype(jnp.float32) - MATRIX_RATE * update
            qkv_mom[number] = momentum
        else:
            out_new[...] = out_ref[...].astype(jnp.float32) - MATRIX_RATE * update
            out_mom[...] = momentum


def finish_call(kernel, name, place, parts, weights, blocks, indices):
    dims = [shape_of(block) for block in blocks]
    return pl.pallas_call(
        kernel,
        grid_spec=pltpu.PrefetchScalarGridSpec(
            num_scalar_prefetch=1,
            grid=(1,),
            in_specs=[pl.BlockSpec(part.shape, lambda step, place: (0, 0)) for part in parts]
            + [pl.BlockSpec(block, index) for block, index in zip(blocks, indices)],
            out_specs=[
                pl.BlockSpec(block, lambda step, place, count=len(block): (0,) * count)
                for block in blocks + blocks
            ],
        ),
        out_shape=dims + dims,
        compiler_params=pltpu.CompilerParams(vmem_limit_bytes=VMEM_LIMIT),
        name=name,
    )(place, *parts, *weights)


def finish_big(place, parts, up_weight, down_weight):
    rows, width = parts[0].shape
    up_rows = rows * width // up_weight.shape[1]
    own = lambda step, place: (place[1], 0)
    return finish_call(
        finish_big_kernel,
        "finish_big",
        place,
        parts,
        (up_weight, down_weight),
        [(up_rows, up_weight.shape[1]), (rows, width)],
        [own, own],
    )


def finish_small(place, parts, qkv_weight, out_weight):
    rows, width = parts[0].shape
    return finish_call(
        finish_small_kernel,
        "finish_small",
        place,
        parts,
        (qkv_weight, out_weight),
        [(3, rows, width), (rows, width)],
        [lambda step, place: (0, place[1], 0), lambda step, place: (place[1], 0)],
    )


def local(
    tokens,
    patch_mask,
    keep_mask,
    image_map,
    qkv_weight,
    out_weight,
    up_weight,
    down_weight,
    vectors,
    qkv_mom,
    out_mom,
    up_mom,
    down_mom,
    vec_mom,
    cotangent,
):
    windows = tokens.shape[1]
    seq_len = tokens.shape[2]
    model_width = tokens.shape[3]
    hidden_width = up_weight.shape[1]
    folds = hidden_width // model_width
    shard_rows = out_mom.shape[0]
    ff_rows = down_mom.shape[0]
    vec_rows = vec_mom.shape[0]
    padded = (seq_len + 7) // 8 * 8
    region_rows = (windows + 7) // 8 * 8
    row_count = windows * padded
    win_count = lax.axis_size("win")
    win_index = lax.axis_index("win")
    place = jnp.stack([lax.axis_index("rep"), win_index]).astype(jnp.int32)

    def pad_rows(values, rows, fill=0):
        widths = ((0, rows - values.shape[0]),) + ((0, 0),) * (values.ndim - 1)
        return jnp.pad(values, widths, constant_values=fill)

    region_own = pad_rows(tokens[0, :, 0], region_rows)
    regions = gather_blocks(region_own)
    keeper = keep_mask[0].astype(jnp.float32) / KEEP_SHARE
    images = image_map[0].reshape(win_count, windows)[win_index ^ jnp.array(gather_masks())]
    images = jnp.pad(images, ((0, 0), (0, region_rows - windows)), constant_values=-1)
    key_images = images.reshape(-1, 1)
    own_images = jnp.tile(images[:1], (1, GROUP_HEADS))
    region_keep = pad_rows(keeper[:, 0:1], region_rows)

    big_moms = (
        MOMENTUM_DECAY * fold_columns(up_mom, model_width),
        MOMENTUM_DECAY * down_mom,
    )
    small_old_moms = MOMENTUM_DECAY * jnp.concatenate([qkv_mom, out_mom[None]])
    own_pair = jnp.where(lax.axis_index("rep") == 0, small_old_moms[:2], small_old_moms[2:])
    kept, sent = pick_owner(win_index % 2 == 0, own_pair[0], own_pair[1])
    small_pair_mom = jnp.concatenate(
        pick_owner(win_index % 2 == 0, kept, swap(sent, "win", 0))
    )
    regions, big_moms, small_pair_mom = tie(regions, big_moms, small_pair_mom)

    region_norm, region_proj, region_mix, region_new = region_forward(
        regions, region_own, region_keep, key_images, own_images, qkv_weight, out_weight, vectors
    )

    key_valid = jnp.concatenate([jnp.ones((windows, 1), jnp.int32), patch_mask[0]], axis=1) == 1
    key_bias = jnp.where(key_valid, 0.0, -1e30)
    key_bias = jnp.pad(key_bias, ((0, 0), (0, padded - seq_len)), constant_values=-1e30)
    key_bias = key_bias[:, :, None]
    keep_window = keeper[:, 1].reshape(windows, 1, 1)
    seq_norm, seq_proj, local_mix, after_attn = window_forward(
        tokens, region_new, key_bias, keep_window, qkv_weight, out_weight, vectors, padded
    )
    seq_norm = seq_norm.reshape(row_count, model_width)
    local_mix = local_mix.reshape(row_count, model_width)
    after_attn = after_attn.reshape(row_count, model_width)

    out_tokens, attn_res_grad, mlp_sums, big_halves = mlp(
        place,
        after_attn,
        cotangent,
        keeper[:, 2].reshape(windows, 1, 1),
        vectors,
        up_weight,
        down_weight,
        padded,
        win_count,
    )

    steps = windows // window_step(windows)
    cuts = [0, steps * 2 // 5, steps * 4 // 5, steps]
    after_grad = attn_res_grad.reshape(windows, padded, model_width)
    two_owners = lax.axis_size("rep") == 2 and len(far_bits()) == 2
    order = Order()
    big_taken = order.launch((big_halves[1], "win", 1))
    before = (None, mlp_sums, None)
    proj_grads, branch_grads = [], []
    for piece in range(3):
        region_new_grad, sums, seq_grad, proj_grad, branch_grad, *region_parts = window_backward(
            tokens,
            region_new,
            key_bias,
            keep_window,
            qkv_weight,
            out_weight,
            vectors,
            seq_proj,
            after_grad,
            region_keep,
            before,
            (cuts[piece], cuts[piece + 1]),
            padded,
        )
        before = (seq_grad, sums, region_new_grad)
        proj_grads.append(proj_grad.reshape(-1, 3 * model_width))
        branch_grads.append(branch_grad.reshape(-1, model_width))
        if piece == 0:
            big_taken, after_grad = tie(big_taken, after_grad)
            big_total = big_halves[0] + wide(big_taken[0])
            if two_owners:
                big_kept, hops = first_parts(big_total)
                big_taken = order.launch(*hops)
        if piece == 1 and two_owners:
            big_taken, after_grad = tie(big_taken, after_grad)
            big_kept, hops = second_parts(*add_pair(big_kept, big_taken))
            hops, after_grad = tie([array for array, _, _ in hops], after_grad)
            big_taken = order.launch((hops[0], "win", 2), (hops[1], "rep", 1))
    region_branch_grad, region_mix_grad = region_parts
    if two_owners:
        mix_taken = order.launch(*spread_far(region_mix_grad))

    first = lax.axis_index("rep") == 0
    low_core = win_index % 2 == 0
    kept, sent = pair_gradients(
        place,
        row_pieces(seq_norm, proj_grads, 0),
        row_pieces(seq_norm, proj_grads, 1),
        model_width,
    )
    small_kept = [kept]
    small_taken = order.launch((sent, "win", 1))
    if two_owners:
        mixes = [far_piece(region_mix_grad, order.land(mix_taken))]
        mix_taken = order.launch((mixes[0], "win", 2))
        big_kept, hops = far_parts(join_halves(add_pair(big_kept, order.land(big_taken))))
        hops, mix_out = tie([array for array, _, _ in hops], region_mix)
        big_taken = order.launch(*[(hop, "win", 4 * (i + 1)) for i, hop in enumerate(hops)])
    else:
        mix_out = region_mix
    kept, sent = pair_gradients(
        place,
        row_pieces(seq_norm, proj_grads, 2),
        row_pieces(local_mix, branch_grads, 0)
        + [(mix_out, 0, region_branch_grad, 0, region_rows)],
        model_width,
    )
    small_kept.append(kept)
    small_taken += order.launch((sent, "win", 1))
    if two_owners:
        mixes += order.land(mix_taken)
        mix_taken = order.launch(*[(piece, "win", 1) for piece in mixes])
    small_totals = [
        (kept + wide(taken)).reshape(-1, 2 * shard_rows, model_width)
        for kept, taken in zip(small_kept, order.land(small_taken))
    ]
    if two_owners:
        small_kept, hops = first_parts_of_two(small_totals)
        small_taken = order.launch(*hops)
        big_mom = jnp.where(first, big_moms[0], big_moms[1])
        big_mom = big_mom + add_far(big_kept, order.land(big_taken))
        big_low = bfloat(big_mom)
        big_taken = order.launch(*spread_far(big_low))
        mixes += order.land(mix_taken)
        mixes = order.land(mixes)
    else:
        mixes = gather_blocks(region_mix_grad)

    region_grad, region_weight_grad, region_sums = region_backward(
        place,
        regions,
        mixes,
        region_norm,
        region_proj,
        key_images,
        key_images.reshape(1, -1),
        region_new_grad,
        qkv_weight,
        vectors,
        2 * shard_rows,
    )

    if two_owners:
        def spread_pair(mine):
            mine = mine.reshape(2, shard_rows, model_width)
            kept, sent = pick_owner(low_core, mine[0], mine[1])
            taken = order.launch((sent, "win", 1), (kept, "rep", 1), (sent, ("win", "rep"), 3))
            return kept, taken

        rep_rows = jnp.stack(
            [
                jnp.where(low_core, region_weight_grad[0], region_weight_grad[1]),
                jnp.where(low_core, region_weight_grad[2], 0.0),
            ]
        )
        rep = lax.axis_index("rep")
        vec_mine = rounded(region_sums)
        small_kept, hops = second_parts(*add_pair(small_kept, order.land(small_taken)))
        small_taken = order.launch(*hops)
        vec_taken = order.launch(
            (bfloat(jnp.concatenate([pick(rep_rows, 1 - rep), vec_mine])), "rep", 1)
        )
        big_pieces = [far_piece(big_low, order.land(big_taken))]
        big_taken = order.launch((big_pieces[0], "win", 2))
        small_kept, hops = far_parts(join_halves(add_pair(small_kept, order.land(small_taken))))
        small_taken = order.launch(*hops)
        vec_taken = wide(vec_taken[0])
        region_rows_sum = pick(rep_rows, rep) + vec_taken[: 2 * shard_rows]
        vec_sum = vec_mine + vec_taken[2 * shard_rows :]
        big_pieces += order.land(big_taken)
        big_taken = order.launch(*[(piece, "win", 1) for piece in big_pieces])
        small_mom = add_far(small_kept, order.land(small_taken)) + region_rows_sum
        small_mom = small_pair_mom + small_mom
        small_low = bfloat(small_mom)
        small_taken = order.launch(*spread_far(small_low))
        input_grad = insert_regions(seq_grad, after(region_grad, *order.sent))
        input_grad = input_grad.reshape(tokens.shape)
        small_pieces = [far_piece(small_low, order.land(small_taken))]
        small_taken = order.launch((small_pieces[0], "win", 2))
        mom_parts = spread_pair(small_mom)
        other_mom = order.launch((big_mom, "rep", 1))[0]
        big_pieces += order.land(big_taken)
        big_mine = big_update(place, big_pieces, folds, gather_masks())

        other_update = order.launch((big_mine, "rep", 1))[0]
        small_pieces += order.land(small_taken)
        small_pieces, mom_parts, other_mom = tie(small_pieces, mom_parts, other_mom)
        small_mine = small_update(
            place, [piece[:, None] for piece in small_pieces], gather_masks(1)
        )[0]
        update_parts = spread_pair(small_mine)
        other_update = order.land(other_update)
        finish_place = jnp.concatenate([place, place[1:] & 1])
        big_parts = [big_mine, other_update, big_mom, other_mom]
        small_parts = [update_parts[0], *update_parts[1], mom_parts[0], *mom_parts[1]]
    else:
        input_grad = insert_regions(seq_grad, region_grad).reshape(tokens.shape)
        big_total = pick(sum_everywhere(big_total), win_index >> 1, 1)
        folded_up_mom = big_moms[0] + big_total[0]
        new_down_mom = big_moms[1] + big_total[1]
        small_total = sum_everywhere(jnp.stack(small_totals))
        other = swap(bfloat(small_total), "win", 0)
        pairs = jnp.stack(pick_owner(low_core, bfloat(small_total), other), axis=1)
        pairs = pairs.reshape(4, -1, 2 * shard_rows, model_width)
        region_pairs = jnp.pad(region_weight_grad, ((0, 1), (0, 0), (0, 0)))
        vec_sum = region_sums
        for bit in range(bit_count("rep")):
            region_pairs = same_sum(region_pairs, "rep", bit)
            vec_sum = same_sum(vec_sum, "rep", bit)
        rows = wide(pick(pairs, win_index >> 1, 1)) + region_pairs
        rows = rows.reshape(4, 2, shard_rows, model_width)
        small_moms = small_old_moms + pick(rows, win_index & 1, 1)
        up_update, down_update, updates = every_update(
            place, (folded_up_mom, new_down_mom), small_moms, folds
        )
        finish_place = jnp.stack([0 * win_index, win_index, 0 * win_index]).astype(jnp.int32)
        big_parts = [up_update, down_update, folded_up_mom, new_down_mom]
        small_parts = [*updates, *small_moms]
    new_up, new_down, new_up_mom, new_down_mom = finish_big(
        finish_place, big_parts, up_weight, down_weight
    )
    new_qkv, new_out, new_qkv_mom, new_out_mom = finish_small(
        finish_place, small_parts, qkv_weight, out_weight
    )
    vec_total = lax.dynamic_slice_in_dim(vec_sum.reshape(-1), win_index * vec_rows, vec_rows)
    new_vec_mom = MOMENTUM_DECAY * vec_mom + vec_total
    new_vectors = (
        lax.dynamic_slice_in_dim(vectors.reshape(-1), win_index * vec_rows, vec_rows)
        - VECTOR_RATE * new_vec_mom
    )

    return (
        out_tokens,
        input_grad,
        new_qkv_mom,
        new_qkv,
        new_out_mom,
        new_out,
        new_up_mom,
        new_up,
        new_down_mom,
        new_down,
        new_vec_mom,
        new_vectors,
    )


def solution(mesh):
    placed = (
        P("rep", "win", None, None),
        P("rep", "win", None),
        P("rep", "win", None),
        P("rep", None),
        P(),
        P(),
        P(),
        P(),
        P(),
        P(None, "win", None),
        P("win", None),
        P("win", None),
        P("win", None),
        P("win"),
        P("rep", "win", None, None),
    )
    return jax.shard_map(
        local,
        mesh=mesh,
        in_specs=placed,
        out_specs=(
            P("rep", "win", None, None),
            P("rep", "win", None, None),
            P(None, "win", None),
            P(None, "win", None),
            P("win", None),
            P("win", None),
            P("win", None),
            P("win", None),
            P("win", None),
            P("win", None),
            P("win"),
            P("win"),
        ),
        check_vma=False,
    )
```

```python
import functools

import jax
import jax.numpy as jnp
from jax import lax
from jax.experimental import pallas as pl
from jax.experimental.pallas import tpu as pltpu
from jax.sharding import PartitionSpec as P

HEADS = 16
HEAD_DIM = 32


EPSILON = 1e-06
MOMENTUM_DECAY = 0.95
MATRIX_RATE = 0.5
VECTOR_RATE = 0.0002
KEEP_SHARE = 0.75
NEWTON_COEFFS = (3.4445, -4.775, 2.0315)


def bfloat(values):
    return values.astype(jnp.bfloat16)


def product(left_side, right_side):
    return jnp.dot(left_side, right_side, preferred_element_type=jnp.float32)


def norm_rows(values, gain_row, shift_row):
    center = values - jnp.mean(values, -1, keepdims=True)
    spread = jnp.mean(center * center, -1, keepdims=True)
    return center * lax.rsqrt(spread + EPSILON) * gain_row + shift_row


def bit_count(axis):
    return lax.axis_size(axis).bit_length() - 1


def swap(values, axis, bit):
    size = lax.axis_size(axis)
    return lax.ppermute(values, axis, [(i, i ^ (1 << bit)) for i in range(size)])


def my_bit(axis, bit):
    return (lax.axis_index(axis) >> bit) & 1


def far_bits():
    return list(range(2, bit_count("win")))


def gather_masks(low=0):
    masks = [0]
    for bit in far_bits() + [1, 0]:
        if bit >= low:
            masks += [mask | (1 << bit) for mask in masks]
    return masks


def gather_far(values):
    size = lax.axis_size("win")
    values = values[None]
    if len(far_bits()) == 2:
        others = [
            lax.ppermute(values, "win", [(i, i ^ mask) for i in range(size)]) for mask in (4, 8, 12)
        ]
        return [jnp.concatenate([values] + others)]
    for bit in far_bits():
        values = jnp.concatenate([values, swap(values, "win", bit)])
    return [values]


def gather_bit(pieces, bit):
    return pieces + [swap(piece, "win", bit) for piece in pieces]


def gather_stages(low=0):
    stages = [gather_far]
    for bit in (1, 0):
        if bit >= low:
            stages.append(functools.partial(gather_bit, bit=bit))
    return stages


def gather_blocks(values, low=0):
    for stage in gather_stages(low):
        values = stage(values)
    return values


def index_order(pieces):
    masks = gather_masks()
    by_mask = sorted(range(len(masks)), key=masks.__getitem__)
    places = lax.axis_index("win") ^ jnp.arange(len(masks))
    return [jnp.concatenate(pieces)[jnp.array(by_mask)][places]]


def tie(*values):
    return lax.optimization_barrier(values)


def after(value, *others):
    return lax.optimization_barrier((value,) + others)[0]


class Order:
    def __init__(self):
        self.sent = ()

    def launch(self, *hops):
        self.sent = tuple(array for array, _, _ in hops)
        return [
            lax.ppermute(array, axis, [(i, i ^ mask) for i in range(lax.axis_size(axis))])
            for array, axis, mask in hops
        ]

    def land(self, values):
        return after(values, *self.sent)


def pick(values, index, axis=0):
    return lax.dynamic_index_in_dim(values, index, axis, keepdims=False)


def wide(values):
    return values.astype(jnp.float32)


def rounded(values):
    return lax.reduce_precision(values, 8, 7)


def same_sum(values, axis, bit):
    low = rounded(values)
    return low + wide(swap(bfloat(low), axis, bit))


def place_bits():
    win_index = lax.axis_index("win")
    return lax.axis_index("rep"), win_index >> 2, (win_index >> 1) & 1, win_index & 1


def first_parts(total):
    rep, _, side, _ = place_bits()
    half = total.shape[-1] // 2
    left, right = total[..., :half], total[..., half:]
    right = right.reshape(2, -1, 2, right.shape[2], half)
    kept = pick(left, rep), pick(right, side, 2)
    sent = bfloat(pick(left, 1 - rep)), bfloat(pick(right, 1 - side, 2))
    return kept, ((sent[0], "rep", 1), (sent[1], "win", 2))


def first_parts_of_two(totals):
    rep, _, side, _ = place_bits()
    half = totals[0].shape[-1] // 2
    left = [total[..., :half] for total in totals]
    right = [total[..., half:].reshape(-1, 2, total.shape[1], half) for total in totals]
    own, other = pick_owner(rep == 0, *left)
    kept = own, jnp.stack([pick(part, side, 1) for part in right])
    sent = bfloat(other), bfloat(jnp.stack([pick(part, 1 - side, 1) for part in right]))
    return kept, ((sent[0], "rep", 1), (sent[1], "win", 2))


def second_parts(left, right):
    rep, _, side, _ = place_bits()
    left = left.reshape(-1, 2, *left.shape[1:])
    kept = pick(left, side, 1), pick(right, rep)
    sent = bfloat(pick(left, 1 - side, 1)), bfloat(pick(right, 1 - rep))
    return kept, ((sent[0], "win", 2), (sent[1], "rep", 1))


def far_parts(total):
    far = place_bits()[1]
    hops = tuple((bfloat(pick(total, far ^ mask)), "win", mask << 2) for mask in (1, 2, 3))
    return pick(total, far), hops


def add_pair(kept, taken):
    return kept[0] + wide(taken[0]), kept[1] + wide(taken[1])


def add_far(kept, taken):
    return (kept + wide(taken[0])) + (wide(taken[1]) + wide(taken[2]))


def join_halves(pair):
    return jnp.concatenate(pair, axis=-1)


def spread_far(values):
    return tuple((values[None], "win", mask) for mask in (4, 8, 12))


def far_piece(values, taken):
    return jnp.concatenate([values[None], *taken])


def sum_everywhere(values, skip_core=True):
    for bit in range(1 if skip_core else 0, bit_count("win")):
        values = same_sum(values, "win", bit)
    for bit in range(bit_count("rep")):
        values = same_sum(values, "rep", bit)
    return values


def off_diagonal_step(iterate, exact):
    high = bfloat(iterate)
    gram = dot_as(high, high, NT)
    if exact:
        rest = bfloat(iterate - high.astype(jnp.float32))
        gram = gram + dot_as(high, rest, NT) + dot_as(rest, high, NT)
    size = gram.shape[0]
    row_ids = lax.broadcasted_iota(jnp.int32, (size, size), 0)
    on_diagonal = row_ids == lax.broadcasted_iota(jnp.int32, (size, size), 1)
    own = jnp.where(on_diagonal, gram, 0.0)
    own_column = jnp.sum(own, 1, keepdims=True)
    own_row = jnp.sum(own, 0, keepdims=True)
    off = jnp.where(on_diagonal, 0.0, gram)
    off_low = bfloat(off)
    square = product(off_low, off_low) + (own_column + own_row) * off
    poly = NEWTON_COEFFS[1] * off + NEWTON_COEFFS[2] * square
    poly_own = jnp.sum(jnp.where(on_diagonal, poly, 0.0), 1, keepdims=True)
    factor = (
        NEWTON_COEFFS[0]
        + poly_own
        + own_column * (NEWTON_COEFFS[1] + NEWTON_COEFFS[2] * own_column)
    )
    poly = jnp.where(on_diagonal, 0.0, poly)
    poly_high = bfloat(poly)
    moved = product(poly_high, high)
    if exact:
        poly_rest = bfloat(poly - poly_high.astype(jnp.float32))
        moved = moved + product(poly_high, rest) + product(poly_rest, high)
    return factor * iterate + moved


def unit_scale(values):
    total = jnp.sum(jnp.sum(values * values, 1, keepdims=True), 0, keepdims=True)
    return values * (1.0 / (jnp.sqrt(total) + EPSILON))


def block_start(place_ref, masks, block, rows, shift=0):
    if masks is None:
        return block * rows
    return pl.multiple_of(((place_ref[1] ^ masks[block]) >> shift) * rows, rows)


def numbered_blocks(piece_refs):
    for piece, piece_ref in enumerate(piece_refs):
        blocks = piece_ref.shape[0]
        for block in range(blocks):
            yield piece * blocks + block, piece_ref.at[block]


def big_newton_kernel(folds, masks, place_ref, *refs):
    piece_refs, (out_ref, iterate_ref, turned_ref) = refs[:-3], refs[-3:]
    _, rows, width = piece_refs[0].shape
    part = rows // folds

    @pl.when(place_ref[0] == 0)
    def _():
        for block, block_ref in numbered_blocks(piece_refs):
            start = block_start(place_ref, masks, block, part)
            for fold in range(folds):
                lanes = slice(fold * width, (fold + 1) * width)
                inner = slice(fold * part, (fold + 1) * part)
                iterate_ref[pl.ds(start, part), lanes] = block_ref[inner, :].astype(jnp.float32)

    @pl.when(place_ref[0] != 0)
    def _():
        for block, block_ref in numbered_blocks(piece_refs):
            start = block_start(place_ref, masks, block, rows)
            iterate_ref[:, pl.ds(start, rows)] = block_ref[...].astype(jnp.float32).T

    iterate_ref[...] = unit_scale(iterate_ref[...])

    @pl.loop(0, 5)
    def _(_):
        iterate_ref[...] = off_diagonal_step(iterate_ref[...], False)

    @pl.when(place_ref[0] == 0)
    def _():
        start = pl.multiple_of(place_ref[1] * part, part)
        for fold in range(folds):
            out_ref[fold * part : (fold + 1) * part, :] = bfloat(
                iterate_ref[pl.ds(start, part), fold * width : (fold + 1) * width]
            )

    @pl.when(place_ref[0] != 0)
    def _():
        span = max(rows, 128)
        start = pl.multiple_of(place_ref[1] * rows // span * span, span)
        turned_ref[...] = iterate_ref[:, pl.ds(start, span)].T * float(folds) ** 0.5
        inner = pl.multiple_of(place_ref[1] * rows - start, rows)
        out_ref[...] = bfloat(turned_ref[pl.ds(inner, rows), :])


def small_newton_kernel(masks, place_ref, *refs):
    piece_refs, (out_ref, iterate_ref) = refs[:-2], refs[-2:]
    _, matrices, rows, width = piece_refs[0].shape
    for block, block_ref in numbered_blocks(piece_refs):
        start = block_start(place_ref, masks, block, rows, 1)
        for number in range(matrices):
            iterate_ref[number, pl.ds(start, rows), :] = block_ref[number].astype(jnp.float32)

    @pl.loop(0, matrices)
    def _(number):
        iterate_ref[number] = unit_scale(iterate_ref[number])

        @pl.loop(0, 2)
        def _(_):
            iterate_ref[number] = off_diagonal_step(iterate_ref[number], False)

        @pl.loop(0, 3)
        def _(_):
            iterate_ref[number] = off_diagonal_step(iterate_ref[number], True)

    start = pl.multiple_of((place_ref[1] if masks is None else place_ref[1] >> 1) * rows, rows)
    for number in range(matrices):
        out_ref[number] = bfloat(iterate_ref[number, pl.ds(start, rows), :])


def newton_call(kernel, name, place, pieces, out_dims, scratch_dims, cost):
    return pl.pallas_call(
        kernel,
        in_specs=[pl.BlockSpec(memory_space=pltpu.SMEM)]
        + [pl.BlockSpec(memory_space=pltpu.VMEM)] * len(pieces),
        out_specs=pl.BlockSpec(memory_space=pltpu.VMEM),
        out_shape=shape_of(out_dims, jnp.bfloat16),
        scratch_shapes=[pltpu.VMEM(dims, jnp.float32) for dims in scratch_dims],
        compiler_params=pltpu.CompilerParams(vmem_limit_bytes=VMEM_LIMIT),
        cost_estimate=lasting(cost),
        name=name,
    )(place, *pieces)


def big_update(place, pieces, folds, masks):
    blocks, rows, width = pieces[0].shape
    columns = len(pieces) * blocks * rows
    return newton_call(
        functools.partial(big_newton_kernel, folds, masks),
        "big_newton",
        place,
        pieces,
        (rows, width),
        [(width, columns), (max(rows, 128), width)],
        16,
    )


def small_update(place, pieces, masks):
    _, matrices, rows, width = pieces[0].shape
    return newton_call(
        functools.partial(small_newton_kernel, masks),
        "small_newton",
        place,
        pieces,
        (matrices, rows, width),
        [(matrices, width, width)],
        10 * matrices,
    )


def fold_columns(rows, width):
    count, columns = rows.shape
    return rows.reshape(count, columns // width, width).swapaxes(0, 1).reshape(-1, width)


def pick_owner(first, here, there):
    return jnp.where(first, here, there), jnp.where(first, there, here)


def every_update(place, big_rows, small_rows, folds):
    updates = []
    for number, rows in enumerate(big_rows):
        here = jnp.stack([jnp.int32(number), place[1]])
        blocks = index_order(gather_blocks(bfloat(rows)))
        updates.append(big_update(here, blocks, folds, None))
    blocks = index_order(gather_blocks(bfloat(small_rows)))
    return updates[0], updates[1], small_update(place, blocks, None)


GROUP_HEADS = 128 // HEAD_DIM
SCORE_SCALE = HEAD_DIM ** (-0.5)
LOG2_E = 1.4426950408889634
VMEM_LIMIT = 44 * 1024 * 1024
VECTOR_ROWS = 16
NT = (((1,), (1,)), ((), ()))
TN = (((0,), (0,)), ((), ()))


def dot_as(left_side, right_side, dims):
    return lax.dot_general(left_side, right_side, dims, preferred_element_type=jnp.float32)


def spread_heads(part, lane_head):
    return bfloat(
        jnp.concatenate(
            [jnp.where(lane_head == head, part, 0.0) for head in range(GROUP_HEADS)], axis=0
        )
    )


def join_heads(spread, lane_head, rows):
    joined = spread[:rows]
    for head in range(1, GROUP_HEADS):
        joined = jnp.where(lane_head == head, spread[head * rows : (head + 1) * rows], joined)
    return joined


def column_softmax(scores, bias_column):
    scores = scores + bias_column
    raised = jnp.exp2((scores - jnp.max(scores, 0, keepdims=True)) * (SCORE_SCALE * LOG2_E))
    return raised * (1.0 / jnp.sum(raised, 0, keepdims=True))


def load_windows(tokens_ref, region_ref, fill_ref, count, seq_len, padded, step):
    for window in range(count):
        base = window * padded
        fill_ref[base : base + seq_len, :] = tokens_ref[0, window].astype(jnp.float32)
        fill_ref[base : base + 1, :] = region_ref[pl.ds(step * count + window, 1), :]


def window_forward_kernel(
    count,
    seq_len,
    padded,
    tokens_ref,
    region_ref,
    bias_ref,
    keep_ref,
    qkv_ref,
    out_ref,
    vec_ref,
    norm_out,
    proj_out,
    mix_out,
    after_out,
    fill_ref,
    mix_ref,
    scores_ref,
    probs_ref,
):
    step = pl.program_id(0)
    width = tokens_ref.shape[-1]

    @pl.when(step == 0)
    def _():
        fill_ref[...] = jnp.zeros_like(fill_ref)

    load_windows(tokens_ref, region_ref, fill_ref, count, seq_len, padded, step)
    flat = fill_ref[...]
    normed = bfloat(norm_rows(flat, vec_ref[2:3, :], vec_ref[3:4, :]))
    lane_head = lax.broadcasted_iota(jnp.int32, (padded, 128), 1) // HEAD_DIM
    query = product(normed, qkv_ref[0]) + vec_ref[6:7, :]
    keyset = product(normed, qkv_ref[1])
    values = product(normed, qkv_ref[2]) + vec_ref[7:8, :]
    pairs = [(window, group) for window in range(count) for group in range(width // 128)]
    for window in range(count):
        rows = slice(window * padded, (window + 1) * padded)
        norm_out[window] = normed[rows]
        proj_out[window, :, :width] = bfloat(query[rows])
        proj_out[window, :, width : 2 * width] = bfloat(keyset[rows])
        proj_out[window, :, 2 * width :] = bfloat(values[rows])
    for number, (window, group) in enumerate(pairs):
        rows = slice(window * padded, (window + 1) * padded)
        lanes = slice(group * 128, (group + 1) * 128)
        spread = spread_heads(query[rows, lanes], lane_head)
        scores_ref[number] = dot_as(bfloat(keyset[rows, lanes]), spread, NT)
    for number, (window, group) in enumerate(pairs):
        probs_ref[number] = bfloat(column_softmax(scores_ref[number], bias_ref[window]))
    for number, (window, group) in enumerate(pairs):
        rows = slice(window * padded, (window + 1) * padded)
        lanes = slice(group * 128, (group + 1) * 128)
        mixed = dot_as(probs_ref[number], bfloat(values[rows, lanes]), TN)
        mix_ref[rows, lanes] = join_heads(mixed, lane_head, padded)
    mixed_low = bfloat(mix_ref[...])
    branch = product(mixed_low, out_ref[...]) + vec_ref[8:9, :]
    for window in range(count):
        rows = slice(window * padded, (window + 1) * padded)
        mix_out[window] = mixed_low[rows]
        after_out[window] = flat[rows] + keep_ref[window] * branch[rows]


def window_backward_kernel(
    count,
    first_step,
    last,
    seq_len,
    padded,
    tokens_ref,
    region_ref,
    bias_ref,
    keep_ref,
    qkv_ref,
    out_ref,
    vec_ref,
    proj_ref,
    after_grad_ref,
    region_keep_ref,
    sums_before_ref,
    *rest,
):
    scratch_count = 8
    if last:
        region_branch_out, region_mix_out = rest[-scratch_count - 2 : -scratch_count]
        rest = rest[: -scratch_count - 2] + rest[-scratch_count:]
    (
        region_grad_out,
        sums_out,
        grad_out,
        proj_grad_out,
        branch_grad_out,
        fill_ref,
        proj_grad_ref,
        spread_ref,
        spread_grad_ref,
        scores_ref,
        probs_grad_ref,
        probs_ref,
        score_grad_ref,
    ) = rest[-13:]
    step = pl.program_id(0) + first_step
    width = tokens_ref.shape[-1]

    @pl.when(pl.program_id(0) == 0)
    def _():
        fill_ref[...] = jnp.zeros_like(fill_ref)
        sums_out[...] = sums_before_ref[...]
        if first_step == 0:
            region_grad_out[...] = jnp.zeros_like(region_grad_out)
        else:
            region_grad_out[...] = rest[0][...]

    load_windows(tokens_ref, region_ref, fill_ref, count, seq_len, padded, step)
    lane_head = lax.broadcasted_iota(jnp.int32, (padded, 128), 1) // HEAD_DIM
    branch_grad = bfloat(
        jnp.concatenate(
            [keep_ref[window] * after_grad_ref[window] for window in range(count)], axis=0
        )
    )
    mix_grad = dot_as(branch_grad, out_ref[...], NT)
    for window in range(count):
        branch_grad_out[window] = branch_grad[window * padded : (window + 1) * padded]
    pairs = [(window, group) for window in range(count) for group in range(width // 128)]

    def lanes_of(part, group):
        return slice(part * width + group * 128, part * width + (group + 1) * 128)

    for number, (window, group) in enumerate(pairs):
        query = proj_ref[window, :, lanes_of(0, group)].astype(jnp.float32)
        spread_ref[number] = spread_heads(query, lane_head)
        rows = slice(window * padded, (window + 1) * padded)
        spread_grad_ref[number] = spread_heads(mix_grad[rows, lanes_of(0, group)], lane_head)
    for number, (window, group) in enumerate(pairs):
        scores_ref[number] = dot_as(
            proj_ref[window, :, lanes_of(1, group)], spread_ref[number], NT
        )
        probs_grad_ref[number] = dot_as(
            proj_ref[window, :, lanes_of(2, group)], spread_grad_ref[number], NT
        )
    for number, (window, group) in enumerate(pairs):
        probs = column_softmax(scores_ref[number], bias_ref[window])
        weighted = probs * probs_grad_ref[number]
        probs_ref[number] = bfloat(probs)
        score_grad_ref[number] = bfloat(weighted - probs * jnp.sum(weighted, 0, keepdims=True))
    for number, (window, group) in enumerate(pairs):
        rows = slice(window * padded, (window + 1) * padded)
        proj_grad_ref[rows, lanes_of(2, group)] = product(
            probs_ref[number], spread_grad_ref[number]
        )
        proj_grad_ref[rows, lanes_of(1, group)] = (
            product(score_grad_ref[number], spread_ref[number]) * SCORE_SCALE
        )
    for number, (window, group) in enumerate(pairs):
        rows = slice(window * padded, (window + 1) * padded)
        query_grad = dot_as(score_grad_ref[number], proj_ref[window, :, lanes_of(1, group)], TN)
        proj_grad_ref[rows, lanes_of(0, group)] = (
            join_heads(query_grad, lane_head, padded) * SCORE_SCALE
        )
    proj_grad = bfloat(proj_grad_ref[...])
    norm_grad = sum(
        dot_as(proj_grad[:, number * width : (number + 1) * width], qkv_ref[number], NT)
        for number in range(3)
    )
    flat = fill_ref[...]
    center = flat - jnp.mean(flat, -1, keepdims=True)
    scale = lax.rsqrt(jnp.mean(center * center, -1, keepdims=True) + EPSILON)
    hat = center * scale
    hat_grad = norm_grad * vec_ref[2:3, :]
    flat_grad = scale * (
        hat_grad
        - jnp.mean(hat_grad, -1, keepdims=True)
        - hat * jnp.mean(hat_grad * hat, -1, keepdims=True)
    )
    proj_sums = jnp.sum(proj_grad.astype(jnp.float32), 0, keepdims=True)
    sums_out[2:3, :] += jnp.sum(norm_grad * hat, 0, keepdims=True)
    sums_out[3:4, :] += jnp.sum(norm_grad, 0, keepdims=True)
    sums_out[6:7, :] += proj_sums[:, :width]
    sums_out[7:8, :] += proj_sums[:, 2 * width :]
    sums_out[8:9, :] += jnp.sum(branch_grad.astype(jnp.float32), 0, keepdims=True)
    for window in range(count):
        rows = slice(window * padded, (window + 1) * padded)
        proj_grad_out[window] = proj_grad[rows]
        seq_grad = after_grad_ref[window] + flat_grad[rows]
        for group in range(width // 128):
            lanes = slice(group * 128, (group + 1) * 128)
            grad_out[window, pl.ds(group, seq_len, stride=width // 128), :] = seq_grad[
                :seq_len, lanes
            ]
        region_grad_out[pl.ds(step * count + window, 1), :] = seq_grad[0:1]

    if last:

        @pl.when(pl.program_id(0) == pl.num_programs(0) - 1)
        def _():
            region_branch = bfloat(region_keep_ref[...] * region_grad_out[...])
            sums_out[8:9, :] += jnp.sum(region_branch.astype(jnp.float32), 0, keepdims=True)
            region_branch_out[...] = region_branch
            regions = region_branch.shape[0]
            spare_rows = region_mix_out.shape[0] - regions - sums_out.shape[0]
            region_mix_out[:regions, :] = bfloat(dot_as(region_branch, out_ref[...], NT))
            sums_low = jnp.concatenate(
                [sums_out[...], jnp.zeros((spare_rows, width), jnp.float32)], axis=0
            )
            region_mix_out[regions:, :] = bfloat(sums_low)


def window_step(windows):
    return next(count for count in (4, 2, 1) if windows % count == 0)


def whole_spec(shape):
    return pl.BlockSpec(shape, lambda step: (0,) * len(shape))


def step_spec(count, *rest):
    return pl.BlockSpec((count,) + rest, lambda step: (step,) + (0,) * len(rest))


def token_spec(count, *rest):
    return pl.BlockSpec((1, count) + rest, lambda step: (0, step) + (0,) * len(rest))


def kept_spec():
    return pl.BlockSpec(memory_space=pltpu.VMEM)


def lasting(microseconds):
    return pl.CostEstimate(flops=microseconds * 10**9, bytes_accessed=10**6, transcendentals=0)


def in_hbm(values):
    return pltpu.with_memory_space_constraint(values, pltpu.HBM)


def hbm_shape(dims, kind=jnp.float32):
    return pltpu.HBM(dims, kind)


def shape_of(dims, kind=jnp.float32):
    return jax.ShapeDtypeStruct(dims, kind)


def window_forward(tokens, region, bias, keep, qkv_weight, out_weight, vectors, padded):
    _, windows, seq_len, width = tokens.shape
    count = window_step(windows)
    pairs = count * width // 128
    return pl.pallas_call(
        functools.partial(window_forward_kernel, count, seq_len, padded),
        grid=(windows // count,),
        in_specs=[
            token_spec(count, seq_len, width),
            whole_spec(region.shape),
            step_spec(count, padded, 1),
            step_spec(count, 1, 1),
            kept_spec(),
            kept_spec(),
            whole_spec(vectors.shape),
        ],
        out_specs=[
            step_spec(count, padded, width),
            step_spec(count, padded, 3 * width),
            step_spec(count, padded, width),
            step_spec(count, padded, width),
        ],
        out_shape=[
            hbm_shape((windows, padded, width), jnp.bfloat16),
            hbm_shape((windows, padded, 3 * width), jnp.bfloat16),
            hbm_shape((windows, padded, width), jnp.bfloat16),
            hbm_shape((windows, padded, width)),
        ],
        scratch_shapes=[
            pltpu.VMEM((count * padded, width), jnp.float32),
            pltpu.VMEM((count * padded, width), jnp.float32),
            pltpu.VMEM((pairs, padded, GROUP_HEADS * padded), jnp.float32),
            pltpu.VMEM((pairs, padded, GROUP_HEADS * padded), jnp.bfloat16),
        ],
        compiler_params=pltpu.CompilerParams(vmem_limit_bytes=VMEM_LIMIT),
        name="window_forward",
    )(in_hbm(tokens), region, bias, keep, qkv_weight, out_weight, vectors)


def window_backward(
    tokens,
    region,
    bias,
    keep,
    qkv_weight,
    out_weight,
    vectors,
    proj,
    after_grad,
    region_keep,
    before,
    steps,
    padded,
):
    _, windows, seq_len, width = tokens.shape
    count = window_step(windows)
    first_step, last_step = steps
    here = (last_step - first_step) * count
    pairs = count * width // 128
    spread_rows = GROUP_HEADS * padded

    def moved(*dims, lead=0):
        zeros = (0,) * (len(dims) - 1)
        if lead:
            return pl.BlockSpec((1,) + dims, lambda step: (0, step + first_step) + zeros)
        return pl.BlockSpec(dims, lambda step: (step + first_step,) + zeros)

    flat_rows = seq_len * width // 128

    grad_before, sums_before, region_before = before
    operands = [in_hbm(tokens), region, bias, keep, qkv_weight, out_weight, vectors]
    operands += [in_hbm(proj), in_hbm(after_grad), region_keep, in_hbm(sums_before)]
    in_specs = [
        moved(count, seq_len, width, lead=1),
        whole_spec(region.shape),
        moved(count, padded, 1),
        moved(count, 1, 1),
        kept_spec(),
        kept_spec(),
        whole_spec(vectors.shape),
        moved(count, padded, 3 * width),
        moved(count, padded, width),
        whole_spec(region_keep.shape),
        whole_spec(sums_before.shape),
    ]
    aliases = {}
    if first_step:
        aliases = {len(operands) + 1: 2}
        operands += [in_hbm(region_before), in_hbm(grad_before)]
        in_specs += [whole_spec(region.shape), pl.BlockSpec(memory_space=pl.ANY)]
    last = last_step * count == windows
    out_specs = [
        whole_spec(region.shape),
        whole_spec(vectors.shape),
        moved(count, flat_rows, 128),
        step_spec(count, padded, 3 * width),
        step_spec(count, padded, width),
    ]
    out_shape = [
        hbm_shape(region.shape),
        hbm_shape(vectors.shape),
        hbm_shape((windows, flat_rows, 128)),
        hbm_shape((here, padded, 3 * width), jnp.bfloat16),
        hbm_shape((here, padded, width), jnp.bfloat16),
    ]
    if last:
        payload = (region.shape[0] + VECTOR_ROWS, width)
        out_specs += [whole_spec(region.shape), whole_spec(payload)]
        out_shape += [shape_of(region.shape, jnp.bfloat16), shape_of(payload, jnp.bfloat16)]
    return pl.pallas_call(
        functools.partial(window_backward_kernel, count, first_step, last, seq_len, padded),
        grid=(last_step - first_step,),
        in_specs=in_specs,
        out_specs=out_specs,
        out_shape=out_shape,
        scratch_shapes=[
            pltpu.VMEM((count * padded, width), jnp.float32),
            pltpu.VMEM((count * padded, 3 * width), jnp.float32),
            pltpu.VMEM((pairs, spread_rows, 128), jnp.bfloat16),
            pltpu.VMEM((pairs, spread_rows, 128), jnp.bfloat16),
            pltpu.VMEM((pairs, padded, spread_rows), jnp.float32),
            pltpu.VMEM((pairs, padded, spread_rows), jnp.float32),
            pltpu.VMEM((pairs, padded, spread_rows), jnp.bfloat16),
            pltpu.VMEM((pairs, padded, spread_rows), jnp.bfloat16),
        ],
        input_output_aliases=aliases,
        compiler_params=pltpu.CompilerParams(vmem_limit_bytes=VMEM_LIMIT),
        cost_estimate=lasting(here),
        name="window_backward",
    )(*operands)


def insert_kernel(rows_ref, region_ref, out_ref):
    out_ref[...] = rows_ref[...]
    for window in range(rows_ref.shape[0]):
        for group in range(region_ref.shape[1] // 128):
            out_ref[window, group : group + 1, :] = region_ref[
                window : window + 1, group * 128 : (group + 1) * 128
            ]


def insert_regions(grad, region_grad):
    rows = pl.BlockSpec((grad.shape[0], 8, 128), lambda step: (0, 0, 0))
    return pl.pallas_call(
        insert_kernel,
        grid=(1,),
        in_specs=[rows, whole_spec(region_grad.shape)],
        out_specs=rows,
        out_shape=shape_of(grad.shape),
        input_output_aliases={0: 0},
        compiler_params=pltpu.CompilerParams(vmem_limit_bytes=VMEM_LIMIT),
        name="insert_regions",
    )(grad, region_grad)


GELU_IN = 0.7978845608028654
GELU_CUBE = 0.044715


def gelu_both(values):
    square = values * values
    bent = jnp.tanh(values * (GELU_IN + (GELU_IN * GELU_CUBE) * square))
    share = 0.5 + 0.5 * bent
    slope = share + (0.5 * values) * (1.0 - bent * bent) * (
        GELU_IN + (3.0 * GELU_IN * GELU_CUBE) * square
    )
    return values * share, slope


def split_cores(values, core):
    own_first = core == 0
    kept = jnp.where(own_first, values[:, 0], values[:, 1])
    sent = jnp.where(own_first, values[:, 1], values[:, 0])
    return kept, bfloat(sent)


def mlp_kernel(
    count,
    seq_len,
    padded,
    place_ref,
    after_ref,
    cot_ref,
    keep_ref,
    vec_ref,
    up_ref,
    down_ref,
    out_ref,
    grad_ref,
    sums_ref,
    kept_ref,
    sent_ref,
    cot_fill,
    up_total,
    down_total,
):
    step = pl.program_id(0)
    width = up_ref.shape[0]
    folds = up_ref.shape[1] // width

    @pl.when(step == 0)
    def _():
        cot_fill[...] = jnp.zeros_like(cot_fill)
        sums_ref[...] = jnp.zeros_like(sums_ref)
        up_total[...] = jnp.zeros_like(up_total)
        down_total[...] = jnp.zeros_like(down_total)

    keeps = []
    for window in range(count):
        base = window * padded
        cot_fill[base : base + seq_len, :] = cot_ref[0, window].astype(jnp.float32)
        keeps.append(jnp.broadcast_to(keep_ref[window], (padded, 1)))
    keep = jnp.concatenate(keeps, axis=0)
    flat = after_ref[...]
    center = flat - jnp.mean(flat, -1, keepdims=True)
    scale = lax.rsqrt(jnp.mean(center * center, -1, keepdims=True) + EPSILON)
    hat = center * scale
    normed = bfloat(hat * vec_ref[4:5, :] + vec_ref[5:6, :])
    normed_turned = normed.T
    cot = cot_fill[...]
    branch_grad = bfloat(keep * cot)
    branch = jnp.zeros_like(flat)
    norm_grad = jnp.zeros_like(flat)
    for fold in range(folds):
        lanes = slice(fold * width, (fold + 1) * width)
        up_part, down_part = up_ref[:, lanes], down_ref[lanes, :]
        hidden = product(normed, up_part) + vec_ref[10 + fold : 11 + fold, :]
        act, slope = gelu_both(hidden)
        act = bfloat(act)
        branch += product(act, down_part)
        hidden_grad = bfloat(slope * dot_as(branch_grad, down_part, NT))
        norm_grad += dot_as(hidden_grad, up_part, NT)
        up_total[fold] += product(normed_turned, hidden_grad)
        down_total[fold] += dot_as(act, branch_grad, TN)
        sums_ref[10 + fold : 11 + fold, :] += jnp.sum(
            hidden_grad.astype(jnp.float32), 0, keepdims=True
        )
    output = bfloat(flat + keep * (branch + vec_ref[9:10, :]))
    hat_grad = norm_grad * vec_ref[4:5, :]
    flat_grad = cot + scale * (
        hat_grad
        - jnp.mean(hat_grad, -1, keepdims=True)
        - hat * jnp.mean(hat_grad * hat, -1, keepdims=True)
    )
    sums_ref[4:5, :] += jnp.sum(norm_grad * hat, 0, keepdims=True)
    sums_ref[5:6, :] += jnp.sum(norm_grad, 0, keepdims=True)
    sums_ref[9:10, :] += jnp.sum(branch_grad.astype(jnp.float32), 0, keepdims=True)
    grad_ref[...] = flat_grad
    for window in range(count):
        out_ref[0, window] = output[window * padded : window * padded + seq_len]

    @pl.when(step == pl.num_programs(0) - 1)
    def _():
        core = place_ref[1] % 2
        _, blocks, rows, _ = kept_ref.shape
        part, here = rows // folds, blocks // folds
        for fold in range(folds):
            total = up_total[fold].reshape(blocks, 2, part, width)
            inner = slice(fold * part, (fold + 1) * part)
            kept_ref[0, :, inner], sent_ref[0, :, inner] = split_cores(total, core)
        for fold in range(folds):
            total = down_total[fold].reshape(here, 2, rows, width)
            inner = slice(fold * here, (fold + 1) * here)
            kept_ref[1, inner], sent_ref[1, inner] = split_cores(total, core)


def mlp(place, after, cotangent, keep, vectors, up_weight, down_weight, padded, win_count):
    _, windows, seq_len, width = cotangent.shape
    count = window_step(windows)
    rows = count * padded
    folds = up_weight.shape[1] // width
    half = win_count // 2
    up_rows = width // win_count
    dims = (2, half, up_rows * folds, width)
    flat_rows = pl.BlockSpec((rows, width), lambda step: (step, 0))
    output, grad, sums, kept, sent = pl.pallas_call(
        functools.partial(mlp_kernel, count, seq_len, padded),
        grid=(windows // count,),
        in_specs=[
            pl.BlockSpec(memory_space=pltpu.SMEM),
            flat_rows,
            token_spec(count, seq_len, width),
            step_spec(count, 1, 1),
            whole_spec(vectors.shape),
            kept_spec(),
            kept_spec(),
        ],
        out_specs=[
            token_spec(count, seq_len, width),
            flat_rows,
            whole_spec(vectors.shape),
            whole_spec(dims),
            whole_spec(dims),
        ],
        out_shape=[
            hbm_shape(cotangent.shape, jnp.bfloat16),
            hbm_shape(after.shape),
            hbm_shape(vectors.shape),
            hbm_shape(dims),
            hbm_shape(dims, jnp.bfloat16),
        ],
        scratch_shapes=[
            pltpu.VMEM((rows, width), jnp.float32),
            pltpu.VMEM((folds, width, width), jnp.float32),
            pltpu.VMEM((folds, width, width), jnp.float32),
        ],
        compiler_params=pltpu.CompilerParams(vmem_limit_bytes=VMEM_LIMIT),
        cost_estimate=lasting(30),
        name="mlp",
    )(place, in_hbm(after), in_hbm(cotangent), keep, vectors, up_weight, down_weight)
    return output, grad, sums, (kept, sent)


def image_bias(keys_ref, queries_ref):
    return jnp.where(keys_ref[...] == queries_ref[...], 0.0, -1e30)


def region_forward_kernel(
    pieces,
    *refs,
):
    piece_refs, refs = refs[:pieces], refs[pieces:]
    region_forward_rows(piece_refs, *refs)


def region_forward_rows(
    piece_refs,
    own_ref,
    keep_ref,
    key_image_ref,
    query_image_ref,
    qkv_ref,
    out_ref,
    vec_ref,
    norm_out,
    proj_out,
    mix_out,
    new_out,
    all_ref,
):
    rows, width = own_ref.shape
    vec = vec_ref[...]
    for block, block_ref in numbered_blocks(piece_refs):
        all_ref[block * rows : (block + 1) * rows, :] = block_ref[...].astype(jnp.float32)
    normed = bfloat(norm_rows(all_ref[...], vec[0:1], vec[1:2]))
    norm_out[...] = normed
    query = bfloat(product(normed, qkv_ref[0]) + vec[6:7])
    keyset = bfloat(product(normed, qkv_ref[1]))
    values = bfloat(product(normed, qkv_ref[2]) + vec[7:8])
    proj_out[:, :width] = query
    proj_out[:, width : 2 * width] = keyset
    proj_out[:, 2 * width :] = values
    region = own_ref[...].astype(jnp.float32)
    own_norm = bfloat(norm_rows(region, vec[0:1], vec[1:2]))
    own_query = product(own_norm, qkv_ref[0]) + vec[6:7]
    bias = image_bias(key_image_ref, query_image_ref)
    lane_head = lax.broadcasted_iota(jnp.int32, (rows, 128), 1) // HEAD_DIM
    parts = []
    for group in range(width // 128):
        lanes = slice(group * 128, (group + 1) * 128)
        spread = spread_heads(own_query[:, lanes], lane_head)
        probs = column_softmax(dot_as(keyset[:, lanes], spread, NT), bias)
        mixed = dot_as(bfloat(probs), values[:, lanes], TN)
        parts.append(join_heads(mixed, lane_head, rows))
    mixed_low = bfloat(jnp.concatenate(parts, axis=1))
    mix_out[...] = mixed_low
    branch = product(mixed_low, out_ref[...]) + vec[8:9]
    new_out[...] = region + keep_ref[...] * branch


def region_forward(pieces, own, keep, key_images, query_images, qkv_weight, out_weight, vectors):
    rows, width = own.shape
    total = len(pieces) * pieces[0].shape[0] * rows
    return pl.pallas_call(
        functools.partial(region_forward_kernel, len(pieces)),
        out_shape=[
            hbm_shape((total, width), jnp.bfloat16),
            hbm_shape((total, 3 * width), jnp.bfloat16),
            hbm_shape(own.shape, jnp.bfloat16),
            shape_of(own.shape),
        ],
        scratch_shapes=[pltpu.VMEM((total, width), jnp.float32)],
        compiler_params=pltpu.CompilerParams(vmem_limit_bytes=VMEM_LIMIT),
        name="region_forward",
    )(*pieces, own, keep, key_images, query_images, qkv_weight, out_weight, vectors)


def region_backward_kernel(pieces, place_ref, *refs):
    region_refs, refs = refs[:pieces], refs[pieces:]
    gathered_refs, refs = refs[:pieces], refs[pieces:]
    region_backward_rows(place_ref, region_refs, gathered_refs, *refs)


def region_backward_rows(
    place_ref,
    region_refs,
    gathered_refs,
    norm_ref,
    proj_ref,
    key_image_ref,
    query_image_ref,
    new_grad_ref,
    qkv_ref,
    vec_ref,
    grad_out,
    weight_out,
    sums_out,
    bias_ref,
    proj_grad_ref,
    region_grad_ref,
    weight_ref,
    mix_grad_ref,
    all_ref,
    scores_ref,
    probs_grad_ref,
    probs_ref,
    score_grad_ref,
):
    total, width = all_ref.shape
    rows = new_grad_ref.shape[0]
    bias_ref[...] = image_bias(key_image_ref, query_image_ref)
    lane_head = lax.broadcasted_iota(jnp.int32, (total, 128), 1) // HEAD_DIM
    for block, block_ref in numbered_blocks(region_refs):
        all_ref[block * rows : (block + 1) * rows, :] = block_ref[...].astype(jnp.float32)
    vector_sum = jnp.zeros((VECTOR_ROWS, width), jnp.float32)
    for block, block_ref in numbered_blocks(gathered_refs):
        part = block_ref[...].astype(jnp.float32)
        mix_grad_ref[block * rows : (block + 1) * rows, :] = part[:rows]
        vector_sum += part[rows:]

    @pl.loop(0, width // 128)
    def _(group):
        query_lanes = pl.ds(pl.multiple_of(group * 128, 128), 128)
        key_lanes = pl.ds(pl.multiple_of(width + group * 128, 128), 128)
        value_lanes = pl.ds(pl.multiple_of(2 * width + group * 128, 128), 128)
        key_low = proj_ref[:, key_lanes]
        value_low = proj_ref[:, value_lanes]
        spread = spread_heads(proj_ref[:, query_lanes].astype(jnp.float32), lane_head)
        spread_grad = spread_heads(mix_grad_ref[:, query_lanes], lane_head)
        scores_ref[...] = dot_as(key_low, spread, NT)
        probs_grad_ref[...] = dot_as(value_low, spread_grad, NT)
        for head in range(GROUP_HEADS):
            lanes = slice(head * total, (head + 1) * total)
            probs = column_softmax(scores_ref[:, lanes], bias_ref[...])
            weighted = probs * probs_grad_ref[:, lanes]
            probs_ref[:, lanes] = bfloat(probs)
            score_grad_ref[:, lanes] = bfloat(
                weighted - probs * jnp.sum(weighted, 0, keepdims=True)
            )
        value_grad = product(probs_ref[...], spread_grad)
        key_grad = product(score_grad_ref[...], spread)
        turned = product(key_low.T, score_grad_ref[...])
        query_grad = jnp.concatenate(
            [
                turned[head * HEAD_DIM : (head + 1) * HEAD_DIM, head * total : (head + 1) * total]
                for head in range(GROUP_HEADS)
            ],
            axis=0,
        ).T
        proj_grad_ref[:, query_lanes] = bfloat(query_grad * SCORE_SCALE)
        proj_grad_ref[:, key_lanes] = bfloat(key_grad * SCORE_SCALE)
        proj_grad_ref[:, value_lanes] = bfloat(value_grad)

    proj_grad = proj_grad_ref[...]
    norm_grad = sum(
        dot_as(proj_grad[:, number * width : (number + 1) * width], qkv_ref[number], NT)
        for number in range(3)
    )
    region = all_ref[...]
    center = region - jnp.mean(region, -1, keepdims=True)
    scale = lax.rsqrt(jnp.mean(center * center, -1, keepdims=True) + EPSILON)
    hat = center * scale
    hat_grad = norm_grad * vec_ref[0:1, :]
    region_grad_ref[...] = scale * (
        hat_grad
        - jnp.mean(hat_grad, -1, keepdims=True)
        - hat * jnp.mean(hat_grad * hat, -1, keepdims=True)
    )
    grad_out[...] = new_grad_ref[...] + region_grad_ref[:rows, :]
    bias_sums = jnp.sum(proj_grad.astype(jnp.float32), 0, keepdims=True)
    sums_out[...] = vector_sum
    sums_out[0:1, :] += jnp.sum(norm_grad * hat, 0, keepdims=True)
    sums_out[1:2, :] += jnp.sum(norm_grad, 0, keepdims=True)
    sums_out[6:7, :] += bias_sums[:, :width]
    sums_out[7:8, :] += bias_sums[:, 2 * width :]
    weight_ref[...] = dot_as(norm_ref[...], proj_grad, TN)
    weight_rows = weight_out.shape[1]
    weight_start = pl.multiple_of((place_ref[1] >> 1) * weight_rows, 8)
    for number in range(3):
        weight_out[number] = weight_ref[
            pl.ds(weight_start, weight_rows), number * width : (number + 1) * width
        ]


def region_backward(
    place,
    regions,
    gathered,
    normed,
    proj,
    key_images,
    query_images,
    new_grad,
    qkv_weight,
    vectors,
    weight_rows,
):
    total, width = normed.shape
    vmem = pl.BlockSpec(memory_space=pltpu.VMEM)
    operands = [*regions, *gathered, in_hbm(normed), in_hbm(proj), key_images, query_images]
    operands += [new_grad, qkv_weight, vectors]
    return pl.pallas_call(
        functools.partial(region_backward_kernel, len(regions)),
        grid=(1,),
        in_specs=[pl.BlockSpec(memory_space=pltpu.SMEM)]
        + [whole_spec(operand.shape) for operand in operands[:-2]]
        + [vmem, whole_spec(vectors.shape)],
        out_specs=[vmem] * 3,
        out_shape=[
            shape_of(new_grad.shape),
            shape_of((3, weight_rows, width)),
            shape_of((VECTOR_ROWS, width)),
        ],
        scratch_shapes=[
            pltpu.VMEM((total, total), jnp.float32),
            pltpu.VMEM((total, 3 * width), jnp.bfloat16),
            pltpu.VMEM((total, width), jnp.float32),
            pltpu.VMEM((width, 3 * width), jnp.float32),
            pltpu.VMEM((total, width), jnp.float32),
            pltpu.VMEM((total, width), jnp.float32),
            pltpu.VMEM((total, GROUP_HEADS * total), jnp.float32),
            pltpu.VMEM((total, GROUP_HEADS * total), jnp.float32),
            pltpu.VMEM((total, GROUP_HEADS * total), jnp.bfloat16),
            pltpu.VMEM((total, GROUP_HEADS * total), jnp.bfloat16),
        ],
        compiler_params=pltpu.CompilerParams(vmem_limit_bytes=VMEM_LIMIT),
        cost_estimate=lasting(14),
        name="region_backward",
    )(place, *operands)


def pair_gradient_kernel(first_count, second_count, place_ref, *refs):
    own_first = place_ref[1] % 2 == 0
    kept, sent = refs[-2:]

    def total(pairs):
        lefts, rights = pairs[0::2], pairs[1::2]
        return sum(dot_as(left[...], right[...], TN) for left, right in zip(lefts, rights))

    first = total(refs[: 2 * first_count])
    second = total(refs[2 * first_count : 2 * (first_count + second_count)])
    kept[...] = jnp.where(own_first, first, second)
    sent[...] = bfloat(jnp.where(own_first, second, first))


def pair_gradients(place, first, second, width):
    operands, in_specs = [place], [pl.BlockSpec(memory_space=pltpu.SMEM)]
    for left, row, right, column, rows in first + second:
        operands += [in_hbm(left), in_hbm(right)]
        in_specs.append(pl.BlockSpec((rows, width), lambda step, row=row: (row, 0)))
        in_specs.append(pl.BlockSpec((rows, width), lambda step, column=column: (0, column)))
    return pl.pallas_call(
        functools.partial(pair_gradient_kernel, len(first), len(second)),
        grid=(1,),
        in_specs=in_specs,
        out_specs=[whole_spec((width, width))] * 2,
        out_shape=[hbm_shape((width, width)), hbm_shape((width, width), jnp.bfloat16)],
        compiler_params=pltpu.CompilerParams(vmem_limit_bytes=VMEM_LIMIT),
        cost_estimate=lasting(5),
        name="pair_gradients",
    )(*operands)


def row_pieces(whole, rights, column):
    pairs, start = [], 0
    for right in rights:
        rows = right.shape[0]
        left, row = (whole, start // rows) if start % rows == 0 else (whole[start : start + rows], 0)
        pairs.append((left, row, right, column, rows))
        start += rows
    return pairs


def finish_big_kernel(
    place_ref, mine, other, mom_mine, mom_other, up_ref, down_ref, up_new, down_new, up_mom, down_mom
):
    first = place_ref[0] == 0

    def ordered(here, there):
        return jnp.where(first, here, there), jnp.where(first, there, here)

    updates = ordered(mine[...].astype(jnp.float32), other[...].astype(jnp.float32))
    momenta = ordered(mom_mine[...], mom_other[...])
    down_new[...] = down_ref[...].astype(jnp.float32) - MATRIX_RATE * updates[1]
    down_mom[...] = momenta[1]
    rows, columns = up_ref.shape
    width = down_ref.shape[1]
    for fold in range(columns // width):
        lanes = slice(fold * width, (fold + 1) * width)
        inner = slice(fold * rows, (fold + 1) * rows)
        up_new[:, lanes] = up_ref[:, lanes].astype(jnp.float32) - MATRIX_RATE * updates[0][inner]
        up_mom[:, lanes] = momenta[0][inner]


def finish_small_kernel(place_ref, *refs):
    updates, momenta = refs[:4], refs[4:8]
    qkv_ref, out_ref, qkv_new, out_new, qkv_mom, out_mom = refs[8:]
    first, low = place_ref[0] == 0, place_ref[2] == 0

    def ordered(parts):
        own, side, across, corner = [part[...].astype(jnp.float32) for part in parts]
        here = jnp.where(low, own, side), jnp.where(low, side, own)
        there = jnp.where(low, across, corner), jnp.where(low, corner, across)
        return [jnp.where(first, one, two) for one, two in zip(here + there, there + here)]

    for number, (update, momentum) in enumerate(zip(ordered(updates), ordered(momenta))):
        if number < 3:
            qkv_new[number] = qkv_ref[number].astype(jnp.float32) - MATRIX_RATE * update
            qkv_mom[number] = momentum
        else:
            out_new[...] = out_ref[...].astype(jnp.float32) - MATRIX_RATE * update
            out_mom[...] = momentum


def finish_call(kernel, name, place, parts, weights, blocks, indices):
    dims = [shape_of(block) for block in blocks]
    return pl.pallas_call(
        kernel,
        grid_spec=pltpu.PrefetchScalarGridSpec(
            num_scalar_prefetch=1,
            grid=(1,),
            in_specs=[pl.BlockSpec(part.shape, lambda step, place: (0, 0)) for part in parts]
            + [pl.BlockSpec(block, index) for block, index in zip(blocks, indices)],
            out_specs=[
                pl.BlockSpec(block, lambda step, place, count=len(block): (0,) * count)
                for block in blocks + blocks
            ],
        ),
        out_shape=dims + dims,
        compiler_params=pltpu.CompilerParams(vmem_limit_bytes=VMEM_LIMIT),
        name=name,
    )(place, *parts, *weights)


def finish_big(place, parts, up_weight, down_weight):
    rows, width = parts[0].shape
    up_rows = rows * width // up_weight.shape[1]
    own = lambda step, place: (place[1], 0)
    return finish_call(
        finish_big_kernel,
        "finish_big",
        place,
        parts,
        (up_weight, down_weight),
        [(up_rows, up_weight.shape[1]), (rows, width)],
        [own, own],
    )


def finish_small(place, parts, qkv_weight, out_weight):
    rows, width = parts[0].shape
    return finish_call(
        finish_small_kernel,
        "finish_small",
        place,
        parts,
        (qkv_weight, out_weight),
        [(3, rows, width), (rows, width)],
        [lambda step, place: (0, place[1], 0), lambda step, place: (place[1], 0)],
    )


def local(
    tokens,
    patch_mask,
    keep_mask,
    image_map,
    qkv_weight,
    out_weight,
    up_weight,
    down_weight,
    vectors,
    qkv_mom,
    out_mom,
    up_mom,
    down_mom,
    vec_mom,
    cotangent,
):
    windows = tokens.shape[1]
    seq_len = tokens.shape[2]
    model_width = tokens.shape[3]
    hidden_width = up_weight.shape[1]
    folds = hidden_width // model_width
    shard_rows = out_mom.shape[0]
    ff_rows = down_mom.shape[0]
    vec_rows = vec_mom.shape[0]
    padded = (seq_len + 7) // 8 * 8
    region_rows = (windows + 7) // 8 * 8
    row_count = windows * padded
    win_count = lax.axis_size("win")
    win_index = lax.axis_index("win")
    place = jnp.stack([lax.axis_index("rep"), win_index]).astype(jnp.int32)

    def pad_rows(values, rows, fill=0):
        widths = ((0, rows - values.shape[0]),) + ((0, 0),) * (values.ndim - 1)
        return jnp.pad(values, widths, constant_values=fill)

    region_own = pad_rows(tokens[0, :, 0], region_rows)
    regions = gather_blocks(region_own)
    keeper = keep_mask[0].astype(jnp.float32) / KEEP_SHARE
    images = image_map[0].reshape(win_count, windows)[win_index ^ jnp.array(gather_masks())]
    images = jnp.pad(images, ((0, 0), (0, region_rows - windows)), constant_values=-1)
    key_images = images.reshape(-1, 1)
    own_images = jnp.tile(images[:1], (1, GROUP_HEADS))
    region_keep = pad_rows(keeper[:, 0:1], region_rows)

    big_moms = (
        MOMENTUM_DECAY * fold_columns(up_mom, model_width),
        MOMENTUM_DECAY * down_mom,
    )
    small_old_moms = MOMENTUM_DECAY * jnp.concatenate([qkv_mom, out_mom[None]])
    own_pair = jnp.where(lax.axis_index("rep") == 0, small_old_moms[:2], small_old_moms[2:])
    kept, sent = pick_owner(win_index % 2 == 0, own_pair[0], own_pair[1])
    small_pair_mom = jnp.concatenate(
        pick_owner(win_index % 2 == 0, kept, swap(sent, "win", 0))
    )
    regions, big_moms, small_pair_mom = tie(regions, big_moms, small_pair_mom)

    region_norm, region_proj, region_mix, region_new = region_forward(
        regions, region_own, region_keep, key_images, own_images, qkv_weight, out_weight, vectors
    )

    key_valid = jnp.concatenate([jnp.ones((windows, 1), jnp.int32), patch_mask[0]], axis=1) == 1
    key_bias = jnp.where(key_valid, 0.0, -1e30)
    key_bias = jnp.pad(key_bias, ((0, 0), (0, padded - seq_len)), constant_values=-1e30)
    key_bias = key_bias[:, :, None]
    keep_window = keeper[:, 1].reshape(windows, 1, 1)
    seq_norm, seq_proj, local_mix, after_attn = window_forward(
        tokens, region_new, key_bias, keep_window, qkv_weight, out_weight, vectors, padded
    )
    seq_norm = seq_norm.reshape(row_count, model_width)
    local_mix = local_mix.reshape(row_count, model_width)
    after_attn = after_attn.reshape(row_count, model_width)

    out_tokens, attn_res_grad, mlp_sums, big_halves = mlp(
        place,
        after_attn,
        cotangent,
        keeper[:, 2].reshape(windows, 1, 1),
        vectors,
        up_weight,
        down_weight,
        padded,
        win_count,
    )

    steps = windows // window_step(windows)
    cuts = [0, steps * 2 // 5, steps * 4 // 5, steps]
    after_grad = attn_res_grad.reshape(windows, padded, model_width)
    two_owners = lax.axis_size("rep") == 2 and len(far_bits()) == 2
    order = Order()
    big_taken = order.launch((big_halves[1], "win", 1))
    before = (None, mlp_sums, None)
    proj_grads, branch_grads = [], []
    for piece in range(3):
        region_new_grad, sums, seq_grad, proj_grad, branch_grad, *region_parts = window_backward(
            tokens,
            region_new,
            key_bias,
            keep_window,
            qkv_weight,
            out_weight,
            vectors,
            seq_proj,
            after_grad,
            region_keep,
            before,
            (cuts[piece], cuts[piece + 1]),
            padded,
        )
        before = (seq_grad, sums, region_new_grad)
        proj_grads.append(proj_grad.reshape(-1, 3 * model_width))
        branch_grads.append(branch_grad.reshape(-1, model_width))
        if piece == 0:
            big_taken, after_grad = tie(big_taken, after_grad)
            big_total = big_halves[0] + wide(big_taken[0])
            if two_owners:
                big_kept, hops = first_parts(big_total)
                big_taken = order.launch(*hops)
        if piece == 1 and two_owners:
            big_taken, after_grad = tie(big_taken, after_grad)
            big_kept, hops = second_parts(*add_pair(big_kept, big_taken))
            hops, after_grad = tie([array for array, _, _ in hops], after_grad)
            big_taken = order.launch((hops[0], "win", 2), (hops[1], "rep", 1))
    region_branch_grad, region_mix_grad = region_parts
    norm_rows_ready, mix_ready = seq_norm, local_mix
    if two_owners:
        mix_taken = order.launch(*spread_far(region_mix_grad))
        big_kept, hops = far_parts(join_halves(add_pair(big_kept, big_taken)))
        hops, norm_rows_ready = tie([array for array, _, _ in hops], seq_norm)
        big_taken = order.launch(*[(hop, "win", 4 * (i + 1)) for i, hop in enumerate(hops)])

    first = lax.axis_index("rep") == 0
    low_core = win_index % 2 == 0
    kept, sent = pair_gradients(
        place,
        row_pieces(norm_rows_ready, proj_grads, 0),
        row_pieces(norm_rows_ready, proj_grads, 1),
        model_width,
    )
    if two_owners:
        kept, sent, mix_taken = tie(kept, sent, mix_taken)
        mixes = [far_piece(region_mix_grad, mix_taken)]
        mixes, mix_ready = tie(mixes, local_mix)
        mix_taken = order.launch((mixes[0], "win", 2))
    small_kept = [kept]
    small_taken = order.launch((sent, "win", 1))
    kept, sent = pair_gradients(
        place,
        row_pieces(seq_norm, proj_grads, 2),
        row_pieces(mix_ready, branch_grads, 0)
        + [(region_mix, 0, region_branch_grad, 0, region_rows)],
        model_width,
    )
    if two_owners:
        kept, sent, mix_taken, big_taken = tie(kept, sent, mix_taken, big_taken)
    small_kept.append(kept)
    small_taken += order.launch((sent, "win", 1))
    if two_owners:
        mixes += mix_taken
        mix_taken = order.launch(*[(piece, "win", 1) for piece in mixes])
    small_totals = [
        (kept + wide(taken)).reshape(-1, 2 * shard_rows, model_width)
        for kept, taken in zip(small_kept, order.land(small_taken))
    ]
    if two_owners:
        small_kept, hops = first_parts_of_two(small_totals)
        small_sent = [array for array, _, _ in hops]
        small_taken = order.launch(*hops)
        big_mom = jnp.where(first, big_moms[0], big_moms[1])
        big_mom = big_mom + add_far(big_kept, big_taken)
        big_low = bfloat(big_mom)
        big_taken = order.launch(*spread_far(big_low))
        mixes += mix_taken
        mixes = after(mixes, small_sent, big_low)
    else:
        mixes = gather_blocks(region_mix_grad)

    region_grad, region_weight_grad, region_sums = region_backward(
        place,
        regions,
        mixes,
        region_norm,
        region_proj,
        key_images,
        key_images.reshape(1, -1),
        region_new_grad,
        qkv_weight,
        vectors,
        2 * shard_rows,
    )

    if two_owners:
        region_weight_grad, small_taken, big_taken = tie(region_weight_grad, small_taken, big_taken)
        def spread_pair(mine):
            mine = mine.reshape(2, shard_rows, model_width)
            kept, sent = pick_owner(low_core, mine[0], mine[1])
            taken = order.launch((sent, "win", 1), (kept, "rep", 1), (sent, ("win", "rep"), 3))
            return kept, taken

        rep_rows = jnp.stack(
            [
                jnp.where(low_core, region_weight_grad[0], region_weight_grad[1]),
                jnp.where(low_core, region_weight_grad[2], 0.0),
            ]
        )
        rep = lax.axis_index("rep")
        vec_mine = rounded(region_sums)
        small_kept, hops = second_parts(*add_pair(small_kept, small_taken))
        small_taken = order.launch(*hops)
        vec_taken = order.launch(
            (bfloat(jnp.concatenate([pick(rep_rows, 1 - rep), vec_mine])), "rep", 1)
        )
        big_pieces = [far_piece(big_low, order.land(big_taken))]
        big_taken = order.launch((big_pieces[0], "win", 2))
        small_kept, hops = far_parts(join_halves(add_pair(small_kept, order.land(small_taken))))
        small_taken = order.launch(*hops)
        vec_taken = wide(vec_taken[0])
        region_rows_sum = pick(rep_rows, rep) + vec_taken[: 2 * shard_rows]
        vec_sum = vec_mine + vec_taken[2 * shard_rows :]
        big_pieces += order.land(big_taken)
        big_taken = order.launch(*[(piece, "win", 1) for piece in big_pieces])
        small_mom = add_far(small_kept, order.land(small_taken)) + region_rows_sum
        small_mom = small_pair_mom + small_mom
        small_low = bfloat(small_mom)
        small_taken = order.launch(*spread_far(small_low))
        input_grad = insert_regions(seq_grad, after(region_grad, *order.sent))
        input_grad = input_grad.reshape(tokens.shape)
        small_pieces = [far_piece(small_low, order.land(small_taken))]
        small_taken = order.launch((small_pieces[0], "win", 2))
        mom_parts = spread_pair(small_mom)
        other_mom = order.launch((big_mom, "rep", 1))[0]
        big_pieces += order.land(big_taken)
        big_mine = big_update(place, big_pieces, folds, gather_masks())

        other_update = order.launch((big_mine, "rep", 1))[0]
        small_pieces += order.land(small_taken)
        small_pieces, mom_parts, other_mom = tie(small_pieces, mom_parts, other_mom)
        small_mine = small_update(
            place, [piece[:, None] for piece in small_pieces], gather_masks(1)
        )[0]
        update_parts = spread_pair(small_mine)
        other_update = order.land(other_update)
        finish_place = jnp.concatenate([place, place[1:] & 1])
        big_parts = [big_mine, other_update, big_mom, other_mom]
        small_parts = [update_parts[0], *update_parts[1], mom_parts[0], *mom_parts[1]]
    else:
        input_grad = insert_regions(seq_grad, region_grad).reshape(tokens.shape)
        big_total = pick(sum_everywhere(big_total), win_index >> 1, 1)
        folded_up_mom = big_moms[0] + big_total[0]
        new_down_mom = big_moms[1] + big_total[1]
        small_total = sum_everywhere(jnp.stack(small_totals))
        other = swap(bfloat(small_total), "win", 0)
        pairs = jnp.stack(pick_owner(low_core, bfloat(small_total), other), axis=1)
        pairs = pairs.reshape(4, -1, 2 * shard_rows, model_width)
        region_pairs = jnp.pad(region_weight_grad, ((0, 1), (0, 0), (0, 0)))
        vec_sum = region_sums
        for bit in range(bit_count("rep")):
            region_pairs = same_sum(region_pairs, "rep", bit)
            vec_sum = same_sum(vec_sum, "rep", bit)
        rows = wide(pick(pairs, win_index >> 1, 1)) + region_pairs
        rows = rows.reshape(4, 2, shard_rows, model_width)
        small_moms = small_old_moms + pick(rows, win_index & 1, 1)
        up_update, down_update, updates = every_update(
            place, (folded_up_mom, new_down_mom), small_moms, folds
        )
        finish_place = jnp.stack([0 * win_index, win_index, 0 * win_index]).astype(jnp.int32)
        big_parts = [up_update, down_update, folded_up_mom, new_down_mom]
        small_parts = [*updates, *small_moms]
    new_up, new_down, new_up_mom, new_down_mom = finish_big(
        finish_place, big_parts, up_weight, down_weight
    )
    new_qkv, new_out, new_qkv_mom, new_out_mom = finish_small(
        finish_place, small_parts, qkv_weight, out_weight
    )
    vec_total = lax.dynamic_slice_in_dim(vec_sum.reshape(-1), win_index * vec_rows, vec_rows)
    new_vec_mom = MOMENTUM_DECAY * vec_mom + vec_total
    new_vectors = (
        lax.dynamic_slice_in_dim(vectors.reshape(-1), win_index * vec_rows, vec_rows)
        - VECTOR_RATE * new_vec_mom
    )

    return (
        out_tokens,
        input_grad,
        new_qkv_mom,
        new_qkv,
        new_out_mom,
        new_out,
        new_up_mom,
        new_up,
        new_down_mom,
        new_down,
        new_vec_mom,
        new_vectors,
    )


def solution(mesh):
    placed = (
        P("rep", "win", None, None),
        P("rep", "win", None),
        P("rep", "win", None),
        P("rep", None),
        P(),
        P(),
        P(),
        P(),
        P(),
        P(None, "win", None),
        P("win", None),
        P("win", None),
        P("win", None),
        P("win"),
        P("rep", "win", None, None),
    )
    return jax.shard_map(
        local,
        mesh=mesh,
        in_specs=placed,
        out_specs=(
            P("rep", "win", None, None),
            P("rep", "win", None, None),
            P(None, "win", None),
            P(None, "win", None),
            P("win", None),
            P("win", None),
            P("win", None),
            P("win", None),
            P("win", None),
            P("win", None),
            P("win"),
            P("win"),
        ),
        check_vma=False,
    )
```

```python
import functools

import jax
import jax.numpy as jnp
from jax import lax
from jax.experimental import pallas as pl
from jax.experimental.pallas import tpu as pltpu
from jax.sharding import PartitionSpec as P

HEADS = 16
HEAD_DIM = 32


EPSILON = 1e-06
MOMENTUM_DECAY = 0.95
MATRIX_RATE = 0.5
VECTOR_RATE = 0.0002
KEEP_SHARE = 0.75
NEWTON_COEFFS = (3.4445, -4.775, 2.0315)


def bfloat(values):
    return values.astype(jnp.bfloat16)


def product(left_side, right_side):
    return jnp.dot(left_side, right_side, preferred_element_type=jnp.float32)


def norm_rows(values, gain_row, shift_row):
    center = values - jnp.mean(values, -1, keepdims=True)
    spread = jnp.mean(center * center, -1, keepdims=True)
    return center * lax.rsqrt(spread + EPSILON) * gain_row + shift_row


def bit_count(axis):
    return lax.axis_size(axis).bit_length() - 1


def swap(values, axis, bit):
    size = lax.axis_size(axis)
    return lax.ppermute(values, axis, [(i, i ^ (1 << bit)) for i in range(size)])


def my_bit(axis, bit):
    return (lax.axis_index(axis) >> bit) & 1


def far_bits():
    return list(range(2, bit_count("win")))


def gather_masks(low=0):
    masks = [0]
    for bit in far_bits() + [1, 0]:
        if bit >= low:
            masks += [mask | (1 << bit) for mask in masks]
    return masks


def gather_far(values):
    size = lax.axis_size("win")
    values = values[None]
    if len(far_bits()) == 2:
        others = [
            lax.ppermute(values, "win", [(i, i ^ mask) for i in range(size)]) for mask in (4, 8, 12)
        ]
        return [jnp.concatenate([values] + others)]
    for bit in far_bits():
        values = jnp.concatenate([values, swap(values, "win", bit)])
    return [values]


def gather_bit(pieces, bit):
    return pieces + [swap(piece, "win", bit) for piece in pieces]


def gather_stages(low=0):
    stages = [gather_far]
    for bit in (1, 0):
        if bit >= low:
            stages.append(functools.partial(gather_bit, bit=bit))
    return stages


def gather_blocks(values, low=0):
    for stage in gather_stages(low):
        values = stage(values)
    return values


def index_order(pieces):
    masks = gather_masks()
    by_mask = sorted(range(len(masks)), key=masks.__getitem__)
    places = lax.axis_index("win") ^ jnp.arange(len(masks))
    return [jnp.concatenate(pieces)[jnp.array(by_mask)][places]]


def tie(*values):
    return lax.optimization_barrier(values)


def after(value, *others):
    return lax.optimization_barrier((value,) + others)[0]


class Order:
    def __init__(self):
        self.sent = ()

    def launch(self, *hops):
        self.sent = tuple(array for array, _, _ in hops)
        return [
            lax.ppermute(array, axis, [(i, i ^ mask) for i in range(lax.axis_size(axis))])
            for array, axis, mask in hops
        ]

    def land(self, values):
        return after(values, *self.sent)


def pick(values, index, axis=0):
    return lax.dynamic_index_in_dim(values, index, axis, keepdims=False)


def wide(values):
    return values.astype(jnp.float32)


def rounded(values):
    return lax.reduce_precision(values, 8, 7)


def same_sum(values, axis, bit):
    low = rounded(values)
    return low + wide(swap(bfloat(low), axis, bit))


def place_bits():
    win_index = lax.axis_index("win")
    return lax.axis_index("rep"), win_index >> 2, (win_index >> 1) & 1, win_index & 1


def first_parts(total):
    rep, _, side, _ = place_bits()
    half = total.shape[-1] // 2
    left, right = total[..., :half], total[..., half:]
    right = right.reshape(2, -1, 2, right.shape[2], half)
    kept = pick(left, rep), pick(right, side, 2)
    sent = bfloat(pick(left, 1 - rep)), bfloat(pick(right, 1 - side, 2))
    return kept, ((sent[0], "rep", 1), (sent[1], "win", 2))


def first_parts_of_two(totals):
    rep, _, side, _ = place_bits()
    half = totals[0].shape[-1] // 2
    left = [total[..., :half] for total in totals]
    right = [total[..., half:].reshape(-1, 2, total.shape[1], half) for total in totals]
    own, other = pick_owner(rep == 0, *left)
    kept = own, jnp.stack([pick(part, side, 1) for part in right])
    sent = bfloat(other), bfloat(jnp.stack([pick(part, 1 - side, 1) for part in right]))
    return kept, ((sent[0], "rep", 1), (sent[1], "win", 2))


def second_parts(left, right):
    rep, _, side, _ = place_bits()
    left = left.reshape(-1, 2, *left.shape[1:])
    kept = pick(left, side, 1), pick(right, rep)
    sent = bfloat(pick(left, 1 - side, 1)), bfloat(pick(right, 1 - rep))
    return kept, ((sent[0], "win", 2), (sent[1], "rep", 1))


def far_parts(total):
    far = place_bits()[1]
    hops = tuple((bfloat(pick(total, far ^ mask)), "win", mask << 2) for mask in (1, 2, 3))
    return pick(total, far), hops


def add_pair(kept, taken):
    return kept[0] + wide(taken[0]), kept[1] + wide(taken[1])


def add_far(kept, taken):
    return (kept + wide(taken[0])) + (wide(taken[1]) + wide(taken[2]))


def join_halves(pair):
    return jnp.concatenate(pair, axis=-1)


def spread_far(values):
    return tuple((values[None], "win", mask) for mask in (4, 8, 12))


def far_piece(values, taken):
    return jnp.concatenate([values[None], *taken])


def sum_everywhere(values, skip_core=True):
    for bit in range(1 if skip_core else 0, bit_count("win")):
        values = same_sum(values, "win", bit)
    for bit in range(bit_count("rep")):
        values = same_sum(values, "rep", bit)
    return values


def off_diagonal_step(iterate, exact):
    high = bfloat(iterate)
    gram = dot_as(high, high, NT)
    if exact:
        rest = bfloat(iterate - high.astype(jnp.float32))
        gram = gram + dot_as(high, rest, NT) + dot_as(rest, high, NT)
    size = gram.shape[0]
    row_ids = lax.broadcasted_iota(jnp.int32, (size, size), 0)
    on_diagonal = row_ids == lax.broadcasted_iota(jnp.int32, (size, size), 1)
    own = jnp.where(on_diagonal, gram, 0.0)
    own_column = jnp.sum(own, 1, keepdims=True)
    own_row = jnp.sum(own, 0, keepdims=True)
    off = jnp.where(on_diagonal, 0.0, gram)
    off_low = bfloat(off)
    square = product(off_low, off_low) + (own_column + own_row) * off
    poly = NEWTON_COEFFS[1] * off + NEWTON_COEFFS[2] * square
    poly_own = jnp.sum(jnp.where(on_diagonal, poly, 0.0), 1, keepdims=True)
    factor = (
        NEWTON_COEFFS[0]
        + poly_own
        + own_column * (NEWTON_COEFFS[1] + NEWTON_COEFFS[2] * own_column)
    )
    poly = jnp.where(on_diagonal, 0.0, poly)
    poly_high = bfloat(poly)
    moved = product(poly_high, high)
    return factor * iterate + moved


def unit_scale(values):
    total = jnp.sum(jnp.sum(values * values, 1, keepdims=True), 0, keepdims=True)
    return values * (1.0 / (jnp.sqrt(total) + EPSILON))


def block_start(place_ref, masks, block, rows, shift=0):
    if masks is None:
        return block * rows
    return pl.multiple_of(((place_ref[1] ^ masks[block]) >> shift) * rows, rows)


def numbered_blocks(piece_refs):
    for piece, piece_ref in enumerate(piece_refs):
        blocks = piece_ref.shape[0]
        for block in range(blocks):
            yield piece * blocks + block, piece_ref.at[block]


def big_newton_kernel(folds, masks, place_ref, *refs):
    piece_refs, (out_ref, iterate_ref, turned_ref) = refs[:-3], refs[-3:]
    _, rows, width = piece_refs[0].shape
    part = rows // folds

    @pl.when(place_ref[0] == 0)
    def _():
        for block, block_ref in numbered_blocks(piece_refs):
            start = block_start(place_ref, masks, block, part)
            for fold in range(folds):
                lanes = slice(fold * width, (fold + 1) * width)
                inner = slice(fold * part, (fold + 1) * part)
                iterate_ref[pl.ds(start, part), lanes] = block_ref[inner, :].astype(jnp.float32)

    @pl.when(place_ref[0] != 0)
    def _():
        for block, block_ref in numbered_blocks(piece_refs):
            start = block_start(place_ref, masks, block, rows)
            iterate_ref[:, pl.ds(start, rows)] = block_ref[...].astype(jnp.float32).T

    iterate_ref[...] = unit_scale(iterate_ref[...])

    @pl.loop(0, 5)
    def _(_):
        iterate_ref[...] = off_diagonal_step(iterate_ref[...], False)

    @pl.when(place_ref[0] == 0)
    def _():
        start = pl.multiple_of(place_ref[1] * part, part)
        for fold in range(folds):
            out_ref[fold * part : (fold + 1) * part, :] = bfloat(
                iterate_ref[pl.ds(start, part), fold * width : (fold + 1) * width]
            )

    @pl.when(place_ref[0] != 0)
    def _():
        span = max(rows, 128)
        start = pl.multiple_of(place_ref[1] * rows // span * span, span)
        turned_ref[...] = iterate_ref[:, pl.ds(start, span)].T * float(folds) ** 0.5
        inner = pl.multiple_of(place_ref[1] * rows - start, rows)
        out_ref[...] = bfloat(turned_ref[pl.ds(inner, rows), :])


def small_newton_kernel(masks, place_ref, *refs):
    piece_refs, (out_ref, iterate_ref) = refs[:-2], refs[-2:]
    _, matrices, rows, width = piece_refs[0].shape
    for block, block_ref in numbered_blocks(piece_refs):
        start = block_start(place_ref, masks, block, rows, 1)
        for number in range(matrices):
            iterate_ref[number, pl.ds(start, rows), :] = block_ref[number].astype(jnp.float32)

    @pl.loop(0, matrices)
    def _(number):
        iterate_ref[number] = unit_scale(iterate_ref[number])

        @pl.loop(0, 2)
        def _(_):
            iterate_ref[number] = off_diagonal_step(iterate_ref[number], False)

        @pl.loop(0, 3)
        def _(_):
            iterate_ref[number] = off_diagonal_step(iterate_ref[number], True)

    start = pl.multiple_of((place_ref[1] if masks is None else place_ref[1] >> 1) * rows, rows)
    for number in range(matrices):
        out_ref[number] = bfloat(iterate_ref[number, pl.ds(start, rows), :])


def newton_call(kernel, name, place, pieces, out_dims, scratch_dims, cost):
    return pl.pallas_call(
        kernel,
        in_specs=[pl.BlockSpec(memory_space=pltpu.SMEM)]
        + [pl.BlockSpec(memory_space=pltpu.VMEM)] * len(pieces),
        out_specs=pl.BlockSpec(memory_space=pltpu.VMEM),
        out_shape=shape_of(out_dims, jnp.bfloat16),
        scratch_shapes=[pltpu.VMEM(dims, jnp.float32) for dims in scratch_dims],
        compiler_params=pltpu.CompilerParams(vmem_limit_bytes=VMEM_LIMIT),
        cost_estimate=lasting(cost),
        name=name,
    )(place, *pieces)


def big_update(place, pieces, folds, masks):
    blocks, rows, width = pieces[0].shape
    columns = len(pieces) * blocks * rows
    return newton_call(
        functools.partial(big_newton_kernel, folds, masks),
        "big_newton",
        place,
        pieces,
        (rows, width),
        [(width, columns), (max(rows, 128), width)],
        16,
    )


def small_update(place, pieces, masks):
    _, matrices, rows, width = pieces[0].shape
    return newton_call(
        functools.partial(small_newton_kernel, masks),
        "small_newton",
        place,
        pieces,
        (matrices, rows, width),
        [(matrices, width, width)],
        10 * matrices,
    )


def fold_columns(rows, width):
    count, columns = rows.shape
    return rows.reshape(count, columns // width, width).swapaxes(0, 1).reshape(-1, width)


def pick_owner(first, here, there):
    return jnp.where(first, here, there), jnp.where(first, there, here)


def every_update(place, big_rows, small_rows, folds):
    updates = []
    for number, rows in enumerate(big_rows):
        here = jnp.stack([jnp.int32(number), place[1]])
        blocks = index_order(gather_blocks(bfloat(rows)))
        updates.append(big_update(here, blocks, folds, None))
    blocks = index_order(gather_blocks(bfloat(small_rows)))
    return updates[0], updates[1], small_update(place, blocks, None)


GROUP_HEADS = 128 // HEAD_DIM
SCORE_SCALE = HEAD_DIM ** (-0.5)
LOG2_E = 1.4426950408889634
VMEM_LIMIT = 44 * 1024 * 1024
VECTOR_ROWS = 16
NT = (((1,), (1,)), ((), ()))
TN = (((0,), (0,)), ((), ()))


def dot_as(left_side, right_side, dims):
    return lax.dot_general(left_side, right_side, dims, preferred_element_type=jnp.float32)


def spread_heads(part, lane_head):
    return bfloat(
        jnp.concatenate(
            [jnp.where(lane_head == head, part, 0.0) for head in range(GROUP_HEADS)], axis=0
        )
    )


def join_heads(spread, lane_head, rows):
    joined = spread[:rows]
    for head in range(1, GROUP_HEADS):
        joined = jnp.where(lane_head == head, spread[head * rows : (head + 1) * rows], joined)
    return joined


def column_softmax(scores, bias_column):
    scores = scores + bias_column
    raised = jnp.exp2((scores - jnp.max(scores, 0, keepdims=True)) * (SCORE_SCALE * LOG2_E))
    return raised * (1.0 / jnp.sum(raised, 0, keepdims=True))


def load_windows(tokens_ref, region_ref, fill_ref, count, seq_len, padded, step):
    for window in range(count):
        base = window * padded
        fill_ref[base : base + seq_len, :] = tokens_ref[0, window].astype(jnp.float32)
        fill_ref[base : base + 1, :] = region_ref[pl.ds(step * count + window, 1), :]


def window_forward_kernel(
    count,
    seq_len,
    padded,
    tokens_ref,
    region_ref,
    bias_ref,
    keep_ref,
    qkv_ref,
    out_ref,
    vec_ref,
    norm_out,
    proj_out,
    mix_out,
    after_out,
    fill_ref,
    mix_ref,
    scores_ref,
    probs_ref,
):
    step = pl.program_id(0)
    width = tokens_ref.shape[-1]

    @pl.when(step == 0)
    def _():
        fill_ref[...] = jnp.zeros_like(fill_ref)

    load_windows(tokens_ref, region_ref, fill_ref, count, seq_len, padded, step)
    flat = fill_ref[...]
    normed = bfloat(norm_rows(flat, vec_ref[2:3, :], vec_ref[3:4, :]))
    lane_head = lax.broadcasted_iota(jnp.int32, (padded, 128), 1) // HEAD_DIM
    query = product(normed, qkv_ref[0]) + vec_ref[6:7, :]
    keyset = product(normed, qkv_ref[1])
    values = product(normed, qkv_ref[2]) + vec_ref[7:8, :]
    pairs = [(window, group) for window in range(count) for group in range(width // 128)]
    for window in range(count):
        rows = slice(window * padded, (window + 1) * padded)
        norm_out[window] = normed[rows]
        proj_out[window, :, :width] = bfloat(query[rows])
        proj_out[window, :, width : 2 * width] = bfloat(keyset[rows])
        proj_out[window, :, 2 * width :] = bfloat(values[rows])
    for number, (window, group) in enumerate(pairs):
        rows = slice(window * padded, (window + 1) * padded)
        lanes = slice(group * 128, (group + 1) * 128)
        spread = spread_heads(query[rows, lanes], lane_head)
        scores_ref[number] = dot_as(bfloat(keyset[rows, lanes]), spread, NT)
    for number, (window, group) in enumerate(pairs):
        probs_ref[number] = bfloat(column_softmax(scores_ref[number], bias_ref[window]))
    for number, (window, group) in enumerate(pairs):
        rows = slice(window * padded, (window + 1) * padded)
        lanes = slice(group * 128, (group + 1) * 128)
        mixed = dot_as(probs_ref[number], bfloat(values[rows, lanes]), TN)
        mix_ref[rows, lanes] = join_heads(mixed, lane_head, padded)
    mixed_low = bfloat(mix_ref[...])
    branch = product(mixed_low, out_ref[...]) + vec_ref[8:9, :]
    for window in range(count):
        rows = slice(window * padded, (window + 1) * padded)
        mix_out[window] = mixed_low[rows]
        after_out[window] = flat[rows] + keep_ref[window] * branch[rows]


def window_backward_kernel(
    count,
    first_step,
    last,
    seq_len,
    padded,
    tokens_ref,
    region_ref,
    bias_ref,
    keep_ref,
    qkv_ref,
    out_ref,
    vec_ref,
    proj_ref,
    after_grad_ref,
    region_keep_ref,
    sums_before_ref,
    *rest,
):
    scratch_count = 8
    if last:
        region_branch_out, region_mix_out = rest[-scratch_count - 2 : -scratch_count]
        rest = rest[: -scratch_count - 2] + rest[-scratch_count:]
    (
        region_grad_out,
        sums_out,
        grad_out,
        proj_grad_out,
        branch_grad_out,
        fill_ref,
        proj_grad_ref,
        spread_ref,
        spread_grad_ref,
        scores_ref,
        probs_grad_ref,
        probs_ref,
        score_grad_ref,
    ) = rest[-13:]
    step = pl.program_id(0) + first_step
    width = tokens_ref.shape[-1]

    @pl.when(pl.program_id(0) == 0)
    def _():
        fill_ref[...] = jnp.zeros_like(fill_ref)
        sums_out[...] = sums_before_ref[...]
        if first_step == 0:
            region_grad_out[...] = jnp.zeros_like(region_grad_out)
        else:
            region_grad_out[...] = rest[0][...]

    load_windows(tokens_ref, region_ref, fill_ref, count, seq_len, padded, step)
    lane_head = lax.broadcasted_iota(jnp.int32, (padded, 128), 1) // HEAD_DIM
    branch_grad = bfloat(
        jnp.concatenate(
            [keep_ref[window] * after_grad_ref[window] for window in range(count)], axis=0
        )
    )
    mix_grad = dot_as(branch_grad, out_ref[...], NT)
    for window in range(count):
        branch_grad_out[window] = branch_grad[window * padded : (window + 1) * padded]
    pairs = [(window, group) for window in range(count) for group in range(width // 128)]

    def lanes_of(part, group):
        return slice(part * width + group * 128, part * width + (group + 1) * 128)

    for number, (window, group) in enumerate(pairs):
        query = proj_ref[window, :, lanes_of(0, group)].astype(jnp.float32)
        spread_ref[number] = spread_heads(query, lane_head)
        rows = slice(window * padded, (window + 1) * padded)
        spread_grad_ref[number] = spread_heads(mix_grad[rows, lanes_of(0, group)], lane_head)
    for number, (window, group) in enumerate(pairs):
        scores_ref[number] = dot_as(
            proj_ref[window, :, lanes_of(1, group)], spread_ref[number], NT
        )
        probs_grad_ref[number] = dot_as(
            proj_ref[window, :, lanes_of(2, group)], spread_grad_ref[number], NT
        )
    for number, (window, group) in enumerate(pairs):
        probs = column_softmax(scores_ref[number], bias_ref[window])
        weighted = probs * probs_grad_ref[number]
        probs_ref[number] = bfloat(probs)
        score_grad_ref[number] = bfloat(weighted - probs * jnp.sum(weighted, 0, keepdims=True))
    for number, (window, group) in enumerate(pairs):
        rows = slice(window * padded, (window + 1) * padded)
        proj_grad_ref[rows, lanes_of(2, group)] = product(
            probs_ref[number], spread_grad_ref[number]
        )
        proj_grad_ref[rows, lanes_of(1, group)] = (
            product(score_grad_ref[number], spread_ref[number]) * SCORE_SCALE
        )
    for number, (window, group) in enumerate(pairs):
        rows = slice(window * padded, (window + 1) * padded)
        query_grad = dot_as(score_grad_ref[number], proj_ref[window, :, lanes_of(1, group)], TN)
        proj_grad_ref[rows, lanes_of(0, group)] = (
            join_heads(query_grad, lane_head, padded) * SCORE_SCALE
        )
    proj_grad = bfloat(proj_grad_ref[...])
    norm_grad = sum(
        dot_as(proj_grad[:, number * width : (number + 1) * width], qkv_ref[number], NT)
        for number in range(3)
    )
    flat = fill_ref[...]
    center = flat - jnp.mean(flat, -1, keepdims=True)
    scale = lax.rsqrt(jnp.mean(center * center, -1, keepdims=True) + EPSILON)
    hat = center * scale
    hat_grad = norm_grad * vec_ref[2:3, :]
    flat_grad = scale * (
        hat_grad
        - jnp.mean(hat_grad, -1, keepdims=True)
        - hat * jnp.mean(hat_grad * hat, -1, keepdims=True)
    )
    proj_sums = jnp.sum(proj_grad.astype(jnp.float32), 0, keepdims=True)
    sums_out[2:3, :] += jnp.sum(norm_grad * hat, 0, keepdims=True)
    sums_out[3:4, :] += jnp.sum(norm_grad, 0, keepdims=True)
    sums_out[6:7, :] += proj_sums[:, :width]
    sums_out[7:8, :] += proj_sums[:, 2 * width :]
    sums_out[8:9, :] += jnp.sum(branch_grad.astype(jnp.float32), 0, keepdims=True)
    for window in range(count):
        rows = slice(window * padded, (window + 1) * padded)
        proj_grad_out[window] = proj_grad[rows]
        seq_grad = after_grad_ref[window] + flat_grad[rows]
        for group in range(width // 128):
            lanes = slice(group * 128, (group + 1) * 128)
            grad_out[window, pl.ds(group, seq_len, stride=width // 128), :] = seq_grad[
                :seq_len, lanes
            ]
        region_grad_out[pl.ds(step * count + window, 1), :] = seq_grad[0:1]

    if last:

        @pl.when(pl.program_id(0) == pl.num_programs(0) - 1)
        def _():
            region_branch = bfloat(region_keep_ref[...] * region_grad_out[...])
            sums_out[8:9, :] += jnp.sum(region_branch.astype(jnp.float32), 0, keepdims=True)
            region_branch_out[...] = region_branch
            regions = region_branch.shape[0]
            spare_rows = region_mix_out.shape[0] - regions - sums_out.shape[0]
            region_mix_out[:regions, :] = bfloat(dot_as(region_branch, out_ref[...], NT))
            sums_low = jnp.concatenate(
                [sums_out[...], jnp.zeros((spare_rows, width), jnp.float32)], axis=0
            )
            region_mix_out[regions:, :] = bfloat(sums_low)


def window_step(windows, most=4):
    return next(count for count in (10, 4, 2, 1) if count <= most and windows % count == 0)


def whole_spec(shape):
    return pl.BlockSpec(shape, lambda step: (0,) * len(shape))


def step_spec(count, *rest):
    return pl.BlockSpec((count,) + rest, lambda step: (step,) + (0,) * len(rest))


def token_spec(count, *rest):
    return pl.BlockSpec((1, count) + rest, lambda step: (0, step) + (0,) * len(rest))


def kept_spec():
    return pl.BlockSpec(memory_space=pltpu.VMEM)


def lasting(microseconds):
    return pl.CostEstimate(flops=microseconds * 10**9, bytes_accessed=10**6, transcendentals=0)


def in_hbm(values):
    return pltpu.with_memory_space_constraint(values, pltpu.HBM)


def hbm_shape(dims, kind=jnp.float32):
    return pltpu.HBM(dims, kind)


def shape_of(dims, kind=jnp.float32):
    return jax.ShapeDtypeStruct(dims, kind)


def window_forward(tokens, region, bias, keep, qkv_weight, out_weight, vectors, padded):
    _, windows, seq_len, width = tokens.shape
    count = window_step(windows, 10)
    pairs = count * width // 128
    return pl.pallas_call(
        functools.partial(window_forward_kernel, count, seq_len, padded),
        grid=(windows // count,),
        in_specs=[
            token_spec(count, seq_len, width),
            whole_spec(region.shape),
            step_spec(count, padded, 1),
            step_spec(count, 1, 1),
            kept_spec(),
            kept_spec(),
            whole_spec(vectors.shape),
        ],
        out_specs=[
            step_spec(count, padded, width),
            step_spec(count, padded, 3 * width),
            step_spec(count, padded, width),
            step_spec(count, padded, width),
        ],
        out_shape=[
            hbm_shape((windows, padded, width), jnp.bfloat16),
            hbm_shape((windows, padded, 3 * width), jnp.bfloat16),
            hbm_shape((windows, padded, width), jnp.bfloat16),
            hbm_shape((windows, padded, width)),
        ],
        scratch_shapes=[
            pltpu.VMEM((count * padded, width), jnp.float32),
            pltpu.VMEM((count * padded, width), jnp.float32),
            pltpu.VMEM((pairs, padded, GROUP_HEADS * padded), jnp.float32),
            pltpu.VMEM((pairs, padded, GROUP_HEADS * padded), jnp.bfloat16),
        ],
        compiler_params=pltpu.CompilerParams(vmem_limit_bytes=VMEM_LIMIT),
        name="window_forward",
    )(in_hbm(tokens), region, bias, keep, qkv_weight, out_weight, vectors)


def window_backward(
    tokens,
    region,
    bias,
    keep,
    qkv_weight,
    out_weight,
    vectors,
    proj,
    after_grad,
    region_keep,
    before,
    steps,
    padded,
):
    _, windows, seq_len, width = tokens.shape
    count = window_step(windows)
    first_step, last_step = steps
    here = (last_step - first_step) * count
    pairs = count * width // 128
    spread_rows = GROUP_HEADS * padded

    def moved(*dims, lead=0):
        zeros = (0,) * (len(dims) - 1)
        if lead:
            return pl.BlockSpec((1,) + dims, lambda step: (0, step + first_step) + zeros)
        return pl.BlockSpec(dims, lambda step: (step + first_step,) + zeros)

    flat_rows = seq_len * width // 128

    grad_before, sums_before, region_before = before
    operands = [in_hbm(tokens), region, bias, keep, qkv_weight, out_weight, vectors]
    operands += [in_hbm(proj), in_hbm(after_grad), region_keep, in_hbm(sums_before)]
    in_specs = [
        moved(count, seq_len, width, lead=1),
        whole_spec(region.shape),
        moved(count, padded, 1),
        moved(count, 1, 1),
        kept_spec(),
        kept_spec(),
        whole_spec(vectors.shape),
        moved(count, padded, 3 * width),
        moved(count, padded, width),
        whole_spec(region_keep.shape),
        whole_spec(sums_before.shape),
    ]
    aliases = {}
    if first_step:
        aliases = {len(operands) + 1: 2}
        operands += [in_hbm(region_before), in_hbm(grad_before)]
        in_specs += [whole_spec(region.shape), pl.BlockSpec(memory_space=pl.ANY)]
    last = last_step * count == windows
    out_specs = [
        whole_spec(region.shape),
        whole_spec(vectors.shape),
        moved(count, flat_rows, 128),
        step_spec(count, padded, 3 * width),
        step_spec(count, padded, width),
    ]
    out_shape = [
        hbm_shape(region.shape),
        hbm_shape(vectors.shape),
        hbm_shape((windows, flat_rows, 128)),
        hbm_shape((here, padded, 3 * width), jnp.bfloat16),
        hbm_shape((here, padded, width), jnp.bfloat16),
    ]
    if last:
        payload = (region.shape[0] + VECTOR_ROWS, width)
        out_specs += [whole_spec(region.shape), whole_spec(payload)]
        out_shape += [shape_of(region.shape, jnp.bfloat16), shape_of(payload, jnp.bfloat16)]
    return pl.pallas_call(
        functools.partial(window_backward_kernel, count, first_step, last, seq_len, padded),
        grid=(last_step - first_step,),
        in_specs=in_specs,
        out_specs=out_specs,
        out_shape=out_shape,
        scratch_shapes=[
            pltpu.VMEM((count * padded, width), jnp.float32),
            pltpu.VMEM((count * padded, 3 * width), jnp.float32),
            pltpu.VMEM((pairs, spread_rows, 128), jnp.bfloat16),
            pltpu.VMEM((pairs, spread_rows, 128), jnp.bfloat16),
            pltpu.VMEM((pairs, padded, spread_rows), jnp.float32),
            pltpu.VMEM((pairs, padded, spread_rows), jnp.float32),
            pltpu.VMEM((pairs, padded, spread_rows), jnp.bfloat16),
            pltpu.VMEM((pairs, padded, spread_rows), jnp.bfloat16),
        ],
        input_output_aliases=aliases,
        compiler_params=pltpu.CompilerParams(vmem_limit_bytes=VMEM_LIMIT),
        cost_estimate=lasting(here),
        name="window_backward",
    )(*operands)


def insert_kernel(rows_ref, region_ref, out_ref):
    out_ref[...] = rows_ref[...]
    for window in range(rows_ref.shape[0]):
        for group in range(region_ref.shape[1] // 128):
            out_ref[window, group : group + 1, :] = region_ref[
                window : window + 1, group * 128 : (group + 1) * 128
            ]


def insert_regions(grad, region_grad):
    rows = pl.BlockSpec((grad.shape[0], 8, 128), lambda step: (0, 0, 0))
    return pl.pallas_call(
        insert_kernel,
        grid=(1,),
        in_specs=[rows, whole_spec(region_grad.shape)],
        out_specs=rows,
        out_shape=shape_of(grad.shape),
        input_output_aliases={0: 0},
        compiler_params=pltpu.CompilerParams(vmem_limit_bytes=VMEM_LIMIT),
        name="insert_regions",
    )(grad, region_grad)


GELU_IN = 0.7978845608028654
GELU_CUBE = 0.044715


def gelu_both(values):
    square = values * values
    bent = jnp.tanh(values * (GELU_IN + (GELU_IN * GELU_CUBE) * square))
    share = 0.5 + 0.5 * bent
    slope = share + (0.5 * values) * (1.0 - bent * bent) * (
        GELU_IN + (3.0 * GELU_IN * GELU_CUBE) * square
    )
    return values * share, slope


def split_cores(values, core):
    own_first = core == 0
    kept = jnp.where(own_first, values[:, 0], values[:, 1])
    sent = jnp.where(own_first, values[:, 1], values[:, 0])
    return kept, bfloat(sent)


def mlp_kernel(
    place_ref,
    after_ref,
    cot_ref,
    keep_ref,
    vec_ref,
    up_ref,
    down_ref,
    sums_ref,
    out_hbm,
    grad_hbm,
    kept_hbm,
    sent_hbm,
    cot_fill,
    act_ref,
    hidden_grad_ref,
    out_ref,
    grad_ref,
    kept_ref,
    sent_ref,
    sems,
):
    _, windows, seq_len, width = cot_ref.shape
    padded = after_ref.shape[0] // windows
    folds = up_ref.shape[1] // width
    core = place_ref[1] % 2
    copies = []

    def write_out(source, target):
        copy = pltpu.make_async_copy(source, target, sems.at[len(copies)])
        copy.start()
        copies.append(copy)

    cot_fill[...] = jnp.zeros_like(cot_fill)
    keeps = []
    for window in range(windows):
        base = window * padded
        cot_fill[base : base + seq_len, :] = cot_ref[0, window].astype(jnp.float32)
        keeps.append(jnp.broadcast_to(keep_ref[window], (padded, 1)))
    keep = jnp.concatenate(keeps, axis=0)
    flat = after_ref[...]
    center = flat - jnp.mean(flat, -1, keepdims=True)
    scale = lax.rsqrt(jnp.mean(center * center, -1, keepdims=True) + EPSILON)
    hat = center * scale
    normed = bfloat(hat * vec_ref[4:5, :] + vec_ref[5:6, :])
    normed_turned = normed.T
    cot = cot_fill[...]
    branch_grad = bfloat(keep * cot)
    branch = jnp.zeros_like(flat)
    norm_grad = jnp.zeros_like(flat)
    for fold in range(folds):
        lanes = slice(fold * width, (fold + 1) * width)
        up_part, down_part = up_ref[:, lanes], down_ref[lanes, :]
        hidden = product(normed, up_part) + vec_ref[10 + fold : 11 + fold, :]
        act, slope = gelu_both(hidden)
        act = bfloat(act)
        act_ref[:, lanes] = act
        branch += product(act, down_part)
        hidden_grad = bfloat(slope * dot_as(branch_grad, down_part, NT))
        hidden_grad_ref[:, lanes] = hidden_grad
        norm_grad += dot_as(hidden_grad, up_part, NT)
        sums_ref[10 + fold : 11 + fold, :] = jnp.sum(
            hidden_grad.astype(jnp.float32), 0, keepdims=True
        )
    output = bfloat(flat + keep * (branch + vec_ref[9:10, :]))
    for window in range(windows):
        out_ref[window] = output[window * padded : window * padded + seq_len]
    write_out(out_ref, out_hbm.at[0])
    hat_grad = norm_grad * vec_ref[4:5, :]
    grad_ref[...] = cot + scale * (
        hat_grad
        - jnp.mean(hat_grad, -1, keepdims=True)
        - hat * jnp.mean(hat_grad * hat, -1, keepdims=True)
    )
    write_out(grad_ref, grad_hbm)
    sums_ref[0:4, :] = jnp.zeros((4, width), jnp.float32)
    sums_ref[4:5, :] = jnp.sum(norm_grad * hat, 0, keepdims=True)
    sums_ref[5:6, :] = jnp.sum(norm_grad, 0, keepdims=True)
    sums_ref[6:9, :] = jnp.zeros((3, width), jnp.float32)
    sums_ref[9:10, :] = jnp.sum(branch_grad.astype(jnp.float32), 0, keepdims=True)
    _, blocks, rows, _ = kept_ref.shape
    part, here = rows // folds, blocks // folds
    for fold in range(folds):
        lanes = slice(fold * width, (fold + 1) * width)
        total = product(normed_turned, hidden_grad_ref[:, lanes])
        inner = pl.ds(fold * part, part)
        kept, sent = split_cores(total.reshape(blocks, 2, part, width), core)
        kept_ref[0, :, inner], sent_ref[0, :, inner] = kept, sent
        write_out(kept_ref.at[0, :, inner], kept_hbm.at[0, :, inner])
        write_out(sent_ref.at[0, :, inner], sent_hbm.at[0, :, inner])
    for fold in range(folds):
        lanes = slice(fold * width, (fold + 1) * width)
        total = dot_as(act_ref[:, lanes], branch_grad, TN)
        inner = pl.ds(fold * here, here)
        kept, sent = split_cores(total.reshape(here, 2, rows, width), core)
        kept_ref[1, inner], sent_ref[1, inner] = kept, sent
        write_out(kept_ref.at[1, inner], kept_hbm.at[1, inner])
        write_out(sent_ref.at[1, inner], sent_hbm.at[1, inner])
    for copy in copies:
        copy.wait()


def mlp(place, after, cotangent, keep, vectors, up_weight, down_weight, padded, win_count):
    _, windows, seq_len, width = cotangent.shape
    rows = after.shape[0]
    folds = up_weight.shape[1] // width
    dims = (2, win_count // 2, width // win_count * folds, width)
    anywhere = pl.BlockSpec(memory_space=pl.ANY)
    sums, output, grad, kept, sent = pl.pallas_call(
        mlp_kernel,
        grid=(1,),
        in_specs=[
            pl.BlockSpec(memory_space=pltpu.SMEM),
            whole_spec(after.shape),
            whole_spec(cotangent.shape),
            whole_spec(keep.shape),
            whole_spec(vectors.shape),
            kept_spec(),
            kept_spec(),
        ],
        out_specs=[whole_spec(vectors.shape)] + [anywhere] * 4,
        out_shape=[
            hbm_shape(vectors.shape),
            hbm_shape(cotangent.shape, jnp.bfloat16),
            hbm_shape(after.shape),
            hbm_shape(dims),
            hbm_shape(dims, jnp.bfloat16),
        ],
        scratch_shapes=[
            pltpu.VMEM((rows, width), jnp.float32),
            pltpu.VMEM((rows, folds * width), jnp.bfloat16),
            pltpu.VMEM((rows, folds * width), jnp.bfloat16),
            pltpu.VMEM((windows, seq_len, width), jnp.bfloat16),
            pltpu.VMEM((rows, width), jnp.float32),
            pltpu.VMEM(dims, jnp.float32),
            pltpu.VMEM(dims, jnp.bfloat16),
            pltpu.SemaphoreType.DMA((2 + 4 * folds,)),
        ],
        compiler_params=pltpu.CompilerParams(vmem_limit_bytes=VMEM_LIMIT),
        cost_estimate=lasting(25),
        name="mlp",
    )(place, in_hbm(after), in_hbm(cotangent), keep, vectors, up_weight, down_weight)
    return output, grad, sums, (kept, sent)


def image_bias(keys_ref, queries_ref):
    return jnp.where(keys_ref[...] == queries_ref[...], 0.0, -1e30)


def region_forward_kernel(
    pieces,
    *refs,
):
    piece_refs, refs = refs[:pieces], refs[pieces:]
    region_forward_rows(piece_refs, *refs)


def region_forward_rows(
    piece_refs,
    own_ref,
    keep_ref,
    key_image_ref,
    query_image_ref,
    qkv_ref,
    out_ref,
    vec_ref,
    norm_out,
    proj_out,
    mix_out,
    new_out,
    all_ref,
):
    rows, width = own_ref.shape
    vec = vec_ref[...]
    for block, block_ref in numbered_blocks(piece_refs):
        all_ref[block * rows : (block + 1) * rows, :] = block_ref[...].astype(jnp.float32)
    normed = bfloat(norm_rows(all_ref[...], vec[0:1], vec[1:2]))
    norm_out[...] = normed
    query = bfloat(product(normed, qkv_ref[0]) + vec[6:7])
    keyset = bfloat(product(normed, qkv_ref[1]))
    values = bfloat(product(normed, qkv_ref[2]) + vec[7:8])
    proj_out[:, :width] = query
    proj_out[:, width : 2 * width] = keyset
    proj_out[:, 2 * width :] = values
    region = own_ref[...].astype(jnp.float32)
    own_norm = bfloat(norm_rows(region, vec[0:1], vec[1:2]))
    own_query = product(own_norm, qkv_ref[0]) + vec[6:7]
    bias = image_bias(key_image_ref, query_image_ref)
    lane_head = lax.broadcasted_iota(jnp.int32, (rows, 128), 1) // HEAD_DIM
    parts = []
    for group in range(width // 128):
        lanes = slice(group * 128, (group + 1) * 128)
        spread = spread_heads(own_query[:, lanes], lane_head)
        probs = column_softmax(dot_as(keyset[:, lanes], spread, NT), bias)
        mixed = dot_as(bfloat(probs), values[:, lanes], TN)
        parts.append(join_heads(mixed, lane_head, rows))
    mixed_low = bfloat(jnp.concatenate(parts, axis=1))
    mix_out[...] = mixed_low
    branch = product(mixed_low, out_ref[...]) + vec[8:9]
    new_out[...] = region + keep_ref[...] * branch


def region_forward(pieces, own, keep, key_images, query_images, qkv_weight, out_weight, vectors):
    rows, width = own.shape
    total = len(pieces) * pieces[0].shape[0] * rows
    return pl.pallas_call(
        functools.partial(region_forward_kernel, len(pieces)),
        out_shape=[
            hbm_shape((total, width), jnp.bfloat16),
            hbm_shape((total, 3 * width), jnp.bfloat16),
            hbm_shape(own.shape, jnp.bfloat16),
            shape_of(own.shape),
        ],
        scratch_shapes=[pltpu.VMEM((total, width), jnp.float32)],
        compiler_params=pltpu.CompilerParams(vmem_limit_bytes=VMEM_LIMIT),
        name="region_forward",
    )(*pieces, own, keep, key_images, query_images, qkv_weight, out_weight, vectors)


def region_backward_kernel(pieces, place_ref, *refs):
    region_refs, refs = refs[:pieces], refs[pieces:]
    gathered_refs, refs = refs[:pieces], refs[pieces:]
    region_backward_rows(place_ref, region_refs, gathered_refs, *refs)


def region_backward_rows(
    place_ref,
    region_refs,
    gathered_refs,
    norm_ref,
    proj_ref,
    key_image_ref,
    query_image_ref,
    new_grad_ref,
    qkv_ref,
    vec_ref,
    grad_out,
    weight_out,
    sums_out,
    bias_ref,
    proj_grad_ref,
    region_grad_ref,
    weight_ref,
    mix_grad_ref,
    all_ref,
    scores_ref,
    probs_grad_ref,
    probs_ref,
    score_grad_ref,
):
    total, width = all_ref.shape
    rows = new_grad_ref.shape[0]
    bias_ref[...] = image_bias(key_image_ref, query_image_ref)
    lane_head = lax.broadcasted_iota(jnp.int32, (total, 128), 1) // HEAD_DIM
    for block, block_ref in numbered_blocks(region_refs):
        all_ref[block * rows : (block + 1) * rows, :] = block_ref[...].astype(jnp.float32)
    vector_sum = jnp.zeros((VECTOR_ROWS, width), jnp.float32)
    for block, block_ref in numbered_blocks(gathered_refs):
        part = block_ref[...].astype(jnp.float32)
        mix_grad_ref[block * rows : (block + 1) * rows, :] = part[:rows]
        vector_sum += part[rows:]

    @pl.loop(0, width // 128)
    def _(group):
        query_lanes = pl.ds(pl.multiple_of(group * 128, 128), 128)
        key_lanes = pl.ds(pl.multiple_of(width + group * 128, 128), 128)
        value_lanes = pl.ds(pl.multiple_of(2 * width + group * 128, 128), 128)
        key_low = proj_ref[:, key_lanes]
        value_low = proj_ref[:, value_lanes]
        spread = spread_heads(proj_ref[:, query_lanes].astype(jnp.float32), lane_head)
        spread_grad = spread_heads(mix_grad_ref[:, query_lanes], lane_head)
        scores_ref[...] = dot_as(key_low, spread, NT)
        probs_grad_ref[...] = dot_as(value_low, spread_grad, NT)
        for head in range(GROUP_HEADS):
            lanes = slice(head * total, (head + 1) * total)
            probs = column_softmax(scores_ref[:, lanes], bias_ref[...])
            weighted = probs * probs_grad_ref[:, lanes]
            probs_ref[:, lanes] = bfloat(probs)
            score_grad_ref[:, lanes] = bfloat(
                weighted - probs * jnp.sum(weighted, 0, keepdims=True)
            )
        value_grad = product(probs_ref[...], spread_grad)
        key_grad = product(score_grad_ref[...], spread)
        turned = product(key_low.T, score_grad_ref[...])
        query_grad = jnp.concatenate(
            [
                turned[head * HEAD_DIM : (head + 1) * HEAD_DIM, head * total : (head + 1) * total]
                for head in range(GROUP_HEADS)
            ],
            axis=0,
        ).T
        proj_grad_ref[:, query_lanes] = bfloat(query_grad * SCORE_SCALE)
        proj_grad_ref[:, key_lanes] = bfloat(key_grad * SCORE_SCALE)
        proj_grad_ref[:, value_lanes] = bfloat(value_grad)

    proj_grad = proj_grad_ref[...]
    norm_grad = sum(
        dot_as(proj_grad[:, number * width : (number + 1) * width], qkv_ref[number], NT)
        for number in range(3)
    )
    region = all_ref[...]
    center = region - jnp.mean(region, -1, keepdims=True)
    scale = lax.rsqrt(jnp.mean(center * center, -1, keepdims=True) + EPSILON)
    hat = center * scale
    hat_grad = norm_grad * vec_ref[0:1, :]
    region_grad_ref[...] = scale * (
        hat_grad
        - jnp.mean(hat_grad, -1, keepdims=True)
        - hat * jnp.mean(hat_grad * hat, -1, keepdims=True)
    )
    grad_out[...] = new_grad_ref[...] + region_grad_ref[:rows, :]
    bias_sums = jnp.sum(proj_grad.astype(jnp.float32), 0, keepdims=True)
    sums_out[...] = vector_sum
    sums_out[0:1, :] += jnp.sum(norm_grad * hat, 0, keepdims=True)
    sums_out[1:2, :] += jnp.sum(norm_grad, 0, keepdims=True)
    sums_out[6:7, :] += bias_sums[:, :width]
    sums_out[7:8, :] += bias_sums[:, 2 * width :]
    weight_ref[...] = dot_as(norm_ref[...], proj_grad, TN)
    weight_rows = weight_out.shape[1]
    weight_start = pl.multiple_of((place_ref[1] >> 1) * weight_rows, 8)
    for number in range(3):
        weight_out[number] = weight_ref[
            pl.ds(weight_start, weight_rows), number * width : (number + 1) * width
        ]


def region_backward(
    place,
    regions,
    gathered,
    normed,
    proj,
    key_images,
    query_images,
    new_grad,
    qkv_weight,
    vectors,
    weight_rows,
):
    total, width = normed.shape
    vmem = pl.BlockSpec(memory_space=pltpu.VMEM)
    operands = [*regions, *gathered, in_hbm(normed), in_hbm(proj), key_images, query_images]
    operands += [new_grad, qkv_weight, vectors]
    return pl.pallas_call(
        functools.partial(region_backward_kernel, len(regions)),
        grid=(1,),
        in_specs=[pl.BlockSpec(memory_space=pltpu.SMEM)]
        + [whole_spec(operand.shape) for operand in operands[:-2]]
        + [vmem, whole_spec(vectors.shape)],
        out_specs=[vmem] * 3,
        out_shape=[
            shape_of(new_grad.shape),
            shape_of((3, weight_rows, width)),
            shape_of((VECTOR_ROWS, width)),
        ],
        scratch_shapes=[
            pltpu.VMEM((total, total), jnp.float32),
            pltpu.VMEM((total, 3 * width), jnp.bfloat16),
            pltpu.VMEM((total, width), jnp.float32),
            pltpu.VMEM((width, 3 * width), jnp.float32),
            pltpu.VMEM((total, width), jnp.float32),
            pltpu.VMEM((total, width), jnp.float32),
            pltpu.VMEM((total, GROUP_HEADS * total), jnp.float32),
            pltpu.VMEM((total, GROUP_HEADS * total), jnp.float32),
            pltpu.VMEM((total, GROUP_HEADS * total), jnp.bfloat16),
            pltpu.VMEM((total, GROUP_HEADS * total), jnp.bfloat16),
        ],
        compiler_params=pltpu.CompilerParams(vmem_limit_bytes=VMEM_LIMIT),
        cost_estimate=lasting(14),
        name="region_backward",
    )(place, *operands)


def pair_gradient_kernel(first_count, second_count, place_ref, *refs):
    own_first = place_ref[1] % 2 == 0
    kept, sent = refs[-2:]

    def total(pairs):
        lefts, rights = pairs[0::2], pairs[1::2]
        return sum(dot_as(left[...], right[...], TN) for left, right in zip(lefts, rights))

    first = total(refs[: 2 * first_count])
    second = total(refs[2 * first_count : 2 * (first_count + second_count)])
    kept[...] = jnp.where(own_first, first, second)
    sent[...] = bfloat(jnp.where(own_first, second, first))


def pair_gradients(place, first, second, width):
    operands, in_specs = [place], [pl.BlockSpec(memory_space=pltpu.SMEM)]
    for left, row, right, column, rows in first + second:
        operands += [in_hbm(left), in_hbm(right)]
        in_specs.append(pl.BlockSpec((rows, width), lambda step, row=row: (row, 0)))
        in_specs.append(pl.BlockSpec((rows, width), lambda step, column=column: (0, column)))
    return pl.pallas_call(
        functools.partial(pair_gradient_kernel, len(first), len(second)),
        grid=(1,),
        in_specs=in_specs,
        out_specs=[whole_spec((width, width))] * 2,
        out_shape=[hbm_shape((width, width)), hbm_shape((width, width), jnp.bfloat16)],
        compiler_params=pltpu.CompilerParams(vmem_limit_bytes=VMEM_LIMIT),
        cost_estimate=lasting(5),
        name="pair_gradients",
    )(*operands)


def row_pieces(whole, rights, column):
    pairs, start = [], 0
    for right in rights:
        rows = right.shape[0]
        left, row = (whole, start // rows) if start % rows == 0 else (whole[start : start + rows], 0)
        pairs.append((left, row, right, column, rows))
        start += rows
    return pairs


def finish_big_kernel(
    place_ref, mine, other, mom_mine, mom_other, up_ref, down_ref, up_new, down_new, up_mom, down_mom
):
    first = place_ref[0] == 0

    def ordered(here, there):
        return jnp.where(first, here, there), jnp.where(first, there, here)

    updates = ordered(mine[...].astype(jnp.float32), other[...].astype(jnp.float32))
    momenta = ordered(mom_mine[...], mom_other[...])
    down_new[...] = down_ref[...].astype(jnp.float32) - MATRIX_RATE * updates[1]
    down_mom[...] = momenta[1]
    rows, columns = up_ref.shape
    width = down_ref.shape[1]
    for fold in range(columns // width):
        lanes = slice(fold * width, (fold + 1) * width)
        inner = slice(fold * rows, (fold + 1) * rows)
        up_new[:, lanes] = up_ref[:, lanes].astype(jnp.float32) - MATRIX_RATE * updates[0][inner]
        up_mom[:, lanes] = momenta[0][inner]


def finish_small_kernel(place_ref, *refs):
    updates, momenta = refs[:4], refs[4:8]
    qkv_ref, out_ref, qkv_new, out_new, qkv_mom, out_mom = refs[8:]
    first, low = place_ref[0] == 0, place_ref[2] == 0

    def ordered(parts):
        own, side, across, corner = [part[...].astype(jnp.float32) for part in parts]
        here = jnp.where(low, own, side), jnp.where(low, side, own)
        there = jnp.where(low, across, corner), jnp.where(low, corner, across)
        return [jnp.where(first, one, two) for one, two in zip(here + there, there + here)]

    for number, (update, momentum) in enumerate(zip(ordered(updates), ordered(momenta))):
        if number < 3:
            qkv_new[number] = qkv_ref[number].astype(jnp.float32) - MATRIX_RATE * update
            qkv_mom[number] = momentum
        else:
            out_new[...] = out_ref[...].astype(jnp.float32) - MATRIX_RATE * update
            out_mom[...] = momentum


def finish_call(kernel, name, place, parts, weights, blocks, indices):
    dims = [shape_of(block) for block in blocks]
    return pl.pallas_call(
        kernel,
        grid_spec=pltpu.PrefetchScalarGridSpec(
            num_scalar_prefetch=1,
            grid=(1,),
            in_specs=[pl.BlockSpec(part.shape, lambda step, place: (0, 0)) for part in parts]
            + [pl.BlockSpec(block, index) for block, index in zip(blocks, indices)],
            out_specs=[
                pl.BlockSpec(block, lambda step, place, count=len(block): (0,) * count)
                for block in blocks + blocks
            ],
        ),
        out_shape=dims + dims,
        compiler_params=pltpu.CompilerParams(vmem_limit_bytes=VMEM_LIMIT),
        name=name,
    )(place, *parts, *weights)


def finish_big(place, parts, up_weight, down_weight):
    rows, width = parts[0].shape
    up_rows = rows * width // up_weight.shape[1]
    own = lambda step, place: (place[1], 0)
    return finish_call(
        finish_big_kernel,
        "finish_big",
        place,
        parts,
        (up_weight, down_weight),
        [(up_rows, up_weight.shape[1]), (rows, width)],
        [own, own],
    )


def finish_small(place, parts, qkv_weight, out_weight):
    rows, width = parts[0].shape
    return finish_call(
        finish_small_kernel,
        "finish_small",
        place,
        parts,
        (qkv_weight, out_weight),
        [(3, rows, width), (rows, width)],
        [lambda step, place: (0, place[1], 0), lambda step, place: (place[1], 0)],
    )


def local(
    tokens,
    patch_mask,
    keep_mask,
    image_map,
    qkv_weight,
    out_weight,
    up_weight,
    down_weight,
    vectors,
    qkv_mom,
    out_mom,
    up_mom,
    down_mom,
    vec_mom,
    cotangent,
):
    windows = tokens.shape[1]
    seq_len = tokens.shape[2]
    model_width = tokens.shape[3]
    hidden_width = up_weight.shape[1]
    folds = hidden_width // model_width
    shard_rows = out_mom.shape[0]
    ff_rows = down_mom.shape[0]
    vec_rows = vec_mom.shape[0]
    padded = (seq_len + 7) // 8 * 8
    region_rows = (windows + 7) // 8 * 8
    row_count = windows * padded
    win_count = lax.axis_size("win")
    win_index = lax.axis_index("win")
    place = jnp.stack([lax.axis_index("rep"), win_index]).astype(jnp.int32)

    def pad_rows(values, rows, fill=0):
        widths = ((0, rows - values.shape[0]),) + ((0, 0),) * (values.ndim - 1)
        return jnp.pad(values, widths, constant_values=fill)

    region_own = pad_rows(tokens[0, :, 0], region_rows)
    regions = gather_far(region_own)
    up_old, down_old = after((up_mom, down_mom), regions)
    for bit in (1, 0):
        regions = gather_bit(regions, bit)
    keeper = keep_mask[0].astype(jnp.float32) / KEEP_SHARE
    images = image_map[0].reshape(win_count, windows)[win_index ^ jnp.array(gather_masks())]
    images = jnp.pad(images, ((0, 0), (0, region_rows - windows)), constant_values=-1)
    key_images = images.reshape(-1, 1)
    own_images = jnp.tile(images[:1], (1, GROUP_HEADS))
    region_keep = pad_rows(keeper[:, 0:1], region_rows)

    big_moms = (
        MOMENTUM_DECAY * fold_columns(up_old, model_width),
        MOMENTUM_DECAY * down_old,
    )
    small_old_moms = MOMENTUM_DECAY * jnp.concatenate([qkv_mom, out_mom[None]])
    own_pair = jnp.where(lax.axis_index("rep") == 0, small_old_moms[:2], small_old_moms[2:])
    kept, sent = pick_owner(win_index % 2 == 0, own_pair[0], own_pair[1])
    small_pair_mom = jnp.concatenate(
        pick_owner(win_index % 2 == 0, kept, swap(sent, "win", 0))
    )
    regions, big_moms, small_pair_mom = tie(regions, big_moms, small_pair_mom)

    region_norm, region_proj, region_mix, region_new = region_forward(
        regions, region_own, region_keep, key_images, own_images, qkv_weight, out_weight, vectors
    )

    key_valid = jnp.concatenate([jnp.ones((windows, 1), jnp.int32), patch_mask[0]], axis=1) == 1
    key_bias = jnp.where(key_valid, 0.0, -1e30)
    key_bias = jnp.pad(key_bias, ((0, 0), (0, padded - seq_len)), constant_values=-1e30)
    key_bias = key_bias[:, :, None]
    keep_window = keeper[:, 1].reshape(windows, 1, 1)
    seq_norm, seq_proj, local_mix, after_attn = window_forward(
        tokens, region_new, key_bias, keep_window, qkv_weight, out_weight, vectors, padded
    )
    seq_norm = seq_norm.reshape(row_count, model_width)
    local_mix = local_mix.reshape(row_count, model_width)
    after_attn = after_attn.reshape(row_count, model_width)

    out_tokens, attn_res_grad, mlp_sums, big_halves = mlp(
        place,
        after_attn,
        cotangent,
        keeper[:, 2].reshape(windows, 1, 1),
        vectors,
        up_weight,
        down_weight,
        padded,
        win_count,
    )

    steps = windows // window_step(windows)
    cuts = [0, steps * 2 // 5, steps * 4 // 5, steps]
    after_grad = attn_res_grad.reshape(windows, padded, model_width)
    two_owners = lax.axis_size("rep") == 2 and len(far_bits()) == 2
    order = Order()
    big_taken = order.launch((big_halves[1], "win", 1))
    before = (None, mlp_sums, None)
    proj_grads, branch_grads = [], []
    for piece in range(3):
        region_new_grad, sums, seq_grad, proj_grad, branch_grad, *region_parts = window_backward(
            tokens,
            region_new,
            key_bias,
            keep_window,
            qkv_weight,
            out_weight,
            vectors,
            seq_proj,
            after_grad,
            region_keep,
            before,
            (cuts[piece], cuts[piece + 1]),
            padded,
        )
        before = (seq_grad, sums, region_new_grad)
        proj_grads.append(proj_grad.reshape(-1, 3 * model_width))
        branch_grads.append(branch_grad.reshape(-1, model_width))
        if piece == 0:
            big_taken, after_grad = tie(big_taken, after_grad)
            big_total = big_halves[0] + wide(big_taken[0])
            if two_owners:
                big_kept, hops = first_parts(big_total)
                big_taken = order.launch(*hops)
        if piece == 1 and two_owners:
            big_taken, after_grad = tie(big_taken, after_grad)
            big_kept, hops = second_parts(*add_pair(big_kept, big_taken))
            hops, after_grad = tie([array for array, _, _ in hops], after_grad)
            big_taken = order.launch((hops[0], "win", 2), (hops[1], "rep", 1))
    region_branch_grad, region_mix_grad = region_parts
    norm_rows_ready, mix_ready = seq_norm, local_mix
    if two_owners:
        mix_taken = order.launch(*spread_far(region_mix_grad))
        big_kept, hops = far_parts(join_halves(add_pair(big_kept, big_taken)))
        hops, norm_rows_ready = tie([array for array, _, _ in hops], seq_norm)
        big_taken = order.launch(*[(hop, "win", 4 * (i + 1)) for i, hop in enumerate(hops)])

    first = lax.axis_index("rep") == 0
    low_core = win_index % 2 == 0
    kept, sent = pair_gradients(
        place,
        row_pieces(norm_rows_ready, proj_grads, 0),
        row_pieces(norm_rows_ready, proj_grads, 1),
        model_width,
    )
    if two_owners:
        kept, sent, mix_taken = tie(kept, sent, mix_taken)
        mixes = [far_piece(region_mix_grad, mix_taken)]
        mixes, mix_ready = tie(mixes, local_mix)
        mix_taken = order.launch((mixes[0], "win", 2))
    small_kept = [kept]
    small_taken = order.launch((sent, "win", 1))
    kept, sent = pair_gradients(
        place,
        row_pieces(seq_norm, proj_grads, 2),
        row_pieces(mix_ready, branch_grads, 0)
        + [(region_mix, 0, region_branch_grad, 0, region_rows)],
        model_width,
    )
    if two_owners:
        kept, sent, mix_taken, big_taken = tie(kept, sent, mix_taken, big_taken)
    small_kept.append(kept)
    small_taken += order.launch((sent, "win", 1))
    if two_owners:
        mixes += mix_taken
        mix_taken = order.launch(*[(piece, "win", 1) for piece in mixes])
    small_totals = [
        (kept + wide(taken)).reshape(-1, 2 * shard_rows, model_width)
        for kept, taken in zip(small_kept, order.land(small_taken))
    ]
    if two_owners:
        small_kept, hops = first_parts_of_two(small_totals)
        small_sent = [array for array, _, _ in hops]
        small_taken = order.launch(*hops)
        big_mom = jnp.where(first, big_moms[0], big_moms[1])
        big_mom = big_mom + add_far(big_kept, big_taken)
        big_low = bfloat(big_mom)
        big_taken = order.launch(*spread_far(big_low))
        mixes += mix_taken
        mixes = after(mixes, small_sent, big_low)
    else:
        mixes = gather_blocks(region_mix_grad)

    region_grad, region_weight_grad, region_sums = region_backward(
        place,
        regions,
        mixes,
        region_norm,
        region_proj,
        key_images,
        key_images.reshape(1, -1),
        region_new_grad,
        qkv_weight,
        vectors,
        2 * shard_rows,
    )

    if two_owners:
        region_weight_grad, small_taken, big_taken = tie(region_weight_grad, small_taken, big_taken)
        def spread_pair(mine):
            mine = mine.reshape(2, shard_rows, model_width)
            kept, sent = pick_owner(low_core, mine[0], mine[1])
            taken = order.launch((sent, "win", 1), (kept, "rep", 1), (sent, ("win", "rep"), 3))
            return kept, taken

        rep_rows = jnp.stack(
            [
                jnp.where(low_core, region_weight_grad[0], region_weight_grad[1]),
                jnp.where(low_core, region_weight_grad[2], 0.0),
            ]
        )
        rep = lax.axis_index("rep")
        vec_mine = rounded(region_sums)
        small_kept, hops = second_parts(*add_pair(small_kept, small_taken))
        small_taken = order.launch(*hops)
        vec_taken = order.launch(
            (bfloat(jnp.concatenate([pick(rep_rows, 1 - rep), vec_mine])), "rep", 1)
        )
        big_pieces = [far_piece(big_low, order.land(big_taken))]
        big_taken = order.launch((big_pieces[0], "win", 2))
        small_kept, hops = far_parts(join_halves(add_pair(small_kept, order.land(small_taken))))
        small_taken = order.launch(*hops)
        vec_taken = wide(vec_taken[0])
        region_rows_sum = pick(rep_rows, rep) + vec_taken[: 2 * shard_rows]
        vec_sum = vec_mine + vec_taken[2 * shard_rows :]
        big_pieces += order.land(big_taken)
        big_taken = order.launch(*[(piece, "win", 1) for piece in big_pieces])
        small_mom = add_far(small_kept, order.land(small_taken)) + region_rows_sum
        small_mom = small_pair_mom + small_mom
        small_low = bfloat(small_mom)
        small_taken = order.launch(*spread_far(small_low))
        input_grad = insert_regions(seq_grad, after(region_grad, *order.sent))
        input_grad = input_grad.reshape(tokens.shape)
        small_pieces = [far_piece(small_low, order.land(small_taken))]
        small_taken = order.launch((small_pieces[0], "win", 2))
        mom_parts = spread_pair(small_mom)
        other_mom = order.launch((big_mom, "rep", 1))[0]
        big_pieces += order.land(big_taken)
        big_mine = big_update(place, big_pieces, folds, gather_masks())

        other_update = order.launch((big_mine, "rep", 1))[0]
        small_pieces += order.land(small_taken)
        small_pieces, mom_parts, other_mom = tie(small_pieces, mom_parts, other_mom)
        small_mine = small_update(
            place, [piece[:, None] for piece in small_pieces], gather_masks(1)
        )[0]
        update_parts = spread_pair(small_mine)
        other_update = order.land(other_update)
        finish_place = jnp.concatenate([place, place[1:] & 1])
        big_parts = [big_mine, other_update, big_mom, other_mom]
        small_parts = [update_parts[0], *update_parts[1], mom_parts[0], *mom_parts[1]]
    else:
        input_grad = insert_regions(seq_grad, region_grad).reshape(tokens.shape)
        big_total = pick(sum_everywhere(big_total), win_index >> 1, 1)
        folded_up_mom = big_moms[0] + big_total[0]
        new_down_mom = big_moms[1] + big_total[1]
        small_total = sum_everywhere(jnp.stack(small_totals))
        other = swap(bfloat(small_total), "win", 0)
        pairs = jnp.stack(pick_owner(low_core, bfloat(small_total), other), axis=1)
        pairs = pairs.reshape(4, -1, 2 * shard_rows, model_width)
        region_pairs = jnp.pad(region_weight_grad, ((0, 1), (0, 0), (0, 0)))
        vec_sum = region_sums
        for bit in range(bit_count("rep")):
            region_pairs = same_sum(region_pairs, "rep", bit)
            vec_sum = same_sum(vec_sum, "rep", bit)
        rows = wide(pick(pairs, win_index >> 1, 1)) + region_pairs
        rows = rows.reshape(4, 2, shard_rows, model_width)
        small_moms = small_old_moms + pick(rows, win_index & 1, 1)
        up_update, down_update, updates = every_update(
            place, (folded_up_mom, new_down_mom), small_moms, folds
        )
        finish_place = jnp.stack([0 * win_index, win_index, 0 * win_index]).astype(jnp.int32)
        big_parts = [up_update, down_update, folded_up_mom, new_down_mom]
        small_parts = [*updates, *small_moms]
    new_up, new_down, new_up_mom, new_down_mom = finish_big(
        finish_place, big_parts, up_weight, down_weight
    )
    new_qkv, new_out, new_qkv_mom, new_out_mom = finish_small(
        finish_place, small_parts, qkv_weight, out_weight
    )
    vec_total = lax.dynamic_slice_in_dim(vec_sum.reshape(-1), win_index * vec_rows, vec_rows)
    new_vec_mom = MOMENTUM_DECAY * vec_mom + vec_total
    new_vectors = (
        lax.dynamic_slice_in_dim(vectors.reshape(-1), win_index * vec_rows, vec_rows)
        - VECTOR_RATE * new_vec_mom
    )

    return (
        out_tokens,
        input_grad,
        new_qkv_mom,
        new_qkv,
        new_out_mom,
        new_out,
        new_up_mom,
        new_up,
        new_down_mom,
        new_down,
        new_vec_mom,
        new_vectors,
    )


def solution(mesh):
    placed = (
        P("rep", "win", None, None),
        P("rep", "win", None),
        P("rep", "win", None),
        P("rep", None),
        P(),
        P(),
        P(),
        P(),
        P(),
        P(None, "win", None),
        P("win", None),
        P("win", None),
        P("win", None),
        P("win"),
        P("rep", "win", None, None),
    )
    return jax.shard_map(
        local,
        mesh=mesh,
        in_specs=placed,
        out_specs=(
            P("rep", "win", None, None),
            P("rep", "win", None, None),
            P(None, "win", None),
            P(None, "win", None),
            P("win", None),
            P("win", None),
            P("win", None),
            P("win", None),
            P("win", None),
            P("win", None),
            P("win"),
            P("win"),
        ),
        check_vma=False,
    )
```

```python
import functools

import jax
import jax.numpy as jnp
from jax import lax
from jax.experimental import pallas as pl
from jax.experimental.pallas import tpu as pltpu
from jax.sharding import PartitionSpec as P

HEADS = 16
HEAD_DIM = 32


EPSILON = 1e-06
MOMENTUM_DECAY = 0.95
MATRIX_RATE = 0.5
VECTOR_RATE = 0.0002
KEEP_SHARE = 0.75
NEWTON_COEFFS = (3.4445, -4.775, 2.0315)


def bfloat(values):
    return values.astype(jnp.bfloat16)


def product(left_side, right_side):
    return jnp.dot(left_side, right_side, preferred_element_type=jnp.float32)


def norm_rows(values, gain_row, shift_row):
    center = values - jnp.mean(values, -1, keepdims=True)
    spread = jnp.mean(center * center, -1, keepdims=True)
    return center * lax.rsqrt(spread + EPSILON) * gain_row + shift_row


def bit_count(axis):
    return lax.axis_size(axis).bit_length() - 1


def swap(values, axis, bit):
    size = lax.axis_size(axis)
    return lax.ppermute(values, axis, [(i, i ^ (1 << bit)) for i in range(size)])


def my_bit(axis, bit):
    return (lax.axis_index(axis) >> bit) & 1


def far_bits():
    return list(range(2, bit_count("win")))


def gather_masks(low=0):
    masks = [0]
    for bit in far_bits() + [1, 0]:
        if bit >= low:
            masks += [mask | (1 << bit) for mask in masks]
    return masks


def gather_far(values):
    size = lax.axis_size("win")
    values = values[None]
    if len(far_bits()) == 2:
        others = [
            lax.ppermute(values, "win", [(i, i ^ mask) for i in range(size)]) for mask in (4, 8, 12)
        ]
        return [jnp.concatenate([values] + others)]
    for bit in far_bits():
        values = jnp.concatenate([values, swap(values, "win", bit)])
    return [values]


def gather_bit(pieces, bit):
    return pieces + [swap(piece, "win", bit) for piece in pieces]


def gather_stages(low=0):
    stages = [gather_far]
    for bit in (1, 0):
        if bit >= low:
            stages.append(functools.partial(gather_bit, bit=bit))
    return stages


def gather_blocks(values, low=0):
    for stage in gather_stages(low):
        values = stage(values)
    return values


def index_order(pieces):
    masks = gather_masks()
    by_mask = sorted(range(len(masks)), key=masks.__getitem__)
    places = lax.axis_index("win") ^ jnp.arange(len(masks))
    return [jnp.concatenate(pieces)[jnp.array(by_mask)][places]]


def tie(*values):
    return lax.optimization_barrier(values)


def after(value, *others):
    return lax.optimization_barrier((value,) + others)[0]


class Order:
    def __init__(self):
        self.sent = ()

    def launch(self, *hops):
        self.sent = tuple(array for array, _, _ in hops)
        return [
            lax.ppermute(array, axis, [(i, i ^ mask) for i in range(lax.axis_size(axis))])
            for array, axis, mask in hops
        ]

    def land(self, values):
        return after(values, *self.sent)


def pick(values, index, axis=0):
    return lax.dynamic_index_in_dim(values, index, axis, keepdims=False)


def wide(values):
    return values.astype(jnp.float32)


def rounded(values):
    return lax.reduce_precision(values, 8, 7)


def same_sum(values, axis, bit):
    low = rounded(values)
    return low + wide(swap(bfloat(low), axis, bit))


def place_bits():
    win_index = lax.axis_index("win")
    return lax.axis_index("rep"), win_index >> 2, (win_index >> 1) & 1, win_index & 1


def first_parts(total):
    rep, _, side, _ = place_bits()
    half = total.shape[-1] // 2
    left, right = total[..., :half], total[..., half:]
    right = right.reshape(2, -1, 2, right.shape[2], half)
    kept = pick(left, rep), pick(right, side, 2)
    sent = bfloat(pick(left, 1 - rep)), bfloat(pick(right, 1 - side, 2))
    return kept, ((sent[0], "rep", 1), (sent[1], "win", 2))


def first_parts_of_two(totals):
    rep, _, side, _ = place_bits()
    half = totals[0].shape[-1] // 2
    left = [total[..., :half] for total in totals]
    right = [total[..., half:].reshape(-1, 2, total.shape[1], half) for total in totals]
    own, other = pick_owner(rep == 0, *left)
    kept = own, jnp.stack([pick(part, side, 1) for part in right])
    sent = bfloat(other), bfloat(jnp.stack([pick(part, 1 - side, 1) for part in right]))
    return kept, ((sent[0], "rep", 1), (sent[1], "win", 2))


def second_parts(left, right):
    rep, _, side, _ = place_bits()
    left = left.reshape(-1, 2, *left.shape[1:])
    kept = pick(left, side, 1), pick(right, rep)
    sent = bfloat(pick(left, 1 - side, 1)), bfloat(pick(right, 1 - rep))
    return kept, ((sent[0], "win", 2), (sent[1], "rep", 1))


def far_parts(total):
    far = place_bits()[1]
    hops = tuple((bfloat(pick(total, far ^ mask)), "win", mask << 2) for mask in (1, 2, 3))
    return pick(total, far), hops


def add_pair(kept, taken):
    return kept[0] + wide(taken[0]), kept[1] + wide(taken[1])


def add_far(kept, taken):
    return (kept + wide(taken[0])) + (wide(taken[1]) + wide(taken[2]))


def join_halves(pair):
    return jnp.concatenate(pair, axis=-1)


def spread_far(values):
    return tuple((values[None], "win", mask) for mask in (4, 8, 12))


def far_piece(values, taken):
    return jnp.concatenate([values[None], *taken])


def sum_everywhere(values, skip_core=True):
    for bit in range(1 if skip_core else 0, bit_count("win")):
        values = same_sum(values, "win", bit)
    for bit in range(bit_count("rep")):
        values = same_sum(values, "rep", bit)
    return values


def off_diagonal_step(iterate, exact):
    high = bfloat(iterate)
    gram = dot_as(high, high, NT)
    if exact:
        rest = bfloat(iterate - high.astype(jnp.float32))
        gram = gram + dot_as(high, rest, NT) + dot_as(rest, high, NT)
    size = gram.shape[0]
    row_ids = lax.broadcasted_iota(jnp.int32, (size, size), 0)
    on_diagonal = row_ids == lax.broadcasted_iota(jnp.int32, (size, size), 1)
    own = jnp.where(on_diagonal, gram, 0.0)
    own_column = jnp.sum(own, 1, keepdims=True)
    own_row = jnp.sum(own, 0, keepdims=True)
    off = jnp.where(on_diagonal, 0.0, gram)
    off_low = bfloat(off)
    square = product(off_low, off_low) + (own_column + own_row) * off
    poly = NEWTON_COEFFS[1] * off + NEWTON_COEFFS[2] * square
    poly_own = jnp.sum(jnp.where(on_diagonal, poly, 0.0), 1, keepdims=True)
    factor = (
        NEWTON_COEFFS[0]
        + poly_own
        + own_column * (NEWTON_COEFFS[1] + NEWTON_COEFFS[2] * own_column)
    )
    poly = jnp.where(on_diagonal, 0.0, poly)
    poly_high = bfloat(poly)
    moved = product(poly_high, high)
    return factor * iterate + moved


def unit_scale(values):
    total = jnp.sum(jnp.sum(values * values, 1, keepdims=True), 0, keepdims=True)
    return values * (1.0 / (jnp.sqrt(total) + EPSILON))


def block_start(place_ref, masks, block, rows, shift=0):
    if masks is None:
        return block * rows
    return pl.multiple_of(((place_ref[1] ^ masks[block]) >> shift) * rows, rows)


def numbered_blocks(piece_refs):
    for piece, piece_ref in enumerate(piece_refs):
        blocks = piece_ref.shape[0]
        for block in range(blocks):
            yield piece * blocks + block, piece_ref.at[block]


def big_newton_kernel(folds, masks, place_ref, *refs):
    piece_refs, (out_ref, iterate_ref, turned_ref) = refs[:-3], refs[-3:]
    _, rows, width = piece_refs[0].shape
    part = rows // folds

    @pl.when(place_ref[0] == 0)
    def _():
        for block, block_ref in numbered_blocks(piece_refs):
            start = block_start(place_ref, masks, block, part)
            for fold in range(folds):
                lanes = slice(fold * width, (fold + 1) * width)
                inner = slice(fold * part, (fold + 1) * part)
                iterate_ref[pl.ds(start, part), lanes] = block_ref[inner, :].astype(jnp.float32)

    @pl.when(place_ref[0] != 0)
    def _():
        for block, block_ref in numbered_blocks(piece_refs):
            start = block_start(place_ref, masks, block, rows)
            iterate_ref[:, pl.ds(start, rows)] = block_ref[...].astype(jnp.float32).T

    iterate_ref[...] = unit_scale(iterate_ref[...])

    @pl.loop(0, 5)
    def _(_):
        iterate_ref[...] = off_diagonal_step(iterate_ref[...], False)

    @pl.when(place_ref[0] == 0)
    def _():
        start = pl.multiple_of(place_ref[1] * part, part)
        for fold in range(folds):
            out_ref[fold * part : (fold + 1) * part, :] = bfloat(
                iterate_ref[pl.ds(start, part), fold * width : (fold + 1) * width]
            )

    @pl.when(place_ref[0] != 0)
    def _():
        span = max(rows, 128)
        start = pl.multiple_of(place_ref[1] * rows // span * span, span)
        turned_ref[...] = iterate_ref[:, pl.ds(start, span)].T * float(folds) ** 0.5
        inner = pl.multiple_of(place_ref[1] * rows - start, rows)
        out_ref[...] = bfloat(turned_ref[pl.ds(inner, rows), :])


def small_newton_kernel(masks, place_ref, *refs):
    piece_refs, (out_ref, iterate_ref) = refs[:-2], refs[-2:]
    _, matrices, rows, width = piece_refs[0].shape
    for block, block_ref in numbered_blocks(piece_refs):
        start = block_start(place_ref, masks, block, rows, 1)
        for number in range(matrices):
            iterate_ref[number, pl.ds(start, rows), :] = block_ref[number].astype(jnp.float32)

    @pl.loop(0, matrices)
    def _(number):
        iterate_ref[number] = unit_scale(iterate_ref[number])

        @pl.loop(0, 2)
        def _(_):
            iterate_ref[number] = off_diagonal_step(iterate_ref[number], False)

        @pl.loop(0, 3)
        def _(_):
            iterate_ref[number] = off_diagonal_step(iterate_ref[number], True)

    start = pl.multiple_of((place_ref[1] if masks is None else place_ref[1] >> 1) * rows, rows)
    for number in range(matrices):
        out_ref[number] = bfloat(iterate_ref[number, pl.ds(start, rows), :])


def newton_call(kernel, name, place, pieces, out_dims, scratch_dims, cost):
    return pl.pallas_call(
        kernel,
        in_specs=[pl.BlockSpec(memory_space=pltpu.SMEM)]
        + [pl.BlockSpec(memory_space=pltpu.VMEM)] * len(pieces),
        out_specs=pl.BlockSpec(memory_space=pltpu.VMEM),
        out_shape=shape_of(out_dims, jnp.bfloat16),
        scratch_shapes=[pltpu.VMEM(dims, jnp.float32) for dims in scratch_dims],
        compiler_params=pltpu.CompilerParams(vmem_limit_bytes=VMEM_LIMIT),
        cost_estimate=lasting(cost),
        name=name,
    )(place, *pieces)


def big_update(place, pieces, folds, masks):
    blocks, rows, width = pieces[0].shape
    columns = len(pieces) * blocks * rows
    return newton_call(
        functools.partial(big_newton_kernel, folds, masks),
        "big_newton",
        place,
        pieces,
        (rows, width),
        [(width, columns), (max(rows, 128), width)],
        16,
    )


def small_update(place, pieces, masks):
    _, matrices, rows, width = pieces[0].shape
    return newton_call(
        functools.partial(small_newton_kernel, masks),
        "small_newton",
        place,
        pieces,
        (matrices, rows, width),
        [(matrices, width, width)],
        10 * matrices,
    )


def fold_columns(rows, width):
    count, columns = rows.shape
    return rows.reshape(count, columns // width, width).swapaxes(0, 1).reshape(-1, width)


def pick_owner(first, here, there):
    return jnp.where(first, here, there), jnp.where(first, there, here)


def every_update(place, big_rows, small_rows, folds):
    updates = []
    for number, rows in enumerate(big_rows):
        here = jnp.stack([jnp.int32(number), place[1]])
        blocks = index_order(gather_blocks(bfloat(rows)))
        updates.append(big_update(here, blocks, folds, None))
    blocks = index_order(gather_blocks(bfloat(small_rows)))
    return updates[0], updates[1], small_update(place, blocks, None)


GROUP_HEADS = 128 // HEAD_DIM
SCORE_SCALE = HEAD_DIM ** (-0.5)
LOG2_E = 1.4426950408889634
VMEM_LIMIT = 44 * 1024 * 1024
VECTOR_ROWS = 16
NT = (((1,), (1,)), ((), ()))
TN = (((0,), (0,)), ((), ()))


def dot_as(left_side, right_side, dims):
    return lax.dot_general(left_side, right_side, dims, preferred_element_type=jnp.float32)


def spread_heads(part, lane_head):
    return bfloat(
        jnp.concatenate(
            [jnp.where(lane_head == head, part, 0.0) for head in range(GROUP_HEADS)], axis=0
        )
    )


def join_heads(spread, lane_head, rows):
    joined = spread[:rows]
    for head in range(1, GROUP_HEADS):
        joined = jnp.where(lane_head == head, spread[head * rows : (head + 1) * rows], joined)
    return joined


def column_softmax(scores, bias_column):
    scores = scores + bias_column
    raised = jnp.exp2((scores - jnp.max(scores, 0, keepdims=True)) * (SCORE_SCALE * LOG2_E))
    return raised * (1.0 / jnp.sum(raised, 0, keepdims=True))


def load_windows(tokens_ref, region_ref, fill_ref, count, seq_len, padded, step):
    for window in range(count):
        base = window * padded
        fill_ref[base : base + seq_len, :] = tokens_ref[0, window].astype(jnp.float32)
        fill_ref[base : base + 1, :] = region_ref[pl.ds(step * count + window, 1), :]


def window_forward_kernel(
    count,
    seq_len,
    padded,
    tokens_ref,
    region_ref,
    bias_ref,
    keep_ref,
    qkv_ref,
    out_ref,
    vec_ref,
    norm_out,
    proj_out,
    mix_out,
    after_out,
    fill_ref,
    mix_ref,
    scores_ref,
    probs_ref,
):
    step = pl.program_id(0)
    width = tokens_ref.shape[-1]

    @pl.when(step == 0)
    def _():
        fill_ref[...] = jnp.zeros_like(fill_ref)

    load_windows(tokens_ref, region_ref, fill_ref, count, seq_len, padded, step)
    flat = fill_ref[...]
    normed = bfloat(norm_rows(flat, vec_ref[2:3, :], vec_ref[3:4, :]))
    lane_head = lax.broadcasted_iota(jnp.int32, (padded, 128), 1) // HEAD_DIM
    query = product(normed, qkv_ref[0]) + vec_ref[6:7, :]
    keyset = product(normed, qkv_ref[1])
    values = product(normed, qkv_ref[2]) + vec_ref[7:8, :]
    pairs = [(window, group) for window in range(count) for group in range(width // 128)]
    for window in range(count):
        rows = slice(window * padded, (window + 1) * padded)
        norm_out[window] = normed[rows]
        proj_out[window, :, :width] = bfloat(query[rows])
        proj_out[window, :, width : 2 * width] = bfloat(keyset[rows])
        proj_out[window, :, 2 * width :] = bfloat(values[rows])
    for number, (window, group) in enumerate(pairs):
        rows = slice(window * padded, (window + 1) * padded)
        lanes = slice(group * 128, (group + 1) * 128)
        spread = spread_heads(query[rows, lanes], lane_head)
        scores_ref[number] = dot_as(bfloat(keyset[rows, lanes]), spread, NT)
    for number, (window, group) in enumerate(pairs):
        probs_ref[number] = bfloat(column_softmax(scores_ref[number], bias_ref[window]))
    for number, (window, group) in enumerate(pairs):
        rows = slice(window * padded, (window + 1) * padded)
        lanes = slice(group * 128, (group + 1) * 128)
        mixed = dot_as(probs_ref[number], bfloat(values[rows, lanes]), TN)
        mix_ref[rows, lanes] = join_heads(mixed, lane_head, padded)
    mixed_low = bfloat(mix_ref[...])
    branch = product(mixed_low, out_ref[...]) + vec_ref[8:9, :]
    for window in range(count):
        rows = slice(window * padded, (window + 1) * padded)
        mix_out[window] = mixed_low[rows]
        after_out[window] = flat[rows] + keep_ref[window] * branch[rows]


def window_backward_kernel(
    count,
    first_step,
    last,
    seq_len,
    padded,
    tokens_ref,
    region_ref,
    bias_ref,
    keep_ref,
    qkv_ref,
    out_ref,
    vec_ref,
    proj_ref,
    after_grad_ref,
    region_keep_ref,
    sums_before_ref,
    *rest,
):
    scratch_count = 8
    if last:
        region_branch_out, region_mix_out = rest[-scratch_count - 2 : -scratch_count]
        rest = rest[: -scratch_count - 2] + rest[-scratch_count:]
    (
        region_grad_out,
        sums_out,
        grad_out,
        proj_grad_out,
        branch_grad_out,
        fill_ref,
        proj_grad_ref,
        spread_ref,
        spread_grad_ref,
        scores_ref,
        probs_grad_ref,
        probs_ref,
        score_grad_ref,
    ) = rest[-13:]
    step = pl.program_id(0) + first_step
    width = tokens_ref.shape[-1]

    @pl.when(pl.program_id(0) == 0)
    def _():
        fill_ref[...] = jnp.zeros_like(fill_ref)
        sums_out[...] = sums_before_ref[...]
        if first_step == 0:
            region_grad_out[...] = jnp.zeros_like(region_grad_out)
        else:
            region_grad_out[...] = rest[0][...]

    load_windows(tokens_ref, region_ref, fill_ref, count, seq_len, padded, step)
    lane_head = lax.broadcasted_iota(jnp.int32, (padded, 128), 1) // HEAD_DIM
    branch_grad = bfloat(
        jnp.concatenate(
            [keep_ref[window] * after_grad_ref[window] for window in range(count)], axis=0
        )
    )
    mix_grad = dot_as(branch_grad, out_ref[...], NT)
    for window in range(count):
        branch_grad_out[window] = branch_grad[window * padded : (window + 1) * padded]
    pairs = [(window, group) for window in range(count) for group in range(width // 128)]

    def lanes_of(part, group):
        return slice(part * width + group * 128, part * width + (group + 1) * 128)

    for number, (window, group) in enumerate(pairs):
        query = proj_ref[window, :, lanes_of(0, group)].astype(jnp.float32)
        spread_ref[number] = spread_heads(query, lane_head)
        rows = slice(window * padded, (window + 1) * padded)
        spread_grad_ref[number] = spread_heads(mix_grad[rows, lanes_of(0, group)], lane_head)
    for number, (window, group) in enumerate(pairs):
        scores_ref[number] = dot_as(
            proj_ref[window, :, lanes_of(1, group)], spread_ref[number], NT
        )
        probs_grad_ref[number] = dot_as(
            proj_ref[window, :, lanes_of(2, group)], spread_grad_ref[number], NT
        )
    for number, (window, group) in enumerate(pairs):
        probs = column_softmax(scores_ref[number], bias_ref[window])
        weighted = probs * probs_grad_ref[number]
        probs_ref[number] = bfloat(probs)
        score_grad_ref[number] = bfloat(weighted - probs * jnp.sum(weighted, 0, keepdims=True))
    for number, (window, group) in enumerate(pairs):
        rows = slice(window * padded, (window + 1) * padded)
        proj_grad_ref[rows, lanes_of(2, group)] = product(
            probs_ref[number], spread_grad_ref[number]
        )
        proj_grad_ref[rows, lanes_of(1, group)] = (
            product(score_grad_ref[number], spread_ref[number]) * SCORE_SCALE
        )
    for number, (window, group) in enumerate(pairs):
        rows = slice(window * padded, (window + 1) * padded)
        query_grad = dot_as(score_grad_ref[number], proj_ref[window, :, lanes_of(1, group)], TN)
        proj_grad_ref[rows, lanes_of(0, group)] = (
            join_heads(query_grad, lane_head, padded) * SCORE_SCALE
        )
    proj_grad = bfloat(proj_grad_ref[...])
    norm_grad = sum(
        dot_as(proj_grad[:, number * width : (number + 1) * width], qkv_ref[number], NT)
        for number in range(3)
    )
    flat = fill_ref[...]
    center = flat - jnp.mean(flat, -1, keepdims=True)
    scale = lax.rsqrt(jnp.mean(center * center, -1, keepdims=True) + EPSILON)
    hat = center * scale
    hat_grad = norm_grad * vec_ref[2:3, :]
    flat_grad = scale * (
        hat_grad
        - jnp.mean(hat_grad, -1, keepdims=True)
        - hat * jnp.mean(hat_grad * hat, -1, keepdims=True)
    )
    proj_sums = jnp.sum(proj_grad.astype(jnp.float32), 0, keepdims=True)
    sums_out[2:3, :] += jnp.sum(norm_grad * hat, 0, keepdims=True)
    sums_out[3:4, :] += jnp.sum(norm_grad, 0, keepdims=True)
    sums_out[6:7, :] += proj_sums[:, :width]
    sums_out[7:8, :] += proj_sums[:, 2 * width :]
    sums_out[8:9, :] += jnp.sum(branch_grad.astype(jnp.float32), 0, keepdims=True)
    for window in range(count):
        rows = slice(window * padded, (window + 1) * padded)
        proj_grad_out[window] = proj_grad[rows]
        seq_grad = after_grad_ref[window] + flat_grad[rows]
        for group in range(width // 128):
            lanes = slice(group * 128, (group + 1) * 128)
            grad_out[window, pl.ds(group, seq_len, stride=width // 128), :] = seq_grad[
                :seq_len, lanes
            ]
        region_grad_out[pl.ds(step * count + window, 1), :] = seq_grad[0:1]

    if last:

        @pl.when(pl.program_id(0) == pl.num_programs(0) - 1)
        def _():
            region_branch = bfloat(region_keep_ref[...] * region_grad_out[...])
            sums_out[8:9, :] += jnp.sum(region_branch.astype(jnp.float32), 0, keepdims=True)
            region_branch_out[...] = region_branch
            regions = region_branch.shape[0]
            spare_rows = region_mix_out.shape[0] - regions - sums_out.shape[0]
            region_mix_out[:regions, :] = bfloat(dot_as(region_branch, out_ref[...], NT))
            sums_low = jnp.concatenate(
                [sums_out[...], jnp.zeros((spare_rows, width), jnp.float32)], axis=0
            )
            region_mix_out[regions:, :] = bfloat(sums_low)


def window_step(windows, most=4):
    return next(count for count in (10, 5, 4, 2, 1) if count <= most and windows % count == 0)


def whole_spec(shape):
    return pl.BlockSpec(shape, lambda step: (0,) * len(shape))


def step_spec(count, *rest):
    return pl.BlockSpec((count,) + rest, lambda step: (step,) + (0,) * len(rest))


def token_spec(count, *rest):
    return pl.BlockSpec((1, count) + rest, lambda step: (0, step) + (0,) * len(rest))


def kept_spec():
    return pl.BlockSpec(memory_space=pltpu.VMEM)


def lasting(microseconds):
    return pl.CostEstimate(flops=microseconds * 10**9, bytes_accessed=10**6, transcendentals=0)


def in_hbm(values):
    return pltpu.with_memory_space_constraint(values, pltpu.HBM)


def hbm_shape(dims, kind=jnp.float32):
    return pltpu.HBM(dims, kind)


def shape_of(dims, kind=jnp.float32):
    return jax.ShapeDtypeStruct(dims, kind)


def window_forward(tokens, region, bias, keep, qkv_weight, out_weight, vectors, padded):
    _, windows, seq_len, width = tokens.shape
    count = window_step(windows, 10)
    pairs = count * width // 128
    return pl.pallas_call(
        functools.partial(window_forward_kernel, count, seq_len, padded),
        grid=(windows // count,),
        in_specs=[
            token_spec(count, seq_len, width),
            whole_spec(region.shape),
            step_spec(count, padded, 1),
            step_spec(count, 1, 1),
            kept_spec(),
            kept_spec(),
            whole_spec(vectors.shape),
        ],
        out_specs=[
            step_spec(count, padded, width),
            step_spec(count, padded, 3 * width),
            step_spec(count, padded, width),
            step_spec(count, padded, width),
        ],
        out_shape=[
            hbm_shape((windows, padded, width), jnp.bfloat16),
            hbm_shape((windows, padded, 3 * width), jnp.bfloat16),
            hbm_shape((windows, padded, width), jnp.bfloat16),
            hbm_shape((windows, padded, width)),
        ],
        scratch_shapes=[
            pltpu.VMEM((count * padded, width), jnp.float32),
            pltpu.VMEM((count * padded, width), jnp.float32),
            pltpu.VMEM((pairs, padded, GROUP_HEADS * padded), jnp.float32),
            pltpu.VMEM((pairs, padded, GROUP_HEADS * padded), jnp.bfloat16),
        ],
        compiler_params=pltpu.CompilerParams(vmem_limit_bytes=VMEM_LIMIT),
        name="window_forward",
    )(in_hbm(tokens), region, bias, keep, qkv_weight, out_weight, vectors)


def window_backward(
    tokens,
    region,
    bias,
    keep,
    qkv_weight,
    out_weight,
    vectors,
    proj,
    after_grad,
    region_keep,
    before,
    steps,
    padded,
):
    _, windows, seq_len, width = tokens.shape
    count = window_step(windows, 5)
    first_step, last_step = steps
    here = (last_step - first_step) * count
    pairs = count * width // 128
    spread_rows = GROUP_HEADS * padded

    def moved(*dims, lead=0):
        zeros = (0,) * (len(dims) - 1)
        if lead:
            return pl.BlockSpec((1,) + dims, lambda step: (0, step + first_step) + zeros)
        return pl.BlockSpec(dims, lambda step: (step + first_step,) + zeros)

    flat_rows = seq_len * width // 128

    grad_before, sums_before, region_before = before
    operands = [in_hbm(tokens), region, bias, keep, qkv_weight, out_weight, vectors]
    operands += [in_hbm(proj), in_hbm(after_grad), region_keep, in_hbm(sums_before)]
    in_specs = [
        moved(count, seq_len, width, lead=1),
        whole_spec(region.shape),
        moved(count, padded, 1),
        moved(count, 1, 1),
        kept_spec(),
        kept_spec(),
        whole_spec(vectors.shape),
        moved(count, padded, 3 * width),
        moved(count, padded, width),
        whole_spec(region_keep.shape),
        whole_spec(sums_before.shape),
    ]
    aliases = {}
    if first_step:
        aliases = {len(operands) + 1: 2}
        operands += [in_hbm(region_before), in_hbm(grad_before)]
        in_specs += [whole_spec(region.shape), pl.BlockSpec(memory_space=pl.ANY)]
    last = last_step * count == windows
    out_specs = [
        whole_spec(region.shape),
        whole_spec(vectors.shape),
        moved(count, flat_rows, 128),
        step_spec(count, padded, 3 * width),
        step_spec(count, padded, width),
    ]
    out_shape = [
        hbm_shape(region.shape),
        hbm_shape(vectors.shape),
        hbm_shape((windows, flat_rows, 128)),
        hbm_shape((here, padded, 3 * width), jnp.bfloat16),
        hbm_shape((here, padded, width), jnp.bfloat16),
    ]
    if last:
        payload = (region.shape[0] + VECTOR_ROWS, width)
        out_specs += [whole_spec(region.shape), whole_spec(payload)]
        out_shape += [shape_of(region.shape, jnp.bfloat16), shape_of(payload, jnp.bfloat16)]
    return pl.pallas_call(
        functools.partial(window_backward_kernel, count, first_step, last, seq_len, padded),
        grid=(last_step - first_step,),
        in_specs=in_specs,
        out_specs=out_specs,
        out_shape=out_shape,
        scratch_shapes=[
            pltpu.VMEM((count * padded, width), jnp.float32),
            pltpu.VMEM((count * padded, 3 * width), jnp.float32),
            pltpu.VMEM((pairs, spread_rows, 128), jnp.bfloat16),
            pltpu.VMEM((pairs, spread_rows, 128), jnp.bfloat16),
            pltpu.VMEM((pairs, padded, spread_rows), jnp.float32),
            pltpu.VMEM((pairs, padded, spread_rows), jnp.float32),
            pltpu.VMEM((pairs, padded, spread_rows), jnp.bfloat16),
            pltpu.VMEM((pairs, padded, spread_rows), jnp.bfloat16),
        ],
        input_output_aliases=aliases,
        compiler_params=pltpu.CompilerParams(vmem_limit_bytes=VMEM_LIMIT),
        cost_estimate=lasting(here),
        name="window_backward",
    )(*operands)


def insert_kernel(rows_ref, region_ref, out_ref):
    out_ref[...] = rows_ref[...]
    for window in range(rows_ref.shape[0]):
        for group in range(region_ref.shape[1] // 128):
            out_ref[window, group : group + 1, :] = region_ref[
                window : window + 1, group * 128 : (group + 1) * 128
            ]


def insert_regions(grad, region_grad):
    rows = pl.BlockSpec((grad.shape[0], 8, 128), lambda step: (0, 0, 0))
    return pl.pallas_call(
        insert_kernel,
        grid=(1,),
        in_specs=[rows, whole_spec(region_grad.shape)],
        out_specs=rows,
        out_shape=shape_of(grad.shape),
        input_output_aliases={0: 0},
        compiler_params=pltpu.CompilerParams(vmem_limit_bytes=VMEM_LIMIT),
        name="insert_regions",
    )(grad, region_grad)


GELU_IN = 0.7978845608028654
GELU_CUBE = 0.044715


def gelu_both(values):
    square = values * values
    bent = jnp.tanh(values * (GELU_IN + (GELU_IN * GELU_CUBE) * square))
    share = 0.5 + 0.5 * bent
    slope = share + (0.5 * values) * (1.0 - bent * bent) * (
        GELU_IN + (3.0 * GELU_IN * GELU_CUBE) * square
    )
    return values * share, slope


def split_cores(values, core):
    own_first = core == 0
    kept = jnp.where(own_first, values[:, 0], values[:, 1])
    sent = jnp.where(own_first, values[:, 1], values[:, 0])
    return kept, bfloat(sent)


def mlp_kernel(
    place_ref,
    after_ref,
    cot_ref,
    keep_ref,
    vec_ref,
    up_ref,
    down_ref,
    sums_ref,
    out_hbm,
    grad_hbm,
    kept_hbm,
    sent_hbm,
    cot_fill,
    act_ref,
    hidden_grad_ref,
    out_ref,
    grad_ref,
    kept_ref,
    sent_ref,
    sems,
):
    _, windows, seq_len, width = cot_ref.shape
    padded = after_ref.shape[0] // windows
    folds = up_ref.shape[1] // width
    core = place_ref[1] % 2
    copies = []

    def write_out(source, target):
        copy = pltpu.make_async_copy(source, target, sems.at[len(copies)])
        copy.start()
        copies.append(copy)

    cot_fill[...] = jnp.zeros_like(cot_fill)
    keeps = []
    for window in range(windows):
        base = window * padded
        cot_fill[base : base + seq_len, :] = cot_ref[0, window].astype(jnp.float32)
        keeps.append(jnp.broadcast_to(keep_ref[window], (padded, 1)))
    keep = jnp.concatenate(keeps, axis=0)
    flat = after_ref[...]
    center = flat - jnp.mean(flat, -1, keepdims=True)
    scale = lax.rsqrt(jnp.mean(center * center, -1, keepdims=True) + EPSILON)
    hat = center * scale
    normed = bfloat(hat * vec_ref[4:5, :] + vec_ref[5:6, :])
    normed_turned = normed.T
    cot = cot_fill[...]
    branch_grad = bfloat(keep * cot)
    branch = jnp.zeros_like(flat)
    norm_grad = jnp.zeros_like(flat)
    for fold in range(folds):
        lanes = slice(fold * width, (fold + 1) * width)
        up_part, down_part = up_ref[:, lanes], down_ref[lanes, :]
        hidden = product(normed, up_part) + vec_ref[10 + fold : 11 + fold, :]
        act, slope = gelu_both(hidden)
        act = bfloat(act)
        act_ref[:, lanes] = act
        branch += product(act, down_part)
        hidden_grad = bfloat(slope * dot_as(branch_grad, down_part, NT))
        hidden_grad_ref[:, lanes] = hidden_grad
        norm_grad += dot_as(hidden_grad, up_part, NT)
        sums_ref[10 + fold : 11 + fold, :] = jnp.sum(
            hidden_grad.astype(jnp.float32), 0, keepdims=True
        )
    output = bfloat(flat + keep * (branch + vec_ref[9:10, :]))
    for window in range(windows):
        out_ref[window] = output[window * padded : window * padded + seq_len]
    write_out(out_ref, out_hbm.at[0])
    hat_grad = norm_grad * vec_ref[4:5, :]
    grad_ref[...] = cot + scale * (
        hat_grad
        - jnp.mean(hat_grad, -1, keepdims=True)
        - hat * jnp.mean(hat_grad * hat, -1, keepdims=True)
    )
    write_out(grad_ref, grad_hbm)
    sums_ref[0:4, :] = jnp.zeros((4, width), jnp.float32)
    sums_ref[4:5, :] = jnp.sum(norm_grad * hat, 0, keepdims=True)
    sums_ref[5:6, :] = jnp.sum(norm_grad, 0, keepdims=True)
    sums_ref[6:9, :] = jnp.zeros((3, width), jnp.float32)
    sums_ref[9:10, :] = jnp.sum(branch_grad.astype(jnp.float32), 0, keepdims=True)
    _, blocks, rows, _ = kept_ref.shape
    part, here = rows // folds, blocks // folds
    for fold in range(folds):
        lanes = slice(fold * width, (fold + 1) * width)
        total = product(normed_turned, hidden_grad_ref[:, lanes])
        inner = pl.ds(fold * part, part)
        kept, sent = split_cores(total.reshape(blocks, 2, part, width), core)
        kept_ref[0, :, inner], sent_ref[0, :, inner] = kept, sent
        write_out(kept_ref.at[0, :, inner], kept_hbm.at[0, :, inner])
        write_out(sent_ref.at[0, :, inner], sent_hbm.at[0, :, inner])
    for fold in range(folds):
        lanes = slice(fold * width, (fold + 1) * width)
        total = dot_as(act_ref[:, lanes], branch_grad, TN)
        inner = pl.ds(fold * here, here)
        kept, sent = split_cores(total.reshape(here, 2, rows, width), core)
        kept_ref[1, inner], sent_ref[1, inner] = kept, sent
        write_out(kept_ref.at[1, inner], kept_hbm.at[1, inner])
        write_out(sent_ref.at[1, inner], sent_hbm.at[1, inner])
    for copy in copies:
        copy.wait()


def mlp(place, after, cotangent, keep, vectors, up_weight, down_weight, padded, win_count):
    _, windows, seq_len, width = cotangent.shape
    rows = after.shape[0]
    folds = up_weight.shape[1] // width
    dims = (2, win_count // 2, width // win_count * folds, width)
    anywhere = pl.BlockSpec(memory_space=pl.ANY)
    sums, output, grad, kept, sent = pl.pallas_call(
        mlp_kernel,
        grid=(1,),
        in_specs=[
            pl.BlockSpec(memory_space=pltpu.SMEM),
            whole_spec(after.shape),
            whole_spec(cotangent.shape),
            whole_spec(keep.shape),
            whole_spec(vectors.shape),
            kept_spec(),
            kept_spec(),
        ],
        out_specs=[whole_spec(vectors.shape)] + [anywhere] * 4,
        out_shape=[
            hbm_shape(vectors.shape),
            hbm_shape(cotangent.shape, jnp.bfloat16),
            hbm_shape(after.shape),
            hbm_shape(dims),
            hbm_shape(dims, jnp.bfloat16),
        ],
        scratch_shapes=[
            pltpu.VMEM((rows, width), jnp.float32),
            pltpu.VMEM((rows, folds * width), jnp.bfloat16),
            pltpu.VMEM((rows, folds * width), jnp.bfloat16),
            pltpu.VMEM((windows, seq_len, width), jnp.bfloat16),
            pltpu.VMEM((rows, width), jnp.float32),
            pltpu.VMEM(dims, jnp.float32),
            pltpu.VMEM(dims, jnp.bfloat16),
            pltpu.SemaphoreType.DMA((2 + 4 * folds,)),
        ],
        compiler_params=pltpu.CompilerParams(vmem_limit_bytes=VMEM_LIMIT),
        cost_estimate=lasting(25),
        name="mlp",
    )(place, in_hbm(after), in_hbm(cotangent), keep, vectors, up_weight, down_weight)
    return output, grad, sums, (kept, sent)


def image_bias(keys_ref, queries_ref):
    return jnp.where(keys_ref[...] == queries_ref[...], 0.0, -1e30)


def region_forward_kernel(
    pieces,
    *refs,
):
    piece_refs, refs = refs[:pieces], refs[pieces:]
    region_forward_rows(piece_refs, *refs)


def region_forward_rows(
    piece_refs,
    own_ref,
    keep_ref,
    key_image_ref,
    query_image_ref,
    qkv_ref,
    out_ref,
    vec_ref,
    norm_out,
    proj_out,
    mix_out,
    new_out,
    all_ref,
):
    rows, width = own_ref.shape
    vec = vec_ref[...]
    for block, block_ref in numbered_blocks(piece_refs):
        all_ref[block * rows : (block + 1) * rows, :] = block_ref[...].astype(jnp.float32)
    normed = bfloat(norm_rows(all_ref[...], vec[0:1], vec[1:2]))
    norm_out[...] = normed
    query = bfloat(product(normed, qkv_ref[0]) + vec[6:7])
    keyset = bfloat(product(normed, qkv_ref[1]))
    values = bfloat(product(normed, qkv_ref[2]) + vec[7:8])
    proj_out[:, :width] = query
    proj_out[:, width : 2 * width] = keyset
    proj_out[:, 2 * width :] = values
    region = own_ref[...].astype(jnp.float32)
    own_norm = bfloat(norm_rows(region, vec[0:1], vec[1:2]))
    own_query = product(own_norm, qkv_ref[0]) + vec[6:7]
    bias = image_bias(key_image_ref, query_image_ref)
    lane_head = lax.broadcasted_iota(jnp.int32, (rows, 128), 1) // HEAD_DIM
    parts = []
    for group in range(width // 128):
        lanes = slice(group * 128, (group + 1) * 128)
        spread = spread_heads(own_query[:, lanes], lane_head)
        probs = column_softmax(dot_as(keyset[:, lanes], spread, NT), bias)
        mixed = dot_as(bfloat(probs), values[:, lanes], TN)
        parts.append(join_heads(mixed, lane_head, rows))
    mixed_low = bfloat(jnp.concatenate(parts, axis=1))
    mix_out[...] = mixed_low
    branch = product(mixed_low, out_ref[...]) + vec[8:9]
    new_out[...] = region + keep_ref[...] * branch


def region_forward(pieces, own, keep, key_images, query_images, qkv_weight, out_weight, vectors):
    rows, width = own.shape
    total = len(pieces) * pieces[0].shape[0] * rows
    return pl.pallas_call(
        functools.partial(region_forward_kernel, len(pieces)),
        out_shape=[
            hbm_shape((total, width), jnp.bfloat16),
            hbm_shape((total, 3 * width), jnp.bfloat16),
            hbm_shape(own.shape, jnp.bfloat16),
            shape_of(own.shape),
        ],
        scratch_shapes=[pltpu.VMEM((total, width), jnp.float32)],
        compiler_params=pltpu.CompilerParams(vmem_limit_bytes=VMEM_LIMIT),
        name="region_forward",
    )(*pieces, own, keep, key_images, query_images, qkv_weight, out_weight, vectors)


def region_backward_kernel(pieces, place_ref, *refs):
    region_refs, refs = refs[:pieces], refs[pieces:]
    gathered_refs, refs = refs[:pieces], refs[pieces:]
    region_backward_rows(place_ref, region_refs, gathered_refs, *refs)


def region_backward_rows(
    place_ref,
    region_refs,
    gathered_refs,
    norm_ref,
    proj_ref,
    key_image_ref,
    query_image_ref,
    new_grad_ref,
    qkv_ref,
    vec_ref,
    grad_out,
    weight_out,
    sums_out,
    bias_ref,
    proj_grad_ref,
    region_grad_ref,
    weight_ref,
    mix_grad_ref,
    all_ref,
    scores_ref,
    probs_grad_ref,
    probs_ref,
    score_grad_ref,
):
    total, width = all_ref.shape
    rows = new_grad_ref.shape[0]
    bias_ref[...] = image_bias(key_image_ref, query_image_ref)
    lane_head = lax.broadcasted_iota(jnp.int32, (total, 128), 1) // HEAD_DIM
    for block, block_ref in numbered_blocks(region_refs):
        all_ref[block * rows : (block + 1) * rows, :] = block_ref[...].astype(jnp.float32)
    vector_sum = jnp.zeros((VECTOR_ROWS, width), jnp.float32)
    for block, block_ref in numbered_blocks(gathered_refs):
        part = block_ref[...].astype(jnp.float32)
        mix_grad_ref[block * rows : (block + 1) * rows, :] = part[:rows]
        vector_sum += part[rows:]

    @pl.loop(0, width // 128)
    def _(group):
        query_lanes = pl.ds(pl.multiple_of(group * 128, 128), 128)
        key_lanes = pl.ds(pl.multiple_of(width + group * 128, 128), 128)
        value_lanes = pl.ds(pl.multiple_of(2 * width + group * 128, 128), 128)
        key_low = proj_ref[:, key_lanes]
        value_low = proj_ref[:, value_lanes]
        spread = spread_heads(proj_ref[:, query_lanes].astype(jnp.float32), lane_head)
        spread_grad = spread_heads(mix_grad_ref[:, query_lanes], lane_head)
        scores_ref[...] = dot_as(key_low, spread, NT)
        probs_grad_ref[...] = dot_as(value_low, spread_grad, NT)
        for head in range(GROUP_HEADS):
            lanes = slice(head * total, (head + 1) * total)
            probs = column_softmax(scores_ref[:, lanes], bias_ref[...])
            weighted = probs * probs_grad_ref[:, lanes]
            probs_ref[:, lanes] = bfloat(probs)
            score_grad_ref[:, lanes] = bfloat(
                weighted - probs * jnp.sum(weighted, 0, keepdims=True)
            )
        value_grad = product(probs_ref[...], spread_grad)
        key_grad = product(score_grad_ref[...], spread)
        turned = product(key_low.T, score_grad_ref[...])
        query_grad = jnp.concatenate(
            [
                turned[head * HEAD_DIM : (head + 1) * HEAD_DIM, head * total : (head + 1) * total]
                for head in range(GROUP_HEADS)
            ],
            axis=0,
        ).T
        proj_grad_ref[:, query_lanes] = bfloat(query_grad * SCORE_SCALE)
        proj_grad_ref[:, key_lanes] = bfloat(key_grad * SCORE_SCALE)
        proj_grad_ref[:, value_lanes] = bfloat(value_grad)

    proj_grad = proj_grad_ref[...]
    norm_grad = sum(
        dot_as(proj_grad[:, number * width : (number + 1) * width], qkv_ref[number], NT)
        for number in range(3)
    )
    region = all_ref[...]
    center = region - jnp.mean(region, -1, keepdims=True)
    scale = lax.rsqrt(jnp.mean(center * center, -1, keepdims=True) + EPSILON)
    hat = center * scale
    hat_grad = norm_grad * vec_ref[0:1, :]
    region_grad_ref[...] = scale * (
        hat_grad
        - jnp.mean(hat_grad, -1, keepdims=True)
        - hat * jnp.mean(hat_grad * hat, -1, keepdims=True)
    )
    grad_out[...] = new_grad_ref[...] + region_grad_ref[:rows, :]
    bias_sums = jnp.sum(proj_grad.astype(jnp.float32), 0, keepdims=True)
    sums_out[...] = vector_sum
    sums_out[0:1, :] += jnp.sum(norm_grad * hat, 0, keepdims=True)
    sums_out[1:2, :] += jnp.sum(norm_grad, 0, keepdims=True)
    sums_out[6:7, :] += bias_sums[:, :width]
    sums_out[7:8, :] += bias_sums[:, 2 * width :]
    weight_ref[...] = dot_as(norm_ref[...], proj_grad, TN)
    weight_rows = weight_out.shape[1]
    weight_start = pl.multiple_of((place_ref[1] >> 1) * weight_rows, 8)
    for number in range(3):
        weight_out[number] = weight_ref[
            pl.ds(weight_start, weight_rows), number * width : (number + 1) * width
        ]


def region_backward(
    place,
    regions,
    gathered,
    normed,
    proj,
    key_images,
    query_images,
    new_grad,
    qkv_weight,
    vectors,
    weight_rows,
):
    total, width = normed.shape
    vmem = pl.BlockSpec(memory_space=pltpu.VMEM)
    operands = [*regions, *gathered, in_hbm(normed), in_hbm(proj), key_images, query_images]
    operands += [new_grad, qkv_weight, vectors]
    return pl.pallas_call(
        functools.partial(region_backward_kernel, len(regions)),
        grid=(1,),
        in_specs=[pl.BlockSpec(memory_space=pltpu.SMEM)]
        + [whole_spec(operand.shape) for operand in operands[:-2]]
        + [vmem, whole_spec(vectors.shape)],
        out_specs=[vmem] * 3,
        out_shape=[
            shape_of(new_grad.shape),
            shape_of((3, weight_rows, width)),
            shape_of((VECTOR_ROWS, width)),
        ],
        scratch_shapes=[
            pltpu.VMEM((total, total), jnp.float32),
            pltpu.VMEM((total, 3 * width), jnp.bfloat16),
            pltpu.VMEM((total, width), jnp.float32),
            pltpu.VMEM((width, 3 * width), jnp.float32),
            pltpu.VMEM((total, width), jnp.float32),
            pltpu.VMEM((total, width), jnp.float32),
            pltpu.VMEM((total, GROUP_HEADS * total), jnp.float32),
            pltpu.VMEM((total, GROUP_HEADS * total), jnp.float32),
            pltpu.VMEM((total, GROUP_HEADS * total), jnp.bfloat16),
            pltpu.VMEM((total, GROUP_HEADS * total), jnp.bfloat16),
        ],
        compiler_params=pltpu.CompilerParams(vmem_limit_bytes=VMEM_LIMIT),
        cost_estimate=lasting(14),
        name="region_backward",
    )(place, *operands)


def pair_gradient_kernel(first_count, second_count, place_ref, *refs):
    own_first = place_ref[1] % 2 == 0
    kept, sent = refs[-2:]

    def total(pairs):
        lefts, rights = pairs[0::2], pairs[1::2]
        return sum(dot_as(left[...], right[...], TN) for left, right in zip(lefts, rights))

    first = total(refs[: 2 * first_count])
    second = total(refs[2 * first_count : 2 * (first_count + second_count)])
    kept[...] = jnp.where(own_first, first, second)
    sent[...] = bfloat(jnp.where(own_first, second, first))


def pair_gradients(place, first, second, width):
    operands, in_specs = [place], [pl.BlockSpec(memory_space=pltpu.SMEM)]
    for left, row, right, column, rows in first + second:
        operands += [in_hbm(left), in_hbm(right)]
        in_specs.append(pl.BlockSpec((rows, width), lambda step, row=row: (row, 0)))
        in_specs.append(pl.BlockSpec((rows, width), lambda step, column=column: (0, column)))
    return pl.pallas_call(
        functools.partial(pair_gradient_kernel, len(first), len(second)),
        grid=(1,),
        in_specs=in_specs,
        out_specs=[whole_spec((width, width))] * 2,
        out_shape=[hbm_shape((width, width)), hbm_shape((width, width), jnp.bfloat16)],
        compiler_params=pltpu.CompilerParams(vmem_limit_bytes=VMEM_LIMIT),
        cost_estimate=lasting(5),
        name="pair_gradients",
    )(*operands)


def row_pieces(whole, rights, column):
    pairs, start = [], 0
    for right in rights:
        rows = right.shape[0]
        left, row = (whole, start // rows) if start % rows == 0 else (whole[start : start + rows], 0)
        pairs.append((left, row, right, column, rows))
        start += rows
    return pairs


def finish_big_kernel(
    place_ref, mine, other, mom_mine, mom_other, up_ref, down_ref, up_new, down_new, up_mom, down_mom
):
    first = place_ref[0] == 0

    def ordered(here, there):
        return jnp.where(first, here, there), jnp.where(first, there, here)

    updates = ordered(mine[...].astype(jnp.float32), other[...].astype(jnp.float32))
    momenta = ordered(mom_mine[...], mom_other[...])
    down_new[...] = down_ref[...].astype(jnp.float32) - MATRIX_RATE * updates[1]
    down_mom[...] = momenta[1]
    rows, columns = up_ref.shape
    width = down_ref.shape[1]
    for fold in range(columns // width):
        lanes = slice(fold * width, (fold + 1) * width)
        inner = slice(fold * rows, (fold + 1) * rows)
        up_new[:, lanes] = up_ref[:, lanes].astype(jnp.float32) - MATRIX_RATE * updates[0][inner]
        up_mom[:, lanes] = momenta[0][inner]


def finish_small_kernel(place_ref, *refs):
    updates, momenta = refs[:4], refs[4:8]
    qkv_ref, out_ref, qkv_new, out_new, qkv_mom, out_mom = refs[8:]
    first, low = place_ref[0] == 0, place_ref[2] == 0

    def ordered(parts):
        own, side, across, corner = [part[...].astype(jnp.float32) for part in parts]
        here = jnp.where(low, own, side), jnp.where(low, side, own)
        there = jnp.where(low, across, corner), jnp.where(low, corner, across)
        return [jnp.where(first, one, two) for one, two in zip(here + there, there + here)]

    for number, (update, momentum) in enumerate(zip(ordered(updates), ordered(momenta))):
        if number < 3:
            qkv_new[number] = qkv_ref[number].astype(jnp.float32) - MATRIX_RATE * update
            qkv_mom[number] = momentum
        else:
            out_new[...] = out_ref[...].astype(jnp.float32) - MATRIX_RATE * update
            out_mom[...] = momentum


def finish_call(kernel, name, place, parts, weights, blocks, indices):
    dims = [shape_of(block) for block in blocks]
    return pl.pallas_call(
        kernel,
        grid_spec=pltpu.PrefetchScalarGridSpec(
            num_scalar_prefetch=1,
            grid=(1,),
            in_specs=[pl.BlockSpec(part.shape, lambda step, place: (0, 0)) for part in parts]
            + [pl.BlockSpec(block, index) for block, index in zip(blocks, indices)],
            out_specs=[
                pl.BlockSpec(block, lambda step, place, count=len(block): (0,) * count)
                for block in blocks + blocks
            ],
        ),
        out_shape=dims + dims,
        compiler_params=pltpu.CompilerParams(vmem_limit_bytes=VMEM_LIMIT),
        name=name,
    )(place, *parts, *weights)


def finish_big(place, parts, up_weight, down_weight):
    rows, width = parts[0].shape
    up_rows = rows * width // up_weight.shape[1]
    own = lambda step, place: (place[1], 0)
    return finish_call(
        finish_big_kernel,
        "finish_big",
        place,
        parts,
        (up_weight, down_weight),
        [(up_rows, up_weight.shape[1]), (rows, width)],
        [own, own],
    )


def finish_small(place, parts, qkv_weight, out_weight):
    rows, width = parts[0].shape
    return finish_call(
        finish_small_kernel,
        "finish_small",
        place,
        parts,
        (qkv_weight, out_weight),
        [(3, rows, width), (rows, width)],
        [lambda step, place: (0, place[1], 0), lambda step, place: (place[1], 0)],
    )


def local(
    tokens,
    patch_mask,
    keep_mask,
    image_map,
    qkv_weight,
    out_weight,
    up_weight,
    down_weight,
    vectors,
    qkv_mom,
    out_mom,
    up_mom,
    down_mom,
    vec_mom,
    cotangent,
):
    windows = tokens.shape[1]
    seq_len = tokens.shape[2]
    model_width = tokens.shape[3]
    hidden_width = up_weight.shape[1]
    folds = hidden_width // model_width
    shard_rows = out_mom.shape[0]
    ff_rows = down_mom.shape[0]
    vec_rows = vec_mom.shape[0]
    padded = (seq_len + 7) // 8 * 8
    region_rows = (windows + 7) // 8 * 8
    row_count = windows * padded
    win_count = lax.axis_size("win")
    win_index = lax.axis_index("win")
    place = jnp.stack([lax.axis_index("rep"), win_index]).astype(jnp.int32)

    def pad_rows(values, rows, fill=0):
        widths = ((0, rows - values.shape[0]),) + ((0, 0),) * (values.ndim - 1)
        return jnp.pad(values, widths, constant_values=fill)

    region_own = pad_rows(tokens[0, :, 0], region_rows)
    regions = gather_far(region_own)
    up_old, down_old = after((up_mom, down_mom), regions)
    for bit in (1, 0):
        regions = gather_bit(regions, bit)
    keeper = keep_mask[0].astype(jnp.float32) / KEEP_SHARE
    images = image_map[0].reshape(win_count, windows)[win_index ^ jnp.array(gather_masks())]
    images = jnp.pad(images, ((0, 0), (0, region_rows - windows)), constant_values=-1)
    key_images = images.reshape(-1, 1)
    own_images = jnp.tile(images[:1], (1, GROUP_HEADS))
    region_keep = pad_rows(keeper[:, 0:1], region_rows)

    big_moms = (
        MOMENTUM_DECAY * fold_columns(up_old, model_width),
        MOMENTUM_DECAY * down_old,
    )
    small_old_moms = MOMENTUM_DECAY * jnp.concatenate([qkv_mom, out_mom[None]])
    own_pair = jnp.where(lax.axis_index("rep") == 0, small_old_moms[:2], small_old_moms[2:])
    kept, sent = pick_owner(win_index % 2 == 0, own_pair[0], own_pair[1])
    small_pair_mom = jnp.concatenate(
        pick_owner(win_index % 2 == 0, kept, swap(sent, "win", 0))
    )
    regions, big_moms, small_pair_mom = tie(regions, big_moms, small_pair_mom)

    region_norm, region_proj, region_mix, region_new = region_forward(
        regions, region_own, region_keep, key_images, own_images, qkv_weight, out_weight, vectors
    )

    key_valid = jnp.concatenate([jnp.ones((windows, 1), jnp.int32), patch_mask[0]], axis=1) == 1
    key_bias = jnp.where(key_valid, 0.0, -1e30)
    key_bias = jnp.pad(key_bias, ((0, 0), (0, padded - seq_len)), constant_values=-1e30)
    key_bias = key_bias[:, :, None]
    keep_window = keeper[:, 1].reshape(windows, 1, 1)
    seq_norm, seq_proj, local_mix, after_attn = window_forward(
        tokens, region_new, key_bias, keep_window, qkv_weight, out_weight, vectors, padded
    )
    seq_norm = seq_norm.reshape(row_count, model_width)
    local_mix = local_mix.reshape(row_count, model_width)
    after_attn = after_attn.reshape(row_count, model_width)

    out_tokens, attn_res_grad, mlp_sums, big_halves = mlp(
        place,
        after_attn,
        cotangent,
        keeper[:, 2].reshape(windows, 1, 1),
        vectors,
        up_weight,
        down_weight,
        padded,
        win_count,
    )

    steps = windows // window_step(windows, 5)
    cuts = [0, steps // 2, steps]
    after_grad = attn_res_grad.reshape(windows, padded, model_width)
    two_owners = lax.axis_size("rep") == 2 and len(far_bits()) == 2
    order = Order()
    big_taken = order.launch((big_halves[1], "win", 1))
    before = (None, mlp_sums, None)
    proj_grads, branch_grads = [], []
    for piece in range(2):
        region_new_grad, sums, seq_grad, proj_grad, branch_grad, *region_parts = window_backward(
            tokens,
            region_new,
            key_bias,
            keep_window,
            qkv_weight,
            out_weight,
            vectors,
            seq_proj,
            after_grad,
            region_keep,
            before,
            (cuts[piece], cuts[piece + 1]),
            padded,
        )
        before = (seq_grad, sums, region_new_grad)
        proj_grads.append(proj_grad.reshape(-1, 3 * model_width))
        branch_grads.append(branch_grad.reshape(-1, model_width))
        if piece == 0:
            big_taken, after_grad = tie(big_taken, after_grad)
            big_total = big_halves[0] + wide(big_taken[0])
            if two_owners:
                big_kept, hops = first_parts(big_total)
                big_taken = order.launch(*hops)
    region_branch_grad, region_mix_grad = region_parts
    norm_rows_ready, mix_ready = seq_norm, local_mix
    if two_owners:
        region_mix_grad, big_taken = tie(region_mix_grad, big_taken)
        big_kept, hops = second_parts(*add_pair(big_kept, big_taken))
        hops, norm_rows_ready = tie([array for array, _, _ in hops], seq_norm)
        big_taken = order.launch((hops[0], "win", 2), (hops[1], "rep", 1))
        mix_taken = order.launch(*spread_far(region_mix_grad))

    first = lax.axis_index("rep") == 0
    low_core = win_index % 2 == 0
    kept, sent = pair_gradients(
        place,
        row_pieces(norm_rows_ready, proj_grads, 0),
        row_pieces(norm_rows_ready, proj_grads, 1),
        model_width,
    )
    if two_owners:
        kept, sent, mix_taken, big_taken = tie(kept, sent, mix_taken, big_taken)
        mixes = [far_piece(region_mix_grad, mix_taken)]
        big_kept, hops = far_parts(join_halves(add_pair(big_kept, big_taken)))
        hops, mixes, mix_ready = tie([array for array, _, _ in hops], mixes, local_mix)
        big_taken = order.launch(*[(hop, "win", 4 * (i + 1)) for i, hop in enumerate(hops)])
        mix_taken = order.launch((mixes[0], "win", 2))
    small_kept = [kept]
    small_taken = order.launch((sent, "win", 1))
    kept, sent = pair_gradients(
        place,
        row_pieces(seq_norm, proj_grads, 2),
        row_pieces(mix_ready, branch_grads, 0)
        + [(region_mix, 0, region_branch_grad, 0, region_rows)],
        model_width,
    )
    if two_owners:
        kept, sent, mix_taken, big_taken = tie(kept, sent, mix_taken, big_taken)
    small_kept.append(kept)
    small_taken += order.launch((sent, "win", 1))
    if two_owners:
        mixes += mix_taken
        mix_taken = order.launch(*[(piece, "win", 1) for piece in mixes])
    small_totals = [
        (kept + wide(taken)).reshape(-1, 2 * shard_rows, model_width)
        for kept, taken in zip(small_kept, order.land(small_taken))
    ]
    if two_owners:
        small_kept, hops = first_parts_of_two(small_totals)
        small_sent = [array for array, _, _ in hops]
        small_taken = order.launch(*hops)
        big_mom = jnp.where(first, big_moms[0], big_moms[1])
        big_mom = big_mom + add_far(big_kept, big_taken)
        big_low = bfloat(big_mom)
        big_taken = order.launch(*spread_far(big_low))
        mixes += mix_taken
        mixes = after(mixes, small_sent, big_low)
    else:
        mixes = gather_blocks(region_mix_grad)

    region_grad, region_weight_grad, region_sums = region_backward(
        place,
        regions,
        mixes,
        region_norm,
        region_proj,
        key_images,
        key_images.reshape(1, -1),
        region_new_grad,
        qkv_weight,
        vectors,
        2 * shard_rows,
    )

    if two_owners:
        region_weight_grad, small_taken, big_taken = tie(region_weight_grad, small_taken, big_taken)
        def spread_pair(mine):
            mine = mine.reshape(2, shard_rows, model_width)
            kept, sent = pick_owner(low_core, mine[0], mine[1])
            taken = order.launch((sent, "win", 1), (kept, "rep", 1), (sent, ("win", "rep"), 3))
            return kept, taken

        rep_rows = jnp.stack(
            [
                jnp.where(low_core, region_weight_grad[0], region_weight_grad[1]),
                jnp.where(low_core, region_weight_grad[2], 0.0),
            ]
        )
        rep = lax.axis_index("rep")
        vec_mine = rounded(region_sums)
        small_kept, hops = second_parts(*add_pair(small_kept, small_taken))
        small_taken = order.launch(*hops)
        vec_taken = order.launch(
            (bfloat(jnp.concatenate([pick(rep_rows, 1 - rep), vec_mine])), "rep", 1)
        )
        big_pieces = [far_piece(big_low, order.land(big_taken))]
        big_taken = order.launch((big_pieces[0], "win", 2))
        small_kept, hops = far_parts(join_halves(add_pair(small_kept, order.land(small_taken))))
        small_taken = order.launch(*hops)
        vec_taken = wide(vec_taken[0])
        region_rows_sum = pick(rep_rows, rep) + vec_taken[: 2 * shard_rows]
        vec_sum = vec_mine + vec_taken[2 * shard_rows :]
        big_pieces += order.land(big_taken)
        big_taken = order.launch(*[(piece, "win", 1) for piece in big_pieces])
        small_mom = add_far(small_kept, order.land(small_taken)) + region_rows_sum
        small_mom = small_pair_mom + small_mom
        small_low = bfloat(small_mom)
        small_taken = order.launch(*spread_far(small_low))
        input_grad = insert_regions(seq_grad, after(region_grad, *order.sent))
        input_grad = input_grad.reshape(tokens.shape)
        small_pieces = [far_piece(small_low, order.land(small_taken))]
        small_taken = order.launch((small_pieces[0], "win", 2))
        mom_parts = spread_pair(small_mom)
        other_mom = order.launch((big_mom, "rep", 1))[0]
        big_pieces += order.land(big_taken)
        big_mine = big_update(place, big_pieces, folds, gather_masks())

        other_update = order.launch((big_mine, "rep", 1))[0]
        small_pieces += order.land(small_taken)
        small_pieces, mom_parts, other_mom = tie(small_pieces, mom_parts, other_mom)
        small_mine = small_update(
            place, [piece[:, None] for piece in small_pieces], gather_masks(1)
        )[0]
        update_parts = spread_pair(small_mine)
        other_update = order.land(other_update)
        finish_place = jnp.concatenate([place, place[1:] & 1])
        big_parts = [big_mine, other_update, big_mom, other_mom]
        small_parts = [update_parts[0], *update_parts[1], mom_parts[0], *mom_parts[1]]
    else:
        input_grad = insert_regions(seq_grad, region_grad).reshape(tokens.shape)
        big_total = pick(sum_everywhere(big_total), win_index >> 1, 1)
        folded_up_mom = big_moms[0] + big_total[0]
        new_down_mom = big_moms[1] + big_total[1]
        small_total = sum_everywhere(jnp.stack(small_totals))
        other = swap(bfloat(small_total), "win", 0)
        pairs = jnp.stack(pick_owner(low_core, bfloat(small_total), other), axis=1)
        pairs = pairs.reshape(4, -1, 2 * shard_rows, model_width)
        region_pairs = jnp.pad(region_weight_grad, ((0, 1), (0, 0), (0, 0)))
        vec_sum = region_sums
        for bit in range(bit_count("rep")):
            region_pairs = same_sum(region_pairs, "rep", bit)
            vec_sum = same_sum(vec_sum, "rep", bit)
        rows = wide(pick(pairs, win_index >> 1, 1)) + region_pairs
        rows = rows.reshape(4, 2, shard_rows, model_width)
        small_moms = small_old_moms + pick(rows, win_index & 1, 1)
        up_update, down_update, updates = every_update(
            place, (folded_up_mom, new_down_mom), small_moms, folds
        )
        finish_place = jnp.stack([0 * win_index, win_index, 0 * win_index]).astype(jnp.int32)
        big_parts = [up_update, down_update, folded_up_mom, new_down_mom]
        small_parts = [*updates, *small_moms]
    new_up, new_down, new_up_mom, new_down_mom = finish_big(
        finish_place, big_parts, up_weight, down_weight
    )
    new_qkv, new_out, new_qkv_mom, new_out_mom = finish_small(
        finish_place, small_parts, qkv_weight, out_weight
    )
    vec_total = lax.dynamic_slice_in_dim(vec_sum.reshape(-1), win_index * vec_rows, vec_rows)
    new_vec_mom = MOMENTUM_DECAY * vec_mom + vec_total
    new_vectors = (
        lax.dynamic_slice_in_dim(vectors.reshape(-1), win_index * vec_rows, vec_rows)
        - VECTOR_RATE * new_vec_mom
    )

    return (
        out_tokens,
        input_grad,
        new_qkv_mom,
        new_qkv,
        new_out_mom,
        new_out,
        new_up_mom,
        new_up,
        new_down_mom,
        new_down,
        new_vec_mom,
        new_vectors,
    )


def solution(mesh):
    placed = (
        P("rep", "win", None, None),
        P("rep", "win", None),
        P("rep", "win", None),
        P("rep", None),
        P(),
        P(),
        P(),
        P(),
        P(),
        P(None, "win", None),
        P("win", None),
        P("win", None),
        P("win", None),
        P("win"),
        P("rep", "win", None, None),
    )
    return jax.shard_map(
        local,
        mesh=mesh,
        in_specs=placed,
        out_specs=(
            P("rep", "win", None, None),
            P("rep", "win", None, None),
            P(None, "win", None),
            P(None, "win", None),
            P("win", None),
            P("win", None),
            P("win", None),
            P("win", None),
            P("win", None),
            P("win", None),
            P("win"),
            P("win"),
        ),
        check_vma=False,
    )
```

```python
import functools

import jax
import jax.numpy as jnp
from jax import lax
from jax.experimental import pallas as pl
from jax.experimental.pallas import tpu as pltpu
from jax.sharding import PartitionSpec as P

HEADS = 16
HEAD_DIM = 32


EPSILON = 1e-06
MOMENTUM_DECAY = 0.95
MATRIX_RATE = 0.5
VECTOR_RATE = 0.0002
KEEP_SHARE = 0.75
NEWTON_COEFFS = (3.4445, -4.775, 2.0315)


def bfloat(values):
    return values.astype(jnp.bfloat16)


def product(left_side, right_side):
    return jnp.dot(left_side, right_side, preferred_element_type=jnp.float32)


def norm_rows(values, gain_row, shift_row):
    center = values - jnp.mean(values, -1, keepdims=True)
    spread = jnp.mean(center * center, -1, keepdims=True)
    return center * lax.rsqrt(spread + EPSILON) * gain_row + shift_row


def bit_count(axis):
    return lax.axis_size(axis).bit_length() - 1


def swap(values, axis, bit):
    size = lax.axis_size(axis)
    return lax.ppermute(values, axis, [(i, i ^ (1 << bit)) for i in range(size)])


def my_bit(axis, bit):
    return (lax.axis_index(axis) >> bit) & 1


def far_bits():
    return list(range(2, bit_count("win")))


def gather_masks(low=0):
    masks = [0]
    for bit in far_bits() + [1, 0]:
        if bit >= low:
            masks += [mask | (1 << bit) for mask in masks]
    return masks


def gather_far(values):
    size = lax.axis_size("win")
    values = values[None]
    if len(far_bits()) == 2:
        others = [
            lax.ppermute(values, "win", [(i, i ^ mask) for i in range(size)]) for mask in (4, 8, 12)
        ]
        return [jnp.concatenate([values] + others)]
    for bit in far_bits():
        values = jnp.concatenate([values, swap(values, "win", bit)])
    return [values]


def gather_bit(pieces, bit):
    return pieces + [swap(piece, "win", bit) for piece in pieces]


def gather_stages(low=0):
    stages = [gather_far]
    for bit in (1, 0):
        if bit >= low:
            stages.append(functools.partial(gather_bit, bit=bit))
    return stages


def gather_blocks(values, low=0):
    for stage in gather_stages(low):
        values = stage(values)
    return values


def index_order(pieces):
    masks = gather_masks()
    by_mask = sorted(range(len(masks)), key=masks.__getitem__)
    places = lax.axis_index("win") ^ jnp.arange(len(masks))
    return [jnp.concatenate(pieces)[jnp.array(by_mask)][places]]


def tie(*values):
    return lax.optimization_barrier(values)


def after(value, *others):
    return lax.optimization_barrier((value,) + others)[0]


class Order:
    def __init__(self):
        self.sent = ()

    def launch(self, *hops):
        self.sent = tuple(array for array, _, _ in hops)
        return [
            lax.ppermute(array, axis, [(i, i ^ mask) for i in range(lax.axis_size(axis))])
            for array, axis, mask in hops
        ]

    def land(self, values):
        return after(values, *self.sent)


def pick(values, index, axis=0):
    return lax.dynamic_index_in_dim(values, index, axis, keepdims=False)


def wide(values):
    return values.astype(jnp.float32)


def rounded(values):
    return lax.reduce_precision(values, 8, 7)


def same_sum(values, axis, bit):
    low = rounded(values)
    return low + wide(swap(bfloat(low), axis, bit))


def place_bits():
    win_index = lax.axis_index("win")
    return lax.axis_index("rep"), win_index >> 2, (win_index >> 1) & 1, win_index & 1


def first_parts(total):
    rep, _, side, _ = place_bits()
    half = total.shape[-1] // 2
    left, right = total[..., :half], total[..., half:]
    right = right.reshape(2, -1, 2, right.shape[2], half)
    kept = pick(left, rep), pick(right, side, 2)
    sent = bfloat(pick(left, 1 - rep)), bfloat(pick(right, 1 - side, 2))
    return kept, ((sent[0], "rep", 1), (sent[1], "win", 2))


def first_parts_of_two(totals):
    rep, _, side, _ = place_bits()
    half = totals[0].shape[-1] // 2
    left = [total[..., :half] for total in totals]
    right = [total[..., half:].reshape(-1, 2, total.shape[1], half) for total in totals]
    own, other = pick_owner(rep == 0, *left)
    kept = own, jnp.stack([pick(part, side, 1) for part in right])
    sent = bfloat(other), bfloat(jnp.stack([pick(part, 1 - side, 1) for part in right]))
    return kept, ((sent[0], "rep", 1), (sent[1], "win", 2))


def second_parts(left, right):
    rep, _, side, _ = place_bits()
    left = left.reshape(-1, 2, *left.shape[1:])
    kept = pick(left, side, 1), pick(right, rep)
    sent = bfloat(pick(left, 1 - side, 1)), bfloat(pick(right, 1 - rep))
    return kept, ((sent[0], "win", 2), (sent[1], "rep", 1))


def far_parts(total):
    far = place_bits()[1]
    hops = tuple((bfloat(pick(total, far ^ mask)), "win", mask << 2) for mask in (1, 2, 3))
    return pick(total, far), hops


def add_pair(kept, taken):
    return kept[0] + wide(taken[0]), kept[1] + wide(taken[1])


def add_far(kept, taken):
    return (kept + wide(taken[0])) + (wide(taken[1]) + wide(taken[2]))


def join_halves(pair):
    return jnp.concatenate(pair, axis=-1)


def spread_far(values):
    return tuple((values[None], "win", mask) for mask in (4, 8, 12))


def far_piece(values, taken):
    return jnp.concatenate([values[None], *taken])


def sum_everywhere(values, skip_core=True):
    for bit in range(1 if skip_core else 0, bit_count("win")):
        values = same_sum(values, "win", bit)
    for bit in range(bit_count("rep")):
        values = same_sum(values, "rep", bit)
    return values


def off_diagonal_step(iterate, exact):
    high = bfloat(iterate)
    gram = dot_as(high, high, NT)
    if exact:
        rest = bfloat(iterate - high.astype(jnp.float32))
        gram = gram + dot_as(high, rest, NT) + dot_as(rest, high, NT)
    size = gram.shape[0]
    row_ids = lax.broadcasted_iota(jnp.int32, (size, size), 0)
    on_diagonal = row_ids == lax.broadcasted_iota(jnp.int32, (size, size), 1)
    own = jnp.where(on_diagonal, gram, 0.0)
    own_column = jnp.sum(own, 1, keepdims=True)
    own_row = jnp.sum(own, 0, keepdims=True)
    off = jnp.where(on_diagonal, 0.0, gram)
    off_low = bfloat(off)
    square = product(off_low, off_low) + (own_column + own_row) * off
    poly = NEWTON_COEFFS[1] * off + NEWTON_COEFFS[2] * square
    poly_own = jnp.sum(jnp.where(on_diagonal, poly, 0.0), 1, keepdims=True)
    factor = (
        NEWTON_COEFFS[0]
        + poly_own
        + own_column * (NEWTON_COEFFS[1] + NEWTON_COEFFS[2] * own_column)
    )
    poly = jnp.where(on_diagonal, 0.0, poly)
    poly_high = bfloat(poly)
    moved = product(poly_high, high)
    return factor * iterate + moved


def unit_scale(values):
    total = jnp.sum(jnp.sum(values * values, 1, keepdims=True), 0, keepdims=True)
    return values * (1.0 / (jnp.sqrt(total) + EPSILON))


def block_start(place_ref, masks, block, rows, shift=0):
    if masks is None:
        return block * rows
    return pl.multiple_of(((place_ref[1] ^ masks[block]) >> shift) * rows, rows)


def numbered_blocks(piece_refs):
    for piece, piece_ref in enumerate(piece_refs):
        blocks = piece_ref.shape[0]
        for block in range(blocks):
            yield piece * blocks + block, piece_ref.at[block]


def big_newton_kernel(folds, masks, place_ref, *refs):
    piece_refs, (out_ref, iterate_ref, turned_ref) = refs[:-3], refs[-3:]
    _, rows, width = piece_refs[0].shape
    part = rows // folds

    @pl.when(place_ref[0] == 0)
    def _():
        for block, block_ref in numbered_blocks(piece_refs):
            start = block_start(place_ref, masks, block, part)
            for fold in range(folds):
                lanes = slice(fold * width, (fold + 1) * width)
                inner = slice(fold * part, (fold + 1) * part)
                iterate_ref[pl.ds(start, part), lanes] = block_ref[inner, :].astype(jnp.float32)

    @pl.when(place_ref[0] != 0)
    def _():
        for block, block_ref in numbered_blocks(piece_refs):
            start = block_start(place_ref, masks, block, rows)
            iterate_ref[:, pl.ds(start, rows)] = block_ref[...].astype(jnp.float32).T

    iterate_ref[...] = unit_scale(iterate_ref[...])

    @pl.loop(0, 5)
    def _(_):
        iterate_ref[...] = off_diagonal_step(iterate_ref[...], False)

    @pl.when(place_ref[0] == 0)
    def _():
        start = pl.multiple_of(place_ref[1] * part, part)
        for fold in range(folds):
            out_ref[fold * part : (fold + 1) * part, :] = bfloat(
                iterate_ref[pl.ds(start, part), fold * width : (fold + 1) * width]
            )

    @pl.when(place_ref[0] != 0)
    def _():
        span = max(rows, 128)
        start = pl.multiple_of(place_ref[1] * rows // span * span, span)
        turned_ref[...] = iterate_ref[:, pl.ds(start, span)].T * float(folds) ** 0.5
        inner = pl.multiple_of(place_ref[1] * rows - start, rows)
        out_ref[...] = bfloat(turned_ref[pl.ds(inner, rows), :])


def small_newton_kernel(masks, place_ref, *refs):
    piece_refs, (out_ref, iterate_ref) = refs[:-2], refs[-2:]
    _, matrices, rows, width = piece_refs[0].shape
    for block, block_ref in numbered_blocks(piece_refs):
        start = block_start(place_ref, masks, block, rows, 1)
        for number in range(matrices):
            iterate_ref[number, pl.ds(start, rows), :] = block_ref[number].astype(jnp.float32)

    @pl.loop(0, matrices)
    def _(number):
        iterate_ref[number] = unit_scale(iterate_ref[number])

        @pl.loop(0, 2)
        def _(_):
            iterate_ref[number] = off_diagonal_step(iterate_ref[number], False)

        @pl.loop(0, 3)
        def _(_):
            iterate_ref[number] = off_diagonal_step(iterate_ref[number], True)

    start = pl.multiple_of((place_ref[1] if masks is None else place_ref[1] >> 1) * rows, rows)
    for number in range(matrices):
        out_ref[number] = bfloat(iterate_ref[number, pl.ds(start, rows), :])


def newton_call(kernel, name, place, pieces, out_dims, scratch_dims, cost):
    return pl.pallas_call(
        kernel,
        in_specs=[pl.BlockSpec(memory_space=pltpu.SMEM)]
        + [pl.BlockSpec(memory_space=pltpu.VMEM)] * len(pieces),
        out_specs=pl.BlockSpec(memory_space=pltpu.VMEM),
        out_shape=shape_of(out_dims, jnp.bfloat16),
        scratch_shapes=[pltpu.VMEM(dims, jnp.float32) for dims in scratch_dims],
        compiler_params=pltpu.CompilerParams(vmem_limit_bytes=VMEM_LIMIT),
        cost_estimate=lasting(cost),
        name=name,
    )(place, *pieces)


def big_update(place, pieces, folds, masks):
    blocks, rows, width = pieces[0].shape
    columns = len(pieces) * blocks * rows
    return newton_call(
        functools.partial(big_newton_kernel, folds, masks),
        "big_newton",
        place,
        pieces,
        (rows, width),
        [(width, columns), (max(rows, 128), width)],
        16,
    )


def small_update(place, pieces, masks):
    _, matrices, rows, width = pieces[0].shape
    return newton_call(
        functools.partial(small_newton_kernel, masks),
        "small_newton",
        place,
        pieces,
        (matrices, rows, width),
        [(matrices, width, width)],
        10 * matrices,
    )


def fold_columns(rows, width):
    count, columns = rows.shape
    return rows.reshape(count, columns // width, width).swapaxes(0, 1).reshape(-1, width)


def pick_owner(first, here, there):
    return jnp.where(first, here, there), jnp.where(first, there, here)


def every_update(place, big_rows, small_rows, folds):
    updates = []
    for number, rows in enumerate(big_rows):
        here = jnp.stack([jnp.int32(number), place[1]])
        blocks = index_order(gather_blocks(bfloat(rows)))
        updates.append(big_update(here, blocks, folds, None))
    blocks = index_order(gather_blocks(bfloat(small_rows)))
    return updates[0], updates[1], small_update(place, blocks, None)


GROUP_HEADS = 128 // HEAD_DIM
SCORE_SCALE = HEAD_DIM ** (-0.5)
LOG2_E = 1.4426950408889634
VMEM_LIMIT = 44 * 1024 * 1024
VECTOR_ROWS = 16
NT = (((1,), (1,)), ((), ()))
TN = (((0,), (0,)), ((), ()))


def dot_as(left_side, right_side, dims):
    return lax.dot_general(left_side, right_side, dims, preferred_element_type=jnp.float32)


def spread_heads(part, lane_head):
    return bfloat(
        jnp.concatenate(
            [jnp.where(lane_head == head, part, 0.0) for head in range(GROUP_HEADS)], axis=0
        )
    )


def join_heads(spread, lane_head, rows):
    joined = spread[:rows]
    for head in range(1, GROUP_HEADS):
        joined = jnp.where(lane_head == head, spread[head * rows : (head + 1) * rows], joined)
    return joined


def column_softmax(scores, bias_column):
    scores = scores + bias_column
    raised = jnp.exp2((scores - jnp.max(scores, 0, keepdims=True)) * (SCORE_SCALE * LOG2_E))
    return raised * (1.0 / jnp.sum(raised, 0, keepdims=True))


def load_windows(tokens_ref, region_ref, fill_ref, count, seq_len, padded, step):
    for window in range(count):
        base = window * padded
        fill_ref[base : base + seq_len, :] = tokens_ref[0, window].astype(jnp.float32)
        fill_ref[base : base + 1, :] = region_ref[pl.ds(step * count + window, 1), :]


def window_forward_kernel(
    count,
    seq_len,
    padded,
    tokens_ref,
    region_ref,
    bias_ref,
    keep_ref,
    qkv_ref,
    out_ref,
    vec_ref,
    norm_out,
    proj_out,
    mix_out,
    after_out,
    fill_ref,
    mix_ref,
    scores_ref,
    probs_ref,
):
    step = pl.program_id(0)
    width = tokens_ref.shape[-1]

    @pl.when(step == 0)
    def _():
        fill_ref[...] = jnp.zeros_like(fill_ref)

    load_windows(tokens_ref, region_ref, fill_ref, count, seq_len, padded, step)
    flat = fill_ref[...]
    normed = bfloat(norm_rows(flat, vec_ref[2:3, :], vec_ref[3:4, :]))
    lane_head = lax.broadcasted_iota(jnp.int32, (padded, 128), 1) // HEAD_DIM
    query = product(normed, qkv_ref[0]) + vec_ref[6:7, :]
    keyset = product(normed, qkv_ref[1])
    values = product(normed, qkv_ref[2]) + vec_ref[7:8, :]
    pairs = [(window, group) for window in range(count) for group in range(width // 128)]
    for window in range(count):
        rows = slice(window * padded, (window + 1) * padded)
        norm_out[window] = normed[rows]
        proj_out[window, :, :width] = bfloat(query[rows])
        proj_out[window, :, width : 2 * width] = bfloat(keyset[rows])
        proj_out[window, :, 2 * width :] = bfloat(values[rows])
    for number, (window, group) in enumerate(pairs):
        rows = slice(window * padded, (window + 1) * padded)
        lanes = slice(group * 128, (group + 1) * 128)
        spread = spread_heads(query[rows, lanes], lane_head)
        scores_ref[number] = dot_as(bfloat(keyset[rows, lanes]), spread, NT)
    for number, (window, group) in enumerate(pairs):
        probs_ref[number] = bfloat(column_softmax(scores_ref[number], bias_ref[window]))
    for number, (window, group) in enumerate(pairs):
        rows = slice(window * padded, (window + 1) * padded)
        lanes = slice(group * 128, (group + 1) * 128)
        mixed = dot_as(probs_ref[number], bfloat(values[rows, lanes]), TN)
        mix_ref[rows, lanes] = join_heads(mixed, lane_head, padded)
    mixed_low = bfloat(mix_ref[...])
    branch = product(mixed_low, out_ref[...]) + vec_ref[8:9, :]
    for window in range(count):
        rows = slice(window * padded, (window + 1) * padded)
        mix_out[window] = mixed_low[rows]
        after_out[window] = flat[rows] + keep_ref[window] * branch[rows]


def window_backward_kernel(
    count,
    first_step,
    last,
    seq_len,
    padded,
    tokens_ref,
    region_ref,
    bias_ref,
    keep_ref,
    qkv_ref,
    out_ref,
    vec_ref,
    proj_ref,
    after_grad_ref,
    region_keep_ref,
    sums_before_ref,
    *rest,
):
    scratch_count = 8
    if last:
        region_branch_out, region_mix_out = rest[-scratch_count - 2 : -scratch_count]
        rest = rest[: -scratch_count - 2] + rest[-scratch_count:]
    (
        region_grad_out,
        sums_out,
        grad_out,
        proj_grad_out,
        branch_grad_out,
        fill_ref,
        proj_grad_ref,
        spread_ref,
        spread_grad_ref,
        scores_ref,
        probs_grad_ref,
        probs_ref,
        score_grad_ref,
    ) = rest[-13:]
    step = pl.program_id(0) + first_step
    width = tokens_ref.shape[-1]

    @pl.when(pl.program_id(0) == 0)
    def _():
        fill_ref[...] = jnp.zeros_like(fill_ref)
        sums_out[...] = sums_before_ref[...]
        if first_step == 0:
            region_grad_out[...] = jnp.zeros_like(region_grad_out)
        else:
            region_grad_out[...] = rest[0][...]

    load_windows(tokens_ref, region_ref, fill_ref, count, seq_len, padded, step)
    lane_head = lax.broadcasted_iota(jnp.int32, (padded, 128), 1) // HEAD_DIM
    branch_grad = bfloat(
        jnp.concatenate(
            [keep_ref[window] * after_grad_ref[window] for window in range(count)], axis=0
        )
    )
    mix_grad = dot_as(branch_grad, out_ref[...], NT)
    for window in range(count):
        branch_grad_out[window] = branch_grad[window * padded : (window + 1) * padded]
    pairs = [(window, group) for window in range(count) for group in range(width // 128)]

    def lanes_of(part, group):
        return slice(part * width + group * 128, part * width + (group + 1) * 128)

    for number, (window, group) in enumerate(pairs):
        query = proj_ref[window, :, lanes_of(0, group)].astype(jnp.float32)
        spread_ref[number] = spread_heads(query, lane_head)
        rows = slice(window * padded, (window + 1) * padded)
        spread_grad_ref[number] = spread_heads(mix_grad[rows, lanes_of(0, group)], lane_head)
    for number, (window, group) in enumerate(pairs):
        scores_ref[number] = dot_as(
            proj_ref[window, :, lanes_of(1, group)], spread_ref[number], NT
        )
        probs_grad_ref[number] = dot_as(
            proj_ref[window, :, lanes_of(2, group)], spread_grad_ref[number], NT
        )
    for number, (window, group) in enumerate(pairs):
        probs = column_softmax(scores_ref[number], bias_ref[window])
        weighted = probs * probs_grad_ref[number]
        probs_ref[number] = bfloat(probs)
        score_grad_ref[number] = bfloat(weighted - probs * jnp.sum(weighted, 0, keepdims=True))
    for number, (window, group) in enumerate(pairs):
        rows = slice(window * padded, (window + 1) * padded)
        proj_grad_ref[rows, lanes_of(2, group)] = product(
            probs_ref[number], spread_grad_ref[number]
        )
        proj_grad_ref[rows, lanes_of(1, group)] = (
            product(score_grad_ref[number], spread_ref[number]) * SCORE_SCALE
        )
    for number, (window, group) in enumerate(pairs):
        rows = slice(window * padded, (window + 1) * padded)
        query_grad = dot_as(score_grad_ref[number], proj_ref[window, :, lanes_of(1, group)], TN)
        proj_grad_ref[rows, lanes_of(0, group)] = (
            join_heads(query_grad, lane_head, padded) * SCORE_SCALE
        )
    proj_grad = bfloat(proj_grad_ref[...])
    norm_grad = sum(
        dot_as(proj_grad[:, number * width : (number + 1) * width], qkv_ref[number], NT)
        for number in range(3)
    )
    flat = fill_ref[...]
    center = flat - jnp.mean(flat, -1, keepdims=True)
    scale = lax.rsqrt(jnp.mean(center * center, -1, keepdims=True) + EPSILON)
    hat = center * scale
    hat_grad = norm_grad * vec_ref[2:3, :]
    flat_grad = scale * (
        hat_grad
        - jnp.mean(hat_grad, -1, keepdims=True)
        - hat * jnp.mean(hat_grad * hat, -1, keepdims=True)
    )
    proj_sums = jnp.sum(proj_grad.astype(jnp.float32), 0, keepdims=True)
    sums_out[2:3, :] += jnp.sum(norm_grad * hat, 0, keepdims=True)
    sums_out[3:4, :] += jnp.sum(norm_grad, 0, keepdims=True)
    sums_out[6:7, :] += proj_sums[:, :width]
    sums_out[7:8, :] += proj_sums[:, 2 * width :]
    sums_out[8:9, :] += jnp.sum(branch_grad.astype(jnp.float32), 0, keepdims=True)
    for window in range(count):
        rows = slice(window * padded, (window + 1) * padded)
        proj_grad_out[window] = proj_grad[rows]
        seq_grad = after_grad_ref[window] + flat_grad[rows]
        for group in range(width // 128):
            lanes = slice(group * 128, (group + 1) * 128)
            grad_out[window, pl.ds(group, seq_len, stride=width // 128), :] = seq_grad[
                :seq_len, lanes
            ]
        region_grad_out[pl.ds(step * count + window, 1), :] = seq_grad[0:1]

    if last:

        @pl.when(pl.program_id(0) == pl.num_programs(0) - 1)
        def _():
            region_branch = bfloat(region_keep_ref[...] * region_grad_out[...])
            sums_out[8:9, :] += jnp.sum(region_branch.astype(jnp.float32), 0, keepdims=True)
            region_branch_out[...] = region_branch
            regions = region_branch.shape[0]
            spare_rows = region_mix_out.shape[0] - regions - sums_out.shape[0]
            region_mix_out[:regions, :] = bfloat(dot_as(region_branch, out_ref[...], NT))
            sums_low = jnp.concatenate(
                [sums_out[...], jnp.zeros((spare_rows, width), jnp.float32)], axis=0
            )
            region_mix_out[regions:, :] = bfloat(sums_low)


def window_step(windows, most=4):
    return next(count for count in (10, 5, 4, 2, 1) if count <= most and windows % count == 0)


def whole_spec(shape):
    return pl.BlockSpec(shape, lambda step: (0,) * len(shape))


def step_spec(count, *rest):
    return pl.BlockSpec((count,) + rest, lambda step: (step,) + (0,) * len(rest))


def token_spec(count, *rest):
    return pl.BlockSpec((1, count) + rest, lambda step: (0, step) + (0,) * len(rest))


def kept_spec():
    return pl.BlockSpec(memory_space=pltpu.VMEM)


def lasting(microseconds):
    return pl.CostEstimate(flops=microseconds * 10**9, bytes_accessed=10**6, transcendentals=0)


def in_hbm(values):
    return pltpu.with_memory_space_constraint(values, pltpu.HBM)


def hbm_shape(dims, kind=jnp.float32):
    return pltpu.HBM(dims, kind)


def shape_of(dims, kind=jnp.float32):
    return jax.ShapeDtypeStruct(dims, kind)


def window_forward(tokens, region, bias, keep, qkv_weight, out_weight, vectors, padded):
    _, windows, seq_len, width = tokens.shape
    count = window_step(windows, 10)
    pairs = count * width // 128
    return pl.pallas_call(
        functools.partial(window_forward_kernel, count, seq_len, padded),
        grid=(windows // count,),
        in_specs=[
            token_spec(count, seq_len, width),
            whole_spec(region.shape),
            step_spec(count, padded, 1),
            step_spec(count, 1, 1),
            kept_spec(),
            kept_spec(),
            whole_spec(vectors.shape),
        ],
        out_specs=[
            step_spec(count, padded, width),
            step_spec(count, padded, 3 * width),
            step_spec(count, padded, width),
            step_spec(count, padded, width),
        ],
        out_shape=[
            hbm_shape((windows, padded, width), jnp.bfloat16),
            hbm_shape((windows, padded, 3 * width), jnp.bfloat16),
            hbm_shape((windows, padded, width), jnp.bfloat16),
            hbm_shape((windows, padded, width)),
        ],
        scratch_shapes=[
            pltpu.VMEM((count * padded, width), jnp.float32),
            pltpu.VMEM((count * padded, width), jnp.float32),
            pltpu.VMEM((pairs, padded, GROUP_HEADS * padded), jnp.float32),
            pltpu.VMEM((pairs, padded, GROUP_HEADS * padded), jnp.bfloat16),
        ],
        compiler_params=pltpu.CompilerParams(vmem_limit_bytes=VMEM_LIMIT),
        name="window_forward",
    )(in_hbm(tokens), region, bias, keep, qkv_weight, out_weight, vectors)


def window_backward(
    tokens,
    region,
    bias,
    keep,
    qkv_weight,
    out_weight,
    vectors,
    proj,
    after_grad,
    region_keep,
    before,
    steps,
    padded,
):
    _, windows, seq_len, width = tokens.shape
    count = window_step(windows, 10)
    first_step, last_step = steps
    here = (last_step - first_step) * count
    pairs = count * width // 128
    spread_rows = GROUP_HEADS * padded

    def moved(*dims, lead=0):
        zeros = (0,) * (len(dims) - 1)
        if lead:
            return pl.BlockSpec((1,) + dims, lambda step: (0, step + first_step) + zeros)
        return pl.BlockSpec(dims, lambda step: (step + first_step,) + zeros)

    flat_rows = seq_len * width // 128

    grad_before, sums_before, region_before = before
    operands = [in_hbm(tokens), region, bias, keep, qkv_weight, out_weight, vectors]
    operands += [in_hbm(proj), in_hbm(after_grad), region_keep, in_hbm(sums_before)]
    in_specs = [
        moved(count, seq_len, width, lead=1),
        whole_spec(region.shape),
        moved(count, padded, 1),
        moved(count, 1, 1),
        kept_spec(),
        kept_spec(),
        whole_spec(vectors.shape),
        moved(count, padded, 3 * width),
        moved(count, padded, width),
        whole_spec(region_keep.shape),
        whole_spec(sums_before.shape),
    ]
    aliases = {}
    if first_step:
        aliases = {len(operands) + 1: 2}
        operands += [in_hbm(region_before), in_hbm(grad_before)]
        in_specs += [whole_spec(region.shape), pl.BlockSpec(memory_space=pl.ANY)]
    last = last_step * count == windows
    out_specs = [
        whole_spec(region.shape),
        whole_spec(vectors.shape),
        moved(count, flat_rows, 128),
        step_spec(count, padded, 3 * width),
        step_spec(count, padded, width),
    ]
    out_shape = [
        hbm_shape(region.shape),
        hbm_shape(vectors.shape),
        hbm_shape((windows, flat_rows, 128)),
        hbm_shape((here, padded, 3 * width), jnp.bfloat16),
        hbm_shape((here, padded, width), jnp.bfloat16),
    ]
    if last:
        payload = (region.shape[0] + VECTOR_ROWS, width)
        out_specs += [whole_spec(region.shape), whole_spec(payload)]
        out_shape += [shape_of(region.shape, jnp.bfloat16), shape_of(payload, jnp.bfloat16)]
    return pl.pallas_call(
        functools.partial(window_backward_kernel, count, first_step, last, seq_len, padded),
        grid=(last_step - first_step,),
        in_specs=in_specs,
        out_specs=out_specs,
        out_shape=out_shape,
        scratch_shapes=[
            pltpu.VMEM((count * padded, width), jnp.float32),
            pltpu.VMEM((count * padded, 3 * width), jnp.float32),
            pltpu.VMEM((pairs, spread_rows, 128), jnp.bfloat16),
            pltpu.VMEM((pairs, spread_rows, 128), jnp.bfloat16),
            pltpu.VMEM((pairs, padded, spread_rows), jnp.float32),
            pltpu.VMEM((pairs, padded, spread_rows), jnp.float32),
            pltpu.VMEM((pairs, padded, spread_rows), jnp.bfloat16),
            pltpu.VMEM((pairs, padded, spread_rows), jnp.bfloat16),
        ],
        input_output_aliases=aliases,
        compiler_params=pltpu.CompilerParams(vmem_limit_bytes=VMEM_LIMIT),
        cost_estimate=lasting(here),
        name="window_backward",
    )(*operands)


def insert_kernel(rows_ref, region_ref, out_ref):
    out_ref[...] = rows_ref[...]
    for window in range(rows_ref.shape[0]):
        for group in range(region_ref.shape[1] // 128):
            out_ref[window, group : group + 1, :] = region_ref[
                window : window + 1, group * 128 : (group + 1) * 128
            ]


def insert_regions(grad, region_grad):
    rows = pl.BlockSpec((grad.shape[0], 8, 128), lambda step: (0, 0, 0))
    return pl.pallas_call(
        insert_kernel,
        grid=(1,),
        in_specs=[rows, whole_spec(region_grad.shape)],
        out_specs=rows,
        out_shape=shape_of(grad.shape),
        input_output_aliases={0: 0},
        compiler_params=pltpu.CompilerParams(vmem_limit_bytes=VMEM_LIMIT),
        name="insert_regions",
    )(grad, region_grad)


GELU_IN = 0.7978845608028654
GELU_CUBE = 0.044715


def gelu_both(values):
    square = values * values
    bent = jnp.tanh(values * (GELU_IN + (GELU_IN * GELU_CUBE) * square))
    share = 0.5 + 0.5 * bent
    slope = share + (0.5 * values) * (1.0 - bent * bent) * (
        GELU_IN + (3.0 * GELU_IN * GELU_CUBE) * square
    )
    return values * share, slope


def split_cores(values, core):
    own_first = core == 0
    kept = jnp.where(own_first, values[:, 0], values[:, 1])
    sent = jnp.where(own_first, values[:, 1], values[:, 0])
    return kept, bfloat(sent)


def mlp_kernel(
    place_ref,
    after_ref,
    cot_ref,
    keep_ref,
    vec_ref,
    up_ref,
    down_ref,
    sums_ref,
    out_hbm,
    grad_hbm,
    kept_hbm,
    sent_hbm,
    cot_fill,
    act_ref,
    hidden_grad_ref,
    out_ref,
    grad_ref,
    kept_ref,
    sent_ref,
    sems,
):
    _, windows, seq_len, width = cot_ref.shape
    padded = after_ref.shape[0] // windows
    folds = up_ref.shape[1] // width
    core = place_ref[1] % 2
    copies = []

    def write_out(source, target):
        copy = pltpu.make_async_copy(source, target, sems.at[len(copies)])
        copy.start()
        copies.append(copy)

    cot_fill[...] = jnp.zeros_like(cot_fill)
    keeps = []
    for window in range(windows):
        base = window * padded
        cot_fill[base : base + seq_len, :] = cot_ref[0, window].astype(jnp.float32)
        keeps.append(jnp.broadcast_to(keep_ref[window], (padded, 1)))
    keep = jnp.concatenate(keeps, axis=0)
    flat = after_ref[...]
    center = flat - jnp.mean(flat, -1, keepdims=True)
    scale = lax.rsqrt(jnp.mean(center * center, -1, keepdims=True) + EPSILON)
    hat = center * scale
    normed = bfloat(hat * vec_ref[4:5, :] + vec_ref[5:6, :])
    normed_turned = normed.T
    cot = cot_fill[...]
    branch_grad = bfloat(keep * cot)
    branch = jnp.zeros_like(flat)
    norm_grad = jnp.zeros_like(flat)
    for fold in range(folds):
        lanes = slice(fold * width, (fold + 1) * width)
        up_part, down_part = up_ref[:, lanes], down_ref[lanes, :]
        hidden = product(normed, up_part) + vec_ref[10 + fold : 11 + fold, :]
        act, slope = gelu_both(hidden)
        act = bfloat(act)
        act_ref[:, lanes] = act
        branch += product(act, down_part)
        hidden_grad = bfloat(slope * dot_as(branch_grad, down_part, NT))
        hidden_grad_ref[:, lanes] = hidden_grad
        norm_grad += dot_as(hidden_grad, up_part, NT)
        sums_ref[10 + fold : 11 + fold, :] = jnp.sum(
            hidden_grad.astype(jnp.float32), 0, keepdims=True
        )
    output = bfloat(flat + keep * (branch + vec_ref[9:10, :]))
    for window in range(windows):
        out_ref[window] = output[window * padded : window * padded + seq_len]
    write_out(out_ref, out_hbm.at[0])
    hat_grad = norm_grad * vec_ref[4:5, :]
    grad_ref[...] = cot + scale * (
        hat_grad
        - jnp.mean(hat_grad, -1, keepdims=True)
        - hat * jnp.mean(hat_grad * hat, -1, keepdims=True)
    )
    write_out(grad_ref, grad_hbm)
    sums_ref[0:4, :] = jnp.zeros((4, width), jnp.float32)
    sums_ref[4:5, :] = jnp.sum(norm_grad * hat, 0, keepdims=True)
    sums_ref[5:6, :] = jnp.sum(norm_grad, 0, keepdims=True)
    sums_ref[6:9, :] = jnp.zeros((3, width), jnp.float32)
    sums_ref[9:10, :] = jnp.sum(branch_grad.astype(jnp.float32), 0, keepdims=True)
    _, blocks, rows, _ = kept_ref.shape
    part, here = rows // folds, blocks // folds
    for fold in range(folds):
        lanes = slice(fold * width, (fold + 1) * width)
        total = product(normed_turned, hidden_grad_ref[:, lanes])
        inner = pl.ds(fold * part, part)
        kept, sent = split_cores(total.reshape(blocks, 2, part, width), core)
        kept_ref[0, :, inner], sent_ref[0, :, inner] = kept, sent
        write_out(kept_ref.at[0, :, inner], kept_hbm.at[0, :, inner])
        write_out(sent_ref.at[0, :, inner], sent_hbm.at[0, :, inner])
    for fold in range(folds):
        lanes = slice(fold * width, (fold + 1) * width)
        total = dot_as(act_ref[:, lanes], branch_grad, TN)
        inner = pl.ds(fold * here, here)
        kept, sent = split_cores(total.reshape(here, 2, rows, width), core)
        kept_ref[1, inner], sent_ref[1, inner] = kept, sent
        write_out(kept_ref.at[1, inner], kept_hbm.at[1, inner])
        write_out(sent_ref.at[1, inner], sent_hbm.at[1, inner])
    for copy in copies:
        copy.wait()


def mlp(place, after, cotangent, keep, vectors, up_weight, down_weight, padded, win_count):
    _, windows, seq_len, width = cotangent.shape
    rows = after.shape[0]
    folds = up_weight.shape[1] // width
    dims = (2, win_count // 2, width // win_count * folds, width)
    anywhere = pl.BlockSpec(memory_space=pl.ANY)
    sums, output, grad, kept, sent = pl.pallas_call(
        mlp_kernel,
        grid=(1,),
        in_specs=[
            pl.BlockSpec(memory_space=pltpu.SMEM),
            whole_spec(after.shape),
            whole_spec(cotangent.shape),
            whole_spec(keep.shape),
            whole_spec(vectors.shape),
            kept_spec(),
            kept_spec(),
        ],
        out_specs=[whole_spec(vectors.shape)] + [anywhere] * 4,
        out_shape=[
            hbm_shape(vectors.shape),
            hbm_shape(cotangent.shape, jnp.bfloat16),
            hbm_shape(after.shape),
            hbm_shape(dims),
            hbm_shape(dims, jnp.bfloat16),
        ],
        scratch_shapes=[
            pltpu.VMEM((rows, width), jnp.float32),
            pltpu.VMEM((rows, folds * width), jnp.bfloat16),
            pltpu.VMEM((rows, folds * width), jnp.bfloat16),
            pltpu.VMEM((windows, seq_len, width), jnp.bfloat16),
            pltpu.VMEM((rows, width), jnp.float32),
            pltpu.VMEM(dims, jnp.float32),
            pltpu.VMEM(dims, jnp.bfloat16),
            pltpu.SemaphoreType.DMA((2 + 4 * folds,)),
        ],
        compiler_params=pltpu.CompilerParams(vmem_limit_bytes=VMEM_LIMIT),
        cost_estimate=lasting(25),
        name="mlp",
    )(place, in_hbm(after), in_hbm(cotangent), keep, vectors, up_weight, down_weight)
    return output, grad, sums, (kept, sent)


def image_bias(keys_ref, queries_ref):
    return jnp.where(keys_ref[...] == queries_ref[...], 0.0, -1e30)


def region_forward_kernel(
    pieces,
    *refs,
):
    piece_refs, refs = refs[:pieces], refs[pieces:]
    region_forward_rows(piece_refs, *refs)


def region_forward_rows(
    piece_refs,
    own_ref,
    keep_ref,
    key_image_ref,
    query_image_ref,
    qkv_ref,
    out_ref,
    vec_ref,
    norm_out,
    proj_out,
    mix_out,
    new_out,
    all_ref,
):
    rows, width = own_ref.shape
    vec = vec_ref[...]
    for block, block_ref in numbered_blocks(piece_refs):
        all_ref[block * rows : (block + 1) * rows, :] = block_ref[...].astype(jnp.float32)
    normed = bfloat(norm_rows(all_ref[...], vec[0:1], vec[1:2]))
    norm_out[...] = normed
    query = bfloat(product(normed, qkv_ref[0]) + vec[6:7])
    keyset = bfloat(product(normed, qkv_ref[1]))
    values = bfloat(product(normed, qkv_ref[2]) + vec[7:8])
    proj_out[:, :width] = query
    proj_out[:, width : 2 * width] = keyset
    proj_out[:, 2 * width :] = values
    region = own_ref[...].astype(jnp.float32)
    own_norm = bfloat(norm_rows(region, vec[0:1], vec[1:2]))
    own_query = product(own_norm, qkv_ref[0]) + vec[6:7]
    bias = image_bias(key_image_ref, query_image_ref)
    lane_head = lax.broadcasted_iota(jnp.int32, (rows, 128), 1) // HEAD_DIM
    parts = []
    for group in range(width // 128):
        lanes = slice(group * 128, (group + 1) * 128)
        spread = spread_heads(own_query[:, lanes], lane_head)
        probs = column_softmax(dot_as(keyset[:, lanes], spread, NT), bias)
        mixed = dot_as(bfloat(probs), values[:, lanes], TN)
        parts.append(join_heads(mixed, lane_head, rows))
    mixed_low = bfloat(jnp.concatenate(parts, axis=1))
    mix_out[...] = mixed_low
    branch = product(mixed_low, out_ref[...]) + vec[8:9]
    new_out[...] = region + keep_ref[...] * branch


def region_forward(pieces, own, keep, key_images, query_images, qkv_weight, out_weight, vectors):
    rows, width = own.shape
    total = len(pieces) * pieces[0].shape[0] * rows
    return pl.pallas_call(
        functools.partial(region_forward_kernel, len(pieces)),
        out_shape=[
            hbm_shape((total, width), jnp.bfloat16),
            hbm_shape((total, 3 * width), jnp.bfloat16),
            hbm_shape(own.shape, jnp.bfloat16),
            shape_of(own.shape),
        ],
        scratch_shapes=[pltpu.VMEM((total, width), jnp.float32)],
        compiler_params=pltpu.CompilerParams(vmem_limit_bytes=VMEM_LIMIT),
        name="region_forward",
    )(*pieces, own, keep, key_images, query_images, qkv_weight, out_weight, vectors)


def region_backward_kernel(pieces, place_ref, *refs):
    region_refs, refs = refs[:pieces], refs[pieces:]
    gathered_refs, refs = refs[:pieces], refs[pieces:]
    region_backward_rows(place_ref, region_refs, gathered_refs, *refs)


def region_backward_rows(
    place_ref,
    region_refs,
    gathered_refs,
    norm_ref,
    proj_ref,
    key_image_ref,
    query_image_ref,
    new_grad_ref,
    qkv_ref,
    vec_ref,
    grad_out,
    weight_out,
    sums_out,
    bias_ref,
    proj_grad_ref,
    region_grad_ref,
    weight_ref,
    mix_grad_ref,
    all_ref,
    scores_ref,
    probs_grad_ref,
    probs_ref,
    score_grad_ref,
):
    total, width = all_ref.shape
    rows = new_grad_ref.shape[0]
    bias_ref[...] = image_bias(key_image_ref, query_image_ref)
    lane_head = lax.broadcasted_iota(jnp.int32, (total, 128), 1) // HEAD_DIM
    for block, block_ref in numbered_blocks(region_refs):
        all_ref[block * rows : (block + 1) * rows, :] = block_ref[...].astype(jnp.float32)
    vector_sum = jnp.zeros((VECTOR_ROWS, width), jnp.float32)
    for block, block_ref in numbered_blocks(gathered_refs):
        part = block_ref[...].astype(jnp.float32)
        mix_grad_ref[block * rows : (block + 1) * rows, :] = part[:rows]
        vector_sum += part[rows:]

    @pl.loop(0, width // 128)
    def _(group):
        query_lanes = pl.ds(pl.multiple_of(group * 128, 128), 128)
        key_lanes = pl.ds(pl.multiple_of(width + group * 128, 128), 128)
        value_lanes = pl.ds(pl.multiple_of(2 * width + group * 128, 128), 128)
        key_low = proj_ref[:, key_lanes]
        value_low = proj_ref[:, value_lanes]
        spread = spread_heads(proj_ref[:, query_lanes].astype(jnp.float32), lane_head)
        spread_grad = spread_heads(mix_grad_ref[:, query_lanes], lane_head)
        scores_ref[...] = dot_as(key_low, spread, NT)
        probs_grad_ref[...] = dot_as(value_low, spread_grad, NT)
        for head in range(GROUP_HEADS):
            lanes = slice(head * total, (head + 1) * total)
            probs = column_softmax(scores_ref[:, lanes], bias_ref[...])
            weighted = probs * probs_grad_ref[:, lanes]
            probs_ref[:, lanes] = bfloat(probs)
            score_grad_ref[:, lanes] = bfloat(
                weighted - probs * jnp.sum(weighted, 0, keepdims=True)
            )
        value_grad = product(probs_ref[...], spread_grad)
        key_grad = product(score_grad_ref[...], spread)
        turned = product(key_low.T, score_grad_ref[...])
        query_grad = jnp.concatenate(
            [
                turned[head * HEAD_DIM : (head + 1) * HEAD_DIM, head * total : (head + 1) * total]
                for head in range(GROUP_HEADS)
            ],
            axis=0,
        ).T
        proj_grad_ref[:, query_lanes] = bfloat(query_grad * SCORE_SCALE)
        proj_grad_ref[:, key_lanes] = bfloat(key_grad * SCORE_SCALE)
        proj_grad_ref[:, value_lanes] = bfloat(value_grad)

    proj_grad = proj_grad_ref[...]
    norm_grad = sum(
        dot_as(proj_grad[:, number * width : (number + 1) * width], qkv_ref[number], NT)
        for number in range(3)
    )
    region = all_ref[...]
    center = region - jnp.mean(region, -1, keepdims=True)
    scale = lax.rsqrt(jnp.mean(center * center, -1, keepdims=True) + EPSILON)
    hat = center * scale
    hat_grad = norm_grad * vec_ref[0:1, :]
    region_grad_ref[...] = scale * (
        hat_grad
        - jnp.mean(hat_grad, -1, keepdims=True)
        - hat * jnp.mean(hat_grad * hat, -1, keepdims=True)
    )
    grad_out[...] = new_grad_ref[...] + region_grad_ref[:rows, :]
    bias_sums = jnp.sum(proj_grad.astype(jnp.float32), 0, keepdims=True)
    sums_out[...] = vector_sum
    sums_out[0:1, :] += jnp.sum(norm_grad * hat, 0, keepdims=True)
    sums_out[1:2, :] += jnp.sum(norm_grad, 0, keepdims=True)
    sums_out[6:7, :] += bias_sums[:, :width]
    sums_out[7:8, :] += bias_sums[:, 2 * width :]
    weight_ref[...] = dot_as(norm_ref[...], proj_grad, TN)
    weight_rows = weight_out.shape[1]
    weight_start = pl.multiple_of((place_ref[1] >> 1) * weight_rows, 8)
    for number in range(3):
        weight_out[number] = weight_ref[
            pl.ds(weight_start, weight_rows), number * width : (number + 1) * width
        ]


def region_backward(
    place,
    regions,
    gathered,
    normed,
    proj,
    key_images,
    query_images,
    new_grad,
    qkv_weight,
    vectors,
    weight_rows,
):
    total, width = normed.shape
    vmem = pl.BlockSpec(memory_space=pltpu.VMEM)
    operands = [*regions, *gathered, in_hbm(normed), in_hbm(proj), key_images, query_images]
    operands += [new_grad, qkv_weight, vectors]
    return pl.pallas_call(
        functools.partial(region_backward_kernel, len(regions)),
        grid=(1,),
        in_specs=[pl.BlockSpec(memory_space=pltpu.SMEM)]
        + [whole_spec(operand.shape) for operand in operands[:-2]]
        + [vmem, whole_spec(vectors.shape)],
        out_specs=[vmem] * 3,
        out_shape=[
            shape_of(new_grad.shape),
            shape_of((3, weight_rows, width)),
            shape_of((VECTOR_ROWS, width)),
        ],
        scratch_shapes=[
            pltpu.VMEM((total, total), jnp.float32),
            pltpu.VMEM((total, 3 * width), jnp.bfloat16),
            pltpu.VMEM((total, width), jnp.float32),
            pltpu.VMEM((width, 3 * width), jnp.float32),
            pltpu.VMEM((total, width), jnp.float32),
            pltpu.VMEM((total, width), jnp.float32),
            pltpu.VMEM((total, GROUP_HEADS * total), jnp.float32),
            pltpu.VMEM((total, GROUP_HEADS * total), jnp.float32),
            pltpu.VMEM((total, GROUP_HEADS * total), jnp.bfloat16),
            pltpu.VMEM((total, GROUP_HEADS * total), jnp.bfloat16),
        ],
        compiler_params=pltpu.CompilerParams(vmem_limit_bytes=VMEM_LIMIT),
        cost_estimate=lasting(14),
        name="region_backward",
    )(place, *operands)


def pair_gradient_kernel(first_count, second_count, place_ref, *refs):
    own_first = place_ref[1] % 2 == 0
    kept, sent = refs[-2:]

    def total(pairs):
        lefts, rights = pairs[0::2], pairs[1::2]
        return sum(dot_as(left[...], right[...], TN) for left, right in zip(lefts, rights))

    first = total(refs[: 2 * first_count])
    second = total(refs[2 * first_count : 2 * (first_count + second_count)])
    kept[...] = jnp.where(own_first, first, second)
    sent[...] = bfloat(jnp.where(own_first, second, first))


def pair_gradients(place, first, second, width):
    operands, in_specs = [place], [pl.BlockSpec(memory_space=pltpu.SMEM)]
    for left, row, right, column, rows in first + second:
        operands += [in_hbm(left), in_hbm(right)]
        in_specs.append(pl.BlockSpec((rows, width), lambda step, row=row: (row, 0)))
        in_specs.append(pl.BlockSpec((rows, width), lambda step, column=column: (0, column)))
    return pl.pallas_call(
        functools.partial(pair_gradient_kernel, len(first), len(second)),
        grid=(1,),
        in_specs=in_specs,
        out_specs=[whole_spec((width, width))] * 2,
        out_shape=[hbm_shape((width, width)), hbm_shape((width, width), jnp.bfloat16)],
        compiler_params=pltpu.CompilerParams(vmem_limit_bytes=VMEM_LIMIT),
        cost_estimate=lasting(5),
        name="pair_gradients",
    )(*operands)


def row_pieces(whole, rights, column):
    pairs, start = [], 0
    for right in rights:
        rows = right.shape[0]
        left, row = (whole, start // rows) if start % rows == 0 else (whole[start : start + rows], 0)
        pairs.append((left, row, right, column, rows))
        start += rows
    return pairs


def finish_big_kernel(
    place_ref, mine, other, mom_mine, mom_other, up_ref, down_ref, up_new, down_new, up_mom, down_mom
):
    first = place_ref[0] == 0

    def ordered(here, there):
        return jnp.where(first, here, there), jnp.where(first, there, here)

    updates = ordered(mine[...].astype(jnp.float32), other[...].astype(jnp.float32))
    momenta = ordered(mom_mine[...], mom_other[...])
    down_new[...] = down_ref[...].astype(jnp.float32) - MATRIX_RATE * updates[1]
    down_mom[...] = momenta[1]
    rows, columns = up_ref.shape
    width = down_ref.shape[1]
    for fold in range(columns // width):
        lanes = slice(fold * width, (fold + 1) * width)
        inner = slice(fold * rows, (fold + 1) * rows)
        up_new[:, lanes] = up_ref[:, lanes].astype(jnp.float32) - MATRIX_RATE * updates[0][inner]
        up_mom[:, lanes] = momenta[0][inner]


def finish_small_kernel(place_ref, *refs):
    updates, momenta = refs[:4], refs[4:8]
    qkv_ref, out_ref, qkv_new, out_new, qkv_mom, out_mom = refs[8:]
    first, low = place_ref[0] == 0, place_ref[2] == 0

    def ordered(parts):
        own, side, across, corner = [part[...].astype(jnp.float32) for part in parts]
        here = jnp.where(low, own, side), jnp.where(low, side, own)
        there = jnp.where(low, across, corner), jnp.where(low, corner, across)
        return [jnp.where(first, one, two) for one, two in zip(here + there, there + here)]

    for number, (update, momentum) in enumerate(zip(ordered(updates), ordered(momenta))):
        if number < 3:
            qkv_new[number] = qkv_ref[number].astype(jnp.float32) - MATRIX_RATE * update
            qkv_mom[number] = momentum
        else:
            out_new[...] = out_ref[...].astype(jnp.float32) - MATRIX_RATE * update
            out_mom[...] = momentum


def finish_call(kernel, name, place, parts, weights, blocks, indices):
    dims = [shape_of(block) for block in blocks]
    return pl.pallas_call(
        kernel,
        grid_spec=pltpu.PrefetchScalarGridSpec(
            num_scalar_prefetch=1,
            grid=(1,),
            in_specs=[pl.BlockSpec(part.shape, lambda step, place: (0, 0)) for part in parts]
            + [pl.BlockSpec(block, index) for block, index in zip(blocks, indices)],
            out_specs=[
                pl.BlockSpec(block, lambda step, place, count=len(block): (0,) * count)
                for block in blocks + blocks
            ],
        ),
        out_shape=dims + dims,
        compiler_params=pltpu.CompilerParams(vmem_limit_bytes=VMEM_LIMIT),
        name=name,
    )(place, *parts, *weights)


def finish_big(place, parts, up_weight, down_weight):
    rows, width = parts[0].shape
    up_rows = rows * width // up_weight.shape[1]
    own = lambda step, place: (place[1], 0)
    return finish_call(
        finish_big_kernel,
        "finish_big",
        place,
        parts,
        (up_weight, down_weight),
        [(up_rows, up_weight.shape[1]), (rows, width)],
        [own, own],
    )


def finish_small(place, parts, qkv_weight, out_weight):
    rows, width = parts[0].shape
    return finish_call(
        finish_small_kernel,
        "finish_small",
        place,
        parts,
        (qkv_weight, out_weight),
        [(3, rows, width), (rows, width)],
        [lambda step, place: (0, place[1], 0), lambda step, place: (place[1], 0)],
    )


def local(
    tokens,
    patch_mask,
    keep_mask,
    image_map,
    qkv_weight,
    out_weight,
    up_weight,
    down_weight,
    vectors,
    qkv_mom,
    out_mom,
    up_mom,
    down_mom,
    vec_mom,
    cotangent,
):
    windows = tokens.shape[1]
    seq_len = tokens.shape[2]
    model_width = tokens.shape[3]
    hidden_width = up_weight.shape[1]
    folds = hidden_width // model_width
    shard_rows = out_mom.shape[0]
    ff_rows = down_mom.shape[0]
    vec_rows = vec_mom.shape[0]
    padded = (seq_len + 7) // 8 * 8
    region_rows = (windows + 7) // 8 * 8
    row_count = windows * padded
    win_count = lax.axis_size("win")
    win_index = lax.axis_index("win")
    place = jnp.stack([lax.axis_index("rep"), win_index]).astype(jnp.int32)

    def pad_rows(values, rows, fill=0):
        widths = ((0, rows - values.shape[0]),) + ((0, 0),) * (values.ndim - 1)
        return jnp.pad(values, widths, constant_values=fill)

    region_own = pad_rows(tokens[0, :, 0], region_rows)
    regions = gather_far(region_own)
    up_old, down_old = after((up_mom, down_mom), regions)
    for bit in (1, 0):
        regions = gather_bit(regions, bit)
    keeper = keep_mask[0].astype(jnp.float32) / KEEP_SHARE
    images = image_map[0].reshape(win_count, windows)[win_index ^ jnp.array(gather_masks())]
    images = jnp.pad(images, ((0, 0), (0, region_rows - windows)), constant_values=-1)
    key_images = images.reshape(-1, 1)
    own_images = jnp.tile(images[:1], (1, GROUP_HEADS))
    region_keep = pad_rows(keeper[:, 0:1], region_rows)

    big_moms = (
        MOMENTUM_DECAY * fold_columns(up_old, model_width),
        MOMENTUM_DECAY * down_old,
    )
    small_old_moms = MOMENTUM_DECAY * jnp.concatenate([qkv_mom, out_mom[None]])
    own_pair = jnp.where(lax.axis_index("rep") == 0, small_old_moms[:2], small_old_moms[2:])
    kept, sent = pick_owner(win_index % 2 == 0, own_pair[0], own_pair[1])
    small_pair_mom = jnp.concatenate(
        pick_owner(win_index % 2 == 0, kept, swap(sent, "win", 0))
    )
    regions, big_moms, small_pair_mom = tie(regions, big_moms, small_pair_mom)

    region_norm, region_proj, region_mix, region_new = region_forward(
        regions, region_own, region_keep, key_images, own_images, qkv_weight, out_weight, vectors
    )

    key_valid = jnp.concatenate([jnp.ones((windows, 1), jnp.int32), patch_mask[0]], axis=1) == 1
    key_bias = jnp.where(key_valid, 0.0, -1e30)
    key_bias = jnp.pad(key_bias, ((0, 0), (0, padded - seq_len)), constant_values=-1e30)
    key_bias = key_bias[:, :, None]
    keep_window = keeper[:, 1].reshape(windows, 1, 1)
    seq_norm, seq_proj, local_mix, after_attn = window_forward(
        tokens, region_new, key_bias, keep_window, qkv_weight, out_weight, vectors, padded
    )
    seq_norm = seq_norm.reshape(row_count, model_width)
    local_mix = local_mix.reshape(row_count, model_width)
    after_attn = after_attn.reshape(row_count, model_width)

    out_tokens, attn_res_grad, mlp_sums, big_halves = mlp(
        place,
        after_attn,
        cotangent,
        keeper[:, 2].reshape(windows, 1, 1),
        vectors,
        up_weight,
        down_weight,
        padded,
        win_count,
    )

    steps = windows // window_step(windows, 10)
    cuts = [0, steps // 2, steps]
    after_grad = attn_res_grad.reshape(windows, padded, model_width)
    two_owners = lax.axis_size("rep") == 2 and len(far_bits()) == 2
    order = Order()
    big_taken = order.launch((big_halves[1], "win", 1))
    before = (None, mlp_sums, None)
    proj_grads, branch_grads = [], []
    for piece in range(2):
        region_new_grad, sums, seq_grad, proj_grad, branch_grad, *region_parts = window_backward(
            tokens,
            region_new,
            key_bias,
            keep_window,
            qkv_weight,
            out_weight,
            vectors,
            seq_proj,
            after_grad,
            region_keep,
            before,
            (cuts[piece], cuts[piece + 1]),
            padded,
        )
        before = (seq_grad, sums, region_new_grad)
        proj_grads.append(proj_grad.reshape(-1, 3 * model_width))
        branch_grads.append(branch_grad.reshape(-1, model_width))
        if piece == 0:
            big_taken, after_grad = tie(big_taken, after_grad)
            big_total = big_halves[0] + wide(big_taken[0])
            if two_owners:
                big_kept, hops = first_parts(big_total)
                big_taken = order.launch(*hops)
    region_branch_grad, region_mix_grad = region_parts
    norm_rows_ready, mix_ready = seq_norm, local_mix
    if two_owners:
        region_mix_grad, big_taken = tie(region_mix_grad, big_taken)
        big_kept, hops = second_parts(*add_pair(big_kept, big_taken))
        hops, norm_rows_ready = tie([array for array, _, _ in hops], seq_norm)
        big_taken = order.launch((hops[0], "win", 2), (hops[1], "rep", 1))
        mix_taken = order.launch(*spread_far(region_mix_grad))

    first = lax.axis_index("rep") == 0
    low_core = win_index % 2 == 0
    kept, sent = pair_gradients(
        place,
        row_pieces(norm_rows_ready, proj_grads, 0),
        row_pieces(norm_rows_ready, proj_grads, 1),
        model_width,
    )
    if two_owners:
        kept, sent, mix_taken, big_taken = tie(kept, sent, mix_taken, big_taken)
        mixes = [far_piece(region_mix_grad, mix_taken)]
        big_kept, hops = far_parts(join_halves(add_pair(big_kept, big_taken)))
        hops, mixes, mix_ready = tie([array for array, _, _ in hops], mixes, local_mix)
        big_taken = order.launch(*[(hop, "win", 4 * (i + 1)) for i, hop in enumerate(hops)])
        mix_taken = order.launch((mixes[0], "win", 2))
    small_kept = [kept]
    small_taken = order.launch((sent, "win", 1))
    kept, sent = pair_gradients(
        place,
        row_pieces(seq_norm, proj_grads, 2),
        row_pieces(mix_ready, branch_grads, 0)
        + [(region_mix, 0, region_branch_grad, 0, region_rows)],
        model_width,
    )
    if two_owners:
        kept, sent, mix_taken, big_taken = tie(kept, sent, mix_taken, big_taken)
    small_kept.append(kept)
    small_taken += order.launch((sent, "win", 1))
    if two_owners:
        mixes += mix_taken
        mix_taken = order.launch(*[(piece, "win", 1) for piece in mixes])
    small_totals = [
        (kept + wide(taken)).reshape(-1, 2 * shard_rows, model_width)
        for kept, taken in zip(small_kept, order.land(small_taken))
    ]
    if two_owners:
        small_kept, hops = first_parts_of_two(small_totals)
        small_sent = [array for array, _, _ in hops]
        small_taken = order.launch(*hops)
        big_mom = jnp.where(first, big_moms[0], big_moms[1])
        big_mom = big_mom + add_far(big_kept, big_taken)
        big_low = bfloat(big_mom)
        big_taken = order.launch(*spread_far(big_low))
        mixes += mix_taken
        mixes = after(mixes, small_sent, big_low)
    else:
        mixes = gather_blocks(region_mix_grad)

    region_grad, region_weight_grad, region_sums = region_backward(
        place,
        regions,
        mixes,
        region_norm,
        region_proj,
        key_images,
        key_images.reshape(1, -1),
        region_new_grad,
        qkv_weight,
        vectors,
        2 * shard_rows,
    )

    def new_vector_rows(vec_sum):
        vec_total = lax.dynamic_slice_in_dim(
            vec_sum.reshape(-1), win_index * vec_rows, vec_rows
        )
        momentum = MOMENTUM_DECAY * vec_mom + vec_total
        old = lax.dynamic_slice_in_dim(vectors.reshape(-1), win_index * vec_rows, vec_rows)
        return momentum, old - VECTOR_RATE * momentum

    if two_owners:
        region_weight_grad, small_taken, big_taken = tie(region_weight_grad, small_taken, big_taken)
        def spread_pair(mine):
            mine = mine.reshape(2, shard_rows, model_width)
            kept, sent = pick_owner(low_core, mine[0], mine[1])
            taken = order.launch((sent, "win", 1), (kept, "rep", 1), (sent, ("win", "rep"), 3))
            return kept, taken

        rep_rows = jnp.stack(
            [
                jnp.where(low_core, region_weight_grad[0], region_weight_grad[1]),
                jnp.where(low_core, region_weight_grad[2], 0.0),
            ]
        )
        rep = lax.axis_index("rep")
        vec_mine = rounded(region_sums)
        small_kept, hops = second_parts(*add_pair(small_kept, small_taken))
        small_taken = order.launch(*hops)
        vec_taken = order.launch(
            (bfloat(jnp.concatenate([pick(rep_rows, 1 - rep), vec_mine])), "rep", 1)
        )
        small_landed = order.land(small_taken)
        big_pieces = [far_piece(big_low, after(big_taken, small_taken[0], *order.sent))]
        big_taken = order.launch((big_pieces[0], "win", 2))
        small_kept, hops = far_parts(join_halves(add_pair(small_kept, small_landed)))
        small_taken = order.launch(*hops)
        vec_taken = wide(vec_taken[0])
        region_rows_sum = pick(rep_rows, rep) + vec_taken[: 2 * shard_rows]
        vec_sum = vec_mine + vec_taken[2 * shard_rows :]
        big_pieces += order.land(big_taken)
        big_taken = order.launch(*[(piece, "win", 1) for piece in big_pieces])
        small_mom = add_far(small_kept, order.land(small_taken)) + region_rows_sum
        small_mom = small_pair_mom + small_mom
        small_low = bfloat(small_mom)
        small_taken = order.launch(*spread_far(small_low))
        input_grad = insert_regions(seq_grad, after(region_grad, *order.sent))
        vector_rows = new_vector_rows(vec_sum)
        small_taken, input_grad, vector_rows = tie(
            order.land(small_taken), input_grad, vector_rows
        )
        small_pieces = [far_piece(small_low, small_taken)]
        small_taken = order.launch((small_pieces[0], "win", 2))
        mom_parts = spread_pair(small_mom)
        other_mom = order.launch((big_mom, "rep", 1))[0]
        big_pieces += order.land(big_taken)
        big_mine = big_update(place, big_pieces, folds, gather_masks())

        other_update = order.launch((big_mine, "rep", 1))[0]
        small_pieces += order.land(small_taken)
        small_pieces, mom_parts, other_mom = tie(small_pieces, mom_parts, other_mom)
        small_mine = small_update(
            place, [piece[:, None] for piece in small_pieces], gather_masks(1)
        )[0]
        update_parts = spread_pair(small_mine)
        other_update = order.land(other_update)
        finish_place = jnp.concatenate([place, place[1:] & 1])
        big_parts = [big_mine, other_update, big_mom, other_mom]
        small_parts = [update_parts[0], *update_parts[1], mom_parts[0], *mom_parts[1]]
    else:
        input_grad = insert_regions(seq_grad, region_grad)
        big_total = pick(sum_everywhere(big_total), win_index >> 1, 1)
        folded_up_mom = big_moms[0] + big_total[0]
        new_down_mom = big_moms[1] + big_total[1]
        small_total = sum_everywhere(jnp.stack(small_totals))
        other = swap(bfloat(small_total), "win", 0)
        pairs = jnp.stack(pick_owner(low_core, bfloat(small_total), other), axis=1)
        pairs = pairs.reshape(4, -1, 2 * shard_rows, model_width)
        region_pairs = jnp.pad(region_weight_grad, ((0, 1), (0, 0), (0, 0)))
        vec_sum = region_sums
        for bit in range(bit_count("rep")):
            region_pairs = same_sum(region_pairs, "rep", bit)
            vec_sum = same_sum(vec_sum, "rep", bit)
        vector_rows = new_vector_rows(vec_sum)
        rows = wide(pick(pairs, win_index >> 1, 1)) + region_pairs
        rows = rows.reshape(4, 2, shard_rows, model_width)
        small_moms = small_old_moms + pick(rows, win_index & 1, 1)
        up_update, down_update, updates = every_update(
            place, (folded_up_mom, new_down_mom), small_moms, folds
        )
        finish_place = jnp.stack([0 * win_index, win_index, 0 * win_index]).astype(jnp.int32)
        big_parts = [up_update, down_update, folded_up_mom, new_down_mom]
        small_parts = [*updates, *small_moms]
    new_up, new_down, new_up_mom, new_down_mom = finish_big(
        finish_place, big_parts, up_weight, down_weight
    )
    new_qkv, new_out, new_qkv_mom, new_out_mom = finish_small(
        finish_place, after(small_parts, new_down), qkv_weight, out_weight
    )
    return (
        out_tokens,
        input_grad.reshape(tokens.shape),
        new_qkv_mom,
        new_qkv,
        new_out_mom,
        new_out,
        new_up_mom,
        new_up,
        new_down_mom,
        new_down,
        *vector_rows,
    )


def solution(mesh):
    placed = (
        P("rep", "win", None, None),
        P("rep", "win", None),
        P("rep", "win", None),
        P("rep", None),
        P(),
        P(),
        P(),
        P(),
        P(),
        P(None, "win", None),
        P("win", None),
        P("win", None),
        P("win", None),
        P("win"),
        P("rep", "win", None, None),
    )
    return jax.shard_map(
        local,
        mesh=mesh,
        in_specs=placed,
        out_specs=(
            P("rep", "win", None, None),
            P("rep", "win", None, None),
            P(None, "win", None),
            P(None, "win", None),
            P("win", None),
            P("win", None),
            P("win", None),
            P("win", None),
            P("win", None),
            P("win", None),
            P("win"),
            P("win"),
        ),
        check_vma=False,
    )
```
